32 devices in a mesh: seq: 8 (over y, x, core), chan: 4 (over z).
Axes of the slice: x: 2, y: 2, z: 4, core: 2. Of those that a mesh axis runs over, the one named last changes fastest.
Arguments:
- values_in: bfloat16 [1024, 4096], P('seq', 'chan'), may hold values from -6 to 6
- gate_values: bfloat16 [1024, 4096], P('seq', 'chan'), may hold values from -6 to 6
- filter_spectrum: float32 [2, 16, 128, 4096], P(None, 'seq', None, 'chan'), may hold values from -6 to 6
- skip_gain: float32 [4096], P('chan'), may hold values from -4 to 4
- out_weight: bfloat16 [4096, 4096], P('chan', 'seq'), may hold values from -0.09375 to 0.09375
Outputs:
- mixed: bfloat16 [1024, 4096], P('seq', 'chan')
The draws below stay inside these ranges and needn't reach their ends.
All inputs are finite; a program needn't handle non-finite values.
Results may differ from the reference program's by a relative error of at most 0.009.
Values may be sent and summed in bfloat16 or wider, within the bound.
No kernel may reach another device: no remote copies, remote signals or barrier semaphores. Data moves between devices by JAX's collectives and lax.ppermute only.
A program may use at most 64 MiB of HBM per device.

```python
import jax
import jax.numpy as jnp
import numpy as np
from jax import lax

D = 4096
LD = 128
SEQ_LEN = 1024
N_SEQ = 8
N_CHAN = 4


def level_of(rng, shape, cuts, smallest, top_value):
    def one(dim, blocks):
        heights = jax.random.uniform(jax.random.fold_in(jax.random.fold_in(rng, 6), dim), (blocks,), jnp.float32, smallest / len(cuts), top_value / len(cuts))
        return jnp.repeat(jnp.exp(heights), shape[dim] // blocks).reshape((-1,) + (1,) * (len(shape) - dim - 1))

    factor_of = one(*cuts[0])
    for cut in cuts[1:]:
        factor_of = factor_of * one(*cut)
    return factor_of


def noise(own_key, dims, deviation, bound, shards=(), kind=jnp.bfloat16):
    factor_of = level_of(own_key, dims, shards, -0.22, 0.18) if shards else 1.0
    values = jax.random.normal(own_key, dims, jnp.float32) * deviation * factor_of
    return jnp.minimum(jnp.maximum(values, -bound), bound).astype(kind)


def setup_inputs(seed: int = 0) -> dict:
    seeds = jax.random.split(jax.random.key(seed), 6)
    return {
        "values_in": noise(seeds[0], (SEQ_LEN, D), 1.0, 6.0, ((0, 8), (1, 4))),
        "gate_values": noise(seeds[1], (SEQ_LEN, D), 1.0, 6.0, ((0, 8), (1, 4))),
        "filter_spectrum": noise(seeds[2], (2, 2 * N_SEQ, LD, D), 1.0, 6.0, ((1, 8), (3, 4)), jnp.float32),
        "skip_gain": noise(seeds[3], (D,), 1.0, 4.0, ((0, 4),), jnp.float32),
        "out_weight": noise(seeds[4], (D, D), D ** -0.5, 0.09375, ((0, 4), (1, 8))),
    }


def frequency_order(count_rows, width_bits):
    row_index = np.arange(count_rows)
    halves = row_index // 2
    flipped = halves * 0
    for bit_place in range(width_bits):
        flipped = flipped + ((halves >> bit_place) & 1) * (1 << (width_bits - 1 - bit_place))
    return 2 * flipped + row_index % 2


def reference(values_in, gate_values, filter_spectrum, skip_gain, out_weight):
    seq_len = LD * N_SEQ
    width_bits = N_SEQ.bit_length() - 1
    row_order = frequency_order(2 * N_SEQ, width_bits)
    natural = filter_spectrum[:, row_order]
    natural = jnp.transpose(natural, (0, 2, 1, 3)).reshape(2, 2 * seq_len, D)
    signal = values_in.astype(jnp.float32)
    block_width = min(D, 512)
    blocks = D // block_width

    def split_blocks(array, length):
        return jnp.transpose(array.reshape(length, blocks, block_width), (1, 0, 2))

    def convolve(block_items):
        block_signal, block_real, block_imag = block_items
        padded = jnp.concatenate([block_signal, jnp.zeros_like(block_signal)], axis=0)
        spectrum = jnp.fft.fft(padded, axis=0)
        product = spectrum * lax.complex(block_real, block_imag)
        return jnp.real(jnp.fft.ifft(product, axis=0))[:seq_len]

    pieces = lax.map(convolve, (split_blocks(signal, seq_len), split_blocks(natural[0], 2 * seq_len), split_blocks(natural[1], 2 * seq_len)))
    convolved = jnp.transpose(pieces, (1, 0, 2)).reshape(seq_len, D)
    gated = (gate_values.astype(jnp.float32) * (convolved + skip_gain * signal)).astype(jnp.bfloat16)
    share_cols = D // N_CHAN

    def accumulate(index, total_sum):
        start = (index * share_cols).astype(jnp.int32)
        rows_part = lax.dynamic_slice_in_dim(gated, start, share_cols, 1)
        weight_part = lax.dynamic_slice_in_dim(out_weight, start, share_cols, 0)
        partial_value = jnp.dot(rows_part, weight_part, preferred_element_type=jnp.float32).astype(jnp.bfloat16)
        partial_value = lax.optimization_barrier(partial_value)
        return total_sum + partial_value.astype(jnp.float32)

    mixed = lax.fori_loop(0, N_CHAN, accumulate, jnp.zeros((seq_len, D), jnp.float32))
    return mixed.astype(jnp.bfloat16)
```

```python
import functools

import jax
import jax.numpy as jnp
import numpy as np
from jax import lax
from jax.experimental import pallas as pl
from jax.experimental.pallas import tpu as pltpu
from jax.sharding import PartitionSpec as P

BF16 = jnp.bfloat16
F32 = jnp.float32


def bit_reversed(number, width_bits):
    flipped = 0
    for bit_place in range(width_bits):
        flipped |= (number >> bit_place & 1) << (width_bits - 1 - bit_place)
    return flipped


def filter_row(residue, width_bits):
    return 2 * bit_reversed(residue // 2, width_bits) + residue % 2


def dft_tables(parts, rows):
    total = 2 * parts * rows
    residue = np.arange(2 * parts)[:, None, None]
    column = np.arange(rows)[None, :, None]
    position = np.arange(rows)[None, None, :]
    phase = 2.0 * np.pi * (position * (residue + 2 * parts * column) % total) / total
    cos, sin = np.cos(phase), np.sin(phase)
    forward = np.concatenate(
        [np.concatenate([cos, sin], axis=2), np.concatenate([-sin, cos], axis=2)], axis=1
    )
    inverse = np.transpose(forward, (0, 2, 1)) / total
    return forward.astype(BF16), inverse.astype(BF16)


def convolve_kernel(parts, rows, moved_ref, skip_ref, forward_ref, inverse_ref, out_ref, waves_ref, back_ref):
    width_bits = parts.bit_length() - 1
    chunk = 16

    def cosine(residue, block):
        return float(np.cos(np.pi * residue * block / parts))

    def sine(residue, block):
        return float(np.sin(np.pi * residue * block / parts))

    def spread(index, carry):
        here = pl.ds(index * chunk, chunk)
        there = pl.ds(rows + index * chunk, chunk)
        blocks = [moved_ref[block, here, :].astype(F32) for block in range(parts)]
        for residue in range(parts + 1):
            real = blocks[0]
            imag = jnp.zeros_like(real)
            for block in range(1, parts):
                real = real + cosine(residue, block) * blocks[block]
                imag = imag - sine(residue, block) * blocks[block]
            waves_ref[residue, here, :] = real.astype(BF16)
            waves_ref[residue, there, :] = imag.astype(BF16)
            if 0 < residue < parts:
                waves_ref[2 * parts - residue, here, :] = real.astype(BF16)
                waves_ref[2 * parts - residue, there, :] = (-imag).astype(BF16)
        return carry

    lax.fori_loop(0, rows // chunk, spread, 0)

    def through(residue):
        wave = jnp.dot(forward_ref[residue], waves_ref[residue], preferred_element_type=F32)
        source, odd = divmod(filter_row(residue, width_bits), 2)
        filter_real = moved_ref[source, pl.ds((2 + odd) * rows, rows), :].astype(F32)
        filter_imag = moved_ref[source, pl.ds((4 + odd) * rows, rows), :].astype(F32)
        real, imag = wave[:rows], wave[rows:]
        product = jnp.concatenate(
            [real * filter_real - imag * filter_imag, real * filter_imag + imag * filter_real], axis=0
        )
        return jnp.dot(inverse_ref[residue], product.astype(BF16), preferred_element_type=F32)

    for residue in range(parts + 1):
        back = through(residue)
        if 0 < residue < parts:
            other = through(2 * parts - residue)
            back_ref[residue, pl.ds(0, rows), :] = back[:rows] + other[:rows]
            back_ref[residue, pl.ds(rows, rows), :] = back[rows:] - other[rows:]
        else:
            back_ref[residue] = back

    skip = skip_ref[...]

    def gather(index, carry):
        here = pl.ds(index * chunk, chunk)
        there = pl.ds(rows + index * chunk, chunk)
        reals = [back_ref[residue, here, :] for residue in range(parts + 1)]
        imags = [back_ref[residue, there, :] for residue in range(parts + 1)]
        for block in range(parts):
            total = reals[0]
            for residue in range(1, parts + 1):
                total = total + cosine(residue, block) * reals[residue]
                if residue < parts and block:
                    total = total - sine(residue, block) * imags[residue]
            signal = moved_ref[block, here, :].astype(F32)
            gate = moved_ref[block, pl.ds(rows + index * chunk, chunk), :].astype(F32)
            out_ref[block, here, :] = (gate * (total + skip * signal)).astype(BF16)
        return carry

    lax.fori_loop(0, rows // chunk, gather, 0)


def convolve(moved, skip):
    parts, stacked, width = moved.shape
    rows = stacked // 6
    forward, inverse = dft_tables(parts, rows)
    whole = pl.BlockSpec(memory_space=pltpu.VMEM)
    return pl.pallas_call(
        functools.partial(convolve_kernel, parts, rows),
        out_shape=jax.ShapeDtypeStruct((parts, rows, width), BF16),
        in_specs=[whole] * 4,
        out_specs=whole,
        scratch_shapes=[
            pltpu.VMEM((2 * parts, 2 * rows, width), BF16),
            pltpu.VMEM((parts + 1, 2 * rows, width), F32),
        ],
        compiler_params=pltpu.CompilerParams(vmem_limit_bytes=40 * 2**20),
    )(moved, skip[None, :], forward, inverse)


def shards(values_in, gate_values, filter_spectrum, skip_gain, out_weight):
    parts = lax.axis_size("seq")
    layers = lax.axis_size("chan")
    rows, width = values_in.shape
    lanes = width // parts
    device = lax.axis_index("seq")

    def by_channel(array):
        return jnp.transpose(array.reshape(array.shape[0], parts, lanes), (1, 0, 2))

    filters = filter_spectrum.astype(BF16).reshape(4 * rows, width)
    packed = jnp.concatenate([by_channel(values_in), by_channel(gate_values), by_channel(filters)], axis=1)
    moved = lax.all_to_all(packed, "seq", 0, 0)
    skip = lax.dynamic_slice_in_dim(skip_gain, device * lanes, lanes)
    gated = convolve(moved, skip)
    gathered = lax.all_gather(gated.reshape(parts * rows, lanes), "seq", axis=1, tiled=True)

    own_cols = out_weight.shape[1]
    share = own_cols * parts // layers // parts
    per_block = parts // layers
    pieces = own_cols // share
    group = device % per_block
    member = device // per_block
    weight = jnp.zeros_like(out_weight)
    for step in range(pieces):
        piece = (member + step) % pieces
        sent = lax.dynamic_slice_in_dim(out_weight, piece * share, share, 1)
        pairs = [
            (source, source % per_block * pieces + (source // per_block + step) % pieces) for source in range(parts)
        ]
        arrived = lax.ppermute(sent, "seq", pairs)
        block = (device % pieces - step) % pieces
        weight = lax.dynamic_update_slice_in_dim(weight, arrived, block * share, 1)
    partials = jnp.dot(gathered, weight, preferred_element_type=F32).astype(BF16)
    mixed = lax.psum_scatter(partials, "chan", scatter_dimension=1, tiled=True)
    return lax.all_to_all(mixed, "seq", 0, 1, tiled=True)


def solution(mesh):
    in_specs = (
        P("seq", "chan"),
        P("seq", "chan"),
        P(None, "seq", None, "chan"),
        P("chan"),
        P("chan", "seq"),
    )
    out_specs = P("seq", "chan")
    return jax.shard_map(shards, mesh=mesh, in_specs=in_specs, out_specs=out_specs, check_vma=False)
```

```python
import functools

import jax
import jax.numpy as jnp
import numpy as np
from jax import lax
from jax.experimental import pallas as pl
from jax.experimental.pallas import tpu as pltpu
from jax.sharding import PartitionSpec as P

BF16 = jnp.bfloat16
F32 = jnp.float32


def bit_reversed(number, width_bits):
    flipped = 0
    for bit_place in range(width_bits):
        flipped |= (number >> bit_place & 1) << (width_bits - 1 - bit_place)
    return flipped


def filter_row(residue, width_bits):
    return 2 * bit_reversed(residue // 2, width_bits) + residue % 2


def dft_tables(parts, rows):
    total = 2 * parts * rows
    residue = np.arange(2 * parts)[:, None, None]
    column = np.arange(rows)[None, :, None]
    position = np.arange(rows)[None, None, :]
    phase = 2.0 * np.pi * (position * (residue + 2 * parts * column) % total) / total
    cos, sin = np.cos(phase), np.sin(phase)
    forward = np.concatenate(
        [np.concatenate([cos, sin], axis=2), np.concatenate([-sin, cos], axis=2)], axis=1
    )
    inverse = np.transpose(forward, (0, 2, 1)) / total
    return forward.astype(BF16), inverse.astype(BF16)


def convolve_kernel(parts, rows, moved_ref, skip_ref, forward_ref, inverse_ref, out_ref, waves_ref, back_ref):
    width_bits = parts.bit_length() - 1
    chunk = 16

    def cosine(residue, block):
        return float(np.cos(np.pi * residue * block / parts))

    def sine(residue, block):
        return float(np.sin(np.pi * residue * block / parts))

    def spread(index, carry):
        here = pl.ds(index * chunk, chunk)
        there = pl.ds(rows + index * chunk, chunk)
        blocks = [moved_ref[block, here, :].astype(F32) for block in range(parts)]
        for residue in range(parts + 1):
            real = blocks[0]
            imag = jnp.zeros_like(real)
            for block in range(1, parts):
                real = real + cosine(residue, block) * blocks[block]
                imag = imag - sine(residue, block) * blocks[block]
            waves_ref[residue, here, :] = real.astype(BF16)
            waves_ref[residue, there, :] = imag.astype(BF16)
            if 0 < residue < parts:
                waves_ref[2 * parts - residue, here, :] = real.astype(BF16)
                waves_ref[2 * parts - residue, there, :] = (-imag).astype(BF16)
        return carry

    lax.fori_loop(0, rows // chunk, spread, 0)

    def through(residue):
        wave = jnp.dot(forward_ref[residue], waves_ref[residue], preferred_element_type=F32)
        source, odd = divmod(filter_row(residue, width_bits), 2)
        filter_real = moved_ref[source, pl.ds((2 + odd) * rows, rows), :].astype(F32)
        filter_imag = moved_ref[source, pl.ds((4 + odd) * rows, rows), :].astype(F32)
        real, imag = wave[:rows], wave[rows:]
        product = jnp.concatenate(
            [real * filter_real - imag * filter_imag, real * filter_imag + imag * filter_real], axis=0
        )
        return jnp.dot(inverse_ref[residue], product.astype(BF16), preferred_element_type=F32)

    for residue in range(parts + 1):
        back = through(residue)
        if 0 < residue < parts:
            other = through(2 * parts - residue)
            back_ref[residue, pl.ds(0, rows), :] = back[:rows] + other[:rows]
            back_ref[residue, pl.ds(rows, rows), :] = back[rows:] - other[rows:]
        else:
            back_ref[residue] = back

    skip = skip_ref[...]

    def gather(index, carry):
        here = pl.ds(index * chunk, chunk)
        there = pl.ds(rows + index * chunk, chunk)
        reals = [back_ref[residue, here, :] for residue in range(parts + 1)]
        imags = [back_ref[residue, there, :] for residue in range(parts + 1)]
        for block in range(parts):
            total = reals[0]
            for residue in range(1, parts + 1):
                total = total + cosine(residue, block) * reals[residue]
                if residue < parts and block:
                    total = total - sine(residue, block) * imags[residue]
            signal = moved_ref[block, here, :].astype(F32)
            gate = moved_ref[block, pl.ds(rows + index * chunk, chunk), :].astype(F32)
            out_ref[block, here, :] = (gate * (total + skip * signal)).astype(BF16)
        return carry

    lax.fori_loop(0, rows // chunk, gather, 0)


def convolve(moved, skip):
    parts, stacked, width = moved.shape
    rows = stacked // 6
    forward, inverse = dft_tables(parts, rows)
    whole = pl.BlockSpec(memory_space=pltpu.VMEM)
    return pl.pallas_call(
        functools.partial(convolve_kernel, parts, rows),
        out_shape=jax.ShapeDtypeStruct((parts, rows, width), BF16),
        in_specs=[whole] * 4,
        out_specs=whole,
        scratch_shapes=[
            pltpu.VMEM((2 * parts, 2 * rows, width), BF16),
            pltpu.VMEM((parts + 1, 2 * rows, width), F32),
        ],
        compiler_params=pltpu.CompilerParams(vmem_limit_bytes=40 * 2**20),
    )(moved, skip[None, :], forward, inverse)


def shards_general(values_in, gate_values, filter_spectrum, skip_gain, out_weight):
    parts = lax.axis_size("seq")
    layers = lax.axis_size("chan")
    rows, width = values_in.shape
    lanes = width // parts
    device = lax.axis_index("seq")

    def by_channel(array):
        return jnp.transpose(array.reshape(array.shape[0], parts, lanes), (1, 0, 2))

    filters = filter_spectrum.astype(BF16).reshape(4 * rows, width)
    packed = jnp.concatenate([by_channel(values_in), by_channel(gate_values), by_channel(filters)], axis=1)
    moved = lax.all_to_all(packed, "seq", 0, 0)
    skip = lax.dynamic_slice_in_dim(skip_gain, device * lanes, lanes)
    gated = convolve(moved, skip)
    gathered = lax.all_gather(gated.reshape(parts * rows, lanes), "seq", axis=1, tiled=True)

    own_cols = out_weight.shape[1]
    share = own_cols * parts // layers // parts
    per_block = parts // layers
    pieces = own_cols // share
    group = device % per_block
    member = device // per_block
    weight = jnp.zeros_like(out_weight)
    for step in range(pieces):
        piece = (member + step) % pieces
        sent = lax.dynamic_slice_in_dim(out_weight, piece * share, share, 1)
        pairs = [
            (source, source % per_block * pieces + (source // per_block + step) % pieces) for source in range(parts)
        ]
        arrived = lax.ppermute(sent, "seq", pairs)
        block = (device % pieces - step) % pieces
        weight = lax.dynamic_update_slice_in_dim(weight, arrived, block * share, 1)
    partials = jnp.dot(gathered, weight, preferred_element_type=F32).astype(BF16)
    mixed = lax.psum_scatter(partials, "chan", scatter_dimension=1, tiled=True)
    return lax.all_to_all(mixed, "seq", 0, 1, tiled=True)


def small_tables(parts, rows):
    total = 2 * parts * rows
    index = np.arange(rows)
    phase = 2.0 * np.pi * (index[:, None] * index[None, :] % rows) / rows
    cos, sin = np.cos(phase), np.sin(phase)
    forward = np.block([[cos, sin], [-sin, cos]])
    turn = 2.0 * np.pi * (index[:, None] * np.arange(2 * parts)[None, :]) / total
    return forward.astype(BF16), forward.T.astype(BF16), np.cos(turn).astype(F32), np.sin(turn).astype(F32)


def cosine(parts, residue, block):
    return float(np.cos(np.pi * residue * block / parts))


def sine(parts, residue, block):
    return float(np.sin(np.pi * residue * block / parts))


def weighted(terms):
    total = None
    for factor, term in terms:
        if abs(factor) < 1e-12:
            continue
        part = term if factor == 1.0 else factor * term
        total = part if total is None else total + part
    return total


def plus(left, right):
    return left if right is None else right if left is None else left + right


def minus(left, right):
    return left if right is None else -right if left is None else left - right


def pack_filters_kernel(parts, lanes, device_ref, filter_ref, *out_refs):
    for offset in range(parts):
        start = pl.multiple_of((device_ref[0] ^ offset) * lanes, lanes)
        out_refs[offset][0] = filter_ref[0, :, pl.ds(start, lanes)].astype(BF16)


def pack_filters(device, filters):
    planes, rows, width = filters.shape
    parts = lax.axis_size("seq")
    lanes = width // parts
    return pl.pallas_call(
        functools.partial(pack_filters_kernel, parts, lanes),
        grid=(planes,),
        in_specs=[
            pl.BlockSpec(memory_space=pltpu.SMEM),
            pl.BlockSpec((1, rows, width), lambda plane: (plane, 0, 0)),
        ],
        out_specs=[pl.BlockSpec((1, rows, lanes), lambda plane: (plane, 0, 0))] * parts,
        out_shape=[jax.ShapeDtypeStruct((planes, rows, lanes), BF16)] * parts,
        name="pack_filters",
    )(device, filters)


def pack_signals_kernel(parts, lanes, device_ref, values_ref, gate_ref, *out_refs):
    for offset in range(parts):
        start = pl.multiple_of((device_ref[0] ^ offset) * lanes, lanes)
        out_refs[offset][0] = values_ref[:, pl.ds(start, lanes)]
        out_refs[offset][1] = gate_ref[:, pl.ds(start, lanes)]


def pack_signals(device, values_in, gate_values):
    rows, width = values_in.shape
    parts = lax.axis_size("seq")
    lanes = width // parts
    return pl.pallas_call(
        functools.partial(pack_signals_kernel, parts, lanes),
        in_specs=[pl.BlockSpec(memory_space=pltpu.SMEM)] + [pl.BlockSpec(memory_space=pltpu.VMEM)] * 2,
        out_specs=[pl.BlockSpec(memory_space=pltpu.VMEM)] * parts,
        out_shape=[jax.ShapeDtypeStruct((2, rows, lanes), BF16)] * parts,
        name="pack_signals",
    )(device, values_in, gate_values)


def forward_kernel(parts, rows, lanes, device_ref, cos_ref, sin_ref, table_ref, *refs):
    signal_refs, out_ref, signal_ref, waves_ref = refs[:parts], refs[parts], refs[parts + 1], refs[parts + 2]
    chunk = 16
    for offset in range(parts):
        signal_ref[device_ref[0] ^ offset] = signal_refs[offset][0]

    def spread(index, carry):
        here = pl.ds(pl.multiple_of(index * chunk, chunk), chunk)
        there = pl.ds(pl.multiple_of(rows + index * chunk, chunk), chunk)
        cos_all, sin_all = cos_ref[here, :], sin_ref[here, :]
        blocks = [signal_ref[block, here, :].astype(F32) for block in range(parts)]

        def store(residue, real, imag):
            if residue:
                cos, sin = cos_all[:, residue : residue + 1], sin_all[:, residue : residue + 1]
                if imag is None:
                    real, imag = real * cos, -(real * sin)
                else:
                    real, imag = real * cos + imag * sin, imag * cos - real * sin
            if imag is None:
                imag = jnp.zeros_like(real)
            columns = pl.ds(residue * lanes, lanes)
            waves_ref[here, columns] = real.astype(BF16)
            waves_ref[there, columns] = imag.astype(BF16)

        def store_both(residue, real, imag):
            store(residue, real, imag)
            if 0 < residue < parts:
                store(2 * parts - residue, real, None if imag is None else -imag)

        for residue in range(parts // 2 + 1):
            even = range(0, parts, 2)
            odd = range(1, parts, 2)
            cos_even = weighted([(cosine(parts, residue, block), blocks[block]) for block in even])
            cos_odd = weighted([(cosine(parts, residue, block), blocks[block]) for block in odd])
            sin_even = weighted([(sine(parts, residue, block), blocks[block]) for block in even])
            sin_odd = weighted([(sine(parts, residue, block), blocks[block]) for block in odd])
            sin_sum = plus(sin_even, sin_odd)
            store_both(residue, plus(cos_even, cos_odd), None if sin_sum is None else -sin_sum)
            if 2 * residue != parts:
                store_both(parts - residue, minus(cos_even, cos_odd), minus(sin_even, sin_odd))
        return carry

    lax.fori_loop(0, rows // chunk, spread, 0)
    for pair in range(parts):
        columns = pl.ds(2 * pair * lanes, 2 * lanes)
        out_ref[:, columns] = jnp.dot(table_ref[...], waves_ref[:, columns], preferred_element_type=F32)


def forward(device, signals, tables):
    parts = len(signals)
    rows, lanes = signals[0].shape[1:]
    forward_table, _, cos, sin = tables
    whole = pl.BlockSpec(memory_space=pltpu.VMEM)
    return pl.pallas_call(
        functools.partial(forward_kernel, parts, rows, lanes),
        in_specs=[pl.BlockSpec(memory_space=pltpu.SMEM)] + [whole] * (3 + parts),
        out_specs=whole,
        out_shape=jax.ShapeDtypeStruct((2 * rows, 2 * parts * lanes), F32),
        scratch_shapes=[
            pltpu.VMEM((parts, rows, lanes), BF16),
            pltpu.VMEM((2 * rows, 2 * parts * lanes), BF16),
        ],
        compiler_params=pltpu.CompilerParams(vmem_limit_bytes=32 * 2**20),
        name="forward",
    )(device, cos, sin, forward_table, *signals)


def backward_kernel(parts, rows, lanes, device_ref, cos_ref, sin_ref, table_ref, spectrum_ref, skip_ref, *refs):
    signal_refs, filter_refs = refs[:parts], refs[parts : 2 * parts]
    mine_ref, other_ref, signal_ref, filter_ref, product_ref, back_ref, gated_ref = refs[2 * parts :]
    width_bits = parts.bit_length() - 1
    chunk = 16
    device = device_ref[0]
    for offset in range(parts):
        signal_ref[device ^ offset] = signal_refs[offset][...]
        filter_ref[device ^ offset] = filter_refs[offset][...]

    for residue in range(2 * parts):
        source, odd = divmod(filter_row(residue, width_bits), 2)
        columns = pl.ds(residue * lanes, lanes)
        filter_real = filter_ref[source, odd].astype(F32)
        filter_imag = filter_ref[source, 2 + odd].astype(F32)
        real = spectrum_ref[pl.ds(0, rows), columns]
        imag = spectrum_ref[pl.ds(rows, rows), columns]
        product_ref[pl.ds(0, rows), columns] = (real * filter_real - imag * filter_imag).astype(BF16)
        product_ref[pl.ds(rows, rows), columns] = (real * filter_imag + imag * filter_real).astype(BF16)
        if residue % 2:
            columns = pl.ds((residue - 1) * lanes, 2 * lanes)
            back_ref[:, columns] = jnp.dot(table_ref[...], product_ref[:, columns], preferred_element_type=F32)

    skip = skip_ref[...]
    scale = 1.0 / (2 * parts * rows)

    def gather(index, carry):
        here = pl.ds(pl.multiple_of(index * chunk, chunk), chunk)
        there = pl.ds(pl.multiple_of(rows + index * chunk, chunk), chunk)
        cos_all, sin_all = cos_ref[here, :] * scale, sin_ref[here, :] * scale

        def turned(residue):
            columns = pl.ds(residue * lanes, lanes)
            real, imag = back_ref[here, columns], back_ref[there, columns]
            if not residue:
                return real * scale, None
            cos, sin = cos_all[:, residue : residue + 1], sin_all[:, residue : residue + 1]
            return real * cos - imag * sin, real * sin + imag * cos

        reals, imags = [], []
        for residue in range(parts + 1):
            real, imag = turned(residue)
            if 0 < residue < parts:
                other_real, other_imag = turned(2 * parts - residue)
                real, imag = real + other_real, imag - other_imag
            reals.append(real)
            imags.append(imag)

        def store(block, total):
            signal = signal_ref[block, 0, here, :].astype(F32)
            gate = signal_ref[block, 1, here, :].astype(F32)
            gated_ref[block, here, :] = (gate * (total + skip * signal)).astype(BF16)

        for block in range(parts // 2 + 1):
            even = range(0, parts + 1, 2)
            odd = range(1, parts + 1, 2)
            cos_even = weighted([(cosine(parts, residue, block), reals[residue]) for residue in even])
            cos_odd = weighted([(cosine(parts, residue, block), reals[residue]) for residue in odd])
            sin_even = weighted([(sine(parts, residue, block), imags[residue]) for residue in even])
            sin_odd = weighted([(sine(parts, residue, block), imags[residue]) for residue in odd])
            store(block, minus(plus(cos_even, cos_odd), plus(sin_even, sin_odd)))
            if 0 < block and 2 * block != parts:
                store(parts - block, plus(minus(cos_even, cos_odd), minus(sin_even, sin_odd)))
        return carry

    lax.fori_loop(0, rows // chunk, gather, 0)
    for chip in range(parts // 2):
        mine_ref[chip] = gated_ref[2 * chip + device % 2]
        other_ref[chip] = gated_ref[2 * chip + 1 - device % 2]


def backward(device, spectrum, skip, signals, filters, tables):
    parts = len(signals)
    rows, lanes = signals[0].shape[1:]
    _, inverse_table, cos, sin = tables
    whole = pl.BlockSpec(memory_space=pltpu.VMEM)
    return pl.pallas_call(
        functools.partial(backward_kernel, parts, rows, lanes),
        in_specs=[pl.BlockSpec(memory_space=pltpu.SMEM)] + [whole] * (5 + 2 * parts),
        out_specs=[whole] * 2,
        out_shape=[jax.ShapeDtypeStruct((parts // 2, rows, lanes), BF16)] * 2,
        scratch_shapes=[
            pltpu.VMEM((parts, 2, rows, lanes), BF16),
            pltpu.VMEM((parts, 4, rows, lanes), BF16),
            pltpu.VMEM((2 * rows, 2 * parts * lanes), BF16),
            pltpu.VMEM((2 * rows, 2 * parts * lanes), F32),
            pltpu.VMEM((parts, rows, lanes), BF16),
        ],
        compiler_params=pltpu.CompilerParams(vmem_limit_bytes=40 * 2**20),
        name="backward",
    )(device, cos, sin, inverse_table, spectrum, skip, *signals, *filters)


def arrange_kernel(layers, share, place_ref, *refs):
    own_refs, other_refs, out_ref = refs[:layers], refs[layers : 2 * layers], refs[2 * layers]
    device, layer = place_ref[0], place_ref[1]
    own_start = pl.multiple_of(device % 2 * share, share)
    other_start = pl.multiple_of((1 - device % 2) * share, share)
    for step in range(layers):
        target = device % layers ^ layer ^ step
        out_ref[target, :, pl.ds(own_start, share)] = own_refs[step][...]
        out_ref[target, :, pl.ds(other_start, share)] = other_refs[step ^ 1][...]


def arrange(place, own, other):
    layers = len(own)
    rows, share = own[0].shape
    whole = pl.BlockSpec(memory_space=pltpu.VMEM)
    return pl.pallas_call(
        functools.partial(arrange_kernel, layers, share),
        in_specs=[pl.BlockSpec(memory_space=pltpu.SMEM)] + [whole] * (2 * layers),
        out_specs=whole,
        out_shape=jax.ShapeDtypeStruct((layers, rows, 2 * share), BF16),
        compiler_params=pltpu.CompilerParams(vmem_limit_bytes=32 * 2**20),
        name="arrange_weights",
    )(place, *own, *other)


def project_kernel(parts, layers, place_ref, weight_ref, *refs):
    gated_refs, out_refs, joined_ref = refs[:parts], refs[parts : parts + layers], refs[parts + layers]
    lanes = gated_refs[0].shape[1]
    for offset in range(parts):
        start = pl.multiple_of((place_ref[0] ^ offset) * lanes, lanes)
        joined_ref[:, pl.ds(start, lanes)] = gated_refs[offset][...]
    for target in reversed(range(layers)):
        out_refs[target][...] = jnp.dot(joined_ref[...], weight_ref[target], preferred_element_type=F32).astype(BF16)


def project(place, weight, gated):
    parts = len(gated)
    layers, depth, columns = weight.shape
    rows = gated[0].shape[0]
    whole = pl.BlockSpec(memory_space=pltpu.VMEM)
    return pl.pallas_call(
        functools.partial(project_kernel, parts, layers),
        in_specs=[pl.BlockSpec(memory_space=pltpu.SMEM)] + [whole] * (1 + parts),
        out_specs=[whole] * layers,
        out_shape=[jax.ShapeDtypeStruct((rows, columns), BF16)] * layers,
        scratch_shapes=[pltpu.VMEM((rows, depth), BF16)],
        compiler_params=pltpu.CompilerParams(vmem_limit_bytes=32 * 2**20),
        name="project",
    )(place, weight, *gated)


def add_kernel(chips, place_ref, *refs):
    in_refs, out_refs = refs[:-chips], refs[-chips:]
    rows = out_refs[0].shape[0]
    for offset in range(chips):
        start = pl.multiple_of((place_ref[0] // 2 ^ offset) * rows, rows)
        here = pl.ds(start, rows)
        total = in_refs[0][here, :].astype(F32)
        for in_ref in in_refs[1:]:
            total = total + in_ref[here, :].astype(F32)
        out_refs[offset][...] = total.astype(BF16)


def add_partials(place, partials, chips):
    rows, columns = partials[0].shape
    whole = pl.BlockSpec(memory_space=pltpu.VMEM)
    return pl.pallas_call(
        functools.partial(add_kernel, chips),
        in_specs=[pl.BlockSpec(memory_space=pltpu.SMEM)] + [whole] * len(partials),
        out_specs=[whole] * chips,
        out_shape=[jax.ShapeDtypeStruct((rows // chips, columns), BF16)] * chips,
        name="add_partials",
    )(place, *partials)


def join_kernel(chips, place_ref, *refs):
    in_refs, out_ref = refs[:chips], refs[chips]
    columns = in_refs[0].shape[1]
    for offset in range(chips):
        start = pl.multiple_of((place_ref[0] // 2 ^ offset) * columns, columns)
        out_ref[:, pl.ds(start, columns)] = in_refs[offset][...]


def join(place, blocks):
    chips = len(blocks)
    rows, columns = blocks[0].shape
    whole = pl.BlockSpec(memory_space=pltpu.VMEM)
    return pl.pallas_call(
        functools.partial(join_kernel, chips),
        in_specs=[pl.BlockSpec(memory_space=pltpu.SMEM)] + [whole] * chips,
        out_specs=whole,
        out_shape=jax.ShapeDtypeStruct((rows, chips * columns), BF16),
        name="join",
    )(place, *blocks)


def swapped(value, axis, offset):
    if not offset:
        return value
    return lax.ppermute(value, axis, [(source, source ^ offset) for source in range(lax.axis_size(axis))])


def shards_direct(values_in, gate_values, filter_spectrum, skip_gain, out_weight):
    parts = lax.axis_size("seq")
    layers = lax.axis_size("chan")
    chips = parts // 2
    rows, width = values_in.shape
    lanes = width // parts
    device = lax.axis_index("seq")
    place = jnp.stack([device, lax.axis_index("chan")])
    tables = small_tables(parts, rows)
    offsets = range(parts)

    signals = [swapped(block, "seq", offset) for offset, block in enumerate(pack_signals(place, values_in, gate_values))]
    filters = pack_filters(place, filter_spectrum.reshape(4, rows, width))
    filters = [swapped(block, "seq", offset) for offset, block in enumerate(filters)]

    share = out_weight.shape[1] // layers
    own_weight = []
    for step in range(layers):
        sent = lax.dynamic_slice_in_dim(out_weight, (device // 2 ^ step) * share, share, 1)
        pairs = [(source, source % 2 * layers + (source // 2 ^ step)) for source in range(parts)]
        own_weight.append(lax.ppermute(sent, "seq", pairs))
    other_weight = [swapped(block, "seq", 1) for block in own_weight]
    weight = arrange(place, own_weight, other_weight)

    skip = lax.dynamic_slice_in_dim(skip_gain, device * lanes, lanes)[None, :]
    spectrum = forward(place, signals, tables)
    mine, other = backward(place, spectrum, skip, signals, filters, tables)
    gated = [swapped(other if offset % 2 else mine, "seq", offset) for offset in offsets]
    gated = [block.reshape(chips * rows, lanes) for block in gated]
    partials = project(place, weight, gated)
    partials = [swapped(block, "chan", offset) for offset, block in enumerate(partials)]
    blocks = add_partials(place, partials, chips)
    blocks = [swapped(block, "seq", 2 * offset) for offset, block in enumerate(blocks)]
    return join(place, blocks)


def shards(values_in, gate_values, filter_spectrum, skip_gain, out_weight):
    parts = lax.axis_size("seq")
    layers = lax.axis_size("chan")
    lanes = values_in.shape[1] // parts
    share = out_weight.shape[1] // layers
    aligned = lanes % 128 == 0 and share % 128 == 0 and values_in.shape[0] % 16 == 0
    run = shards_direct if aligned and parts == 2 * layers else shards_general
    return run(values_in, gate_values, filter_spectrum, skip_gain, out_weight)


def solution(mesh):
    in_specs = (
        P("seq", "chan"),
        P("seq", "chan"),
        P(None, "seq", None, "chan"),
        P("chan"),
        P("chan", "seq"),
    )
    out_specs = P("seq", "chan")
    return jax.shard_map(shards, mesh=mesh, in_specs=in_specs, out_specs=out_specs, check_vma=False)
```

```python
import functools

import jax
import jax.numpy as jnp
import numpy as np
from jax import lax
from jax.experimental import pallas as pl
from jax.experimental.pallas import tpu as pltpu
from jax.sharding import PartitionSpec as P

BF16 = jnp.bfloat16
F32 = jnp.float32


def bit_reversed(number, width_bits):
    flipped = 0
    for bit_place in range(width_bits):
        flipped |= (number >> bit_place & 1) << (width_bits - 1 - bit_place)
    return flipped


def filter_row(residue, width_bits):
    return 2 * bit_reversed(residue // 2, width_bits) + residue % 2


def dft_tables(parts, rows):
    total = 2 * parts * rows
    residue = np.arange(2 * parts)[:, None, None]
    column = np.arange(rows)[None, :, None]
    position = np.arange(rows)[None, None, :]
    phase = 2.0 * np.pi * (position * (residue + 2 * parts * column) % total) / total
    cos, sin = np.cos(phase), np.sin(phase)
    forward = np.concatenate(
        [np.concatenate([cos, sin], axis=2), np.concatenate([-sin, cos], axis=2)], axis=1
    )
    inverse = np.transpose(forward, (0, 2, 1)) / total
    return forward.astype(BF16), inverse.astype(BF16)


def convolve_kernel(parts, rows, moved_ref, skip_ref, forward_ref, inverse_ref, out_ref, waves_ref, back_ref):
    width_bits = parts.bit_length() - 1
    chunk = 16

    def cosine(residue, block):
        return float(np.cos(np.pi * residue * block / parts))

    def sine(residue, block):
        return float(np.sin(np.pi * residue * block / parts))

    def spread(index, carry):
        here = pl.ds(index * chunk, chunk)
        there = pl.ds(rows + index * chunk, chunk)
        blocks = [moved_ref[block, here, :].astype(F32) for block in range(parts)]
        for residue in range(parts + 1):
            real = blocks[0]
            imag = jnp.zeros_like(real)
            for block in range(1, parts):
                real = real + cosine(residue, block) * blocks[block]
                imag = imag - sine(residue, block) * blocks[block]
            waves_ref[residue, here, :] = real.astype(BF16)
            waves_ref[residue, there, :] = imag.astype(BF16)
            if 0 < residue < parts:
                waves_ref[2 * parts - residue, here, :] = real.astype(BF16)
                waves_ref[2 * parts - residue, there, :] = (-imag).astype(BF16)
        return carry

    lax.fori_loop(0, rows // chunk, spread, 0)

    def through(residue):
        wave = jnp.dot(forward_ref[residue], waves_ref[residue], preferred_element_type=F32)
        source, odd = divmod(filter_row(residue, width_bits), 2)
        filter_real = moved_ref[source, pl.ds((2 + odd) * rows, rows), :].astype(F32)
        filter_imag = moved_ref[source, pl.ds((4 + odd) * rows, rows), :].astype(F32)
        real, imag = wave[:rows], wave[rows:]
        product = jnp.concatenate(
            [real * filter_real - imag * filter_imag, real * filter_imag + imag * filter_real], axis=0
        )
        return jnp.dot(inverse_ref[residue], product.astype(BF16), preferred_element_type=F32)

    for residue in range(parts + 1):
        back = through(residue)
        if 0 < residue < parts:
            other = through(2 * parts - residue)
            back_ref[residue, pl.ds(0, rows), :] = back[:rows] + other[:rows]
            back_ref[residue, pl.ds(rows, rows), :] = back[rows:] - other[rows:]
        else:
            back_ref[residue] = back

    skip = skip_ref[...]

    def gather(index, carry):
        here = pl.ds(index * chunk, chunk)
        there = pl.ds(rows + index * chunk, chunk)
        reals = [back_ref[residue, here, :] for residue in range(parts + 1)]
        imags = [back_ref[residue, there, :] for residue in range(parts + 1)]
        for block in range(parts):
            total = reals[0]
            for residue in range(1, parts + 1):
                total = total + cosine(residue, block) * reals[residue]
                if residue < parts and block:
                    total = total - sine(residue, block) * imags[residue]
            signal = moved_ref[block, here, :].astype(F32)
            gate = moved_ref[block, pl.ds(rows + index * chunk, chunk), :].astype(F32)
            out_ref[block, here, :] = (gate * (total + skip * signal)).astype(BF16)
        return carry

    lax.fori_loop(0, rows // chunk, gather, 0)


def convolve(moved, skip):
    parts, stacked, width = moved.shape
    rows = stacked // 6
    forward, inverse = dft_tables(parts, rows)
    whole = pl.BlockSpec(memory_space=pltpu.VMEM)
    return pl.pallas_call(
        functools.partial(convolve_kernel, parts, rows),
        out_shape=jax.ShapeDtypeStruct((parts, rows, width), BF16),
        in_specs=[whole] * 4,
        out_specs=whole,
        scratch_shapes=[
            pltpu.VMEM((2 * parts, 2 * rows, width), BF16),
            pltpu.VMEM((parts + 1, 2 * rows, width), F32),
        ],
        compiler_params=pltpu.CompilerParams(vmem_limit_bytes=40 * 2**20),
    )(moved, skip[None, :], forward, inverse)


def shards_general(values_in, gate_values, filter_spectrum, skip_gain, out_weight):
    parts = lax.axis_size("seq")
    layers = lax.axis_size("chan")
    rows, width = values_in.shape
    lanes = width // parts
    device = lax.axis_index("seq")

    def by_channel(array):
        return jnp.transpose(array.reshape(array.shape[0], parts, lanes), (1, 0, 2))

    filters = filter_spectrum.astype(BF16).reshape(4 * rows, width)
    packed = jnp.concatenate([by_channel(values_in), by_channel(gate_values), by_channel(filters)], axis=1)
    moved = lax.all_to_all(packed, "seq", 0, 0)
    skip = lax.dynamic_slice_in_dim(skip_gain, device * lanes, lanes)
    gated = convolve(moved, skip)
    gathered = lax.all_gather(gated.reshape(parts * rows, lanes), "seq", axis=1, tiled=True)

    own_cols = out_weight.shape[1]
    share = own_cols * parts // layers // parts
    per_block = parts // layers
    pieces = own_cols // share
    group = device % per_block
    member = device // per_block
    weight = jnp.zeros_like(out_weight)
    for step in range(pieces):
        piece = (member + step) % pieces
        sent = lax.dynamic_slice_in_dim(out_weight, piece * share, share, 1)
        pairs = [
            (source, source % per_block * pieces + (source // per_block + step) % pieces) for source in range(parts)
        ]
        arrived = lax.ppermute(sent, "seq", pairs)
        block = (device % pieces - step) % pieces
        weight = lax.dynamic_update_slice_in_dim(weight, arrived, block * share, 1)
    partials = jnp.dot(gathered, weight, preferred_element_type=F32).astype(BF16)
    mixed = lax.psum_scatter(partials, "chan", scatter_dimension=1, tiled=True)
    return lax.all_to_all(mixed, "seq", 0, 1, tiled=True)


WHOLE = pl.BlockSpec(memory_space=pltpu.VMEM)


def small_tables(parts, rows):
    total = 2 * parts * rows
    index = np.arange(rows)
    phase = 2.0 * np.pi * (index[:, None] * index[None, :] % rows) / rows
    cos, sin = np.cos(phase), np.sin(phase)
    forward = np.block([[cos, sin], [-sin, cos]])
    residue = np.arange(2 * parts).reshape(2, 1, parts)
    turn = 2.0 * np.pi * index[None, :, None] * residue / total
    return forward.astype(BF16), forward.T.astype(BF16), np.cos(turn).astype(F32), np.sin(turn).astype(F32)


def cosine(parts, residue, block):
    return float(np.cos(np.pi * residue * block / parts))


def sine(parts, residue, block):
    return float(np.sin(np.pi * residue * block / parts))


def weighted(terms):
    total = None
    for factor, term in terms:
        if abs(factor) < 1e-12:
            continue
        part = term if factor == 1.0 else factor * term
        total = part if total is None else total + part
    return total


def plus(left, right):
    return left if right is None else right if left is None else left + right


def minus(left, right):
    return left if right is None else -right if left is None else left - right


def own_place():
    device = lax.axis_index("seq")
    return device // 2, device % 2


def block_at(index, size):
    return pl.ds(pl.multiple_of(index * size, size), size)


def pack_signals_kernel(chips, values_ref, gate_ref, *out_refs):
    chip, _ = own_place()
    lanes = out_refs[0].shape[2]
    for offset in range(chips):
        out_refs[offset][0] = values_ref[:, block_at(chip ^ offset, lanes)]
        out_refs[offset][1] = gate_ref[:, block_at(chip ^ offset, lanes)]


def pack_signals(values_in, gate_values, chips):
    rows, width = values_in.shape
    return pl.pallas_call(
        functools.partial(pack_signals_kernel, chips),
        in_specs=[WHOLE] * 2,
        out_specs=[WHOLE] * chips,
        out_shape=[jax.ShapeDtypeStruct((2, rows, width // chips), BF16)] * chips,
        name="pack_signals",
    )(values_in, gate_values)


def pack_filter_kernel(offset, filter_ref, out_ref, plane_ref, arrived):
    chip, _ = own_place()
    planes, _, lanes = out_ref.shape
    copies = [
        pltpu.make_async_copy(
            filter_ref.at[plane, :, block_at(chip ^ offset, lanes)], plane_ref.at[plane], arrived.at[plane]
        )
        for plane in range(planes)
    ]
    for copy in copies:
        copy.start()
    for plane, copy in enumerate(copies):
        copy.wait()
        out_ref[plane] = plane_ref[plane].astype(BF16)


def pack_filter(filters, chips, offset):
    planes, rows, width = filters.shape
    shape = (planes, rows, width // chips)
    return pl.pallas_call(
        functools.partial(pack_filter_kernel, offset),
        in_specs=[pl.BlockSpec(memory_space=pl.ANY)],
        out_specs=WHOLE,
        out_shape=jax.ShapeDtypeStruct(shape, BF16),
        scratch_shapes=[pltpu.VMEM(shape, F32), pltpu.SemaphoreType.DMA((planes,))],
        name="pack_filter",
    )(filters)


def forward_kernel(chips, cos_ref, sin_ref, table_ref, own_ref, other_ref, out_ref, signal_ref, waves_ref):
    chip, core = own_place()
    parts = 2 * chips
    rows, lanes = own_ref.shape[1:]
    chunk, width = 16, 128
    for offset in range(chips):
        signal_ref[2 * (chip ^ offset) + core] = own_ref[offset]
        signal_ref[2 * (chip ^ offset) + 1 - core] = other_ref[offset]
    sign = (1 - 2 * core).astype(F32)

    def spread(index, carry):
        here = block_at(index, chunk)
        there = pl.ds(pl.multiple_of(rows + index * chunk, chunk), chunk)
        cos_all, sin_all = cos_ref[core, here, :], sin_ref[core, here, :]
        for start in range(0, lanes, width):
            blocks = [signal_ref[block, here, pl.ds(start, width)].astype(F32) for block in range(parts)]
            blocks = [block * sign if place % 2 else block for place, block in enumerate(blocks)]

            def store(residue, real, imag):
                cos, sin = cos_all[:, residue : residue + 1], sin_all[:, residue : residue + 1]
                if imag is None:
                    real, imag = real * cos, -(real * sin)
                else:
                    real, imag = real * cos + imag * sin, imag * cos - real * sin
                columns = pl.ds(residue * lanes + start, width)
                waves_ref[here, columns] = real.astype(BF16)
                waves_ref[there, columns] = imag.astype(BF16)

            for residue in range(parts // 2 + 1):
                even, odd = range(0, parts, 2), range(1, parts, 2)
                cos_even = weighted([(cosine(parts, residue, block), blocks[block]) for block in even])
                cos_odd = weighted([(cosine(parts, residue, block), blocks[block]) for block in odd])
                sin_even = weighted([(sine(parts, residue, block), blocks[block]) for block in even])
                sin_odd = weighted([(sine(parts, residue, block), blocks[block]) for block in odd])
                sin_sum = plus(sin_even, sin_odd)
                store(residue, plus(cos_even, cos_odd), None if sin_sum is None else -sin_sum)
                if 0 < residue and 2 * residue != parts:
                    store(parts - residue, minus(cos_even, cos_odd), minus(sin_even, sin_odd))
        return carry

    lax.fori_loop(0, rows // chunk, spread, 0)
    for residue in range(parts):
        columns = pl.ds(residue * lanes, lanes)
        out_ref[:, columns] = jnp.dot(table_ref[...], waves_ref[:, columns], preferred_element_type=F32)


def forward(own, other, tables):
    chips, rows, lanes = own.shape
    table, _, cos, sin = tables
    spectrum = (2 * rows, 2 * chips * lanes)
    return pl.pallas_call(
        functools.partial(forward_kernel, chips),
        in_specs=[WHOLE] * 5,
        out_specs=WHOLE,
        out_shape=jax.ShapeDtypeStruct(spectrum, F32),
        scratch_shapes=[pltpu.VMEM((2 * chips, rows, lanes), BF16), pltpu.VMEM(spectrum, BF16)],
        compiler_params=pltpu.CompilerParams(vmem_limit_bytes=32 * 2**20),
        name="forward",
    )(cos, sin, table, own, other)


def backward_kernel(chips, cos_ref, sin_ref, table_ref, spectrum_ref, *refs):
    filter_refs, (keep_ref, send_ref, filter_ref, product_ref, back_ref) = refs[:chips], refs[chips:]
    chip, core = own_place()
    parts = 2 * chips
    rows, lanes = keep_ref.shape[1:]
    chip_bits = chips.bit_length() - 1
    chunk, width = 16, 128
    for offset in range(chips):
        filter_ref[chip ^ offset] = filter_refs[offset][...]

    for residue in range(parts):
        source, odd = bit_reversed(residue // 2, chip_bits), residue % 2
        columns = pl.ds(residue * lanes, lanes)
        filter_real = filter_ref[source, odd].astype(F32)
        filter_imag = filter_ref[source, 2 + odd].astype(F32)
        real = spectrum_ref[pl.ds(0, rows), columns]
        imag = spectrum_ref[pl.ds(rows, rows), columns]
        product_ref[pl.ds(0, rows), columns] = (real * filter_real - imag * filter_imag).astype(BF16)
        product_ref[pl.ds(rows, rows), columns] = (real * filter_imag + imag * filter_real).astype(BF16)
        back_ref[:, columns] = jnp.dot(table_ref[...], product_ref[:, columns], preferred_element_type=F32)

    scale = 1.0 / (2 * parts * rows)
    sign = (1 - 2 * core).astype(F32)
    upper = core == 1

    def gather(index, carry):
        here = block_at(index, chunk)
        there = pl.ds(pl.multiple_of(rows + index * chunk, chunk), chunk)
        cos_all, sin_all = cos_ref[core, here, :] * scale, sin_ref[core, here, :] * scale
        for start in range(0, lanes, width):
            reals, imags = [], []
            for residue in range(parts):
                columns = pl.ds(residue * lanes + start, width)
                real, imag = back_ref[here, columns], back_ref[there, columns]
                cos, sin = cos_all[:, residue : residue + 1], sin_all[:, residue : residue + 1]
                reals.append(real * cos - imag * sin)
                imags.append(real * sin + imag * cos)
            totals = [None] * parts
            for block in range(parts // 2 + 1):
                even, odd = range(0, parts, 2), range(1, parts, 2)
                cos_even = weighted([(cosine(parts, residue, block), reals[residue]) for residue in even])
                cos_odd = weighted([(cosine(parts, residue, block), reals[residue]) for residue in odd])
                sin_even = weighted([(sine(parts, residue, block), imags[residue]) for residue in even])
                sin_odd = weighted([(sine(parts, residue, block), imags[residue]) for residue in odd])
                totals[block] = minus(plus(cos_even, cos_odd), plus(sin_even, sin_odd))
                if 0 < block and 2 * block != parts:
                    totals[parts - block] = plus(minus(cos_even, cos_odd), minus(sin_even, sin_odd))
            lane = pl.ds(start, width)
            for pair in range(chips):
                low, high = totals[2 * pair], totals[2 * pair + 1] * sign
                keep_ref[pair, here, lane] = jnp.where(upper, high, low)
                send_ref[pair, here, lane] = jnp.where(upper, low, high).astype(BF16)
        return carry

    lax.fori_loop(0, rows // chunk, gather, 0)


def backward(spectrum, filters, tables):
    chips = len(filters)
    planes, rows, lanes = filters[0].shape
    _, table, cos, sin = tables
    kept = (chips, rows, lanes)
    return pl.pallas_call(
        functools.partial(backward_kernel, chips),
        in_specs=[WHOLE] * (4 + chips),
        out_specs=[WHOLE] * 2,
        out_shape=[jax.ShapeDtypeStruct(kept, F32), jax.ShapeDtypeStruct(kept, BF16)],
        scratch_shapes=[
            pltpu.VMEM((chips, planes, rows, lanes), BF16),
            pltpu.VMEM(spectrum.shape, BF16),
            pltpu.VMEM(spectrum.shape, F32),
        ],
        compiler_params=pltpu.CompilerParams(vmem_limit_bytes=40 * 2**20),
        name="backward",
    )(cos, sin, table, spectrum, *filters)


def gate_kernel(chips, skip_ref, keep_ref, arrived_ref, *refs):
    signal_refs, out_refs = refs[:chips], refs[chips:]
    chip, _ = own_place()
    rows, lanes = keep_ref.shape[1:]
    step = rows // len(out_refs)
    skip = skip_ref[:, block_at(chip, lanes)]
    for offset in range(chips):
        block = chip ^ offset
        for part, out_ref in enumerate(out_refs):
            here = pl.ds(part * step, step)
            convolved = keep_ref[block, here, :] + arrived_ref[block, here, :].astype(F32)
            signal = signal_refs[offset][0, here, :].astype(F32)
            gate = signal_refs[offset][1, here, :].astype(F32)
            out_ref[block_at(block, step), :] = (gate * (convolved + skip * signal)).astype(BF16)


def gate(skip, keep, arrived, signals, pieces):
    chips, rows, lanes = keep.shape
    return pl.pallas_call(
        functools.partial(gate_kernel, chips),
        in_specs=[WHOLE] * (3 + chips),
        out_specs=[WHOLE] * pieces,
        out_shape=[jax.ShapeDtypeStruct((chips * rows // pieces, lanes), BF16)] * pieces,
        name="gate",
    )(skip, keep, arrived, *signals)


def arrange_kernel(layers, *refs):
    own_refs, other_refs, out_ref = refs[:layers], refs[layers : 2 * layers], refs[2 * layers]
    device, layer = lax.axis_index("seq"), lax.axis_index("chan")
    share = own_refs[0].shape[1]
    for step in range(layers):
        target = device % layers ^ layer ^ step
        out_ref[target, :, block_at(device % 2, share)] = own_refs[step][...]
        out_ref[target, :, block_at(1 - device % 2, share)] = other_refs[step ^ 1][...]


def arrange(own, other):
    layers = len(own)
    rows, share = own[0].shape
    return pl.pallas_call(
        functools.partial(arrange_kernel, layers),
        in_specs=[WHOLE] * (2 * layers),
        out_specs=WHOLE,
        out_shape=jax.ShapeDtypeStruct((layers, rows, 2 * share), BF16),
        compiler_params=pltpu.CompilerParams(vmem_limit_bytes=32 * 2**20),
        name="arrange_weights",
    )(*own, *other)


def project_kernel(chips, weight_ref, *refs):
    gated_refs, (keep_ref, pass_ref, send_ref, joined_ref) = refs[:chips], refs[chips:]
    chip, _ = own_place()
    lanes = gated_refs[0].shape[1]
    for offset in range(chips):
        joined_ref[:, block_at(chip ^ offset, lanes)] = gated_refs[offset][...]

    def partial_of(target):
        return jnp.dot(joined_ref[...], weight_ref[target], preferred_element_type=F32).astype(BF16)

    send_ref[0] = partial_of(1)
    send_ref[1] = partial_of(3)
    pass_ref[...] = partial_of(2)
    keep_ref[...] = partial_of(0)


def project(weight, gated):
    chips = len(gated)
    _, depth, columns = weight.shape
    rows = gated[0].shape[0]
    block = jax.ShapeDtypeStruct((rows, columns), BF16)
    return pl.pallas_call(
        functools.partial(project_kernel, chips),
        in_specs=[WHOLE] * (1 + chips),
        out_specs=[WHOLE] * 3,
        out_shape=[block, block, jax.ShapeDtypeStruct((2, rows, columns), BF16)],
        scratch_shapes=[pltpu.VMEM((rows, depth), BF16)],
        compiler_params=pltpu.CompilerParams(vmem_limit_bytes=32 * 2**20),
        name="project",
    )(weight, *gated)


def finish_kernel(chips, pieces, *refs):
    keep_refs, first_refs, second_refs = refs[:pieces], refs[pieces : 2 * pieces], refs[2 * pieces : 3 * pieces]
    out_refs = refs[3 * pieces :]
    chip, _ = own_place()
    step = keep_refs[0].shape[0] // chips
    for offset in range(chips):
        here = block_at(chip ^ offset, step)
        for part in range(pieces):
            total = keep_refs[part][here, :].astype(F32) + first_refs[part][0, here, :].astype(F32)
            total = total + second_refs[part][here, :].astype(F32)
            out_refs[offset][pl.ds(part * step, step), :] = total.astype(BF16)


def finish(keep, first, second, chips):
    pieces = len(keep)
    rows, columns = keep[0].shape
    return pl.pallas_call(
        functools.partial(finish_kernel, chips, pieces),
        in_specs=[WHOLE] * (3 * pieces),
        out_specs=[WHOLE] * chips,
        out_shape=[jax.ShapeDtypeStruct((rows * pieces // chips, columns), BF16)] * chips,
        name="finish",
    )(*keep, *first, *second)


def join_kernel(chips, *refs):
    in_refs, out_ref = refs[:chips], refs[chips]
    chip, _ = own_place()
    columns = in_refs[0].shape[1]
    for offset in range(chips):
        out_ref[:, block_at(chip ^ offset, columns)] = in_refs[offset][...]


def join(blocks):
    chips = len(blocks)
    rows, columns = blocks[0].shape
    return pl.pallas_call(
        functools.partial(join_kernel, chips),
        in_specs=[WHOLE] * chips,
        out_specs=WHOLE,
        out_shape=jax.ShapeDtypeStruct((rows, chips * columns), BF16),
        name="join",
    )(*blocks)


def swapped(value, axis, offset):
    if not offset:
        return value
    return lax.ppermute(value, axis, [(source, source ^ offset) for source in range(lax.axis_size(axis))])


def to_chips(blocks):
    return [swapped(block, "seq", 2 * offset) for offset, block in enumerate(blocks)]


def shards_direct(values_in, gate_values, filter_spectrum, skip_gain, out_weight):
    parts = lax.axis_size("seq")
    layers = lax.axis_size("chan")
    chips = parts // 2
    pieces = 2
    rows, width = values_in.shape
    device = lax.axis_index("seq")
    tables = small_tables(parts, rows)

    signals = to_chips(pack_signals(values_in, gate_values, chips))
    flat_filters = filter_spectrum.reshape(4, rows, width)
    filters = to_chips([pack_filter(flat_filters, chips, offset) for offset in range(chips)])

    share = out_weight.shape[1] // layers
    own_weight = []
    for step in range(layers):
        sent = lax.dynamic_slice_in_dim(out_weight, (device // 2 ^ step) * share, share, 1)
        pairs = [(source, source % 2 * layers + (source // 2 ^ step)) for source in range(parts)]
        own_weight.append(lax.ppermute(sent, "seq", pairs))
    weight = arrange(own_weight, [swapped(block, "seq", 1) for block in own_weight])

    own = jnp.stack([block[0] for block in signals])
    spectrum = forward(own, swapped(own, "seq", 1), tables)
    keep, send = backward(spectrum, filters, tables)
    gated = gate(skip_gain[None, :], keep, swapped(send, "seq", 1), signals, pieces)

    kept, firsts, seconds = [], [], []
    for piece in gated:
        keep, passed, send = project(weight, to_chips([piece] * chips))
        first = swapped(send, "chan", 1)
        passed = (passed.astype(F32) + first[1].astype(F32)).astype(BF16)
        kept.append(keep)
        firsts.append(first)
        seconds.append(swapped(passed, "chan", 2))
    return join(to_chips(finish(kept, firsts, seconds, chips)))


def shards(values_in, gate_values, filter_spectrum, skip_gain, out_weight):
    parts, layers = lax.axis_size("seq"), lax.axis_size("chan")
    rows, width = values_in.shape
    share = out_weight.shape[1] // layers
    aligned = width // parts % 128 == 0 and share % 128 == 0 and rows % 32 == 0
    run = shards_direct if aligned and layers == 4 and parts == 8 else shards_general
    return run(values_in, gate_values, filter_spectrum, skip_gain, out_weight)


def solution(mesh):
    in_specs = (
        P("seq", "chan"),
        P("seq", "chan"),
        P(None, "seq", None, "chan"),
        P("chan"),
        P("chan", "seq"),
    )
    out_specs = P("seq", "chan")
    return jax.shard_map(shards, mesh=mesh, in_specs=in_specs, out_specs=out_specs, check_vma=False)
```

```python
import functools

import jax
import jax.numpy as jnp
import numpy as np
from jax import lax
from jax.experimental import pallas as pl
from jax.experimental.pallas import tpu as pltpu
from jax.sharding import PartitionSpec as P

BF16 = jnp.bfloat16
F32 = jnp.float32


def bit_reversed(number, width_bits):
    flipped = 0
    for bit_place in range(width_bits):
        flipped |= (number >> bit_place & 1) << (width_bits - 1 - bit_place)
    return flipped


def filter_row(residue, width_bits):
    return 2 * bit_reversed(residue // 2, width_bits) + residue % 2


def dft_tables(parts, rows):
    total = 2 * parts * rows
    residue = np.arange(2 * parts)[:, None, None]
    column = np.arange(rows)[None, :, None]
    position = np.arange(rows)[None, None, :]
    phase = 2.0 * np.pi * (position * (residue + 2 * parts * column) % total) / total
    cos, sin = np.cos(phase), np.sin(phase)
    forward = np.concatenate(
        [np.concatenate([cos, sin], axis=2), np.concatenate([-sin, cos], axis=2)], axis=1
    )
    inverse = np.transpose(forward, (0, 2, 1)) / total
    return forward.astype(BF16), inverse.astype(BF16)


def convolve_kernel(parts, rows, moved_ref, skip_ref, forward_ref, inverse_ref, out_ref, waves_ref, back_ref):
    width_bits = parts.bit_length() - 1
    chunk = 16

    def cosine(residue, block):
        return float(np.cos(np.pi * residue * block / parts))

    def sine(residue, block):
        return float(np.sin(np.pi * residue * block / parts))

    def spread(index, carry):
        here = pl.ds(index * chunk, chunk)
        there = pl.ds(rows + index * chunk, chunk)
        blocks = [moved_ref[block, here, :].astype(F32) for block in range(parts)]
        for residue in range(parts + 1):
            real = blocks[0]
            imag = jnp.zeros_like(real)
            for block in range(1, parts):
                real = real + cosine(residue, block) * blocks[block]
                imag = imag - sine(residue, block) * blocks[block]
            waves_ref[residue, here, :] = real.astype(BF16)
            waves_ref[residue, there, :] = imag.astype(BF16)
            if 0 < residue < parts:
                waves_ref[2 * parts - residue, here, :] = real.astype(BF16)
                waves_ref[2 * parts - residue, there, :] = (-imag).astype(BF16)
        return carry

    lax.fori_loop(0, rows // chunk, spread, 0)

    def through(residue):
        wave = jnp.dot(forward_ref[residue], waves_ref[residue], preferred_element_type=F32)
        source, odd = divmod(filter_row(residue, width_bits), 2)
        filter_real = moved_ref[source, pl.ds((2 + odd) * rows, rows), :].astype(F32)
        filter_imag = moved_ref[source, pl.ds((4 + odd) * rows, rows), :].astype(F32)
        real, imag = wave[:rows], wave[rows:]
        product = jnp.concatenate(
            [real * filter_real - imag * filter_imag, real * filter_imag + imag * filter_real], axis=0
        )
        return jnp.dot(inverse_ref[residue], product.astype(BF16), preferred_element_type=F32)

    for residue in range(parts + 1):
        back = through(residue)
        if 0 < residue < parts:
            other = through(2 * parts - residue)
            back_ref[residue, pl.ds(0, rows), :] = back[:rows] + other[:rows]
            back_ref[residue, pl.ds(rows, rows), :] = back[rows:] - other[rows:]
        else:
            back_ref[residue] = back

    skip = skip_ref[...]

    def gather(index, carry):
        here = pl.ds(index * chunk, chunk)
        there = pl.ds(rows + index * chunk, chunk)
        reals = [back_ref[residue, here, :] for residue in range(parts + 1)]
        imags = [back_ref[residue, there, :] for residue in range(parts + 1)]
        for block in range(parts):
            total = reals[0]
            for residue in range(1, parts + 1):
                total = total + cosine(residue, block) * reals[residue]
                if residue < parts and block:
                    total = total - sine(residue, block) * imags[residue]
            signal = moved_ref[block, here, :].astype(F32)
            gate = moved_ref[block, pl.ds(rows + index * chunk, chunk), :].astype(F32)
            out_ref[block, here, :] = (gate * (total + skip * signal)).astype(BF16)
        return carry

    lax.fori_loop(0, rows // chunk, gather, 0)


def convolve(moved, skip):
    parts, stacked, width = moved.shape
    rows = stacked // 6
    forward, inverse = dft_tables(parts, rows)
    whole = pl.BlockSpec(memory_space=pltpu.VMEM)
    return pl.pallas_call(
        functools.partial(convolve_kernel, parts, rows),
        out_shape=jax.ShapeDtypeStruct((parts, rows, width), BF16),
        in_specs=[whole] * 4,
        out_specs=whole,
        scratch_shapes=[
            pltpu.VMEM((2 * parts, 2 * rows, width), BF16),
            pltpu.VMEM((parts + 1, 2 * rows, width), F32),
        ],
        compiler_params=pltpu.CompilerParams(vmem_limit_bytes=40 * 2**20),
    )(moved, skip[None, :], forward, inverse)


def shards_general(values_in, gate_values, filter_spectrum, skip_gain, out_weight):
    parts = lax.axis_size("seq")
    layers = lax.axis_size("chan")
    rows, width = values_in.shape
    lanes = width // parts
    device = lax.axis_index("seq")

    def by_channel(array):
        return jnp.transpose(array.reshape(array.shape[0], parts, lanes), (1, 0, 2))

    filters = filter_spectrum.astype(BF16).reshape(4 * rows, width)
    packed = jnp.concatenate([by_channel(values_in), by_channel(gate_values), by_channel(filters)], axis=1)
    moved = lax.all_to_all(packed, "seq", 0, 0)
    skip = lax.dynamic_slice_in_dim(skip_gain, device * lanes, lanes)
    gated = convolve(moved, skip)
    gathered = lax.all_gather(gated.reshape(parts * rows, lanes), "seq", axis=1, tiled=True)

    own_cols = out_weight.shape[1]
    share = own_cols * parts // layers // parts
    per_block = parts // layers
    pieces = own_cols // share
    group = device % per_block
    member = device // per_block
    weight = jnp.zeros_like(out_weight)
    for step in range(pieces):
        piece = (member + step) % pieces
        sent = lax.dynamic_slice_in_dim(out_weight, piece * share, share, 1)
        pairs = [
            (source, source % per_block * pieces + (source // per_block + step) % pieces) for source in range(parts)
        ]
        arrived = lax.ppermute(sent, "seq", pairs)
        block = (device % pieces - step) % pieces
        weight = lax.dynamic_update_slice_in_dim(weight, arrived, block * share, 1)
    partials = jnp.dot(gathered, weight, preferred_element_type=F32).astype(BF16)
    mixed = lax.psum_scatter(partials, "chan", scatter_dimension=1, tiled=True)
    return lax.all_to_all(mixed, "seq", 0, 1, tiled=True)


WHOLE = pl.BlockSpec(memory_space=pltpu.VMEM)


def small_tables(parts, rows):
    total = 2 * parts * rows
    index = np.arange(rows)
    phase = 2.0 * np.pi * (index[:, None] * index[None, :] % rows) / rows
    cos, sin = np.cos(phase), np.sin(phase)
    forward = np.block([[cos, sin], [-sin, cos]])
    residue = np.arange(2 * parts).reshape(2, 1, parts)
    turn = 2.0 * np.pi * index[None, :, None] * residue / total
    return forward.astype(BF16), forward.T.astype(BF16), np.cos(turn).astype(F32), np.sin(turn).astype(F32)


def cosine(parts, residue, block):
    return float(np.cos(np.pi * residue * block / parts))


def sine(parts, residue, block):
    return float(np.sin(np.pi * residue * block / parts))


def weighted(terms):
    total = None
    for factor, term in terms:
        if abs(factor) < 1e-12:
            continue
        part = term if factor == 1.0 else factor * term
        total = part if total is None else total + part
    return total


def plus(left, right):
    return left if right is None else right if left is None else left + right


def minus(left, right):
    return left if right is None else -right if left is None else left - right


def own_place():
    device = lax.axis_index("seq")
    return device // 2, device % 2


def block_at(index, size):
    return pl.ds(pl.multiple_of(index * size, size), size)


def pack_signals_kernel(chips, values_ref, gate_ref, *out_refs):
    chip, _ = own_place()
    lanes = out_refs[0].shape[2]
    for offset in range(chips):
        out_refs[offset][0] = values_ref[:, block_at(chip ^ offset, lanes)]
        out_refs[offset][1] = gate_ref[:, block_at(chip ^ offset, lanes)]


def pack_signals(values_in, gate_values, chips):
    rows, width = values_in.shape
    return pl.pallas_call(
        functools.partial(pack_signals_kernel, chips),
        in_specs=[WHOLE] * 2,
        out_specs=[WHOLE] * chips,
        out_shape=[jax.ShapeDtypeStruct((2, rows, width // chips), BF16)] * chips,
        compiler_params=pltpu.CompilerParams(vmem_limit_bytes=4 * 2**20),
        name="pack_signals",
    )(values_in, gate_values)


def pack_filter_kernel(offset, filter_ref, out_ref, plane_ref, arrived):
    chip, _ = own_place()
    planes, _, lanes = out_ref.shape
    copies = [
        pltpu.make_async_copy(
            filter_ref.at[plane, :, block_at(chip ^ offset, lanes)], plane_ref.at[plane], arrived.at[plane]
        )
        for plane in range(planes)
    ]
    for copy in copies:
        copy.start()
    for plane, copy in enumerate(copies):
        copy.wait()
        out_ref[plane] = plane_ref[plane].astype(BF16)


def pack_filter(filters, chips, offset):
    planes, rows, width = filters.shape
    shape = (planes, rows, width // chips)
    return pl.pallas_call(
        functools.partial(pack_filter_kernel, offset),
        in_specs=[pl.BlockSpec(memory_space=pl.ANY)],
        out_specs=WHOLE,
        out_shape=jax.ShapeDtypeStruct(shape, BF16),
        scratch_shapes=[pltpu.VMEM(shape, F32), pltpu.SemaphoreType.DMA((planes,))],
        compiler_params=pltpu.CompilerParams(vmem_limit_bytes=4 * 2**20),
        name="pack_filter",
    )(filters)


def forward_kernel(chips, cos_ref, sin_ref, table_ref, own_ref, other_ref, out_ref, signal_ref, waves_ref):
    chip, core = own_place()
    parts = 2 * chips
    rows, lanes = own_ref.shape[1:]
    chunk, width = 16, 128
    for offset in range(chips):
        signal_ref[2 * (chip ^ offset) + core] = own_ref[offset]
        signal_ref[2 * (chip ^ offset) + 1 - core] = other_ref[offset]
    sign = (1 - 2 * core).astype(F32)

    def spread(index, carry):
        here = block_at(index, chunk)
        there = pl.ds(pl.multiple_of(rows + index * chunk, chunk), chunk)
        cos_all, sin_all = cos_ref[core, here, :], sin_ref[core, here, :]
        for start in range(0, lanes, width):
            blocks = [signal_ref[block, here, pl.ds(start, width)].astype(F32) for block in range(parts)]
            blocks = [block * sign if place % 2 else block for place, block in enumerate(blocks)]

            def store(residue, real, imag):
                cos, sin = cos_all[:, residue : residue + 1], sin_all[:, residue : residue + 1]
                if imag is None:
                    real, imag = real * cos, -(real * sin)
                else:
                    real, imag = real * cos + imag * sin, imag * cos - real * sin
                columns = pl.ds(residue * lanes + start, width)
                waves_ref[here, columns] = real.astype(BF16)
                waves_ref[there, columns] = imag.astype(BF16)

            for residue in range(parts // 2 + 1):
                even, odd = range(0, parts, 2), range(1, parts, 2)
                cos_even = weighted([(cosine(parts, residue, block), blocks[block]) for block in even])
                cos_odd = weighted([(cosine(parts, residue, block), blocks[block]) for block in odd])
                sin_even = weighted([(sine(parts, residue, block), blocks[block]) for block in even])
                sin_odd = weighted([(sine(parts, residue, block), blocks[block]) for block in odd])
                sin_sum = plus(sin_even, sin_odd)
                store(residue, plus(cos_even, cos_odd), None if sin_sum is None else -sin_sum)
                if 0 < residue and 2 * residue != parts:
                    store(parts - residue, minus(cos_even, cos_odd), minus(sin_even, sin_odd))
        return carry

    lax.fori_loop(0, rows // chunk, spread, 0)
    for residue in range(parts):
        columns = pl.ds(residue * lanes, lanes)
        out_ref[:, columns] = jnp.dot(table_ref[...], waves_ref[:, columns], preferred_element_type=F32)


def forward(own, other, tables):
    chips, rows, lanes = own.shape
    table, _, cos, sin = tables
    spectrum = (2 * rows, 2 * chips * lanes)
    return pl.pallas_call(
        functools.partial(forward_kernel, chips),
        in_specs=[WHOLE] * 5,
        out_specs=WHOLE,
        out_shape=jax.ShapeDtypeStruct(spectrum, F32),
        scratch_shapes=[pltpu.VMEM((2 * chips, rows, lanes), BF16), pltpu.VMEM(spectrum, BF16)],
        compiler_params=pltpu.CompilerParams(vmem_limit_bytes=8 * 2**20),
        name="forward",
    )(cos, sin, table, own, other)


def backward_kernel(chips, cos_ref, sin_ref, table_ref, spectrum_ref, *refs):
    filter_refs, (keep_ref, send_ref, filter_ref, product_ref, back_ref) = refs[:chips], refs[chips:]
    chip, core = own_place()
    parts = 2 * chips
    rows, lanes = keep_ref.shape[1:]
    chip_bits = chips.bit_length() - 1
    chunk, width = 16, 128
    for offset in range(chips):
        filter_ref[chip ^ offset] = filter_refs[offset][...]

    for residue in range(parts):
        source, odd = bit_reversed(residue // 2, chip_bits), residue % 2
        columns = pl.ds(residue * lanes, lanes)
        filter_real = filter_ref[source, odd].astype(F32)
        filter_imag = filter_ref[source, 2 + odd].astype(F32)
        real = spectrum_ref[pl.ds(0, rows), columns]
        imag = spectrum_ref[pl.ds(rows, rows), columns]
        product_ref[pl.ds(0, rows), columns] = (real * filter_real - imag * filter_imag).astype(BF16)
        product_ref[pl.ds(rows, rows), columns] = (real * filter_imag + imag * filter_real).astype(BF16)
        back_ref[:, columns] = jnp.dot(table_ref[...], product_ref[:, columns], preferred_element_type=F32)

    scale = 1.0 / (2 * parts * rows)
    sign = (1 - 2 * core).astype(F32)
    upper = core == 1

    def gather(index, carry):
        here = block_at(index, chunk)
        there = pl.ds(pl.multiple_of(rows + index * chunk, chunk), chunk)
        cos_all, sin_all = cos_ref[core, here, :] * scale, sin_ref[core, here, :] * scale
        for start in range(0, lanes, width):
            reals, imags = [], []
            for residue in range(parts):
                columns = pl.ds(residue * lanes + start, width)
                real, imag = back_ref[here, columns], back_ref[there, columns]
                cos, sin = cos_all[:, residue : residue + 1], sin_all[:, residue : residue + 1]
                reals.append(real * cos - imag * sin)
                imags.append(real * sin + imag * cos)
            totals = [None] * parts
            for block in range(parts // 2 + 1):
                even, odd = range(0, parts, 2), range(1, parts, 2)
                cos_even = weighted([(cosine(parts, residue, block), reals[residue]) for residue in even])
                cos_odd = weighted([(cosine(parts, residue, block), reals[residue]) for residue in odd])
                sin_even = weighted([(sine(parts, residue, block), imags[residue]) for residue in even])
                sin_odd = weighted([(sine(parts, residue, block), imags[residue]) for residue in odd])
                totals[block] = minus(plus(cos_even, cos_odd), plus(sin_even, sin_odd))
                if 0 < block and 2 * block != parts:
                    totals[parts - block] = plus(minus(cos_even, cos_odd), minus(sin_even, sin_odd))
            lane = pl.ds(start, width)
            for pair in range(chips):
                low, high = totals[2 * pair], totals[2 * pair + 1] * sign
                keep_ref[pair, here, lane] = jnp.where(upper, high, low)
                send_ref[pair, here, lane] = jnp.where(upper, low, high).astype(BF16)
        return carry

    lax.fori_loop(0, rows // chunk, gather, 0)


def backward(spectrum, filters, tables):
    chips = len(filters)
    planes, rows, lanes = filters[0].shape
    _, table, cos, sin = tables
    kept = (chips, rows, lanes)
    return pl.pallas_call(
        functools.partial(backward_kernel, chips),
        in_specs=[WHOLE] * (4 + chips),
        out_specs=[WHOLE] * 2,
        out_shape=[jax.ShapeDtypeStruct(kept, F32), jax.ShapeDtypeStruct(kept, BF16)],
        scratch_shapes=[
            pltpu.VMEM((chips, planes, rows, lanes), BF16),
            pltpu.VMEM(spectrum.shape, BF16),
            pltpu.VMEM(spectrum.shape, F32),
        ],
        compiler_params=pltpu.CompilerParams(vmem_limit_bytes=12 * 2**20),
        name="backward",
    )(cos, sin, table, spectrum, *filters)


def gate_kernel(chips, skip_ref, keep_ref, arrived_ref, *refs):
    signal_refs, out_refs = refs[:chips], refs[chips:]
    chip, _ = own_place()
    rows, lanes = keep_ref.shape[1:]
    step = rows // len(out_refs)
    skip = skip_ref[:, block_at(chip, lanes)]
    for offset in range(chips):
        block = chip ^ offset
        for part, out_ref in enumerate(out_refs):
            here = pl.ds(part * step, step)
            convolved = keep_ref[block, here, :] + arrived_ref[block, here, :].astype(F32)
            signal = signal_refs[offset][0, here, :].astype(F32)
            gate = signal_refs[offset][1, here, :].astype(F32)
            out_ref[block_at(block, step), :] = (gate * (convolved + skip * signal)).astype(BF16)


def gate(skip, keep, arrived, signals, pieces):
    chips, rows, lanes = keep.shape
    return pl.pallas_call(
        functools.partial(gate_kernel, chips),
        in_specs=[WHOLE] * (3 + chips),
        out_specs=[WHOLE] * pieces,
        out_shape=[jax.ShapeDtypeStruct((chips * rows // pieces, lanes), BF16)] * pieces,
        compiler_params=pltpu.CompilerParams(vmem_limit_bytes=6 * 2**20),
        name="gate",
    )(skip, keep, arrived, *signals)


def arrange_kernel(layers, *refs):
    own_refs, other_refs, out_ref = refs[:layers], refs[layers : 2 * layers], refs[2 * layers]
    device, layer = lax.axis_index("seq"), lax.axis_index("chan")
    share = own_refs[0].shape[1]
    for step in range(layers):
        target = device % layers ^ layer ^ step
        out_ref[target, :, block_at(device % 2, share)] = own_refs[step][...]
        out_ref[target, :, block_at(1 - device % 2, share)] = other_refs[step ^ 1][...]


def arrange(own, other):
    layers = len(own)
    rows, share = own[0].shape
    return pl.pallas_call(
        functools.partial(arrange_kernel, layers),
        in_specs=[WHOLE] * (2 * layers),
        out_specs=WHOLE,
        out_shape=jax.ShapeDtypeStruct((layers, rows, 2 * share), BF16),
        compiler_params=pltpu.CompilerParams(vmem_limit_bytes=8 * 2**20),
        name="arrange_weights",
    )(*own, *other)


def project_kernel(chips, weight_ref, *refs):
    gated_refs, (keep_ref, pass_ref, send_ref, joined_ref) = refs[:chips], refs[chips:]
    chip, _ = own_place()
    lanes = gated_refs[0].shape[1]
    for offset in range(chips):
        joined_ref[:, block_at(chip ^ offset, lanes)] = gated_refs[offset][...]

    def partial_of(target):
        return jnp.dot(joined_ref[...], weight_ref[target], preferred_element_type=F32).astype(BF16)

    send_ref[0] = partial_of(1)
    send_ref[1] = partial_of(3)
    pass_ref[...] = partial_of(2)
    keep_ref[...] = partial_of(0)


def project(weight, gated):
    chips = len(gated)
    _, depth, columns = weight.shape
    rows = gated[0].shape[0]
    block = jax.ShapeDtypeStruct((rows, columns), BF16)
    return pl.pallas_call(
        functools.partial(project_kernel, chips),
        in_specs=[WHOLE] * (1 + chips),
        out_specs=[WHOLE] * 3,
        out_shape=[block, block, jax.ShapeDtypeStruct((2, rows, columns), BF16)],
        scratch_shapes=[pltpu.VMEM((rows, depth), BF16)],
        compiler_params=pltpu.CompilerParams(vmem_limit_bytes=8 * 2**20),
        name="project",
    )(weight, *gated)


def finish_kernel(chips, pieces, *refs):
    keep_refs, first_refs, second_refs = refs[:pieces], refs[pieces : 2 * pieces], refs[2 * pieces : 3 * pieces]
    out_refs = refs[3 * pieces :]
    chip, _ = own_place()
    step = keep_refs[0].shape[0] // chips
    for offset in range(chips):
        here = block_at(chip ^ offset, step)
        for part in range(pieces):
            total = keep_refs[part][here, :].astype(F32) + first_refs[part][0, here, :].astype(F32)
            total = total + second_refs[part][here, :].astype(F32)
            out_refs[offset][pl.ds(part * step, step), :] = total.astype(BF16)


def finish(keep, first, second, chips):
    pieces = len(keep)
    rows, columns = keep[0].shape
    return pl.pallas_call(
        functools.partial(finish_kernel, chips, pieces),
        in_specs=[WHOLE] * (3 * pieces),
        out_specs=[WHOLE] * chips,
        out_shape=[jax.ShapeDtypeStruct((rows * pieces // chips, columns), BF16)] * chips,
        compiler_params=pltpu.CompilerParams(vmem_limit_bytes=4 * 2**20),
        name="finish",
    )(*keep, *first, *second)


def join_kernel(chips, *refs):
    in_refs, out_ref = refs[:chips], refs[chips]
    chip, _ = own_place()
    columns = in_refs[0].shape[1]
    for offset in range(chips):
        out_ref[:, block_at(chip ^ offset, columns)] = in_refs[offset][...]


def join(blocks):
    chips = len(blocks)
    rows, columns = blocks[0].shape
    return pl.pallas_call(
        functools.partial(join_kernel, chips),
        in_specs=[WHOLE] * chips,
        out_specs=WHOLE,
        out_shape=jax.ShapeDtypeStruct((rows, chips * columns), BF16),
        compiler_params=pltpu.CompilerParams(vmem_limit_bytes=2 * 2**20),
        name="join",
    )(*blocks)


def swapped(value, axis, offset):
    if not offset:
        return value
    return lax.ppermute(value, axis, [(source, source ^ offset) for source in range(lax.axis_size(axis))])


def to_chips(blocks):
    return [swapped(block, "seq", 2 * offset) for offset, block in enumerate(blocks)]


def shards_direct(values_in, gate_values, filter_spectrum, skip_gain, out_weight):
    parts = lax.axis_size("seq")
    layers = lax.axis_size("chan")
    chips = parts // 2
    pieces = 2
    early = layers // 2
    rows, width = values_in.shape
    device = lax.axis_index("seq")
    tables = small_tables(parts, rows)

    signals = to_chips(pack_signals(values_in, gate_values, chips))
    flat_filters = filter_spectrum.reshape(4, rows, width)
    filters = to_chips([pack_filter(flat_filters, chips, offset) for offset in range(chips)])

    share = out_weight.shape[1] // layers
    sent = [lax.dynamic_slice_in_dim(out_weight, (device // 2 ^ step) * share, share, 1) for step in range(layers)]

    def weights_from(step, block):
        pairs = [(source, source % 2 * layers + (source // 2 ^ step)) for source in range(parts)]
        return lax.ppermute(block, "seq", pairs)

    own_weight = [weights_from(step, sent[step]) for step in range(early)]

    own = jnp.stack([block[0] for block in signals])
    spectrum = forward(own, swapped(own, "seq", 1), tables)
    keep, send = backward(spectrum, filters, tables)
    late = lax.optimization_barrier((send, *sent[early:]))
    send = late[0]
    own_weight += [weights_from(early + step, block) for step, block in enumerate(late[1:])]
    weight = arrange(own_weight, [swapped(block, "seq", 1) for block in own_weight])
    gated = gate(skip_gain[None, :], keep, swapped(send, "seq", 1), signals, pieces)

    kept, firsts, seconds = [], [], []
    for piece in gated:
        keep, passed, send = project(weight, to_chips([piece] * chips))
        first = swapped(send, "chan", 1)
        passed = (passed.astype(F32) + first[1].astype(F32)).astype(BF16)
        kept.append(keep)
        firsts.append(first)
        seconds.append(swapped(passed, "chan", 2))
    return join(to_chips(finish(kept, firsts, seconds, chips)))


def shards(values_in, gate_values, filter_spectrum, skip_gain, out_weight):
    parts, layers = lax.axis_size("seq"), lax.axis_size("chan")
    rows, width = values_in.shape
    share = out_weight.shape[1] // layers
    aligned = width // parts % 128 == 0 and share % 128 == 0 and rows % 32 == 0
    run = shards_direct if aligned and layers == 4 and parts == 8 else shards_general
    return run(values_in, gate_values, filter_spectrum, skip_gain, out_weight)


def solution(mesh):
    in_specs = (
        P("seq", "chan"),
        P("seq", "chan"),
        P(None, "seq", None, "chan"),
        P("chan"),
        P("chan", "seq"),
    )
    out_specs = P("seq", "chan")
    return jax.shard_map(shards, mesh=mesh, in_specs=in_specs, out_specs=out_specs, check_vma=False)
```

```python
import functools

import jax
import jax.numpy as jnp
import numpy as np
from jax import lax
from jax.experimental import pallas as pl
from jax.experimental.pallas import tpu as pltpu
from jax.sharding import PartitionSpec as P

BF16 = jnp.bfloat16
F32 = jnp.float32


def bit_reversed(number, width_bits):
    flipped = 0
    for bit_place in range(width_bits):
        flipped |= (number >> bit_place & 1) << (width_bits - 1 - bit_place)
    return flipped


def filter_row(residue, width_bits):
    return 2 * bit_reversed(residue // 2, width_bits) + residue % 2


def dft_tables(parts, rows):
    total = 2 * parts * rows
    residue = np.arange(2 * parts)[:, None, None]
    column = np.arange(rows)[None, :, None]
    position = np.arange(rows)[None, None, :]
    phase = 2.0 * np.pi * (position * (residue + 2 * parts * column) % total) / total
    cos, sin = np.cos(phase), np.sin(phase)
    forward = np.concatenate(
        [np.concatenate([cos, sin], axis=2), np.concatenate([-sin, cos], axis=2)], axis=1
    )
    inverse = np.transpose(forward, (0, 2, 1)) / total
    return forward.astype(BF16), inverse.astype(BF16)


def convolve_kernel(parts, rows, moved_ref, skip_ref, forward_ref, inverse_ref, out_ref, waves_ref, back_ref):
    width_bits = parts.bit_length() - 1
    chunk = 16

    def cosine(residue, block):
        return float(np.cos(np.pi * residue * block / parts))

    def sine(residue, block):
        return float(np.sin(np.pi * residue * block / parts))

    def spread(index, carry):
        here = pl.ds(index * chunk, chunk)
        there = pl.ds(rows + index * chunk, chunk)
        blocks = [moved_ref[block, here, :].astype(F32) for block in range(parts)]
        for residue in range(parts + 1):
            real = blocks[0]
            imag = jnp.zeros_like(real)
            for block in range(1, parts):
                real = real + cosine(residue, block) * blocks[block]
                imag = imag - sine(residue, block) * blocks[block]
            waves_ref[residue, here, :] = real.astype(BF16)
            waves_ref[residue, there, :] = imag.astype(BF16)
            if 0 < residue < parts:
                waves_ref[2 * parts - residue, here, :] = real.astype(BF16)
                waves_ref[2 * parts - residue, there, :] = (-imag).astype(BF16)
        return carry

    lax.fori_loop(0, rows // chunk, spread, 0)

    def through(residue):
        wave = jnp.dot(forward_ref[residue], waves_ref[residue], preferred_element_type=F32)
        source, odd = divmod(filter_row(residue, width_bits), 2)
        filter_real = moved_ref[source, pl.ds((2 + odd) * rows, rows), :].astype(F32)
        filter_imag = moved_ref[source, pl.ds((4 + odd) * rows, rows), :].astype(F32)
        real, imag = wave[:rows], wave[rows:]
        product = jnp.concatenate(
            [real * filter_real - imag * filter_imag, real * filter_imag + imag * filter_real], axis=0
        )
        return jnp.dot(inverse_ref[residue], product.astype(BF16), preferred_element_type=F32)

    for residue in range(parts + 1):
        back = through(residue)
        if 0 < residue < parts:
            other = through(2 * parts - residue)
            back_ref[residue, pl.ds(0, rows), :] = back[:rows] + other[:rows]
            back_ref[residue, pl.ds(rows, rows), :] = back[rows:] - other[rows:]
        else:
            back_ref[residue] = back

    skip = skip_ref[...]

    def gather(index, carry):
        here = pl.ds(index * chunk, chunk)
        there = pl.ds(rows + index * chunk, chunk)
        reals = [back_ref[residue, here, :] for residue in range(parts + 1)]
        imags = [back_ref[residue, there, :] for residue in range(parts + 1)]
        for block in range(parts):
            total = reals[0]
            for residue in range(1, parts + 1):
                total = total + cosine(residue, block) * reals[residue]
                if residue < parts and block:
                    total = total - sine(residue, block) * imags[residue]
            signal = moved_ref[block, here, :].astype(F32)
            gate = moved_ref[block, pl.ds(rows + index * chunk, chunk), :].astype(F32)
            out_ref[block, here, :] = (gate * (total + skip * signal)).astype(BF16)
        return carry

    lax.fori_loop(0, rows // chunk, gather, 0)


def convolve(moved, skip):
    parts, stacked, width = moved.shape
    rows = stacked // 6
    forward, inverse = dft_tables(parts, rows)
    whole = pl.BlockSpec(memory_space=pltpu.VMEM)
    return pl.pallas_call(
        functools.partial(convolve_kernel, parts, rows),
        out_shape=jax.ShapeDtypeStruct((parts, rows, width), BF16),
        in_specs=[whole] * 4,
        out_specs=whole,
        scratch_shapes=[
            pltpu.VMEM((2 * parts, 2 * rows, width), BF16),
            pltpu.VMEM((parts + 1, 2 * rows, width), F32),
        ],
        compiler_params=pltpu.CompilerParams(vmem_limit_bytes=40 * 2**20),
    )(moved, skip[None, :], forward, inverse)


def shards_general(values_in, gate_values, filter_spectrum, skip_gain, out_weight):
    parts = lax.axis_size("seq")
    layers = lax.axis_size("chan")
    rows, width = values_in.shape
    lanes = width // parts
    device = lax.axis_index("seq")

    def by_channel(array):
        return jnp.transpose(array.reshape(array.shape[0], parts, lanes), (1, 0, 2))

    filters = filter_spectrum.astype(BF16).reshape(4 * rows, width)
    packed = jnp.concatenate([by_channel(values_in), by_channel(gate_values), by_channel(filters)], axis=1)
    moved = lax.all_to_all(packed, "seq", 0, 0)
    skip = lax.dynamic_slice_in_dim(skip_gain, device * lanes, lanes)
    gated = convolve(moved, skip)
    gathered = lax.all_gather(gated.reshape(parts * rows, lanes), "seq", axis=1, tiled=True)

    own_cols = out_weight.shape[1]
    share = own_cols * parts // layers // parts
    per_block = parts // layers
    pieces = own_cols // share
    group = device % per_block
    member = device // per_block
    weight = jnp.zeros_like(out_weight)
    for step in range(pieces):
        piece = (member + step) % pieces
        sent = lax.dynamic_slice_in_dim(out_weight, piece * share, share, 1)
        pairs = [
            (source, source % per_block * pieces + (source // per_block + step) % pieces) for source in range(parts)
        ]
        arrived = lax.ppermute(sent, "seq", pairs)
        block = (device % pieces - step) % pieces
        weight = lax.dynamic_update_slice_in_dim(weight, arrived, block * share, 1)
    partials = jnp.dot(gathered, weight, preferred_element_type=F32).astype(BF16)
    mixed = lax.psum_scatter(partials, "chan", scatter_dimension=1, tiled=True)
    return lax.all_to_all(mixed, "seq", 0, 1, tiled=True)


WHOLE = pl.BlockSpec(memory_space=pltpu.VMEM)


def small_tables(parts, rows):
    total = 2 * parts * rows
    index = np.arange(rows)
    phase = 2.0 * np.pi * (index[:, None] * index[None, :] % rows) / rows
    cos, sin = np.cos(phase), np.sin(phase)
    forward = np.block([[cos, sin], [-sin, cos]])
    residue = np.arange(2 * parts).reshape(2, 1, parts)
    turn = 2.0 * np.pi * index[None, :, None] * residue / total
    return forward.astype(BF16), forward.T.astype(BF16), np.cos(turn).astype(F32), np.sin(turn).astype(F32)


def cosine(parts, residue, block):
    return float(np.cos(np.pi * residue * block / parts))


def sine(parts, residue, block):
    return float(np.sin(np.pi * residue * block / parts))


def weighted(terms):
    total = None
    for factor, term in terms:
        if abs(factor) < 1e-12:
            continue
        part = term if factor == 1.0 else factor * term
        total = part if total is None else total + part
    return total


def plus(left, right):
    return left if right is None else right if left is None else left + right


def minus(left, right):
    return left if right is None else -right if left is None else left - right


def own_place():
    device = lax.axis_index("seq")
    return device // 2, device % 2


def block_at(index, size):
    return pl.ds(pl.multiple_of(index * size, size), size)


def pack_signals_kernel(chips, values_ref, gate_ref, *refs):
    out_refs, arrived = refs[:chips], refs[chips]
    chip, _ = own_place()
    lanes = out_refs[0].shape[2]
    copies = []
    for offset in range(chips):
        here = block_at(chip ^ offset, lanes)
        for plane, in_ref in enumerate((values_ref, gate_ref)):
            copies.append(
                pltpu.make_async_copy(in_ref.at[:, here], out_refs[offset].at[plane], arrived.at[offset, plane])
            )
    for copy in copies:
        copy.start()
    for copy in copies:
        copy.wait()


def pack_signals(values_in, gate_values, chips):
    rows, width = values_in.shape
    return pl.pallas_call(
        functools.partial(pack_signals_kernel, chips),
        in_specs=[pl.BlockSpec(memory_space=pltpu.HBM)] * 2,
        out_specs=[WHOLE] * chips,
        out_shape=[jax.ShapeDtypeStruct((2, rows, width // chips), BF16)] * chips,
        scratch_shapes=[pltpu.SemaphoreType.DMA((chips, 2))],
        compiler_params=pltpu.CompilerParams(vmem_limit_bytes=4 * 2**20),
        name="pack_signals",
    )(values_in, gate_values)


def pack_filters_kernel(chips, filter_ref, *refs):
    out_refs, (plane_ref, arrived) = refs[:chips], refs[chips:]
    chip, _ = own_place()
    planes, _, lanes = out_refs[0].shape
    order = [(offset, plane) for offset in reversed(range(chips)) for plane in range(planes)]
    copies = [
        pltpu.make_async_copy(
            filter_ref.at[plane, :, block_at(chip ^ offset, lanes)],
            plane_ref.at[offset, plane],
            arrived.at[offset, plane],
        )
        for offset, plane in order
    ]
    for copy in copies:
        copy.start()
    for (offset, plane), copy in zip(order, copies):
        copy.wait()
        out_refs[offset][plane] = plane_ref[offset, plane].astype(BF16)


def pack_filters(filters, chips):
    planes, rows, width = filters.shape
    shape = (planes, rows, width // chips)
    return pl.pallas_call(
        functools.partial(pack_filters_kernel, chips),
        in_specs=[pl.BlockSpec(memory_space=pltpu.HBM)],
        out_specs=[WHOLE] * chips,
        out_shape=[jax.ShapeDtypeStruct(shape, BF16)] * chips,
        scratch_shapes=[pltpu.VMEM((chips, *shape), F32), pltpu.SemaphoreType.DMA((chips, planes))],
        compiler_params=pltpu.CompilerParams(vmem_limit_bytes=8 * 2**20),
        name="pack_filters",
    )(filters)


def forward_kernel(chips, cos_ref, sin_ref, table_ref, own_ref, other_ref, out_ref, signal_ref, waves_ref):
    chip, core = own_place()
    parts = 2 * chips
    rows, lanes = own_ref.shape[1:]
    chunk, width = 16, 128
    for offset in range(chips):
        signal_ref[2 * (chip ^ offset) + core] = own_ref[offset]
        signal_ref[2 * (chip ^ offset) + 1 - core] = other_ref[offset]
    sign = (1 - 2 * core).astype(F32)

    def spread(index, carry):
        here = block_at(index, chunk)
        there = pl.ds(pl.multiple_of(rows + index * chunk, chunk), chunk)
        cos_all, sin_all = cos_ref[core, here, :], sin_ref[core, here, :]
        for start in range(0, lanes, width):
            blocks = [signal_ref[block, here, pl.ds(start, width)].astype(F32) for block in range(parts)]
            blocks = [block * sign if place % 2 else block for place, block in enumerate(blocks)]

            def store(residue, real, imag):
                cos, sin = cos_all[:, residue : residue + 1], sin_all[:, residue : residue + 1]
                if imag is None:
                    real, imag = real * cos, -(real * sin)
                else:
                    real, imag = real * cos + imag * sin, imag * cos - real * sin
                columns = pl.ds(residue * lanes + start, width)
                waves_ref[here, columns] = real.astype(BF16)
                waves_ref[there, columns] = imag.astype(BF16)

            for residue in range(parts // 2 + 1):
                even, odd = range(0, parts, 2), range(1, parts, 2)
                cos_even = weighted([(cosine(parts, residue, block), blocks[block]) for block in even])
                cos_odd = weighted([(cosine(parts, residue, block), blocks[block]) for block in odd])
                sin_even = weighted([(sine(parts, residue, block), blocks[block]) for block in even])
                sin_odd = weighted([(sine(parts, residue, block), blocks[block]) for block in odd])
                sin_sum = plus(sin_even, sin_odd)
                store(residue, plus(cos_even, cos_odd), None if sin_sum is None else -sin_sum)
                if 0 < residue and 2 * residue != parts:
                    store(parts - residue, minus(cos_even, cos_odd), minus(sin_even, sin_odd))
        return carry

    lax.fori_loop(0, rows // chunk, spread, 0)
    for residue in range(parts):
        columns = pl.ds(residue * lanes, lanes)
        out_ref[:, columns] = jnp.dot(table_ref[...], waves_ref[:, columns], preferred_element_type=F32)


def forward(own, other, tables):
    chips, rows, lanes = own.shape
    table, _, cos, sin = tables
    spectrum = (2 * rows, 2 * chips * lanes)
    return pl.pallas_call(
        functools.partial(forward_kernel, chips),
        in_specs=[WHOLE] * 5,
        out_specs=WHOLE,
        out_shape=jax.ShapeDtypeStruct(spectrum, F32),
        scratch_shapes=[pltpu.VMEM((2 * chips, rows, lanes), BF16), pltpu.VMEM(spectrum, BF16)],
        compiler_params=pltpu.CompilerParams(vmem_limit_bytes=32 * 2**20),
        name="forward",
    )(cos, sin, table, own, other)


def backward_kernel(chips, cos_ref, sin_ref, table_ref, spectrum_ref, *refs):
    filter_refs, (keep_ref, send_ref, filter_ref, product_ref, back_ref) = refs[:chips], refs[chips:]
    chip, core = own_place()
    parts = 2 * chips
    rows, lanes = keep_ref.shape[1:]
    chip_bits = chips.bit_length() - 1
    chunk, width = 16, 128
    for offset in range(chips):
        filter_ref[chip ^ offset] = filter_refs[offset][...]

    for residue in range(parts):
        source, odd = bit_reversed(residue // 2, chip_bits), residue % 2
        columns = pl.ds(residue * lanes, lanes)
        filter_real = filter_ref[source, odd].astype(F32)
        filter_imag = filter_ref[source, 2 + odd].astype(F32)
        real = spectrum_ref[pl.ds(0, rows), columns]
        imag = spectrum_ref[pl.ds(rows, rows), columns]
        product_ref[pl.ds(0, rows), columns] = (real * filter_real - imag * filter_imag).astype(BF16)
        product_ref[pl.ds(rows, rows), columns] = (real * filter_imag + imag * filter_real).astype(BF16)
        back_ref[:, columns] = jnp.dot(table_ref[...], product_ref[:, columns], preferred_element_type=F32)

    scale = 1.0 / (2 * parts * rows)
    sign = (1 - 2 * core).astype(F32)
    upper = core == 1

    def gather(index, carry):
        here = block_at(index, chunk)
        there = pl.ds(pl.multiple_of(rows + index * chunk, chunk), chunk)
        cos_all, sin_all = cos_ref[core, here, :] * scale, sin_ref[core, here, :] * scale
        for start in range(0, lanes, width):
            reals, imags = [], []
            for residue in range(parts):
                columns = pl.ds(residue * lanes + start, width)
                real, imag = back_ref[here, columns], back_ref[there, columns]
                cos, sin = cos_all[:, residue : residue + 1], sin_all[:, residue : residue + 1]
                reals.append(real * cos - imag * sin)
                imags.append(real * sin + imag * cos)
            totals = [None] * parts
            for block in range(parts // 2 + 1):
                even, odd = range(0, parts, 2), range(1, parts, 2)
                cos_even = weighted([(cosine(parts, residue, block), reals[residue]) for residue in even])
                cos_odd = weighted([(cosine(parts, residue, block), reals[residue]) for residue in odd])
                sin_even = weighted([(sine(parts, residue, block), imags[residue]) for residue in even])
                sin_odd = weighted([(sine(parts, residue, block), imags[residue]) for residue in odd])
                totals[block] = minus(plus(cos_even, cos_odd), plus(sin_even, sin_odd))
                if 0 < block and 2 * block != parts:
                    totals[parts - block] = plus(minus(cos_even, cos_odd), minus(sin_even, sin_odd))
            lane = pl.ds(start, width)
            for pair in range(chips):
                low, high = totals[2 * pair], totals[2 * pair + 1] * sign
                keep_ref[pair, here, lane] = jnp.where(upper, high, low)
                send_ref[pair, here, lane] = jnp.where(upper, low, high).astype(BF16)
        return carry

    lax.fori_loop(0, rows // chunk, gather, 0)


def backward(spectrum, filters, tables):
    chips = len(filters)
    planes, rows, lanes = filters[0].shape
    _, table, cos, sin = tables
    kept = (chips, rows, lanes)
    return pl.pallas_call(
        functools.partial(backward_kernel, chips),
        in_specs=[WHOLE] * (4 + chips),
        out_specs=[WHOLE] * 2,
        out_shape=[jax.ShapeDtypeStruct(kept, F32), jax.ShapeDtypeStruct(kept, BF16)],
        scratch_shapes=[
            pltpu.VMEM((chips, planes, rows, lanes), BF16),
            pltpu.VMEM(spectrum.shape, BF16),
            pltpu.VMEM(spectrum.shape, F32),
        ],
        compiler_params=pltpu.CompilerParams(vmem_limit_bytes=32 * 2**20),
        name="backward",
    )(cos, sin, table, spectrum, *filters)


def gate_kernel(chips, skip_ref, keep_ref, arrived_ref, *refs):
    signal_refs, out_ref = refs[:chips], refs[chips]
    chip, _ = own_place()
    rows, lanes = keep_ref.shape[1:]
    pieces = out_ref.shape[0]
    step = rows // pieces
    skip = skip_ref[:, block_at(chip, lanes)]
    for offset in range(chips):
        block = chip ^ offset
        for piece in range(pieces):
            here = pl.ds(piece * step, step)
            convolved = keep_ref[block, here, :] + arrived_ref[block, here, :].astype(F32)
            signal = signal_refs[offset][0, here, :].astype(F32)
            gate = signal_refs[offset][1, here, :].astype(F32)
            out_ref[piece, block_at(block, step), :] = (gate * (convolved + skip * signal)).astype(BF16)


def gate(skip, keep, arrived, signals, pieces):
    chips, rows, lanes = keep.shape
    return pl.pallas_call(
        functools.partial(gate_kernel, chips),
        in_specs=[WHOLE] * (3 + chips),
        out_specs=WHOLE,
        out_shape=jax.ShapeDtypeStruct((pieces, chips * rows // pieces, lanes), BF16),
        compiler_params=pltpu.CompilerParams(vmem_limit_bytes=6 * 2**20),
        name="gate",
    )(skip, keep, arrived, *signals)


def arrange_kernel(layers, *refs):
    own_refs, other_refs, out_ref = refs[:layers], refs[layers : 2 * layers], refs[2 * layers]
    device, layer = lax.axis_index("seq"), lax.axis_index("chan")
    share = own_refs[0].shape[1]
    for step in range(layers):
        target = device % layers ^ layer ^ step
        out_ref[target, :, block_at(device % 2, share)] = own_refs[step][...]
        out_ref[target, :, block_at(1 - device % 2, share)] = other_refs[step ^ 1][...]


def arrange(own, other):
    layers = len(own)
    rows, share = own[0].shape
    return pl.pallas_call(
        functools.partial(arrange_kernel, layers),
        in_specs=[WHOLE] * (2 * layers),
        out_specs=WHOLE,
        out_shape=jax.ShapeDtypeStruct((layers, rows, 2 * share), BF16),
        compiler_params=pltpu.CompilerParams(vmem_limit_bytes=8 * 2**20),
        name="arrange_weights",
    )(*own, *other)


def project_kernel(chips, piece, weight_ref, *refs):
    gated_refs, (keep_ref, pass_ref, send_ref, joined_ref) = refs[:chips], refs[chips:]
    chip, _ = own_place()
    lanes = gated_refs[0].shape[2]
    for offset in range(chips):
        joined_ref[:, block_at(chip ^ offset, lanes)] = gated_refs[offset][piece]

    def partial_of(target):
        return jnp.dot(joined_ref[...], weight_ref[target], preferred_element_type=F32).astype(BF16)

    send_ref[0] = partial_of(1)
    send_ref[1] = partial_of(3)
    pass_ref[...] = partial_of(2)
    keep_ref[...] = partial_of(0)


def project(weight, gated, piece):
    chips = len(gated)
    _, depth, columns = weight.shape
    rows = gated[0].shape[1]
    block = jax.ShapeDtypeStruct((rows, columns), BF16)
    return pl.pallas_call(
        functools.partial(project_kernel, chips, piece),
        in_specs=[WHOLE] * (1 + chips),
        out_specs=[WHOLE] * 3,
        out_shape=[block, block, jax.ShapeDtypeStruct((2, rows, columns), BF16)],
        scratch_shapes=[pltpu.VMEM((rows, depth), BF16)],
        compiler_params=pltpu.CompilerParams(vmem_limit_bytes=8 * 2**20),
        name="project",
    )(weight, *gated)


def finish_kernel(chips, pieces, *refs):
    keep_refs, first_refs, second_refs = refs[:pieces], refs[pieces : 2 * pieces], refs[2 * pieces : 3 * pieces]
    out_refs = refs[3 * pieces :]
    chip, _ = own_place()
    step = keep_refs[0].shape[0] // chips
    for offset in range(chips):
        here = block_at(chip ^ offset, step)
        for part in range(pieces):
            total = keep_refs[part][here, :].astype(F32) + first_refs[part][0, here, :].astype(F32)
            total = total + second_refs[part][here, :].astype(F32)
            out_refs[offset][pl.ds(part * step, step), :] = total.astype(BF16)


def finish(keep, first, second, chips):
    pieces = len(keep)
    rows, columns = keep[0].shape
    return pl.pallas_call(
        functools.partial(finish_kernel, chips, pieces),
        in_specs=[WHOLE] * (3 * pieces),
        out_specs=[WHOLE] * chips,
        out_shape=[jax.ShapeDtypeStruct((rows * pieces // chips, columns), BF16)] * chips,
        compiler_params=pltpu.CompilerParams(vmem_limit_bytes=4 * 2**20),
        name="finish",
    )(*keep, *first, *second)


def join_kernel(chips, *refs):
    in_refs, out_ref = refs[:chips], refs[chips]
    chip, _ = own_place()
    columns = in_refs[0].shape[1]
    for offset in range(chips):
        out_ref[:, block_at(chip ^ offset, columns)] = in_refs[offset][...]


def join(blocks):
    chips = len(blocks)
    rows, columns = blocks[0].shape
    return pl.pallas_call(
        functools.partial(join_kernel, chips),
        in_specs=[WHOLE] * chips,
        out_specs=WHOLE,
        out_shape=jax.ShapeDtypeStruct((rows, chips * columns), BF16),
        compiler_params=pltpu.CompilerParams(vmem_limit_bytes=2 * 2**20),
        name="join",
    )(*blocks)


def swapped(value, axis, offset):
    if not offset:
        return value
    return lax.ppermute(value, axis, [(source, source ^ offset) for source in range(lax.axis_size(axis))])


def to_chips(blocks):
    return [swapped(block, "seq", 2 * offset) for offset, block in enumerate(blocks)]


def after(value, *others):
    return lax.optimization_barrier((value, *others))[0]


def shards_direct(values_in, gate_values, filter_spectrum, skip_gain, out_weight):
    parts = lax.axis_size("seq")
    layers = lax.axis_size("chan")
    chips = parts // 2
    pieces = 2
    rows, width = values_in.shape
    device = lax.axis_index("seq")
    tables = small_tables(parts, rows)

    signals = pack_signals(values_in, gate_values, chips)
    filters = pack_filters(after(filter_spectrum.reshape(4, rows, width), signals[0]), chips)
    signals = to_chips(signals)
    own = jnp.stack([after(block, filters[0])[0] for block in signals])
    filters = to_chips(filters)
    spectrum = forward(own, swapped(own, "seq", 1), tables)
    keep, send = backward(spectrum, filters, tables)
    gated = gate(skip_gain[None, :], keep, swapped(send, "seq", 1), signals, pieces)

    share = out_weight.shape[1] // layers
    sent = [
        lax.dynamic_slice_in_dim(after(out_weight, own), (device // 2 ^ step) * share, share, 1)
        for step in range(layers)
    ]
    own_weight = []
    for step, earlier in enumerate((spectrum, send, send, gated)):
        pairs = [(source, source % 2 * layers + (source // 2 ^ step)) for source in range(parts)]
        own_weight.append(lax.ppermute(after(sent[step], earlier), "seq", pairs))
    weight = arrange(own_weight, [swapped(after(block, gated), "seq", 1) for block in own_weight])

    gathered = to_chips([gated] * chips)
    kept, firsts, seconds = [], [], []
    for piece in range(pieces):
        keep, passed, send = project(weight, gathered, piece)
        first = swapped(send, "chan", 1)
        passed = (passed.astype(F32) + first[1].astype(F32)).astype(BF16)
        kept.append(keep)
        firsts.append(first)
        seconds.append(swapped(passed, "chan", 2))
    return join(to_chips(finish(kept, firsts, seconds, chips)))


def shards(values_in, gate_values, filter_spectrum, skip_gain, out_weight):
    parts, layers = lax.axis_size("seq"), lax.axis_size("chan")
    rows, width = values_in.shape
    share = out_weight.shape[1] // layers
    aligned = width // parts % 128 == 0 and share % 128 == 0 and rows % 32 == 0
    run = shards_direct if aligned and layers == 4 and parts == 8 else shards_general
    return run(values_in, gate_values, filter_spectrum, skip_gain, out_weight)


def solution(mesh):
    in_specs = (
        P("seq", "chan"),
        P("seq", "chan"),
        P(None, "seq", None, "chan"),
        P("chan"),
        P("chan", "seq"),
    )
    out_specs = P("seq", "chan")
    return jax.shard_map(shards, mesh=mesh, in_specs=in_specs, out_specs=out_specs, check_vma=False)
```

```python
import functools

import jax
import jax.numpy as jnp
import numpy as np
from jax import lax
from jax.experimental import pallas as pl
from jax.experimental.pallas import tpu as pltpu
from jax.sharding import PartitionSpec as P

BF16 = jnp.bfloat16
F32 = jnp.float32


def bit_reversed(number, width_bits):
    flipped = 0
    for bit_place in range(width_bits):
        flipped |= (number >> bit_place & 1) << (width_bits - 1 - bit_place)
    return flipped


def filter_row(residue, width_bits):
    return 2 * bit_reversed(residue // 2, width_bits) + residue % 2


def dft_tables(parts, rows):
    total = 2 * parts * rows
    residue = np.arange(2 * parts)[:, None, None]
    column = np.arange(rows)[None, :, None]
    position = np.arange(rows)[None, None, :]
    phase = 2.0 * np.pi * (position * (residue + 2 * parts * column) % total) / total
    cos, sin = np.cos(phase), np.sin(phase)
    forward = np.concatenate(
        [np.concatenate([cos, sin], axis=2), np.concatenate([-sin, cos], axis=2)], axis=1
    )
    inverse = np.transpose(forward, (0, 2, 1)) / total
    return forward.astype(BF16), inverse.astype(BF16)


def convolve_kernel(parts, rows, moved_ref, skip_ref, forward_ref, inverse_ref, out_ref, waves_ref, back_ref):
    width_bits = parts.bit_length() - 1
    chunk = 16

    def cosine(residue, block):
        return float(np.cos(np.pi * residue * block / parts))

    def sine(residue, block):
        return float(np.sin(np.pi * residue * block / parts))

    def spread(index, carry):
        here = pl.ds(index * chunk, chunk)
        there = pl.ds(rows + index * chunk, chunk)
        blocks = [moved_ref[block, here, :].astype(F32) for block in range(parts)]
        for residue in range(parts + 1):
            real = blocks[0]
            imag = jnp.zeros_like(real)
            for block in range(1, parts):
                real = real + cosine(residue, block) * blocks[block]
                imag = imag - sine(residue, block) * blocks[block]
            waves_ref[residue, here, :] = real.astype(BF16)
            waves_ref[residue, there, :] = imag.astype(BF16)
            if 0 < residue < parts:
                waves_ref[2 * parts - residue, here, :] = real.astype(BF16)
                waves_ref[2 * parts - residue, there, :] = (-imag).astype(BF16)
        return carry

    lax.fori_loop(0, rows // chunk, spread, 0)

    def through(residue):
        wave = jnp.dot(forward_ref[residue], waves_ref[residue], preferred_element_type=F32)
        source, odd = divmod(filter_row(residue, width_bits), 2)
        filter_real = moved_ref[source, pl.ds((2 + odd) * rows, rows), :].astype(F32)
        filter_imag = moved_ref[source, pl.ds((4 + odd) * rows, rows), :].astype(F32)
        real, imag = wave[:rows], wave[rows:]
        product = jnp.concatenate(
            [real * filter_real - imag * filter_imag, real * filter_imag + imag * filter_real], axis=0
        )
        return jnp.dot(inverse_ref[residue], product.astype(BF16), preferred_element_type=F32)

    for residue in range(parts + 1):
        back = through(residue)
        if 0 < residue < parts:
            other = through(2 * parts - residue)
            back_ref[residue, pl.ds(0, rows), :] = back[:rows] + other[:rows]
            back_ref[residue, pl.ds(rows, rows), :] = back[rows:] - other[rows:]
        else:
            back_ref[residue] = back

    skip = skip_ref[...]

    def gather(index, carry):
        here = pl.ds(index * chunk, chunk)
        there = pl.ds(rows + index * chunk, chunk)
        reals = [back_ref[residue, here, :] for residue in range(parts + 1)]
        imags = [back_ref[residue, there, :] for residue in range(parts + 1)]
        for block in range(parts):
            total = reals[0]
            for residue in range(1, parts + 1):
                total = total + cosine(residue, block) * reals[residue]
                if residue < parts and block:
                    total = total - sine(residue, block) * imags[residue]
            signal = moved_ref[block, here, :].astype(F32)
            gate = moved_ref[block, pl.ds(rows + index * chunk, chunk), :].astype(F32)
            out_ref[block, here, :] = (gate * (total + skip * signal)).astype(BF16)
        return carry

    lax.fori_loop(0, rows // chunk, gather, 0)


def convolve(moved, skip):
    parts, stacked, width = moved.shape
    rows = stacked // 6
    forward, inverse = dft_tables(parts, rows)
    whole = pl.BlockSpec(memory_space=pltpu.VMEM)
    return pl.pallas_call(
        functools.partial(convolve_kernel, parts, rows),
        out_shape=jax.ShapeDtypeStruct((parts, rows, width), BF16),
        in_specs=[whole] * 4,
        out_specs=whole,
        scratch_shapes=[
            pltpu.VMEM((2 * parts, 2 * rows, width), BF16),
            pltpu.VMEM((parts + 1, 2 * rows, width), F32),
        ],
        compiler_params=pltpu.CompilerParams(vmem_limit_bytes=40 * 2**20),
    )(moved, skip[None, :], forward, inverse)


def shards_general(values_in, gate_values, filter_spectrum, skip_gain, out_weight):
    parts = lax.axis_size("seq")
    layers = lax.axis_size("chan")
    rows, width = values_in.shape
    lanes = width // parts
    device = lax.axis_index("seq")

    def by_channel(array):
        return jnp.transpose(array.reshape(array.shape[0], parts, lanes), (1, 0, 2))

    filters = filter_spectrum.astype(BF16).reshape(4 * rows, width)
    packed = jnp.concatenate([by_channel(values_in), by_channel(gate_values), by_channel(filters)], axis=1)
    moved = lax.all_to_all(packed, "seq", 0, 0)
    skip = lax.dynamic_slice_in_dim(skip_gain, device * lanes, lanes)
    gated = convolve(moved, skip)
    gathered = lax.all_gather(gated.reshape(parts * rows, lanes), "seq", axis=1, tiled=True)

    own_cols = out_weight.shape[1]
    share = own_cols * parts // layers // parts
    per_block = parts // layers
    pieces = own_cols // share
    group = device % per_block
    member = device // per_block
    weight = jnp.zeros_like(out_weight)
    for step in range(pieces):
        piece = (member + step) % pieces
        sent = lax.dynamic_slice_in_dim(out_weight, piece * share, share, 1)
        pairs = [
            (source, source % per_block * pieces + (source // per_block + step) % pieces) for source in range(parts)
        ]
        arrived = lax.ppermute(sent, "seq", pairs)
        block = (device % pieces - step) % pieces
        weight = lax.dynamic_update_slice_in_dim(weight, arrived, block * share, 1)
    partials = jnp.dot(gathered, weight, preferred_element_type=F32).astype(BF16)
    mixed = lax.psum_scatter(partials, "chan", scatter_dimension=1, tiled=True)
    return lax.all_to_all(mixed, "seq", 0, 1, tiled=True)


WHOLE = pl.BlockSpec(memory_space=pltpu.VMEM)
CHEAP = pl.CostEstimate(flops=0, transcendentals=0, bytes_accessed=0)


def small_tables(parts, rows):
    total = 2 * parts * rows
    index = np.arange(rows)
    phase = 2.0 * np.pi * (index[:, None] * index[None, :] % rows) / rows
    cos, sin = np.cos(phase), np.sin(phase)
    forward = np.block([[cos, sin], [-sin, cos]])
    residue = np.arange(2 * parts).reshape(2, 1, parts)
    turn = 2.0 * np.pi * index[None, :, None] * residue / total
    return forward.astype(BF16), forward.T.astype(BF16), np.cos(turn).astype(F32), np.sin(turn).astype(F32)


def cosine(parts, residue, block):
    return float(np.cos(np.pi * residue * block / parts))


def sine(parts, residue, block):
    return float(np.sin(np.pi * residue * block / parts))


def weighted(terms):
    total = None
    for factor, term in terms:
        if abs(factor) < 1e-12:
            continue
        part = term if factor == 1.0 else factor * term
        total = part if total is None else total + part
    return total


def plus(left, right):
    return left if right is None else right if left is None else left + right


def minus(left, right):
    return left if right is None else -right if left is None else left - right


def own_place():
    device = lax.axis_index("seq")
    return device // 2, device % 2


def block_at(index, size):
    return pl.ds(pl.multiple_of(index * size, size), size)


def pack_kernel(chips, planes, signal_ref, filter_ref, *refs):
    out_refs, (plane_ref, arrived) = refs[:chips], refs[chips:]
    chip, _ = own_place()
    lanes = out_refs[0].shape[2]
    copies = []
    for offset in reversed(range(chips)):
        here = block_at(chip ^ offset, lanes)
        for place, plane in enumerate(planes):
            copies.append(
                pltpu.make_async_copy(
                    filter_ref.at[plane, :, here], plane_ref.at[offset, place], arrived.at[offset, 1 + place]
                )
            )
        copies.append(
            pltpu.make_async_copy(signal_ref.at[:, here], out_refs[offset].at[0], arrived.at[offset, 0])
        )
    for copy in copies:
        copy.start()
    for copy in copies:
        copy.wait()
    for offset in range(chips):
        for place in range(len(planes)):
            out_refs[offset][1 + place] = plane_ref[offset, place].astype(BF16)


def pack(signal, filters, chips, planes):
    rows, width = signal.shape
    lanes = width // chips
    return pl.pallas_call(
        functools.partial(pack_kernel, chips, planes),
        in_specs=[pl.BlockSpec(memory_space=pltpu.HBM)] * 2,
        out_specs=[WHOLE] * chips,
        out_shape=[jax.ShapeDtypeStruct((1 + len(planes), rows, lanes), BF16)] * chips,
        scratch_shapes=[
            pltpu.VMEM((chips, len(planes), rows, lanes), F32),
            pltpu.SemaphoreType.DMA((chips, 1 + len(planes))),
        ],
        cost_estimate=CHEAP,
        compiler_params=pltpu.CompilerParams(vmem_limit_bytes=8 * 2**20),
        name="pack",
    )(pltpu.with_memory_space_constraint(signal, pltpu.HBM), pltpu.with_memory_space_constraint(filters, pltpu.HBM))


def forward_kernel(chips, cos_ref, sin_ref, table_ref, own_ref, other_ref, out_ref, signal_ref, waves_ref):
    chip, core = own_place()
    parts = 2 * chips
    rows, lanes = own_ref.shape[1:]
    chunk, width = 16, 128
    for offset in range(chips):
        signal_ref[2 * (chip ^ offset) + core] = own_ref[offset]
        signal_ref[2 * (chip ^ offset) + 1 - core] = other_ref[offset]
    sign = (1 - 2 * core).astype(F32)

    def spread(index, carry):
        here = block_at(index, chunk)
        there = pl.ds(pl.multiple_of(rows + index * chunk, chunk), chunk)
        cos_all, sin_all = cos_ref[core, here, :], sin_ref[core, here, :]
        for start in range(0, lanes, width):
            blocks = [signal_ref[block, here, pl.ds(start, width)].astype(F32) for block in range(parts)]
            blocks = [block * sign if place % 2 else block for place, block in enumerate(blocks)]

            def store(residue, real, imag):
                cos, sin = cos_all[:, residue : residue + 1], sin_all[:, residue : residue + 1]
                if imag is None:
                    real, imag = real * cos, -(real * sin)
                else:
                    real, imag = real * cos + imag * sin, imag * cos - real * sin
                columns = pl.ds(residue * lanes + start, width)
                waves_ref[here, columns] = real.astype(BF16)
                waves_ref[there, columns] = imag.astype(BF16)

            for residue in range(parts // 2 + 1):
                even, odd = range(0, parts, 2), range(1, parts, 2)
                cos_even = weighted([(cosine(parts, residue, block), blocks[block]) for block in even])
                cos_odd = weighted([(cosine(parts, residue, block), blocks[block]) for block in odd])
                sin_even = weighted([(sine(parts, residue, block), blocks[block]) for block in even])
                sin_odd = weighted([(sine(parts, residue, block), blocks[block]) for block in odd])
                sin_sum = plus(sin_even, sin_odd)
                store(residue, plus(cos_even, cos_odd), None if sin_sum is None else -sin_sum)
                if 0 < residue and 2 * residue != parts:
                    store(parts - residue, minus(cos_even, cos_odd), minus(sin_even, sin_odd))
        return carry

    lax.fori_loop(0, rows // chunk, spread, 0)
    for residue in range(parts):
        columns = pl.ds(residue * lanes, lanes)
        out_ref[:, columns] = jnp.dot(table_ref[...], waves_ref[:, columns], preferred_element_type=F32)


def forward(own, other, tables):
    chips, rows, lanes = own.shape
    table, _, cos, sin = tables
    spectrum = (2 * rows, 2 * chips * lanes)
    return pl.pallas_call(
        functools.partial(forward_kernel, chips),
        in_specs=[WHOLE] * 5,
        out_specs=WHOLE,
        out_shape=jax.ShapeDtypeStruct(spectrum, F32),
        scratch_shapes=[pltpu.VMEM((2 * chips, rows, lanes), BF16), pltpu.VMEM(spectrum, BF16)],
        cost_estimate=CHEAP,
        compiler_params=pltpu.CompilerParams(vmem_limit_bytes=32 * 2**20),
        name="forward",
    )(cos, sin, table, own, other)


def backward_kernel(chips, cos_ref, sin_ref, table_ref, spectrum_ref, *refs):
    group_refs, (keep_ref, send_ref, filter_ref, product_ref, back_ref) = refs[: 2 * chips], refs[2 * chips :]
    chip, core = own_place()
    parts = 2 * chips
    rows, lanes = keep_ref.shape[1:]
    chip_bits = chips.bit_length() - 1
    chunk, width = 16, 128
    for odd in range(2):
        for offset in range(chips):
            filter_ref[chip ^ offset, odd] = group_refs[odd * chips + offset][pl.ds(1, 2)]

    for residue in range(parts):
        source, odd = bit_reversed(residue // 2, chip_bits), residue % 2
        columns = pl.ds(residue * lanes, lanes)
        filter_real = filter_ref[source, odd, 0].astype(F32)
        filter_imag = filter_ref[source, odd, 1].astype(F32)
        real = spectrum_ref[pl.ds(0, rows), columns]
        imag = spectrum_ref[pl.ds(rows, rows), columns]
        product_ref[pl.ds(0, rows), columns] = (real * filter_real - imag * filter_imag).astype(BF16)
        product_ref[pl.ds(rows, rows), columns] = (real * filter_imag + imag * filter_real).astype(BF16)
        back_ref[:, columns] = jnp.dot(table_ref[...], product_ref[:, columns], preferred_element_type=F32)

    scale = 1.0 / (2 * parts * rows)
    sign = (1 - 2 * core).astype(F32)
    upper = core == 1

    def gather(index, carry):
        here = block_at(index, chunk)
        there = pl.ds(pl.multiple_of(rows + index * chunk, chunk), chunk)
        cos_all, sin_all = cos_ref[core, here, :] * scale, sin_ref[core, here, :] * scale
        for start in range(0, lanes, width):
            reals, imags = [], []
            for residue in range(parts):
                columns = pl.ds(residue * lanes + start, width)
                real, imag = back_ref[here, columns], back_ref[there, columns]
                cos, sin = cos_all[:, residue : residue + 1], sin_all[:, residue : residue + 1]
                reals.append(real * cos - imag * sin)
                imags.append(real * sin + imag * cos)
            totals = [None] * parts
            for block in range(parts // 2 + 1):
                even, odd = range(0, parts, 2), range(1, parts, 2)
                cos_even = weighted([(cosine(parts, residue, block), reals[residue]) for residue in even])
                cos_odd = weighted([(cosine(parts, residue, block), reals[residue]) for residue in odd])
                sin_even = weighted([(sine(parts, residue, block), imags[residue]) for residue in even])
                sin_odd = weighted([(sine(parts, residue, block), imags[residue]) for residue in odd])
                totals[block] = minus(plus(cos_even, cos_odd), plus(sin_even, sin_odd))
                if 0 < block and 2 * block != parts:
                    totals[parts - block] = plus(minus(cos_even, cos_odd), minus(sin_even, sin_odd))
            lane = pl.ds(start, width)
            for pair in range(chips):
                low, high = totals[2 * pair], totals[2 * pair + 1] * sign
                keep_ref[pair, here, lane] = jnp.where(upper, high, low)
                send_ref[pair, here, lane] = jnp.where(upper, low, high).astype(BF16)
        return carry

    lax.fori_loop(0, rows // chunk, gather, 0)


def backward(spectrum, first, second, tables):
    chips = len(first)
    _, rows, lanes = first[0].shape
    _, table, cos, sin = tables
    kept = (chips, rows, lanes)
    return pl.pallas_call(
        functools.partial(backward_kernel, chips),
        in_specs=[WHOLE] * (4 + 2 * chips),
        out_specs=[WHOLE] * 2,
        out_shape=[jax.ShapeDtypeStruct(kept, F32), jax.ShapeDtypeStruct(kept, BF16)],
        scratch_shapes=[
            pltpu.VMEM((chips, 2, 2, rows, lanes), BF16),
            pltpu.VMEM(spectrum.shape, BF16),
            pltpu.VMEM(spectrum.shape, F32),
        ],
        cost_estimate=CHEAP,
        compiler_params=pltpu.CompilerParams(vmem_limit_bytes=32 * 2**20),
        name="backward",
    )(cos, sin, table, spectrum, *first, *second)


def gate_kernel(chips, skip_ref, keep_ref, arrived_ref, *refs):
    signal_refs, gate_refs, out_ref = refs[:chips], refs[chips : 2 * chips], refs[2 * chips]
    chip, _ = own_place()
    rows, lanes = keep_ref.shape[1:]
    pieces = out_ref.shape[0]
    step = rows // pieces
    skip = skip_ref[:, block_at(chip, lanes)]
    for offset in range(chips):
        block = chip ^ offset
        for piece in range(pieces):
            here = pl.ds(piece * step, step)
            convolved = keep_ref[block, here, :] + arrived_ref[block, here, :].astype(F32)
            signal = signal_refs[offset][0, here, :].astype(F32)
            gate = gate_refs[offset][0, here, :].astype(F32)
            out_ref[piece, block_at(block, step), :] = (gate * (convolved + skip * signal)).astype(BF16)


def gate(skip, keep, arrived, first, second, pieces):
    chips, rows, lanes = keep.shape
    return pl.pallas_call(
        functools.partial(gate_kernel, chips),
        in_specs=[WHOLE] * (3 + 2 * chips),
        out_specs=WHOLE,
        out_shape=jax.ShapeDtypeStruct((pieces, chips * rows // pieces, lanes), BF16),
        cost_estimate=CHEAP,
        compiler_params=pltpu.CompilerParams(vmem_limit_bytes=6 * 2**20),
        name="gate",
    )(skip, keep, arrived, *first, *second)


def collect_kernel(layers, *refs):
    in_refs, out_ref = refs[:layers], refs[layers]
    device, layer = lax.axis_index("seq"), lax.axis_index("chan")
    for step in range(layers):
        out_ref[device % layers ^ layer ^ step] = in_refs[step][...]


def collect(blocks):
    layers = len(blocks)
    return pl.pallas_call(
        functools.partial(collect_kernel, layers),
        in_specs=[WHOLE] * layers,
        out_specs=WHOLE,
        out_shape=jax.ShapeDtypeStruct((layers, *blocks[0].shape), BF16),
        cost_estimate=CHEAP,
        compiler_params=pltpu.CompilerParams(vmem_limit_bytes=4 * 2**20),
        name="collect_weights",
    )(*blocks)


def arrange_kernel(own_ref, other_ref, out_ref):
    _, core = own_place()
    share = own_ref.shape[2]
    out_ref[:, :, block_at(core, share)] = own_ref[...]
    out_ref[:, :, block_at(1 - core, share)] = other_ref[...]


def arrange(own, other):
    layers, rows, share = own.shape
    return pl.pallas_call(
        arrange_kernel,
        in_specs=[WHOLE] * 2,
        out_specs=WHOLE,
        out_shape=jax.ShapeDtypeStruct((layers, rows, 2 * share), BF16),
        cost_estimate=CHEAP,
        compiler_params=pltpu.CompilerParams(vmem_limit_bytes=8 * 2**20),
        name="arrange_weights",
    )(own, other)


def project_kernel(chips, piece, weight_ref, *refs):
    gated_refs, out_refs, joined_ref = refs[:chips], refs[chips:-1], refs[-1]
    chip, _ = own_place()
    lanes = gated_refs[0].shape[2]
    for offset in range(chips):
        joined_ref[:, block_at(chip ^ offset, lanes)] = gated_refs[offset][piece]
    order = (3, 2, 1, 0) if len(out_refs) == 4 else (1, 3, 2, 0)
    for target in order:
        partial = jnp.dot(joined_ref[...], weight_ref[target], preferred_element_type=F32).astype(BF16)
        if len(out_refs) == 4:
            out_refs[target][...] = partial
        elif target % 2:
            out_refs[2][target // 2] = partial
        else:
            out_refs[target // 2][...] = partial


def project(weight, gated, piece, paired):
    chips = len(gated)
    layers, depth, columns = weight.shape
    rows = gated[0].shape[1]
    block = jax.ShapeDtypeStruct((rows, columns), BF16)
    pair = jax.ShapeDtypeStruct((2, rows, columns), BF16)
    out_shape = [block, block, pair] if paired else [block] * layers
    return pl.pallas_call(
        functools.partial(project_kernel, chips, piece),
        in_specs=[WHOLE] * (1 + chips),
        out_specs=[WHOLE] * len(out_shape),
        out_shape=out_shape,
        scratch_shapes=[pltpu.VMEM((rows, depth), BF16)],
        cost_estimate=CHEAP,
        compiler_params=pltpu.CompilerParams(vmem_limit_bytes=8 * 2**20),
        name="project",
    )(weight, *gated)


def finish_kernel(chips, direct_refs, paired_refs, out_refs):
    chip, _ = own_place()
    step = direct_refs[0].shape[0] // chips
    for offset in range(chips):
        here = block_at(chip ^ offset, step)
        total = direct_refs[0][here, :].astype(F32)
        for part_ref in direct_refs[1:]:
            total = total + part_ref[here, :].astype(F32)
        out_refs[offset][pl.ds(0, step), :] = total.astype(BF16)
        keep_ref, first_ref, second_ref = paired_refs
        total = keep_ref[here, :].astype(F32) + first_ref[0, here, :].astype(F32) + second_ref[here, :].astype(F32)
        out_refs[offset][pl.ds(step, step), :] = total.astype(BF16)


def finish(direct, paired, chips):
    rows, columns = direct[0].shape

    def kernel(*refs):
        ends = (len(direct), len(direct) + len(paired))
        finish_kernel(chips, refs[: ends[0]], refs[ends[0] : ends[1]], refs[ends[1] :])

    return pl.pallas_call(
        kernel,
        in_specs=[WHOLE] * (len(direct) + len(paired)),
        out_specs=[WHOLE] * chips,
        out_shape=[jax.ShapeDtypeStruct((2 * rows // chips, columns), BF16)] * chips,
        cost_estimate=CHEAP,
        compiler_params=pltpu.CompilerParams(vmem_limit_bytes=4 * 2**20),
        name="finish",
    )(*direct, *paired)


def join_kernel(chips, *refs):
    in_refs, out_ref = refs[:chips], refs[chips]
    chip, _ = own_place()
    columns = in_refs[0].shape[1]
    for offset in range(chips):
        out_ref[:, block_at(chip ^ offset, columns)] = in_refs[offset][...]


def join(blocks):
    chips = len(blocks)
    rows, columns = blocks[0].shape
    return pl.pallas_call(
        functools.partial(join_kernel, chips),
        in_specs=[WHOLE] * chips,
        out_specs=WHOLE,
        out_shape=jax.ShapeDtypeStruct((rows, chips * columns), BF16),
        cost_estimate=CHEAP,
        compiler_params=pltpu.CompilerParams(vmem_limit_bytes=2 * 2**20),
        name="join",
    )(*blocks)


def swapped(value, axis, offset):
    if not offset:
        return value
    return lax.ppermute(value, axis, [(source, source ^ offset) for source in range(lax.axis_size(axis))])


def to_chips(blocks):
    return [swapped(block, "seq", 2 * offset) for offset, block in enumerate(blocks)]


def after(value, *others):
    return lax.optimization_barrier((value, *others))[0]


def shards_direct(values_in, gate_values, filter_spectrum, skip_gain, out_weight):
    parts = lax.axis_size("seq")
    layers = lax.axis_size("chan")
    chips = parts // 2
    rows, width = values_in.shape
    device = lax.axis_index("seq")
    tables = small_tables(parts, rows)

    flat_filters = filter_spectrum.reshape(4, rows, width)
    first = pack(values_in, flat_filters, chips, (0, 2))
    second = pack(after(gate_values, first[0]), flat_filters, chips, (1, 3))
    first = to_chips(first)
    own = jnp.stack([after(block, second[0])[0] for block in first])
    second = to_chips(second)
    spectrum = forward(own, swapped(own, "seq", 1), tables)
    keep, send = backward(spectrum, first, second, tables)
    gated = gate(skip_gain[None, :], keep, swapped(send, "seq", 1), first, second, 2)

    share = out_weight.shape[1] // layers
    own_weight = []
    for step, earlier in enumerate((spectrum, spectrum, send, send)):
        sent = lax.dynamic_slice_in_dim(after(out_weight, second[0]), (device // 2 ^ step) * share, share, 1)
        pairs = [(source, source % 2 * layers + (source // 2 ^ step)) for source in range(parts)]
        own_weight.append(lax.ppermute(after(sent, earlier), "seq", pairs))
    own_weight = collect([after(block, gated) for block in own_weight])
    weight = arrange(own_weight, swapped(own_weight, "seq", 1))

    gathered = to_chips([gated] * chips)
    partials = project(weight, gathered, 0, False)
    direct = [swapped(block, "chan", offset) for offset, block in enumerate(partials)]
    keep, passed, send = project(weight, gathered, 1, True)
    arrived = swapped(send, "chan", 1)
    passed = after((passed.astype(F32) + arrived[1].astype(F32)).astype(BF16), *direct)
    return join(to_chips(finish(direct, (keep, arrived, swapped(passed, "chan", 2)), chips)))


def shards(values_in, gate_values, filter_spectrum, skip_gain, out_weight):
    parts, layers = lax.axis_size("seq"), lax.axis_size("chan")
    rows, width = values_in.shape
    share = out_weight.shape[1] // layers
    aligned = width // parts % 128 == 0 and share % 128 == 0 and rows % 32 == 0
    run = shards_direct if aligned and layers == 4 and parts == 8 else shards_general
    return run(values_in, gate_values, filter_spectrum, skip_gain, out_weight)


def solution(mesh):
    in_specs = (
        P("seq", "chan"),
        P("seq", "chan"),
        P(None, "seq", None, "chan"),
        P("chan"),
        P("chan", "seq"),
    )
    out_specs = P("seq", "chan")
    return jax.shard_map(shards, mesh=mesh, in_specs=in_specs, out_specs=out_specs, check_vma=False)
```

```python
import functools

import jax
import jax.numpy as jnp
import numpy as np
from jax import lax
from jax.experimental import pallas as pl
from jax.experimental.pallas import tpu as pltpu
from jax.sharding import PartitionSpec as P

BF16 = jnp.bfloat16
F32 = jnp.float32


def bit_reversed(number, width_bits):
    flipped = 0
    for bit_place in range(width_bits):
        flipped |= (number >> bit_place & 1) << (width_bits - 1 - bit_place)
    return flipped


def filter_row(residue, width_bits):
    return 2 * bit_reversed(residue // 2, width_bits) + residue % 2


def dft_tables(parts, rows):
    total = 2 * parts * rows
    residue = np.arange(2 * parts)[:, None, None]
    column = np.arange(rows)[None, :, None]
    position = np.arange(rows)[None, None, :]
    phase = 2.0 * np.pi * (position * (residue + 2 * parts * column) % total) / total
    cos, sin = np.cos(phase), np.sin(phase)
    forward = np.concatenate(
        [np.concatenate([cos, sin], axis=2), np.concatenate([-sin, cos], axis=2)], axis=1
    )
    inverse = np.transpose(forward, (0, 2, 1)) / total
    return forward.astype(BF16), inverse.astype(BF16)


def convolve_kernel(parts, rows, moved_ref, skip_ref, forward_ref, inverse_ref, out_ref, waves_ref, back_ref):
    width_bits = parts.bit_length() - 1
    chunk = 16

    def cosine(residue, block):
        return float(np.cos(np.pi * residue * block / parts))

    def sine(residue, block):
        return float(np.sin(np.pi * residue * block / parts))

    def spread(index, carry):
        here = pl.ds(index * chunk, chunk)
        there = pl.ds(rows + index * chunk, chunk)
        blocks = [moved_ref[block, here, :].astype(F32) for block in range(parts)]
        for residue in range(parts + 1):
            real = blocks[0]
            imag = jnp.zeros_like(real)
            for block in range(1, parts):
                real = real + cosine(residue, block) * blocks[block]
                imag = imag - sine(residue, block) * blocks[block]
            waves_ref[residue, here, :] = real.astype(BF16)
            waves_ref[residue, there, :] = imag.astype(BF16)
            if 0 < residue < parts:
                waves_ref[2 * parts - residue, here, :] = real.astype(BF16)
                waves_ref[2 * parts - residue, there, :] = (-imag).astype(BF16)
        return carry

    lax.fori_loop(0, rows // chunk, spread, 0)

    def through(residue):
        wave = jnp.dot(forward_ref[residue], waves_ref[residue], preferred_element_type=F32)
        source, odd = divmod(filter_row(residue, width_bits), 2)
        filter_real = moved_ref[source, pl.ds((2 + odd) * rows, rows), :].astype(F32)
        filter_imag = moved_ref[source, pl.ds((4 + odd) * rows, rows), :].astype(F32)
        real, imag = wave[:rows], wave[rows:]
        product = jnp.concatenate(
            [real * filter_real - imag * filter_imag, real * filter_imag + imag * filter_real], axis=0
        )
        return jnp.dot(inverse_ref[residue], product.astype(BF16), preferred_element_type=F32)

    for residue in range(parts + 1):
        back = through(residue)
        if 0 < residue < parts:
            other = through(2 * parts - residue)
            back_ref[residue, pl.ds(0, rows), :] = back[:rows] + other[:rows]
            back_ref[residue, pl.ds(rows, rows), :] = back[rows:] - other[rows:]
        else:
            back_ref[residue] = back

    skip = skip_ref[...]

    def gather(index, carry):
        here = pl.ds(index * chunk, chunk)
        there = pl.ds(rows + index * chunk, chunk)
        reals = [back_ref[residue, here, :] for residue in range(parts + 1)]
        imags = [back_ref[residue, there, :] for residue in range(parts + 1)]
        for block in range(parts):
            total = reals[0]
            for residue in range(1, parts + 1):
                total = total + cosine(residue, block) * reals[residue]
                if residue < parts and block:
                    total = total - sine(residue, block) * imags[residue]
            signal = moved_ref[block, here, :].astype(F32)
            gate = moved_ref[block, pl.ds(rows + index * chunk, chunk), :].astype(F32)
            out_ref[block, here, :] = (gate * (total + skip * signal)).astype(BF16)
        return carry

    lax.fori_loop(0, rows // chunk, gather, 0)


def convolve(moved, skip):
    parts, stacked, width = moved.shape
    rows = stacked // 6
    forward, inverse = dft_tables(parts, rows)
    whole = pl.BlockSpec(memory_space=pltpu.VMEM)
    return pl.pallas_call(
        functools.partial(convolve_kernel, parts, rows),
        out_shape=jax.ShapeDtypeStruct((parts, rows, width), BF16),
        in_specs=[whole] * 4,
        out_specs=whole,
        scratch_shapes=[
            pltpu.VMEM((2 * parts, 2 * rows, width), BF16),
            pltpu.VMEM((parts + 1, 2 * rows, width), F32),
        ],
        compiler_params=pltpu.CompilerParams(vmem_limit_bytes=40 * 2**20),
    )(moved, skip[None, :], forward, inverse)


def shards_general(values_in, gate_values, filter_spectrum, skip_gain, out_weight):
    parts = lax.axis_size("seq")
    layers = lax.axis_size("chan")
    rows, width = values_in.shape
    lanes = width // parts
    device = lax.axis_index("seq")

    def by_channel(array):
        return jnp.transpose(array.reshape(array.shape[0], parts, lanes), (1, 0, 2))

    filters = filter_spectrum.astype(BF16).reshape(4 * rows, width)
    packed = jnp.concatenate([by_channel(values_in), by_channel(gate_values), by_channel(filters)], axis=1)
    moved = lax.all_to_all(packed, "seq", 0, 0)
    skip = lax.dynamic_slice_in_dim(skip_gain, device * lanes, lanes)
    gated = convolve(moved, skip)
    gathered = lax.all_gather(gated.reshape(parts * rows, lanes), "seq", axis=1, tiled=True)

    own_cols = out_weight.shape[1]
    share = own_cols * parts // layers // parts
    per_block = parts // layers
    pieces = own_cols // share
    group = device % per_block
    member = device // per_block
    weight = jnp.zeros_like(out_weight)
    for step in range(pieces):
        piece = (member + step) % pieces
        sent = lax.dynamic_slice_in_dim(out_weight, piece * share, share, 1)
        pairs = [
            (source, source % per_block * pieces + (source // per_block + step) % pieces) for source in range(parts)
        ]
        arrived = lax.ppermute(sent, "seq", pairs)
        block = (device % pieces - step) % pieces
        weight = lax.dynamic_update_slice_in_dim(weight, arrived, block * share, 1)
    partials = jnp.dot(gathered, weight, preferred_element_type=F32).astype(BF16)
    mixed = lax.psum_scatter(partials, "chan", scatter_dimension=1, tiled=True)
    return lax.all_to_all(mixed, "seq", 0, 1, tiled=True)


WHOLE = pl.BlockSpec(memory_space=pltpu.VMEM)
CHEAP = pl.CostEstimate(flops=0, transcendentals=0, bytes_accessed=0)


def small_tables(parts, rows):
    total = 2 * parts * rows
    index = np.arange(rows)
    phase = 2.0 * np.pi * (index[:, None] * index[None, :] % rows) / rows
    cos, sin = np.cos(phase), np.sin(phase)
    forward = np.block([[cos, sin], [-sin, cos]])
    residue = np.arange(2 * parts).reshape(2, 1, parts)
    turn = 2.0 * np.pi * index[None, :, None] * residue / total
    return forward.astype(BF16), forward.T.astype(BF16), np.cos(turn).astype(F32), np.sin(turn).astype(F32)


def cosine(parts, residue, block):
    return float(np.cos(np.pi * residue * block / parts))


def sine(parts, residue, block):
    return float(np.sin(np.pi * residue * block / parts))


def weighted(terms):
    total = None
    for factor, term in terms:
        if abs(factor) < 1e-12:
            continue
        part = term if factor == 1.0 else factor * term
        total = part if total is None else total + part
    return total


def plus(left, right):
    return left if right is None else right if left is None else left + right


def minus(left, right):
    return left if right is None else -right if left is None else left - right


def own_place():
    device = lax.axis_index("seq")
    return device // 2, device % 2


def block_at(index, size):
    return pl.ds(pl.multiple_of(index * size, size), size)


def pack_signals_kernel(chips, values_ref, filter_ref, *refs):
    out_refs, (plane_ref, arrived) = refs[:chips], refs[chips:]
    chip, _ = own_place()
    planes, rows, _ = filter_ref.shape
    lanes = out_refs[0].shape[2]
    copies = []
    for offset in reversed(range(chips)):
        here = block_at(chip ^ offset, lanes)
        for plane in range(planes):
            copies.append(
                pltpu.make_async_copy(filter_ref.at[plane, :, here], plane_ref.at[offset, plane], arrived.at[offset, plane])
            )
        copies.append(
            pltpu.make_async_copy(values_ref.at[:, here], out_refs[offset].at[planes], arrived.at[offset, planes])
        )
    for copy in copies:
        copy.start()
    for place, copy in enumerate(copies):
        copy.wait()
        offset, plane = chips - 1 - place // (planes + 1), place % (planes + 1)
        if plane < planes:
            out_refs[offset][plane] = plane_ref[offset, plane].astype(BF16)


def pack_signals(values_in, filters, chips):
    planes, rows, width = filters.shape
    lanes = width // chips
    return pl.pallas_call(
        functools.partial(pack_signals_kernel, chips),
        in_specs=[pl.BlockSpec(memory_space=pltpu.HBM)] * 2,
        out_specs=[WHOLE] * chips,
        out_shape=[jax.ShapeDtypeStruct((planes + 1, rows, lanes), BF16)] * chips,
        scratch_shapes=[
            pltpu.VMEM((chips, planes, rows, lanes), F32),
            pltpu.SemaphoreType.DMA((chips, planes + 1)),
        ],
        cost_estimate=CHEAP,
        compiler_params=pltpu.CompilerParams(vmem_limit_bytes=8 * 2**20),
        name="pack_signals",
    )(
        pltpu.with_memory_space_constraint(values_in, pltpu.HBM),
        pltpu.with_memory_space_constraint(filters, pltpu.HBM),
    )


def pack_weights_kernel(chips, gate_ref, weight_ref, other_ref, *refs):
    out_refs, (joined_ref, arrived) = refs[:chips], refs[chips:]
    chip, core = own_place()
    rows = gate_ref.shape[0]
    half, held = other_ref.shape
    lanes = out_refs[0].shape[1]
    copies = [
        pltpu.make_async_copy(
            weight_ref.at[block_at(core, half), :], joined_ref.at[:, block_at(core, held)], arrived.at[chips]
        )
    ]
    for offset in range(chips):
        copies.append(
            pltpu.make_async_copy(
                gate_ref.at[:, block_at(chip ^ offset, lanes)], out_refs[offset].at[pl.ds(0, rows)], arrived.at[offset]
            )
        )
    for copy in copies:
        copy.start()
    joined_ref[:, block_at(1 - core, held)] = other_ref[...]
    for copy in copies:
        copy.wait()
    for offset in range(chips):
        out_refs[offset][pl.ds(rows, half), :] = joined_ref[:, block_at(chip ^ offset, lanes)]


def pack_weights(gate_values, weight, other, chips):
    rows, width = gate_values.shape
    half, held = other.shape
    return pl.pallas_call(
        functools.partial(pack_weights_kernel, chips),
        in_specs=[pl.BlockSpec(memory_space=pltpu.HBM)] * 2 + [WHOLE],
        out_specs=[WHOLE] * chips,
        out_shape=[jax.ShapeDtypeStruct((rows + half, width // chips), BF16)] * chips,
        scratch_shapes=[pltpu.VMEM((half, 2 * held), BF16), pltpu.SemaphoreType.DMA((chips + 1,))],
        cost_estimate=CHEAP,
        compiler_params=pltpu.CompilerParams(vmem_limit_bytes=8 * 2**20),
        name="pack_weights",
    )(
        pltpu.with_memory_space_constraint(gate_values, pltpu.HBM),
        pltpu.with_memory_space_constraint(weight, pltpu.HBM),
        other,
    )


def forward_kernel(chips, cos_ref, sin_ref, table_ref, own_ref, other_ref, out_ref, signal_ref, waves_ref):
    chip, core = own_place()
    parts = 2 * chips
    rows, lanes = own_ref.shape[1:]
    chunk, width = 16, 128
    for offset in range(chips):
        signal_ref[2 * (chip ^ offset) + core] = own_ref[offset]
        signal_ref[2 * (chip ^ offset) + 1 - core] = other_ref[offset]
    sign = (1 - 2 * core).astype(F32)

    def spread(index, carry):
        here = block_at(index, chunk)
        there = pl.ds(pl.multiple_of(rows + index * chunk, chunk), chunk)
        cos_all, sin_all = cos_ref[core, here, :], sin_ref[core, here, :]
        for start in range(0, lanes, width):
            blocks = [signal_ref[block, here, pl.ds(start, width)].astype(F32) for block in range(parts)]
            blocks = [block * sign if place % 2 else block for place, block in enumerate(blocks)]

            def store(residue, real, imag):
                cos, sin = cos_all[:, residue : residue + 1], sin_all[:, residue : residue + 1]
                if imag is None:
                    real, imag = real * cos, -(real * sin)
                else:
                    real, imag = real * cos + imag * sin, imag * cos - real * sin
                columns = pl.ds(residue * lanes + start, width)
                waves_ref[here, columns] = real.astype(BF16)
                waves_ref[there, columns] = imag.astype(BF16)

            for residue in range(parts // 2 + 1):
                even, odd = range(0, parts, 2), range(1, parts, 2)
                cos_even = weighted([(cosine(parts, residue, block), blocks[block]) for block in even])
                cos_odd = weighted([(cosine(parts, residue, block), blocks[block]) for block in odd])
                sin_even = weighted([(sine(parts, residue, block), blocks[block]) for block in even])
                sin_odd = weighted([(sine(parts, residue, block), blocks[block]) for block in odd])
                sin_sum = plus(sin_even, sin_odd)
                store(residue, plus(cos_even, cos_odd), None if sin_sum is None else -sin_sum)
                if 0 < residue and 2 * residue != parts:
                    store(parts - residue, minus(cos_even, cos_odd), minus(sin_even, sin_odd))
        return carry

    lax.fori_loop(0, rows // chunk, spread, 0)
    for residue in range(parts):
        columns = pl.ds(residue * lanes, lanes)
        out_ref[:, columns] = jnp.dot(table_ref[...], waves_ref[:, columns], preferred_element_type=F32)


def forward(own, other, tables):
    chips, rows, lanes = own.shape
    table, _, cos, sin = tables
    spectrum = (2 * rows, 2 * chips * lanes)
    return pl.pallas_call(
        functools.partial(forward_kernel, chips),
        in_specs=[WHOLE] * 5,
        out_specs=WHOLE,
        out_shape=jax.ShapeDtypeStruct(spectrum, F32),
        scratch_shapes=[pltpu.VMEM((2 * chips, rows, lanes), BF16), pltpu.VMEM(spectrum, BF16)],
        cost_estimate=CHEAP,
        compiler_params=pltpu.CompilerParams(vmem_limit_bytes=32 * 2**20),
        name="forward",
    )(cos, sin, table, own, other)


def backward_kernel(chips, cos_ref, sin_ref, table_ref, spectrum_ref, *refs):
    filter_refs, (keep_ref, send_ref, filter_ref, product_ref, back_ref) = refs[:chips], refs[chips:]
    chip, core = own_place()
    parts = 2 * chips
    rows, lanes = keep_ref.shape[1:]
    chip_bits = chips.bit_length() - 1
    chunk, width = 16, 128
    for offset in range(chips):
        filter_ref[chip ^ offset] = filter_refs[offset][pl.ds(0, 4)]

    for residue in range(parts):
        source, odd = bit_reversed(residue // 2, chip_bits), residue % 2
        columns = pl.ds(residue * lanes, lanes)
        filter_real = filter_ref[source, odd].astype(F32)
        filter_imag = filter_ref[source, 2 + odd].astype(F32)
        real = spectrum_ref[pl.ds(0, rows), columns]
        imag = spectrum_ref[pl.ds(rows, rows), columns]
        product_ref[pl.ds(0, rows), columns] = (real * filter_real - imag * filter_imag).astype(BF16)
        product_ref[pl.ds(rows, rows), columns] = (real * filter_imag + imag * filter_real).astype(BF16)
        back_ref[:, columns] = jnp.dot(table_ref[...], product_ref[:, columns], preferred_element_type=F32)

    scale = 1.0 / (2 * parts * rows)
    sign = (1 - 2 * core).astype(F32)
    upper = core == 1

    def gather(index, carry):
        here = block_at(index, chunk)
        there = pl.ds(pl.multiple_of(rows + index * chunk, chunk), chunk)
        cos_all, sin_all = cos_ref[core, here, :] * scale, sin_ref[core, here, :] * scale
        for start in range(0, lanes, width):
            reals, imags = [], []
            for residue in range(parts):
                columns = pl.ds(residue * lanes + start, width)
                real, imag = back_ref[here, columns], back_ref[there, columns]
                cos, sin = cos_all[:, residue : residue + 1], sin_all[:, residue : residue + 1]
                reals.append(real * cos - imag * sin)
                imags.append(real * sin + imag * cos)
            totals = [None] * parts
            for block in range(parts // 2 + 1):
                even, odd = range(0, parts, 2), range(1, parts, 2)
                cos_even = weighted([(cosine(parts, residue, block), reals[residue]) for residue in even])
                cos_odd = weighted([(cosine(parts, residue, block), reals[residue]) for residue in odd])
                sin_even = weighted([(sine(parts, residue, block), imags[residue]) for residue in even])
                sin_odd = weighted([(sine(parts, residue, block), imags[residue]) for residue in odd])
                totals[block] = minus(plus(cos_even, cos_odd), plus(sin_even, sin_odd))
                if 0 < block and 2 * block != parts:
                    totals[parts - block] = plus(minus(cos_even, cos_odd), minus(sin_even, sin_odd))
            lane = pl.ds(start, width)
            for pair in range(chips):
                low, high = totals[2 * pair], totals[2 * pair + 1] * sign
                keep_ref[pair, here, lane] = jnp.where(upper, high, low)
                send_ref[pair, here, lane] = jnp.where(upper, low, high).astype(BF16)
        return carry

    lax.fori_loop(0, rows // chunk, gather, 0)


def backward(spectrum, first, tables):
    chips = len(first)
    _, rows, lanes = first[0].shape
    _, table, cos, sin = tables
    kept = (chips, rows, lanes)
    return pl.pallas_call(
        functools.partial(backward_kernel, chips),
        in_specs=[WHOLE] * (4 + chips),
        out_specs=[WHOLE] * 2,
        out_shape=[jax.ShapeDtypeStruct(kept, F32), jax.ShapeDtypeStruct(kept, BF16)],
        scratch_shapes=[
            pltpu.VMEM((chips, 4, rows, lanes), BF16),
            pltpu.VMEM(spectrum.shape, BF16),
            pltpu.VMEM(spectrum.shape, F32),
        ],
        cost_estimate=CHEAP,
        compiler_params=pltpu.CompilerParams(vmem_limit_bytes=32 * 2**20),
        name="backward",
    )(cos, sin, table, spectrum, *first)


def gate_kernel(chips, skip_ref, keep_ref, arrived_ref, *refs):
    signal_refs, gate_refs, out_ref = refs[:chips], refs[chips : 2 * chips], refs[2 * chips]
    chip, _ = own_place()
    rows, lanes = keep_ref.shape[1:]
    pieces = out_ref.shape[0]
    step = rows // pieces
    skip = skip_ref[:, block_at(chip, lanes)]
    for offset in range(chips):
        block = chip ^ offset
        for piece in range(pieces):
            here = pl.ds(piece * step, step)
            convolved = keep_ref[block, here, :] + arrived_ref[block, here, :].astype(F32)
            signal = signal_refs[offset][4, here, :].astype(F32)
            gate = gate_refs[offset][here, :].astype(F32)
            out_ref[piece, block_at(block, step), :] = (gate * (convolved + skip * signal)).astype(BF16)


def gate(skip, keep, arrived, first, second, pieces):
    chips, rows, lanes = keep.shape
    return pl.pallas_call(
        functools.partial(gate_kernel, chips),
        in_specs=[WHOLE] * (3 + 2 * chips),
        out_specs=WHOLE,
        out_shape=jax.ShapeDtypeStruct((pieces, chips * rows // pieces, lanes), BF16),
        cost_estimate=CHEAP,
        compiler_params=pltpu.CompilerParams(vmem_limit_bytes=6 * 2**20),
        name="gate",
    )(skip, keep, arrived, *first, *second)


def collect_kernel(chips, *refs):
    in_refs, out_ref = refs[:chips], refs[chips]
    chip, _ = own_place()
    layer = lax.axis_index("chan")
    half = out_ref.shape[1]
    start = in_refs[0].shape[0] - half
    for offset in range(chips):
        out_ref[chip ^ layer ^ offset] = in_refs[offset][pl.ds(start, half), :]


def collect(second, half):
    chips = len(second)
    return pl.pallas_call(
        functools.partial(collect_kernel, chips),
        in_specs=[WHOLE] * chips,
        out_specs=WHOLE,
        out_shape=jax.ShapeDtypeStruct((chips, half, second[0].shape[1]), BF16),
        cost_estimate=CHEAP,
        compiler_params=pltpu.CompilerParams(vmem_limit_bytes=4 * 2**20),
        name="collect_weights",
    )(*second)


def project_kernel(chips, piece, own_ref, other_ref, *refs):
    gated_refs, out_refs, joined_ref = refs[:chips], refs[chips:-1], refs[-1]
    chip, core = own_place()
    half = own_ref.shape[1]
    lanes = gated_refs[0].shape[2]
    for offset in range(chips):
        joined_ref[:, block_at(chip ^ offset, lanes)] = gated_refs[offset][piece]
    order = (3, 2, 1, 0) if len(out_refs) == 4 else (1, 3, 2, 0)
    for target in order:
        partial = jnp.dot(joined_ref[:, block_at(core, half)], own_ref[target], preferred_element_type=F32)
        partial += jnp.dot(joined_ref[:, block_at(1 - core, half)], other_ref[target], preferred_element_type=F32)
        partial = partial.astype(BF16)
        if len(out_refs) == 4:
            out_refs[target][...] = partial
        elif target % 2:
            out_refs[2][target // 2] = partial
        else:
            out_refs[target // 2][...] = partial


def project(own, other, gated, piece, paired):
    chips = len(gated)
    layers, half, columns = own.shape
    rows = gated[0].shape[1]
    block = jax.ShapeDtypeStruct((rows, columns), BF16)
    pair = jax.ShapeDtypeStruct((2, rows, columns), BF16)
    out_shape = [block, block, pair] if paired else [block] * layers
    return pl.pallas_call(
        functools.partial(project_kernel, chips, piece),
        in_specs=[WHOLE] * (2 + chips),
        out_specs=[WHOLE] * len(out_shape),
        out_shape=out_shape,
        scratch_shapes=[pltpu.VMEM((rows, 2 * half), BF16)],
        cost_estimate=CHEAP,
        compiler_params=pltpu.CompilerParams(vmem_limit_bytes=8 * 2**20),
        name="project",
    )(own, other, *gated)


def finish_kernel(chips, direct_refs, paired_refs, out_refs):
    chip, _ = own_place()
    step = direct_refs[0].shape[0] // chips
    for offset in range(chips):
        here = block_at(chip ^ offset, step)
        total = direct_refs[0][here, :].astype(F32)
        for part_ref in direct_refs[1:]:
            total = total + part_ref[here, :].astype(F32)
        out_refs[offset][pl.ds(0, step), :] = total.astype(BF16)
        keep_ref, first_ref, second_ref = paired_refs
        total = keep_ref[here, :].astype(F32) + first_ref[0, here, :].astype(F32) + second_ref[here, :].astype(F32)
        out_refs[offset][pl.ds(step, step), :] = total.astype(BF16)


def finish(direct, paired, chips):
    rows, columns = direct[0].shape

    def kernel(*refs):
        ends = (len(direct), len(direct) + len(paired))
        finish_kernel(chips, refs[: ends[0]], refs[ends[0] : ends[1]], refs[ends[1] :])

    return pl.pallas_call(
        kernel,
        in_specs=[WHOLE] * (len(direct) + len(paired)),
        out_specs=[WHOLE] * chips,
        out_shape=[jax.ShapeDtypeStruct((2 * rows // chips, columns), BF16)] * chips,
        cost_estimate=CHEAP,
        compiler_params=pltpu.CompilerParams(vmem_limit_bytes=4 * 2**20),
        name="finish",
    )(*direct, *paired)


def join_kernel(chips, *refs):
    in_refs, out_ref = refs[:chips], refs[chips]
    chip, _ = own_place()
    columns = in_refs[0].shape[1]
    for offset in range(chips):
        out_ref[:, block_at(chip ^ offset, columns)] = in_refs[offset][...]


def join(blocks):
    chips = len(blocks)
    rows, columns = blocks[0].shape
    return pl.pallas_call(
        functools.partial(join_kernel, chips),
        in_specs=[WHOLE] * chips,
        out_specs=WHOLE,
        out_shape=jax.ShapeDtypeStruct((rows, chips * columns), BF16),
        cost_estimate=CHEAP,
        compiler_params=pltpu.CompilerParams(vmem_limit_bytes=2 * 2**20),
        name="join",
    )(*blocks)


def swapped(value, axis, offset):
    if not offset:
        return value
    return lax.ppermute(value, axis, [(source, source ^ offset) for source in range(lax.axis_size(axis))])


def to_chips(blocks):
    return [swapped(block, "seq", 2 * offset) for offset, block in enumerate(blocks)]


def after(value, *others):
    return lax.optimization_barrier((value, *others))[0]


def shards_direct(values_in, gate_values, filter_spectrum, skip_gain, out_weight):
    parts = lax.axis_size("seq")
    chips = parts // 2
    rows, width = values_in.shape
    device = lax.axis_index("seq")
    tables = small_tables(parts, rows)

    first = pack_signals(values_in, filter_spectrum.reshape(4, rows, width), chips)
    half = out_weight.shape[0] // 2
    others_half = lax.dynamic_slice_in_dim(after(out_weight, first[0]), (1 - device % 2) * half, half, 0)
    second = pack_weights(gate_values, out_weight, swapped(others_half, "seq", 1), chips)
    first = to_chips(first)
    own = jnp.stack([after(block, second[0])[4] for block in first])
    second = to_chips(second)
    spectrum = forward(own, swapped(own, "seq", 1), tables)
    keep, send = backward(spectrum, first, tables)
    gated = gate(skip_gain[None, :], keep, swapped(send, "seq", 1), first, second, 2)
    gathered = to_chips([gated] * chips)
    own_weight = collect([after(block, gated) for block in second], half)
    weights = (own_weight, swapped(own_weight, "seq", 1))

    partials = project(*weights, gathered, 0, False)
    direct = [swapped(block, "chan", offset) for offset, block in enumerate(partials)]
    keep, passed, send = project(*weights, gathered, 1, True)
    arrived = swapped(send, "chan", 1)
    passed = (passed.astype(F32) + arrived[1].astype(F32)).astype(BF16)
    return join(to_chips(finish(direct, (keep, arrived, swapped(passed, "chan", 2)), chips)))


def shards(values_in, gate_values, filter_spectrum, skip_gain, out_weight):
    parts, layers = lax.axis_size("seq"), lax.axis_size("chan")
    rows, width = values_in.shape
    share = out_weight.shape[1] // layers
    aligned = width // parts % 128 == 0 and share % 128 == 0 and rows % 32 == 0
    run = shards_direct if aligned and layers == 4 and parts == 8 else shards_general
    return run(values_in, gate_values, filter_spectrum, skip_gain, out_weight)


def solution(mesh):
    in_specs = (
        P("seq", "chan"),
        P("seq", "chan"),
        P(None, "seq", None, "chan"),
        P("chan"),
        P("chan", "seq"),
    )
    out_specs = P("seq", "chan")
    return jax.shard_map(shards, mesh=mesh, in_specs=in_specs, out_specs=out_specs, check_vma=False)
```

```python
import functools

import jax
import jax.numpy as jnp
import numpy as np
from jax import lax
from jax.experimental import pallas as pl
from jax.experimental.pallas import tpu as pltpu
from jax.sharding import PartitionSpec as P

BF16 = jnp.bfloat16
F32 = jnp.float32


def bit_reversed(number, width_bits):
    flipped = 0
    for bit_place in range(width_bits):
        flipped |= (number >> bit_place & 1) << (width_bits - 1 - bit_place)
    return flipped


def filter_row(residue, width_bits):
    return 2 * bit_reversed(residue // 2, width_bits) + residue % 2


def dft_tables(parts, rows):
    total = 2 * parts * rows
    residue = np.arange(2 * parts)[:, None, None]
    column = np.arange(rows)[None, :, None]
    position = np.arange(rows)[None, None, :]
    phase = 2.0 * np.pi * (position * (residue + 2 * parts * column) % total) / total
    cos, sin = np.cos(phase), np.sin(phase)
    forward = np.concatenate(
        [np.concatenate([cos, sin], axis=2), np.concatenate([-sin, cos], axis=2)], axis=1
    )
    inverse = np.transpose(forward, (0, 2, 1)) / total
    return forward.astype(BF16), inverse.astype(BF16)


def convolve_kernel(parts, rows, moved_ref, skip_ref, forward_ref, inverse_ref, out_ref, waves_ref, back_ref):
    width_bits = parts.bit_length() - 1
    chunk = 16

    def cosine(residue, block):
        return float(np.cos(np.pi * residue * block / parts))

    def sine(residue, block):
        return float(np.sin(np.pi * residue * block / parts))

    def spread(index, carry):
        here = pl.ds(index * chunk, chunk)
        there = pl.ds(rows + index * chunk, chunk)
        blocks = [moved_ref[block, here, :].astype(F32) for block in range(parts)]
        for residue in range(parts + 1):
            real = blocks[0]
            imag = jnp.zeros_like(real)
            for block in range(1, parts):
                real = real + cosine(residue, block) * blocks[block]
                imag = imag - sine(residue, block) * blocks[block]
            waves_ref[residue, here, :] = real.astype(BF16)
            waves_ref[residue, there, :] = imag.astype(BF16)
            if 0 < residue < parts:
                waves_ref[2 * parts - residue, here, :] = real.astype(BF16)
                waves_ref[2 * parts - residue, there, :] = (-imag).astype(BF16)
        return carry

    lax.fori_loop(0, rows // chunk, spread, 0)

    def through(residue):
        wave = jnp.dot(forward_ref[residue], waves_ref[residue], preferred_element_type=F32)
        source, odd = divmod(filter_row(residue, width_bits), 2)
        filter_real = moved_ref[source, pl.ds((2 + odd) * rows, rows), :].astype(F32)
        filter_imag = moved_ref[source, pl.ds((4 + odd) * rows, rows), :].astype(F32)
        real, imag = wave[:rows], wave[rows:]
        product = jnp.concatenate(
            [real * filter_real - imag * filter_imag, real * filter_imag + imag * filter_real], axis=0
        )
        return jnp.dot(inverse_ref[residue], product.astype(BF16), preferred_element_type=F32)

    for residue in range(parts + 1):
        back = through(residue)
        if 0 < residue < parts:
            other = through(2 * parts - residue)
            back_ref[residue, pl.ds(0, rows), :] = back[:rows] + other[:rows]
            back_ref[residue, pl.ds(rows, rows), :] = back[rows:] - other[rows:]
        else:
            back_ref[residue] = back

    skip = skip_ref[...]

    def gather(index, carry):
        here = pl.ds(index * chunk, chunk)
        there = pl.ds(rows + index * chunk, chunk)
        reals = [back_ref[residue, here, :] for residue in range(parts + 1)]
        imags = [back_ref[residue, there, :] for residue in range(parts + 1)]
        for block in range(parts):
            total = reals[0]
            for residue in range(1, parts + 1):
                total = total + cosine(residue, block) * reals[residue]
                if residue < parts and block:
                    total = total - sine(residue, block) * imags[residue]
            signal = moved_ref[block, here, :].astype(F32)
            gate = moved_ref[block, pl.ds(rows + index * chunk, chunk), :].astype(F32)
            out_ref[block, here, :] = (gate * (total + skip * signal)).astype(BF16)
        return carry

    lax.fori_loop(0, rows // chunk, gather, 0)


def convolve(moved, skip):
    parts, stacked, width = moved.shape
    rows = stacked // 6
    forward, inverse = dft_tables(parts, rows)
    whole = pl.BlockSpec(memory_space=pltpu.VMEM)
    return pl.pallas_call(
        functools.partial(convolve_kernel, parts, rows),
        out_shape=jax.ShapeDtypeStruct((parts, rows, width), BF16),
        in_specs=[whole] * 4,
        out_specs=whole,
        scratch_shapes=[
            pltpu.VMEM((2 * parts, 2 * rows, width), BF16),
            pltpu.VMEM((parts + 1, 2 * rows, width), F32),
        ],
        compiler_params=pltpu.CompilerParams(vmem_limit_bytes=40 * 2**20),
    )(moved, skip[None, :], forward, inverse)


def shards_general(values_in, gate_values, filter_spectrum, skip_gain, out_weight):
    parts = lax.axis_size("seq")
    layers = lax.axis_size("chan")
    rows, width = values_in.shape
    lanes = width // parts
    device = lax.axis_index("seq")

    def by_channel(array):
        return jnp.transpose(array.reshape(array.shape[0], parts, lanes), (1, 0, 2))

    filters = filter_spectrum.astype(BF16).reshape(4 * rows, width)
    packed = jnp.concatenate([by_channel(values_in), by_channel(gate_values), by_channel(filters)], axis=1)
    moved = lax.all_to_all(packed, "seq", 0, 0)
    skip = lax.dynamic_slice_in_dim(skip_gain, device * lanes, lanes)
    gated = convolve(moved, skip)
    gathered = lax.all_gather(gated.reshape(parts * rows, lanes), "seq", axis=1, tiled=True)

    own_cols = out_weight.shape[1]
    share = own_cols * parts // layers // parts
    per_block = parts // layers
    pieces = own_cols // share
    group = device % per_block
    member = device // per_block
    weight = jnp.zeros_like(out_weight)
    for step in range(pieces):
        piece = (member + step) % pieces
        sent = lax.dynamic_slice_in_dim(out_weight, piece * share, share, 1)
        pairs = [
            (source, source % per_block * pieces + (source // per_block + step) % pieces) for source in range(parts)
        ]
        arrived = lax.ppermute(sent, "seq", pairs)
        block = (device % pieces - step) % pieces
        weight = lax.dynamic_update_slice_in_dim(weight, arrived, block * share, 1)
    partials = jnp.dot(gathered, weight, preferred_element_type=F32).astype(BF16)
    mixed = lax.psum_scatter(partials, "chan", scatter_dimension=1, tiled=True)
    return lax.all_to_all(mixed, "seq", 0, 1, tiled=True)


WHOLE = pl.BlockSpec(memory_space=pltpu.VMEM)
CHEAP = pl.CostEstimate(flops=0, transcendentals=0, bytes_accessed=0)


def small_tables(parts, rows):
    total = 2 * parts * rows
    index = np.arange(rows)
    phase = 2.0 * np.pi * (index[:, None] * index[None, :] % rows) / rows
    cos, sin = np.cos(phase), np.sin(phase)
    forward = np.block([[cos, sin], [-sin, cos]])
    residue = np.arange(2 * parts).reshape(2, 1, parts)
    turn = 2.0 * np.pi * index[None, :, None] * residue / total
    return forward.astype(BF16), forward.T.astype(BF16), np.cos(turn).astype(F32), np.sin(turn).astype(F32)


def cosine(parts, residue, block):
    return float(np.cos(np.pi * residue * block / parts))


def sine(parts, residue, block):
    return float(np.sin(np.pi * residue * block / parts))


def weighted(terms):
    total = None
    for factor, term in terms:
        if abs(factor) < 1e-12:
            continue
        part = term if factor == 1.0 else factor * term
        total = part if total is None else total + part
    return total


def plus(left, right):
    return left if right is None else right if left is None else left + right


def minus(left, right):
    return left if right is None else -right if left is None else left - right


def own_place():
    device = lax.axis_index("seq")
    return device // 2, device % 2


def block_at(index, size):
    return pl.ds(pl.multiple_of(index * size, size), size)


def pack_signals_kernel(offsets, filter_ref, values_ref, *refs):
    out_refs, (plane_ref, arrived) = refs[: len(offsets)], refs[len(offsets) :]
    chip, _ = own_place()
    planes = filter_ref.shape[0]
    lanes = out_refs[0].shape[2]
    copies, work = [], []
    for place, offset in enumerate(offsets):
        here = block_at(chip ^ offset, lanes)
        for plane in range(planes):
            copies.append(
                pltpu.make_async_copy(filter_ref.at[plane, :, here], plane_ref.at[place, plane], arrived.at[place, plane])
            )
            work.append((place, plane))
        copies.append(
            pltpu.make_async_copy(values_ref.at[:, here], out_refs[place].at[planes], arrived.at[place, planes])
        )
        work.append(None)
    for copy in copies:
        copy.start()
    for copy, task in zip(copies, work):
        copy.wait()
        if task:
            place, plane = task
            out_refs[place][plane] = plane_ref[place, plane].astype(BF16)


def pack_signals(values_in, filters, chips, offsets):
    planes, rows, width = filters.shape
    lanes = width // chips
    return pl.pallas_call(
        functools.partial(pack_signals_kernel, offsets),
        in_specs=[pl.BlockSpec(memory_space=pltpu.HBM)] * 2,
        out_specs=[WHOLE] * len(offsets),
        out_shape=[jax.ShapeDtypeStruct((planes + 1, rows, lanes), BF16)] * len(offsets),
        scratch_shapes=[
            pltpu.VMEM((len(offsets), planes, rows, lanes), F32),
            pltpu.SemaphoreType.DMA((len(offsets), planes + 1)),
        ],
        cost_estimate=CHEAP,
        compiler_params=pltpu.CompilerParams(vmem_limit_bytes=8 * 2**20),
        name="pack_signals",
    )(*(pltpu.with_memory_space_constraint(array, pltpu.HBM) for array in (filters, values_in)))


def pack_weights_kernel(chips, gate_ref, weight_ref, *refs):
    out_refs, arrived = refs[:chips], refs[chips]
    chip, _ = own_place()
    rows = gate_ref.shape[0]
    depth, held = weight_ref.shape
    half, share = depth // 2, held // chips
    copies = []
    for offset in range(chips):
        out_ref, target = out_refs[offset], chip ^ offset
        gates = gate_ref.at[:, block_at(target, out_ref.shape[1])]
        copies.append(pltpu.make_async_copy(gates, out_ref.at[pl.ds(0, rows)], arrived.at[offset, 2]))
        for part in range(2):
            source = weight_ref.at[pl.ds(part * half, half), block_at(target, share)]
            sink = out_ref.at[pl.ds(rows, half), pl.ds(part * share, share)]
            copies.append(pltpu.make_async_copy(source, sink, arrived.at[offset, part]))
    for copy in copies:
        copy.start()
    for copy in copies:
        copy.wait()


def pack_weights(gate_values, weight, chips):
    rows, width = gate_values.shape
    depth, held = weight.shape
    shape = (rows + depth // 2, 2 * held // chips)
    return pl.pallas_call(
        functools.partial(pack_weights_kernel, chips),
        in_specs=[pl.BlockSpec(memory_space=pltpu.HBM)] * 2,
        out_specs=[WHOLE] * chips,
        out_shape=[jax.ShapeDtypeStruct(shape, BF16)] * chips,
        scratch_shapes=[pltpu.SemaphoreType.DMA((chips, 3))],
        cost_estimate=CHEAP,
        compiler_params=pltpu.CompilerParams(vmem_limit_bytes=8 * 2**20),
        name="pack_weights",
    )(*(pltpu.with_memory_space_constraint(array, pltpu.HBM) for array in (gate_values, weight)))


def forward_kernel(chips, cos_ref, sin_ref, table_ref, own_ref, other_ref, out_ref, signal_ref, waves_ref):
    chip, core = own_place()
    parts = 2 * chips
    rows, lanes = own_ref.shape[1:]
    chunk, width = 16, 128
    for offset in range(chips):
        signal_ref[2 * (chip ^ offset) + core] = own_ref[offset]
        signal_ref[2 * (chip ^ offset) + 1 - core] = other_ref[offset]
    sign = (1 - 2 * core).astype(F32)

    def spread(index, carry):
        here = block_at(index, chunk)
        there = pl.ds(pl.multiple_of(rows + index * chunk, chunk), chunk)
        cos_all, sin_all = cos_ref[core, here, :], sin_ref[core, here, :]
        for start in range(0, lanes, width):
            blocks = [signal_ref[block, here, pl.ds(start, width)].astype(F32) for block in range(parts)]
            blocks = [block * sign if place % 2 else block for place, block in enumerate(blocks)]

            def store(residue, real, imag):
                cos, sin = cos_all[:, residue : residue + 1], sin_all[:, residue : residue + 1]
                if imag is None:
                    real, imag = real * cos, -(real * sin)
                else:
                    real, imag = real * cos + imag * sin, imag * cos - real * sin
                columns = pl.ds(residue * lanes + start, width)
                waves_ref[here, columns] = real.astype(BF16)
                waves_ref[there, columns] = imag.astype(BF16)

            for residue in range(parts // 2 + 1):
                even, odd = range(0, parts, 2), range(1, parts, 2)
                cos_even = weighted([(cosine(parts, residue, block), blocks[block]) for block in even])
                cos_odd = weighted([(cosine(parts, residue, block), blocks[block]) for block in odd])
                sin_even = weighted([(sine(parts, residue, block), blocks[block]) for block in even])
                sin_odd = weighted([(sine(parts, residue, block), blocks[block]) for block in odd])
                sin_sum = plus(sin_even, sin_odd)
                store(residue, plus(cos_even, cos_odd), None if sin_sum is None else -sin_sum)
                if 0 < residue and 2 * residue != parts:
                    store(parts - residue, minus(cos_even, cos_odd), minus(sin_even, sin_odd))
        return carry

    lax.fori_loop(0, rows // chunk, spread, 0)
    for residue in range(parts):
        columns = pl.ds(residue * lanes, lanes)
        out_ref[:, columns] = jnp.dot(table_ref[...], waves_ref[:, columns], preferred_element_type=F32)


def forward(own, other, tables):
    chips, rows, lanes = own.shape
    table, _, cos, sin = tables
    spectrum = (2 * rows, 2 * chips * lanes)
    return pl.pallas_call(
        functools.partial(forward_kernel, chips),
        in_specs=[WHOLE] * 5,
        out_specs=WHOLE,
        out_shape=jax.ShapeDtypeStruct(spectrum, F32),
        scratch_shapes=[pltpu.VMEM((2 * chips, rows, lanes), BF16), pltpu.VMEM(spectrum, BF16)],
        cost_estimate=CHEAP,
        compiler_params=pltpu.CompilerParams(vmem_limit_bytes=32 * 2**20),
        name="forward",
    )(cos, sin, table, own, other)


def backward_kernel(chips, cos_ref, sin_ref, table_ref, spectrum_ref, *refs):
    filter_refs, (keep_ref, send_ref, filter_ref, product_ref, back_ref) = refs[:chips], refs[chips:]
    chip, core = own_place()
    parts = 2 * chips
    rows, lanes = keep_ref.shape[1:]
    chip_bits = chips.bit_length() - 1
    chunk, width = 16, 128
    for offset in range(chips):
        filter_ref[chip ^ offset] = filter_refs[offset][pl.ds(0, 4)]

    for residue in range(parts):
        source, odd = bit_reversed(residue // 2, chip_bits), residue % 2
        columns = pl.ds(residue * lanes, lanes)
        filter_real = filter_ref[source, odd].astype(F32)
        filter_imag = filter_ref[source, 2 + odd].astype(F32)
        real = spectrum_ref[pl.ds(0, rows), columns]
        imag = spectrum_ref[pl.ds(rows, rows), columns]
        product_ref[pl.ds(0, rows), columns] = (real * filter_real - imag * filter_imag).astype(BF16)
        product_ref[pl.ds(rows, rows), columns] = (real * filter_imag + imag * filter_real).astype(BF16)
        back_ref[:, columns] = jnp.dot(table_ref[...], product_ref[:, columns], preferred_element_type=F32)

    scale = 1.0 / (2 * parts * rows)
    sign = (1 - 2 * core).astype(F32)
    upper = core == 1

    def gather(index, carry):
        here = block_at(index, chunk)
        there = pl.ds(pl.multiple_of(rows + index * chunk, chunk), chunk)
        cos_all, sin_all = cos_ref[core, here, :] * scale, sin_ref[core, here, :] * scale
        for start in range(0, lanes, width):
            reals, imags = [], []
            for residue in range(parts):
                columns = pl.ds(residue * lanes + start, width)
                real, imag = back_ref[here, columns], back_ref[there, columns]
                cos, sin = cos_all[:, residue : residue + 1], sin_all[:, residue : residue + 1]
                reals.append(real * cos - imag * sin)
                imags.append(real * sin + imag * cos)
            totals = [None] * parts
            for block in range(parts // 2 + 1):
                even, odd = range(0, parts, 2), range(1, parts, 2)
                cos_even = weighted([(cosine(parts, residue, block), reals[residue]) for residue in even])
                cos_odd = weighted([(cosine(parts, residue, block), reals[residue]) for residue in odd])
                sin_even = weighted([(sine(parts, residue, block), imags[residue]) for residue in even])
                sin_odd = weighted([(sine(parts, residue, block), imags[residue]) for residue in odd])
                totals[block] = minus(plus(cos_even, cos_odd), plus(sin_even, sin_odd))
                if 0 < block and 2 * block != parts:
                    totals[parts - block] = plus(minus(cos_even, cos_odd), minus(sin_even, sin_odd))
            lane = pl.ds(start, width)
            for pair in range(chips):
                low, high = totals[2 * pair], totals[2 * pair + 1] * sign
                keep_ref[pair, here, lane] = jnp.where(upper, high, low)
                send_ref[pair, here, lane] = jnp.where(upper, low, high).astype(BF16)
        return carry

    lax.fori_loop(0, rows // chunk, gather, 0)


def backward(spectrum, first, tables):
    chips = len(first)
    _, rows, lanes = first[0].shape
    _, table, cos, sin = tables
    kept = (chips, rows, lanes)
    return pl.pallas_call(
        functools.partial(backward_kernel, chips),
        in_specs=[WHOLE] * (4 + chips),
        out_specs=[WHOLE] * 2,
        out_shape=[jax.ShapeDtypeStruct(kept, F32), jax.ShapeDtypeStruct(kept, BF16)],
        scratch_shapes=[
            pltpu.VMEM((chips, 4, rows, lanes), BF16),
            pltpu.VMEM(spectrum.shape, BF16),
            pltpu.VMEM(spectrum.shape, F32),
        ],
        cost_estimate=CHEAP,
        compiler_params=pltpu.CompilerParams(vmem_limit_bytes=32 * 2**20),
        name="backward",
    )(cos, sin, table, spectrum, *first)


def gate_kernel(chips, skip_ref, keep_ref, arrived_ref, *refs):
    signal_refs, gate_refs, out_refs = refs[:chips], refs[chips : 2 * chips], refs[2 * chips :]
    chip, _ = own_place()
    rows, lanes = keep_ref.shape[1:]
    step = rows // len(out_refs)
    skip = skip_ref[:, block_at(chip, lanes)]
    for offset in range(chips):
        block = chip ^ offset
        for piece, out_ref in enumerate(out_refs):
            here = pl.ds(piece * step, step)
            convolved = keep_ref[block, here, :] + arrived_ref[block, here, :].astype(F32)
            signal = signal_refs[offset][4, here, :].astype(F32)
            gate = gate_refs[offset][here, :].astype(F32)
            out_ref[block_at(block, step), :] = (gate * (convolved + skip * signal)).astype(BF16)


def gate(skip, keep, arrived, first, second, pieces):
    chips, rows, lanes = keep.shape
    return pl.pallas_call(
        functools.partial(gate_kernel, chips),
        in_specs=[WHOLE] * (3 + 2 * chips),
        out_specs=[WHOLE] * pieces,
        out_shape=[jax.ShapeDtypeStruct((chips * rows // pieces, lanes), BF16)] * pieces,
        cost_estimate=CHEAP,
        compiler_params=pltpu.CompilerParams(vmem_limit_bytes=6 * 2**20),
        name="gate",
    )(skip, keep, arrived, *first, *second)


def collect_kernel(chips, *refs):
    in_refs, out_ref = refs[:chips], refs[chips]
    chip, _ = own_place()
    layer = lax.axis_index("chan")
    depth, share = out_ref.shape[1:]
    half = depth // 2
    start = in_refs[0].shape[0] - half
    for offset in range(chips):
        for part in range(2):
            block = in_refs[offset][pl.ds(start, half), pl.ds(part * share, share)]
            out_ref[chip ^ layer ^ offset, pl.ds(part * half, half), :] = block


def collect(second, depth):
    chips = len(second)
    return pl.pallas_call(
        functools.partial(collect_kernel, chips),
        in_specs=[WHOLE] * chips,
        out_specs=WHOLE,
        out_shape=jax.ShapeDtypeStruct((chips, depth, second[0].shape[1] // 2), BF16),
        cost_estimate=CHEAP,
        compiler_params=pltpu.CompilerParams(vmem_limit_bytes=4 * 2**20),
        name="collect_weights",
    )(*second)


def arrange_kernel(own_ref, other_ref, out_ref):
    _, core = own_place()
    share = own_ref.shape[2]
    out_ref[:, :, block_at(core, share)] = own_ref[...]
    out_ref[:, :, block_at(1 - core, share)] = other_ref[...]


def arrange(own, other):
    layers, rows, share = own.shape
    return pl.pallas_call(
        arrange_kernel,
        in_specs=[WHOLE] * 2,
        out_specs=WHOLE,
        out_shape=jax.ShapeDtypeStruct((layers, rows, 2 * share), BF16),
        cost_estimate=CHEAP,
        compiler_params=pltpu.CompilerParams(vmem_limit_bytes=8 * 2**20),
        name="arrange_weights",
    )(own, other)


def project_kernel(chips, weight_ref, *refs):
    gated_refs, (keep_ref, pass_ref, send_ref, joined_ref) = refs[:chips], refs[chips:]
    chip, _ = own_place()
    lanes = gated_refs[0].shape[1]
    for offset in range(chips):
        joined_ref[:, block_at(chip ^ offset, lanes)] = gated_refs[offset][...]

    def partial_of(target):
        return jnp.dot(joined_ref[...], weight_ref[target], preferred_element_type=F32).astype(BF16)

    send_ref[0] = partial_of(1)
    send_ref[1] = partial_of(3)
    pass_ref[...] = partial_of(2)
    keep_ref[...] = partial_of(0)


def project(weight, gated):
    chips = len(gated)
    _, depth, columns = weight.shape
    rows = gated[0].shape[0]
    block = jax.ShapeDtypeStruct((rows, columns), BF16)
    return pl.pallas_call(
        functools.partial(project_kernel, chips),
        in_specs=[WHOLE] * (1 + chips),
        out_specs=[WHOLE] * 3,
        out_shape=[block, block, jax.ShapeDtypeStruct((2, rows, columns), BF16)],
        scratch_shapes=[pltpu.VMEM((rows, depth), BF16)],
        cost_estimate=CHEAP,
        compiler_params=pltpu.CompilerParams(vmem_limit_bytes=8 * 2**20),
        name="project",
    )(weight, *gated)


def finish_kernel(chips, pieces, *refs):
    keep_refs, first_refs, second_refs = refs[:pieces], refs[pieces : 2 * pieces], refs[2 * pieces : 3 * pieces]
    out_refs = refs[3 * pieces :]
    chip, _ = own_place()
    step = keep_refs[0].shape[0] // chips
    for offset in range(chips):
        here = block_at(chip ^ offset, step)
        for piece in range(pieces):
            total = keep_refs[piece][here, :].astype(F32) + first_refs[piece][0, here, :].astype(F32)
            total = total + second_refs[piece][here, :].astype(F32)
            out_refs[offset][pl.ds(piece * step, step), :] = total.astype(BF16)


def finish(keep, first, second, chips):
    pieces = len(keep)
    rows, columns = keep[0].shape
    return pl.pallas_call(
        functools.partial(finish_kernel, chips, pieces),
        in_specs=[WHOLE] * (3 * pieces),
        out_specs=[WHOLE] * chips,
        out_shape=[jax.ShapeDtypeStruct((rows * pieces // chips, columns), BF16)] * chips,
        cost_estimate=CHEAP,
        compiler_params=pltpu.CompilerParams(vmem_limit_bytes=4 * 2**20),
        name="finish",
    )(*keep, *first, *second)


def join_kernel(chips, *refs):
    in_refs, out_ref = refs[:chips], refs[chips]
    chip, _ = own_place()
    share = in_refs[0].shape[1] // 2
    for offset in range(chips):
        for part in range(2):
            block = in_refs[offset][:, pl.ds(part * share, share)]
            out_ref[:, block_at(part * chips + (chip ^ offset), share)] = block


def join(blocks):
    chips = len(blocks)
    rows, columns = blocks[0].shape
    return pl.pallas_call(
        functools.partial(join_kernel, chips),
        in_specs=[WHOLE] * chips,
        out_specs=WHOLE,
        out_shape=jax.ShapeDtypeStruct((rows, chips * columns), BF16),
        cost_estimate=CHEAP,
        compiler_params=pltpu.CompilerParams(vmem_limit_bytes=2 * 2**20),
        name="join",
    )(*blocks)


def swapped(value, axis, offset):
    if not offset:
        return value
    return lax.ppermute(value, axis, [(source, source ^ offset) for source in range(lax.axis_size(axis))])


def to_chips(blocks):
    return [swapped(block, "seq", 2 * offset) for offset, block in enumerate(blocks)]


def after(value, *others):
    return lax.optimization_barrier((value, *others))[0]


def shards_direct(values_in, gate_values, filter_spectrum, skip_gain, out_weight):
    parts = lax.axis_size("seq")
    chips = parts // 2
    rows, width = values_in.shape
    tables = small_tables(parts, rows)

    first = pack_signals(values_in, filter_spectrum.reshape(4, rows, width), chips, tuple(range(chips)))
    second = pack_weights(after(gate_values, first[0]), out_weight, chips)
    first = to_chips(first)
    own = jnp.stack([after(block, second[0])[4] for block in first])
    second = to_chips(second)
    spectrum = forward(own, swapped(own, "seq", 1), tables)
    keep, send = backward(spectrum, first, tables)
    gated = gate(skip_gain[None, :], keep, swapped(send, "seq", 1), first, second, 2)
    own_weight = collect([after(block, *gated) for block in second], out_weight.shape[0])
    weight = arrange(own_weight, swapped(own_weight, "seq", 1))

    kept, arrived, passed = [], [], []
    for piece in gated:
        keep, second_keep, send = project(weight, to_chips([piece] * chips))
        kept.append(keep)
        arrived.append(swapped(send, "chan", 1))
        passed.append(swapped((second_keep.astype(F32) + arrived[-1][1].astype(F32)).astype(BF16), "chan", 2))
    return join(to_chips(finish(kept, arrived, passed, chips)))


def shards(values_in, gate_values, filter_spectrum, skip_gain, out_weight):
    parts, layers = lax.axis_size("seq"), lax.axis_size("chan")
    rows, width = values_in.shape
    share = out_weight.shape[1] // layers
    aligned = width // parts % 128 == 0 and share % 128 == 0 and rows % 32 == 0
    run = shards_direct if aligned and layers == 4 and parts == 8 else shards_general
    return run(values_in, gate_values, filter_spectrum, skip_gain, out_weight)


def solution(mesh):
    in_specs = (
        P("seq", "chan"),
        P("seq", "chan"),
        P(None, "seq", None, "chan"),
        P("chan"),
        P("chan", "seq"),
    )
    out_specs = P("seq", "chan")
    return jax.shard_map(shards, mesh=mesh, in_specs=in_specs, out_specs=out_specs, check_vma=False)
```

```python
import functools

import jax
import jax.numpy as jnp
import numpy as np
from jax import lax
from jax.experimental import pallas as pl
from jax.experimental.pallas import tpu as pltpu
from jax.sharding import PartitionSpec as P

BF16 = jnp.bfloat16
F32 = jnp.float32


def bit_reversed(number, width_bits):
    flipped = 0
    for bit_place in range(width_bits):
        flipped |= (number >> bit_place & 1) << (width_bits - 1 - bit_place)
    return flipped


def filter_row(residue, width_bits):
    return 2 * bit_reversed(residue // 2, width_bits) + residue % 2


def dft_tables(parts, rows):
    total = 2 * parts * rows
    residue = np.arange(2 * parts)[:, None, None]
    column = np.arange(rows)[None, :, None]
    position = np.arange(rows)[None, None, :]
    phase = 2.0 * np.pi * (position * (residue + 2 * parts * column) % total) / total
    cos, sin = np.cos(phase), np.sin(phase)
    forward = np.concatenate(
        [np.concatenate([cos, sin], axis=2), np.concatenate([-sin, cos], axis=2)], axis=1
    )
    inverse = np.transpose(forward, (0, 2, 1)) / total
    return forward.astype(BF16), inverse.astype(BF16)


def convolve_kernel(parts, rows, moved_ref, skip_ref, forward_ref, inverse_ref, out_ref, waves_ref, back_ref):
    width_bits = parts.bit_length() - 1
    chunk = 16

    def cosine(residue, block):
        return float(np.cos(np.pi * residue * block / parts))

    def sine(residue, block):
        return float(np.sin(np.pi * residue * block / parts))

    def spread(index, carry):
        here = pl.ds(index * chunk, chunk)
        there = pl.ds(rows + index * chunk, chunk)
        blocks = [moved_ref[block, here, :].astype(F32) for block in range(parts)]
        for residue in range(parts + 1):
            real = blocks[0]
            imag = jnp.zeros_like(real)
            for block in range(1, parts):
                real = real + cosine(residue, block) * blocks[block]
                imag = imag - sine(residue, block) * blocks[block]
            waves_ref[residue, here, :] = real.astype(BF16)
            waves_ref[residue, there, :] = imag.astype(BF16)
            if 0 < residue < parts:
                waves_ref[2 * parts - residue, here, :] = real.astype(BF16)
                waves_ref[2 * parts - residue, there, :] = (-imag).astype(BF16)
        return carry

    lax.fori_loop(0, rows // chunk, spread, 0)

    def through(residue):
        wave = jnp.dot(forward_ref[residue], waves_ref[residue], preferred_element_type=F32)
        source, odd = divmod(filter_row(residue, width_bits), 2)
        filter_real = moved_ref[source, pl.ds((2 + odd) * rows, rows), :].astype(F32)
        filter_imag = moved_ref[source, pl.ds((4 + odd) * rows, rows), :].astype(F32)
        real, imag = wave[:rows], wave[rows:]
        product = jnp.concatenate(
            [real * filter_real - imag * filter_imag, real * filter_imag + imag * filter_real], axis=0
        )
        return jnp.dot(inverse_ref[residue], product.astype(BF16), preferred_element_type=F32)

    for residue in range(parts + 1):
        back = through(residue)
        if 0 < residue < parts:
            other = through(2 * parts - residue)
            back_ref[residue, pl.ds(0, rows), :] = back[:rows] + other[:rows]
            back_ref[residue, pl.ds(rows, rows), :] = back[rows:] - other[rows:]
        else:
            back_ref[residue] = back

    skip = skip_ref[...]

    def gather(index, carry):
        here = pl.ds(index * chunk, chunk)
        there = pl.ds(rows + index * chunk, chunk)
        reals = [back_ref[residue, here, :] for residue in range(parts + 1)]
        imags = [back_ref[residue, there, :] for residue in range(parts + 1)]
        for block in range(parts):
            total = reals[0]
            for residue in range(1, parts + 1):
                total = total + cosine(residue, block) * reals[residue]
                if residue < parts and block:
                    total = total - sine(residue, block) * imags[residue]
            signal = moved_ref[block, here, :].astype(F32)
            gate = moved_ref[block, pl.ds(rows + index * chunk, chunk), :].astype(F32)
            out_ref[block, here, :] = (gate * (total + skip * signal)).astype(BF16)
        return carry

    lax.fori_loop(0, rows // chunk, gather, 0)


def convolve(moved, skip):
    parts, stacked, width = moved.shape
    rows = stacked // 6
    forward, inverse = dft_tables(parts, rows)
    whole = pl.BlockSpec(memory_space=pltpu.VMEM)
    return pl.pallas_call(
        functools.partial(convolve_kernel, parts, rows),
        out_shape=jax.ShapeDtypeStruct((parts, rows, width), BF16),
        in_specs=[whole] * 4,
        out_specs=whole,
        scratch_shapes=[
            pltpu.VMEM((2 * parts, 2 * rows, width), BF16),
            pltpu.VMEM((parts + 1, 2 * rows, width), F32),
        ],
        compiler_params=pltpu.CompilerParams(vmem_limit_bytes=40 * 2**20),
    )(moved, skip[None, :], forward, inverse)


def shards_general(values_in, gate_values, filter_spectrum, skip_gain, out_weight):
    parts = lax.axis_size("seq")
    layers = lax.axis_size("chan")
    rows, width = values_in.shape
    lanes = width // parts
    device = lax.axis_index("seq")

    def by_channel(array):
        return jnp.transpose(array.reshape(array.shape[0], parts, lanes), (1, 0, 2))

    filters = filter_spectrum.astype(BF16).reshape(4 * rows, width)
    packed = jnp.concatenate([by_channel(values_in), by_channel(gate_values), by_channel(filters)], axis=1)
    moved = lax.all_to_all(packed, "seq", 0, 0)
    skip = lax.dynamic_slice_in_dim(skip_gain, device * lanes, lanes)
    gated = convolve(moved, skip)
    gathered = lax.all_gather(gated.reshape(parts * rows, lanes), "seq", axis=1, tiled=True)

    own_cols = out_weight.shape[1]
    share = own_cols * parts // layers // parts
    per_block = parts // layers
    pieces = own_cols // share
    group = device % per_block
    member = device // per_block
    weight = jnp.zeros_like(out_weight)
    for step in range(pieces):
        piece = (member + step) % pieces
        sent = lax.dynamic_slice_in_dim(out_weight, piece * share, share, 1)
        pairs = [
            (source, source % per_block * pieces + (source // per_block + step) % pieces) for source in range(parts)
        ]
        arrived = lax.ppermute(sent, "seq", pairs)
        block = (device % pieces - step) % pieces
        weight = lax.dynamic_update_slice_in_dim(weight, arrived, block * share, 1)
    partials = jnp.dot(gathered, weight, preferred_element_type=F32).astype(BF16)
    mixed = lax.psum_scatter(partials, "chan", scatter_dimension=1, tiled=True)
    return lax.all_to_all(mixed, "seq", 0, 1, tiled=True)


WHOLE = pl.BlockSpec(memory_space=pltpu.VMEM)
CHEAP = pl.CostEstimate(flops=0, transcendentals=0, bytes_accessed=0)


def small_tables(parts, rows):
    total = 2 * parts * rows
    index = np.arange(rows)
    phase = 2.0 * np.pi * (index[:, None] * index[None, :] % rows) / rows
    cos, sin = np.cos(phase), np.sin(phase)
    forward = np.block([[cos, sin], [-sin, cos]])
    residue = np.arange(2 * parts).reshape(2, 1, parts)
    turn = 2.0 * np.pi * index[None, :, None] * residue / total
    return forward.astype(BF16), forward.T.astype(BF16), np.cos(turn).astype(F32), np.sin(turn).astype(F32)


def cosine(parts, residue, block):
    return float(np.cos(np.pi * residue * block / parts))


def sine(parts, residue, block):
    return float(np.sin(np.pi * residue * block / parts))


def weighted(terms):
    total = None
    for factor, term in terms:
        if abs(factor) < 1e-12:
            continue
        part = term if factor == 1.0 else factor * term
        total = part if total is None else total + part
    return total


def plus(left, right):
    return left if right is None else right if left is None else left + right


def minus(left, right):
    return left if right is None else -right if left is None else left - right


def own_place():
    device = lax.axis_index("seq")
    return device // 2, device % 2


def block_at(index, size):
    return pl.ds(pl.multiple_of(index * size, size), size)


def pack_signals_kernel(offsets, filter_ref, values_ref, *refs):
    out_refs, (plane_ref, arrived) = refs[: len(offsets)], refs[len(offsets) :]
    chip, _ = own_place()
    planes = filter_ref.shape[0]
    lanes = out_refs[0].shape[2]
    copies, work = [], []
    for place, offset in enumerate(offsets):
        here = block_at(chip ^ offset, lanes)
        for plane in range(planes):
            copies.append(
                pltpu.make_async_copy(filter_ref.at[plane, :, here], plane_ref.at[place, plane], arrived.at[place, plane])
            )
            work.append((place, plane))
        copies.append(
            pltpu.make_async_copy(values_ref.at[:, here], out_refs[place].at[planes], arrived.at[place, planes])
        )
        work.append(None)
    for copy in copies:
        copy.start()
    for copy, task in zip(copies, work):
        copy.wait()
        if task:
            place, plane = task
            out_refs[place][plane] = plane_ref[place, plane].astype(BF16)


def pack_signals(values_in, filters, chips, offsets):
    planes, rows, width = filters.shape
    lanes = width // chips
    return pl.pallas_call(
        functools.partial(pack_signals_kernel, offsets),
        in_specs=[pl.BlockSpec(memory_space=pltpu.HBM)] * 2,
        out_specs=[WHOLE] * len(offsets),
        out_shape=[jax.ShapeDtypeStruct((planes + 1, rows, lanes), BF16)] * len(offsets),
        scratch_shapes=[
            pltpu.VMEM((len(offsets), planes, rows, lanes), F32),
            pltpu.SemaphoreType.DMA((len(offsets), planes + 1)),
        ],
        cost_estimate=CHEAP,
        compiler_params=pltpu.CompilerParams(vmem_limit_bytes=8 * 2**20),
        name="pack_signals",
    )(*(pltpu.with_memory_space_constraint(array, pltpu.HBM) for array in (filters, values_in)))


def pack_gates_kernel(chips, gate_ref, *refs):
    out_refs, arrived = refs[:chips], refs[chips]
    chip, _ = own_place()
    copies = []
    for offset, out_ref in enumerate(out_refs):
        gates = gate_ref.at[:, block_at(chip ^ offset, out_ref.shape[1])]
        copies.append(pltpu.make_async_copy(gates, out_ref, arrived.at[offset]))
    for copy in copies:
        copy.start()
    for copy in copies:
        copy.wait()


def pack_gates(gate_values, chips):
    rows, width = gate_values.shape
    return pl.pallas_call(
        functools.partial(pack_gates_kernel, chips),
        in_specs=[pl.BlockSpec(memory_space=pltpu.HBM)],
        out_specs=[WHOLE] * chips,
        out_shape=[jax.ShapeDtypeStruct((rows, width // chips), BF16)] * chips,
        scratch_shapes=[pltpu.SemaphoreType.DMA((chips,))],
        cost_estimate=CHEAP,
        compiler_params=pltpu.CompilerParams(vmem_limit_bytes=4 * 2**20),
        name="pack_gates",
    )(pltpu.with_memory_space_constraint(gate_values, pltpu.HBM))


def forward_kernel(chips, cos_ref, sin_ref, table_ref, own_ref, other_ref, out_ref, signal_ref, waves_ref):
    chip, core = own_place()
    parts = 2 * chips
    rows, lanes = own_ref.shape[1:]
    chunk, width = 16, 128
    for offset in range(chips):
        signal_ref[2 * (chip ^ offset) + core] = own_ref[offset]
        signal_ref[2 * (chip ^ offset) + 1 - core] = other_ref[offset]
    sign = (1 - 2 * core).astype(F32)

    def spread(index, carry):
        here = block_at(index, chunk)
        there = pl.ds(pl.multiple_of(rows + index * chunk, chunk), chunk)
        cos_all, sin_all = cos_ref[core, here, :], sin_ref[core, here, :]
        for start in range(0, lanes, width):
            blocks = [signal_ref[block, here, pl.ds(start, width)].astype(F32) for block in range(parts)]
            blocks = [block * sign if place % 2 else block for place, block in enumerate(blocks)]

            def store(residue, real, imag):
                cos, sin = cos_all[:, residue : residue + 1], sin_all[:, residue : residue + 1]
                if imag is None:
                    real, imag = real * cos, -(real * sin)
                else:
                    real, imag = real * cos + imag * sin, imag * cos - real * sin
                columns = pl.ds(residue * lanes + start, width)
                waves_ref[here, columns] = real.astype(BF16)
                waves_ref[there, columns] = imag.astype(BF16)

            for residue in range(parts // 2 + 1):
                even, odd = range(0, parts, 2), range(1, parts, 2)
                cos_even = weighted([(cosine(parts, residue, block), blocks[block]) for block in even])
                cos_odd = weighted([(cosine(parts, residue, block), blocks[block]) for block in odd])
                sin_even = weighted([(sine(parts, residue, block), blocks[block]) for block in even])
                sin_odd = weighted([(sine(parts, residue, block), blocks[block]) for block in odd])
                sin_sum = plus(sin_even, sin_odd)
                store(residue, plus(cos_even, cos_odd), None if sin_sum is None else -sin_sum)
                if 0 < residue and 2 * residue != parts:
                    store(parts - residue, minus(cos_even, cos_odd), minus(sin_even, sin_odd))
        return carry

    lax.fori_loop(0, rows // chunk, spread, 0)
    for residue in range(parts):
        columns = pl.ds(residue * lanes, lanes)
        out_ref[:, columns] = jnp.dot(table_ref[...], waves_ref[:, columns], preferred_element_type=F32)


def forward(own, other, tables):
    chips, rows, lanes = own.shape
    table, _, cos, sin = tables
    spectrum = (2 * rows, 2 * chips * lanes)
    return pl.pallas_call(
        functools.partial(forward_kernel, chips),
        in_specs=[WHOLE] * 5,
        out_specs=WHOLE,
        out_shape=jax.ShapeDtypeStruct(spectrum, F32),
        scratch_shapes=[pltpu.VMEM((2 * chips, rows, lanes), BF16), pltpu.VMEM(spectrum, BF16)],
        cost_estimate=CHEAP,
        compiler_params=pltpu.CompilerParams(vmem_limit_bytes=32 * 2**20),
        name="forward",
    )(cos, sin, table, own, other)


def backward_kernel(chips, cos_ref, sin_ref, table_ref, spectrum_ref, *refs):
    filter_refs, (keep_ref, send_ref, filter_ref, product_ref, back_ref) = refs[:chips], refs[chips:]
    chip, core = own_place()
    parts = 2 * chips
    rows, lanes = keep_ref.shape[1:]
    chip_bits = chips.bit_length() - 1
    chunk, width = 16, 128
    for offset in range(chips):
        filter_ref[chip ^ offset] = filter_refs[offset][pl.ds(0, 4)]

    for residue in range(parts):
        source, odd = bit_reversed(residue // 2, chip_bits), residue % 2
        columns = pl.ds(residue * lanes, lanes)
        filter_real = filter_ref[source, odd].astype(F32)
        filter_imag = filter_ref[source, 2 + odd].astype(F32)
        real = spectrum_ref[pl.ds(0, rows), columns]
        imag = spectrum_ref[pl.ds(rows, rows), columns]
        product_ref[pl.ds(0, rows), columns] = (real * filter_real - imag * filter_imag).astype(BF16)
        product_ref[pl.ds(rows, rows), columns] = (real * filter_imag + imag * filter_real).astype(BF16)
        back_ref[:, columns] = jnp.dot(table_ref[...], product_ref[:, columns], preferred_element_type=F32)

    scale = 1.0 / (2 * parts * rows)
    sign = (1 - 2 * core).astype(F32)
    upper = core == 1

    def gather(index, carry):
        here = block_at(index, chunk)
        there = pl.ds(pl.multiple_of(rows + index * chunk, chunk), chunk)
        cos_all, sin_all = cos_ref[core, here, :] * scale, sin_ref[core, here, :] * scale
        for start in range(0, lanes, width):
            reals, imags = [], []
            for residue in range(parts):
                columns = pl.ds(residue * lanes + start, width)
                real, imag = back_ref[here, columns], back_ref[there, columns]
                cos, sin = cos_all[:, residue : residue + 1], sin_all[:, residue : residue + 1]
                reals.append(real * cos - imag * sin)
                imags.append(real * sin + imag * cos)
            totals = [None] * parts
            for block in range(parts // 2 + 1):
                even, odd = range(0, parts, 2), range(1, parts, 2)
                cos_even = weighted([(cosine(parts, residue, block), reals[residue]) for residue in even])
                cos_odd = weighted([(cosine(parts, residue, block), reals[residue]) for residue in odd])
                sin_even = weighted([(sine(parts, residue, block), imags[residue]) for residue in even])
                sin_odd = weighted([(sine(parts, residue, block), imags[residue]) for residue in odd])
                totals[block] = minus(plus(cos_even, cos_odd), plus(sin_even, sin_odd))
                if 0 < block and 2 * block != parts:
                    totals[parts - block] = plus(minus(cos_even, cos_odd), minus(sin_even, sin_odd))
            lane = pl.ds(start, width)
            for pair in range(chips):
                low, high = totals[2 * pair], totals[2 * pair + 1] * sign
                keep_ref[pair, here, lane] = jnp.where(upper, high, low)
                send_ref[pair, here, lane] = jnp.where(upper, low, high).astype(BF16)
        return carry

    lax.fori_loop(0, rows // chunk, gather, 0)


def backward(spectrum, first, tables):
    chips = len(first)
    _, rows, lanes = first[0].shape
    _, table, cos, sin = tables
    kept = (chips, rows, lanes)
    return pl.pallas_call(
        functools.partial(backward_kernel, chips),
        in_specs=[WHOLE] * (4 + chips),
        out_specs=[WHOLE] * 2,
        out_shape=[jax.ShapeDtypeStruct(kept, F32), jax.ShapeDtypeStruct(kept, BF16)],
        scratch_shapes=[
            pltpu.VMEM((chips, 4, rows, lanes), BF16),
            pltpu.VMEM(spectrum.shape, BF16),
            pltpu.VMEM(spectrum.shape, F32),
        ],
        cost_estimate=CHEAP,
        compiler_params=pltpu.CompilerParams(vmem_limit_bytes=32 * 2**20),
        name="backward",
    )(cos, sin, table, spectrum, *first)


def gate_kernel(chips, skip_ref, keep_ref, arrived_ref, *refs):
    signal_refs, gate_refs, out_ref = refs[:chips], refs[chips : 2 * chips], refs[2 * chips]
    chip, _ = own_place()
    rows, lanes = keep_ref.shape[1:]
    skip = skip_ref[:, block_at(chip, lanes)]
    for offset in range(chips):
        block = chip ^ offset
        convolved = keep_ref[block] + arrived_ref[block].astype(F32)
        signal = signal_refs[offset][4].astype(F32)
        gate = gate_refs[offset][...].astype(F32)
        out_ref[block_at(block, rows), :] = (gate * (convolved + skip * signal)).astype(BF16)


def gate(skip, keep, arrived, first, gates):
    chips, rows, lanes = keep.shape
    return pl.pallas_call(
        functools.partial(gate_kernel, chips),
        in_specs=[WHOLE] * (3 + 2 * chips),
        out_specs=WHOLE,
        out_shape=jax.ShapeDtypeStruct((chips * rows, lanes), BF16),
        cost_estimate=CHEAP,
        compiler_params=pltpu.CompilerParams(vmem_limit_bytes=6 * 2**20),
        name="gate",
    )(skip, keep, arrived, *first, *gates)


def project_kernel(chips, own_ref, other_ref, *refs):
    gated_refs, out_refs, (joined_ref, weight_ref) = refs[:chips], refs[chips : 2 * chips], refs[2 * chips :]
    chip, core = own_place()
    layer = lax.axis_index("chan")
    held = own_ref.shape[1]
    lanes = gated_refs[0].shape[1]
    rows = out_refs[0].shape[0]
    for offset in range(chips):
        joined_ref[:, block_at(chip ^ offset, lanes)] = gated_refs[offset][...]
    weight_ref[:, block_at(core, held)] = own_ref[...]
    weight_ref[:, block_at(1 - core, held)] = other_ref[...]
    for step in range(chips):
        gated = joined_ref[block_at(chip ^ layer ^ step, rows), :]
        out_refs[step][...] = jnp.dot(gated, weight_ref[...], preferred_element_type=F32).astype(BF16)


def project(own, other, gated):
    chips = len(gated)
    depth, held = own.shape
    rows = gated[0].shape[0] // chips
    return pl.pallas_call(
        functools.partial(project_kernel, chips),
        in_specs=[WHOLE] * (2 + chips),
        out_specs=[WHOLE] * chips,
        out_shape=[jax.ShapeDtypeStruct((rows, 2 * held), BF16)] * chips,
        scratch_shapes=[pltpu.VMEM((rows * chips, depth), BF16), pltpu.VMEM((depth, 2 * held), BF16)],
        cost_estimate=CHEAP,
        compiler_params=pltpu.CompilerParams(vmem_limit_bytes=12 * 2**20),
        name="project",
    )(own, other, *gated)


def swapped(value, axis, offset):
    if not offset:
        return value
    return lax.ppermute(value, axis, [(source, source ^ offset) for source in range(lax.axis_size(axis))])


def to_chips(blocks):
    return [swapped(block, "seq", 2 * offset) for offset, block in enumerate(blocks)]


def after(value, *others):
    return lax.optimization_barrier((value, *others))[0]


def to_layers(partials):
    chips = len(partials)
    arrived = []
    for step, partial in enumerate(partials):
        pairs = []
        for chip in range(chips):
            for core in range(2):
                for layer in range(chips):
                    source = (2 * chip + core) * chips + layer
                    pairs.append((source, (2 * (chip ^ layer ^ step) + core) * chips + chip))
        arrived.append(lax.ppermute(partial, ("seq", "chan"), pairs))
    return arrived


def shards_direct(values_in, gate_values, filter_spectrum, skip_gain, out_weight):
    parts = lax.axis_size("seq")
    chips = parts // 2
    rows, width = values_in.shape
    tables = small_tables(parts, rows)

    first = pack_signals(values_in, filter_spectrum.reshape(4, rows, width), chips, tuple(range(chips)))
    gates = pack_gates(after(gate_values, first[0]), chips)
    first = to_chips(first)
    own = jnp.stack([after(block, gates[0])[4] for block in first])
    gates = to_chips(gates)
    spectrum = forward(own, swapped(own, "seq", 1), tables)
    keep, send = backward(spectrum, first, tables)
    gated = gate(skip_gain[None, :], keep, swapped(send, "seq", 1), first, gates)

    partials = project(out_weight, swapped(out_weight, "seq", 1), to_chips([gated] * chips))
    arrived = to_layers(partials)
    total = arrived[0].astype(F32)
    for partial in arrived[1:]:
        total = total + partial.astype(F32)
    return total.astype(BF16)


def shards(values_in, gate_values, filter_spectrum, skip_gain, out_weight):
    parts, layers = lax.axis_size("seq"), lax.axis_size("chan")
    rows, width = values_in.shape
    share = out_weight.shape[1] // layers
    aligned = width // parts % 128 == 0 and share % 128 == 0 and rows % 32 == 0
    run = shards_direct if aligned and layers == 4 and parts == 8 else shards_general
    return run(values_in, gate_values, filter_spectrum, skip_gain, out_weight)


def solution(mesh):
    in_specs = (
        P("seq", "chan"),
        P("seq", "chan"),
        P(None, "seq", None, "chan"),
        P("chan"),
        P("chan", "seq"),
    )
    out_specs = P("seq", "chan")
    return jax.shard_map(shards, mesh=mesh, in_specs=in_specs, out_specs=out_specs, check_vma=False)
```

```python
import functools

import jax
import jax.numpy as jnp
import numpy as np
from jax import lax
from jax.experimental import pallas as pl
from jax.experimental.pallas import tpu as pltpu
from jax.sharding import PartitionSpec as P

BF16 = jnp.bfloat16
F32 = jnp.float32


def bit_reversed(number, width_bits):
    flipped = 0
    for bit_place in range(width_bits):
        flipped |= (number >> bit_place & 1) << (width_bits - 1 - bit_place)
    return flipped


def filter_row(residue, width_bits):
    return 2 * bit_reversed(residue // 2, width_bits) + residue % 2


def dft_tables(parts, rows):
    total = 2 * parts * rows
    residue = np.arange(2 * parts)[:, None, None]
    column = np.arange(rows)[None, :, None]
    position = np.arange(rows)[None, None, :]
    phase = 2.0 * np.pi * (position * (residue + 2 * parts * column) % total) / total
    cos, sin = np.cos(phase), np.sin(phase)
    forward = np.concatenate(
        [np.concatenate([cos, sin], axis=2), np.concatenate([-sin, cos], axis=2)], axis=1
    )
    inverse = np.transpose(forward, (0, 2, 1)) / total
    return forward.astype(BF16), inverse.astype(BF16)


def convolve_kernel(parts, rows, moved_ref, skip_ref, forward_ref, inverse_ref, out_ref, waves_ref, back_ref):
    width_bits = parts.bit_length() - 1
    chunk = 16

    def cosine(residue, block):
        return float(np.cos(np.pi * residue * block / parts))

    def sine(residue, block):
        return float(np.sin(np.pi * residue * block / parts))

    def spread(index, carry):
        here = pl.ds(index * chunk, chunk)
        there = pl.ds(rows + index * chunk, chunk)
        blocks = [moved_ref[block, here, :].astype(F32) for block in range(parts)]
        for residue in range(parts + 1):
            real = blocks[0]
            imag = jnp.zeros_like(real)
            for block in range(1, parts):
                real = real + cosine(residue, block) * blocks[block]
                imag = imag - sine(residue, block) * blocks[block]
            waves_ref[residue, here, :] = real.astype(BF16)
            waves_ref[residue, there, :] = imag.astype(BF16)
            if 0 < residue < parts:
                waves_ref[2 * parts - residue, here, :] = real.astype(BF16)
                waves_ref[2 * parts - residue, there, :] = (-imag).astype(BF16)
        return carry

    lax.fori_loop(0, rows // chunk, spread, 0)

    def through(residue):
        wave = jnp.dot(forward_ref[residue], waves_ref[residue], preferred_element_type=F32)
        source, odd = divmod(filter_row(residue, width_bits), 2)
        filter_real = moved_ref[source, pl.ds((2 + odd) * rows, rows), :].astype(F32)
        filter_imag = moved_ref[source, pl.ds((4 + odd) * rows, rows), :].astype(F32)
        real, imag = wave[:rows], wave[rows:]
        product = jnp.concatenate(
            [real * filter_real - imag * filter_imag, real * filter_imag + imag * filter_real], axis=0
        )
        return jnp.dot(inverse_ref[residue], product.astype(BF16), preferred_element_type=F32)

    for residue in range(parts + 1):
        back = through(residue)
        if 0 < residue < parts:
            other = through(2 * parts - residue)
            back_ref[residue, pl.ds(0, rows), :] = back[:rows] + other[:rows]
            back_ref[residue, pl.ds(rows, rows), :] = back[rows:] - other[rows:]
        else:
            back_ref[residue] = back

    skip = skip_ref[...]

    def gather(index, carry):
        here = pl.ds(index * chunk, chunk)
        there = pl.ds(rows + index * chunk, chunk)
        reals = [back_ref[residue, here, :] for residue in range(parts + 1)]
        imags = [back_ref[residue, there, :] for residue in range(parts + 1)]
        for block in range(parts):
            total = reals[0]
            for residue in range(1, parts + 1):
                total = total + cosine(residue, block) * reals[residue]
                if residue < parts and block:
                    total = total - sine(residue, block) * imags[residue]
            signal = moved_ref[block, here, :].astype(F32)
            gate = moved_ref[block, pl.ds(rows + index * chunk, chunk), :].astype(F32)
            out_ref[block, here, :] = (gate * (total + skip * signal)).astype(BF16)
        return carry

    lax.fori_loop(0, rows // chunk, gather, 0)


def convolve(moved, skip):
    parts, stacked, width = moved.shape
    rows = stacked // 6
    forward, inverse = dft_tables(parts, rows)
    whole = pl.BlockSpec(memory_space=pltpu.VMEM)
    return pl.pallas_call(
        functools.partial(convolve_kernel, parts, rows),
        out_shape=jax.ShapeDtypeStruct((parts, rows, width), BF16),
        in_specs=[whole] * 4,
        out_specs=whole,
        scratch_shapes=[
            pltpu.VMEM((2 * parts, 2 * rows, width), BF16),
            pltpu.VMEM((parts + 1, 2 * rows, width), F32),
        ],
        compiler_params=pltpu.CompilerParams(vmem_limit_bytes=40 * 2**20),
    )(moved, skip[None, :], forward, inverse)


def shards_general(values_in, gate_values, filter_spectrum, skip_gain, out_weight):
    parts = lax.axis_size("seq")
    layers = lax.axis_size("chan")
    rows, width = values_in.shape
    lanes = width // parts
    device = lax.axis_index("seq")

    def by_channel(array):
        return jnp.transpose(array.reshape(array.shape[0], parts, lanes), (1, 0, 2))

    filters = filter_spectrum.astype(BF16).reshape(4 * rows, width)
    packed = jnp.concatenate([by_channel(values_in), by_channel(gate_values), by_channel(filters)], axis=1)
    moved = lax.all_to_all(packed, "seq", 0, 0)
    skip = lax.dynamic_slice_in_dim(skip_gain, device * lanes, lanes)
    gated = convolve(moved, skip)
    gathered = lax.all_gather(gated.reshape(parts * rows, lanes), "seq", axis=1, tiled=True)

    own_cols = out_weight.shape[1]
    share = own_cols * parts // layers // parts
    per_block = parts // layers
    pieces = own_cols // share
    group = device % per_block
    member = device // per_block
    weight = jnp.zeros_like(out_weight)
    for step in range(pieces):
        piece = (member + step) % pieces
        sent = lax.dynamic_slice_in_dim(out_weight, piece * share, share, 1)
        pairs = [
            (source, source % per_block * pieces + (source // per_block + step) % pieces) for source in range(parts)
        ]
        arrived = lax.ppermute(sent, "seq", pairs)
        block = (device % pieces - step) % pieces
        weight = lax.dynamic_update_slice_in_dim(weight, arrived, block * share, 1)
    partials = jnp.dot(gathered, weight, preferred_element_type=F32).astype(BF16)
    mixed = lax.psum_scatter(partials, "chan", scatter_dimension=1, tiled=True)
    return lax.all_to_all(mixed, "seq", 0, 1, tiled=True)


WHOLE = pl.BlockSpec(memory_space=pltpu.VMEM)
CHEAP = pl.CostEstimate(flops=0, transcendentals=0, bytes_accessed=0)


def small_tables(parts, rows):
    total = 2 * parts * rows
    index = np.arange(rows)
    phase = 2.0 * np.pi * (index[:, None] * index[None, :] % rows) / rows
    cos, sin = np.cos(phase), np.sin(phase)
    forward = np.block([[cos, sin], [-sin, cos]])
    residue = np.arange(2 * parts).reshape(2, 1, parts)
    turn = 2.0 * np.pi * index[None, :, None] * residue / total
    return forward.astype(BF16), forward.T.astype(BF16), np.cos(turn).astype(F32), np.sin(turn).astype(F32)


def cosine(parts, residue, block):
    return float(np.cos(np.pi * residue * block / parts))


def sine(parts, residue, block):
    return float(np.sin(np.pi * residue * block / parts))


def weighted(terms):
    total = None
    for factor, term in terms:
        if abs(factor) < 1e-12:
            continue
        part = term if factor == 1.0 else factor * term
        total = part if total is None else total + part
    return total


def plus(left, right):
    return left if right is None else right if left is None else left + right


def minus(left, right):
    return left if right is None else -right if left is None else left - right


def own_place():
    device = lax.axis_index("seq")
    return device // 2, device % 2


def block_at(index, size):
    return pl.ds(pl.multiple_of(index * size, size), size)


def pack_signals_kernel(offsets, filter_ref, values_ref, *refs):
    out_refs, (plane_ref, arrived) = refs[: len(offsets)], refs[len(offsets) :]
    chip, _ = own_place()
    planes = filter_ref.shape[0]
    lanes = out_refs[0].shape[2]
    copies, work = [], []
    for place, offset in enumerate(offsets):
        here = block_at(chip ^ offset, lanes)
        for plane in range(planes):
            copies.append(
                pltpu.make_async_copy(filter_ref.at[plane, :, here], plane_ref.at[place, plane], arrived.at[place, plane])
            )
            work.append((place, plane))
        copies.append(
            pltpu.make_async_copy(values_ref.at[:, here], out_refs[place].at[planes], arrived.at[place, planes])
        )
        work.append(None)
    for copy in copies:
        copy.start()
    for copy, task in zip(copies, work):
        copy.wait()
        if task:
            place, plane = task
            out_refs[place][plane] = plane_ref[place, plane].astype(BF16)


def pack_signals(values_in, filters, chips, offsets):
    planes, rows, width = filters.shape
    lanes = width // chips
    return pl.pallas_call(
        functools.partial(pack_signals_kernel, offsets),
        in_specs=[pl.BlockSpec(memory_space=pltpu.HBM)] * 2,
        out_specs=[WHOLE] * len(offsets),
        out_shape=[jax.ShapeDtypeStruct((planes + 1, rows, lanes), BF16)] * len(offsets),
        scratch_shapes=[
            pltpu.VMEM((len(offsets), planes, rows, lanes), F32),
            pltpu.SemaphoreType.DMA((len(offsets), planes + 1)),
        ],
        cost_estimate=CHEAP,
        compiler_params=pltpu.CompilerParams(vmem_limit_bytes=8 * 2**20),
        name="pack_signals",
    )(*(pltpu.with_memory_space_constraint(array, pltpu.HBM) for array in (filters, values_in)))


def pack_moved_kernel(chips, gate_ref, own_ref, other_ref, *refs):
    out_refs, arrived = refs[:chips], refs[chips]
    chip, core = own_place()
    rows = gate_ref.shape[0]
    depth, held = own_ref.shape
    quarter, share = depth // 4, held // chips

    def copies_from(weight_ref):
        copies = []
        for offset in range(chips):
            out_ref, target = out_refs[offset], chip ^ offset
            gates = gate_ref.at[:, block_at(target, out_ref.shape[1])]
            copies.append(pltpu.make_async_copy(gates, out_ref.at[pl.ds(0, rows)], arrived.at[offset, 2]))
            for part in range(2):
                source = weight_ref.at[block_at(2 * core + part, quarter), block_at(target, share)]
                sink = out_ref.at[pl.ds(rows, quarter), pl.ds(part * share, share)]
                copies.append(pltpu.make_async_copy(source, sink, arrived.at[offset, part]))
        for copy in copies:
            copy.start()
        for copy in copies:
            copy.wait()

    @pl.when(core == 0)
    def _():
        copies_from(own_ref)

    @pl.when(core == 1)
    def _():
        copies_from(other_ref)


def pack_moved(gate_values, own, other, chips):
    rows, width = gate_values.shape
    depth, held = own.shape
    return pl.pallas_call(
        functools.partial(pack_moved_kernel, chips),
        in_specs=[pl.BlockSpec(memory_space=pltpu.HBM)] * 2 + [pl.BlockSpec(memory_space=pl.ANY)],
        out_specs=[WHOLE] * chips,
        out_shape=[jax.ShapeDtypeStruct((rows + depth // 4, 2 * held // chips), BF16)] * chips,
        scratch_shapes=[pltpu.SemaphoreType.DMA((chips, 3))],
        cost_estimate=CHEAP,
        compiler_params=pltpu.CompilerParams(vmem_limit_bytes=8 * 2**20),
        name="pack_moved",
    )(*(pltpu.with_memory_space_constraint(array, pltpu.HBM) for array in (gate_values, own)), other)


def forward_kernel(chips, cos_ref, sin_ref, table_ref, *refs):
    own_refs, other_refs, (out_ref, signal_ref, waves_ref) = refs[:2], refs[2:4], refs[4:]
    chip, core = own_place()
    parts = 2 * chips
    rows, lanes = own_refs[0].shape[1:]
    chunk, width = 16, 128
    for offset in range(chips):
        part, place = divmod(offset, chips // 2)
        signal_ref[2 * (chip ^ offset) + core] = own_refs[part][place]
        signal_ref[2 * (chip ^ offset) + 1 - core] = other_refs[part][place]
    sign = (1 - 2 * core).astype(F32)

    def spread(index, carry):
        here = block_at(index, chunk)
        there = pl.ds(pl.multiple_of(rows + index * chunk, chunk), chunk)
        cos_all, sin_all = cos_ref[core, here, :], sin_ref[core, here, :]
        for start in range(0, lanes, width):
            blocks = [signal_ref[block, here, pl.ds(start, width)].astype(F32) for block in range(parts)]
            blocks = [block * sign if place % 2 else block for place, block in enumerate(blocks)]

            def store(residue, real, imag):
                cos, sin = cos_all[:, residue : residue + 1], sin_all[:, residue : residue + 1]
                if imag is None:
                    real, imag = real * cos, -(real * sin)
                else:
                    real, imag = real * cos + imag * sin, imag * cos - real * sin
                columns = pl.ds(residue * lanes + start, width)
                waves_ref[here, columns] = real.astype(BF16)
                waves_ref[there, columns] = imag.astype(BF16)

            for residue in range(parts // 2 + 1):
                even, odd = range(0, parts, 2), range(1, parts, 2)
                cos_even = weighted([(cosine(parts, residue, block), blocks[block]) for block in even])
                cos_odd = weighted([(cosine(parts, residue, block), blocks[block]) for block in odd])
                sin_even = weighted([(sine(parts, residue, block), blocks[block]) for block in even])
                sin_odd = weighted([(sine(parts, residue, block), blocks[block]) for block in odd])
                sin_sum = plus(sin_even, sin_odd)
                store(residue, plus(cos_even, cos_odd), None if sin_sum is None else -sin_sum)
                if 0 < residue and 2 * residue != parts:
                    store(parts - residue, minus(cos_even, cos_odd), minus(sin_even, sin_odd))
        return carry

    lax.fori_loop(0, rows // chunk, spread, 0)
    for residue in range(parts):
        columns = pl.ds(residue * lanes, lanes)
        out_ref[:, columns] = jnp.dot(table_ref[...], waves_ref[:, columns], preferred_element_type=F32)


def forward(own, other, tables):
    chips, (_, rows, lanes) = 2 * own[0].shape[0], own[0].shape
    table, _, cos, sin = tables
    spectrum = (2 * rows, 2 * chips * lanes)
    return pl.pallas_call(
        functools.partial(forward_kernel, chips),
        in_specs=[WHOLE] * 7,
        out_specs=WHOLE,
        out_shape=jax.ShapeDtypeStruct(spectrum, F32),
        scratch_shapes=[pltpu.VMEM((2 * chips, rows, lanes), BF16), pltpu.VMEM(spectrum, BF16)],
        cost_estimate=CHEAP,
        compiler_params=pltpu.CompilerParams(vmem_limit_bytes=32 * 2**20),
        name="forward",
    )(cos, sin, table, *own, *other)


def backward_kernel(chips, cos_ref, sin_ref, table_ref, spectrum_ref, *refs):
    filter_refs, (keep_ref, *send_refs, filter_ref, product_ref, back_ref) = refs[:chips], refs[chips:]
    chip, core = own_place()
    parts = 2 * chips
    rows, lanes = keep_ref.shape[1:]
    chip_bits = chips.bit_length() - 1
    chunk, width = 16, 128
    for offset in range(chips):
        filter_ref[chip ^ offset] = filter_refs[offset][pl.ds(0, 4)]

    for residue in range(parts):
        source, odd = bit_reversed(residue // 2, chip_bits), residue % 2
        columns = pl.ds(residue * lanes, lanes)
        filter_real = filter_ref[source, odd].astype(F32)
        filter_imag = filter_ref[source, 2 + odd].astype(F32)
        real = spectrum_ref[pl.ds(0, rows), columns]
        imag = spectrum_ref[pl.ds(rows, rows), columns]
        product_ref[pl.ds(0, rows), columns] = (real * filter_real - imag * filter_imag).astype(BF16)
        product_ref[pl.ds(rows, rows), columns] = (real * filter_imag + imag * filter_real).astype(BF16)
        back_ref[:, columns] = jnp.dot(table_ref[...], product_ref[:, columns], preferred_element_type=F32)

    scale = 1.0 / (2 * parts * rows)
    sign = (1 - 2 * core).astype(F32)
    upper = core == 1

    def gather(index, carry):
        here = block_at(index, chunk)
        there = pl.ds(pl.multiple_of(rows + index * chunk, chunk), chunk)
        cos_all, sin_all = cos_ref[core, here, :] * scale, sin_ref[core, here, :] * scale
        for start in range(0, lanes, width):
            reals, imags = [], []
            for residue in range(parts):
                columns = pl.ds(residue * lanes + start, width)
                real, imag = back_ref[here, columns], back_ref[there, columns]
                cos, sin = cos_all[:, residue : residue + 1], sin_all[:, residue : residue + 1]
                reals.append(real * cos - imag * sin)
                imags.append(real * sin + imag * cos)
            totals = [None] * parts
            for block in range(parts // 2 + 1):
                even, odd = range(0, parts, 2), range(1, parts, 2)
                cos_even = weighted([(cosine(parts, residue, block), reals[residue]) for residue in even])
                cos_odd = weighted([(cosine(parts, residue, block), reals[residue]) for residue in odd])
                sin_even = weighted([(sine(parts, residue, block), imags[residue]) for residue in even])
                sin_odd = weighted([(sine(parts, residue, block), imags[residue]) for residue in odd])
                totals[block] = minus(plus(cos_even, cos_odd), plus(sin_even, sin_odd))
                if 0 < block and 2 * block != parts:
                    totals[parts - block] = plus(minus(cos_even, cos_odd), minus(sin_even, sin_odd))
            lane = pl.ds(start, width)
            for pair in range(chips):
                low, high = totals[2 * pair], totals[2 * pair + 1] * sign
                keep_ref[pair, here, lane] = jnp.where(upper, high, low)
                part, place = divmod(pair, chips // 2)
                send_refs[part][place, here, lane] = jnp.where(upper, low, high).astype(BF16)
        return carry

    lax.fori_loop(0, rows // chunk, gather, 0)


def backward(spectrum, first, tables):
    chips = len(first)
    _, rows, lanes = first[0].shape
    _, table, cos, sin = tables
    half = jax.ShapeDtypeStruct((chips // 2, rows, lanes), BF16)
    return pl.pallas_call(
        functools.partial(backward_kernel, chips),
        in_specs=[WHOLE] * (4 + chips),
        out_specs=[WHOLE] * 3,
        out_shape=[jax.ShapeDtypeStruct((chips, rows, lanes), F32), half, half],
        scratch_shapes=[
            pltpu.VMEM((chips, 4, rows, lanes), BF16),
            pltpu.VMEM(spectrum.shape, BF16),
            pltpu.VMEM(spectrum.shape, F32),
        ],
        cost_estimate=CHEAP,
        compiler_params=pltpu.CompilerParams(vmem_limit_bytes=32 * 2**20),
        name="backward",
    )(cos, sin, table, spectrum, *first)


def gate_kernel(chips, skip_ref, keep_ref, low_ref, high_ref, *refs):
    signal_refs, gate_refs, (out_ref, arrived_ref) = refs[:chips], refs[chips : 2 * chips], refs[2 * chips :]
    chip, _ = own_place()
    rows, lanes = keep_ref.shape[1:]
    skip = skip_ref[:, block_at(chip, lanes)]
    arrived_ref[pl.ds(0, chips // 2)] = low_ref[...]
    arrived_ref[pl.ds(chips // 2, chips // 2)] = high_ref[...]
    for offset in range(chips):
        block = chip ^ offset
        convolved = keep_ref[block] + arrived_ref[block].astype(F32)
        signal = signal_refs[offset][4].astype(F32)
        gate = gate_refs[offset][pl.ds(0, rows), :].astype(F32)
        out_ref[block_at(block, rows), :] = (gate * (convolved + skip * signal)).astype(BF16)


def gate(skip, keep, arrived, first, gates):
    chips, rows, lanes = keep.shape
    return pl.pallas_call(
        functools.partial(gate_kernel, chips),
        in_specs=[WHOLE] * (4 + 2 * chips),
        out_specs=WHOLE,
        out_shape=jax.ShapeDtypeStruct((chips * rows, lanes), BF16),
        scratch_shapes=[pltpu.VMEM((chips, rows, lanes), BF16)],
        cost_estimate=CHEAP,
        compiler_params=pltpu.CompilerParams(vmem_limit_bytes=6 * 2**20),
        name="gate",
    )(skip, keep, *arrived, *first, *gates)


def collect_kernel(chips, *refs):
    in_refs, out_ref = refs[:chips], refs[chips]
    chip, _ = own_place()
    layer = lax.axis_index("chan")
    quarter, share = out_ref.shape[0] // 2, out_ref.shape[1] // chips
    start = in_refs[0].shape[0] - quarter
    for offset in range(chips):
        for part in range(2):
            block = in_refs[offset][pl.ds(start, quarter), pl.ds(part * share, share)]
            out_ref[pl.ds(part * quarter, quarter), block_at(chip ^ layer ^ offset, share)] = block


def collect(moved, half):
    chips = len(moved)
    return pl.pallas_call(
        functools.partial(collect_kernel, chips),
        in_specs=[WHOLE] * chips,
        out_specs=WHOLE,
        out_shape=jax.ShapeDtypeStruct((half, chips * moved[0].shape[1] // 2), BF16),
        cost_estimate=CHEAP,
        compiler_params=pltpu.CompilerParams(vmem_limit_bytes=4 * 2**20),
        name="collect_weights",
    )(*moved)


def join_channels(chips, gated_refs, joined_ref):
    chip, _ = own_place()
    lanes = gated_refs[0].shape[1]
    for offset in range(chips):
        joined_ref[:, block_at(chip ^ offset, lanes)] = gated_refs[offset][...]


def project_moved_kernel(chips, own_ref, other_ref, *refs):
    gated_refs, (keep_ref, pass_ref, send_ref, joined_ref) = refs[:chips], refs[chips:]
    _, core = own_place()
    half = own_ref.shape[0]
    share = keep_ref.shape[1]
    join_channels(chips, gated_refs, joined_ref)
    partial = jnp.dot(joined_ref[:, block_at(core, half)], own_ref[...], preferred_element_type=F32)
    partial += jnp.dot(joined_ref[:, block_at(1 - core, half)], other_ref[...], preferred_element_type=F32)
    partial = partial.astype(BF16)
    keep_ref[...] = partial[:, :share]
    send_ref[0] = partial[:, share : 2 * share]
    pass_ref[...] = partial[:, 2 * share : 3 * share]
    send_ref[1] = partial[:, 3 * share :]


def project_moved(own, other, gated):
    chips = len(gated)
    half, columns = own.shape
    rows = gated[0].shape[0]
    block = jax.ShapeDtypeStruct((rows, columns // chips), BF16)
    return pl.pallas_call(
        functools.partial(project_moved_kernel, chips),
        in_specs=[WHOLE] * (2 + chips),
        out_specs=[WHOLE] * 3,
        out_shape=[block, block, jax.ShapeDtypeStruct((2, rows, columns // chips), BF16)],
        scratch_shapes=[pltpu.VMEM((rows, 2 * half), BF16)],
        cost_estimate=CHEAP,
        compiler_params=pltpu.CompilerParams(vmem_limit_bytes=8 * 2**20),
        name="project_moved",
    )(own, other, *gated)


def project_still_kernel(chips, own_ref, other_ref, *refs):
    gated_refs, out_refs, joined_ref = refs[:chips], refs[chips : 2 * chips], refs[2 * chips]
    chip, core = own_place()
    rows = out_refs[0].shape[0]
    join_channels(chips, gated_refs, joined_ref)

    def project_with(weight_ref):
        for offset in range(chips):
            gated = joined_ref[block_at(chip ^ offset, rows), :]
            out_refs[offset][...] = jnp.dot(gated, weight_ref[...], preferred_element_type=F32).astype(BF16)

    @pl.when(core == 0)
    def _():
        project_with(other_ref)

    @pl.when(core == 1)
    def _():
        project_with(own_ref)


def project_still(own, other, gated):
    chips = len(gated)
    depth, held = own.shape
    rows = gated[0].shape[0] // chips
    return pl.pallas_call(
        functools.partial(project_still_kernel, chips),
        in_specs=[WHOLE] * (2 + chips),
        out_specs=[WHOLE] * chips,
        out_shape=[jax.ShapeDtypeStruct((rows, held), BF16)] * chips,
        scratch_shapes=[pltpu.VMEM((rows * chips, depth), BF16)],
        cost_estimate=CHEAP,
        compiler_params=pltpu.CompilerParams(vmem_limit_bytes=12 * 2**20),
        name="project_still",
    )(own, other, *gated)


def sort_kernel(chips, *refs):
    in_refs, (keep_ref, pass_ref, send_ref, sorted_ref) = refs[:chips], refs[chips:]
    chip, _ = own_place()
    layer = lax.axis_index("chan")
    for offset in range(chips):
        sorted_ref[chip ^ layer ^ offset] = in_refs[offset][...]
    keep_ref[...] = sorted_ref[0]
    send_ref[0] = sorted_ref[1]
    pass_ref[...] = sorted_ref[2]
    send_ref[1] = sorted_ref[3]


def sort_blocks(blocks):
    chips = len(blocks)
    block = jax.ShapeDtypeStruct(blocks[0].shape, BF16)
    return pl.pallas_call(
        functools.partial(sort_kernel, chips),
        in_specs=[WHOLE] * chips,
        out_specs=[WHOLE] * 3,
        out_shape=[block, block, jax.ShapeDtypeStruct((2, *block.shape), BF16)],
        scratch_shapes=[pltpu.VMEM((chips, *block.shape), BF16)],
        cost_estimate=CHEAP,
        compiler_params=pltpu.CompilerParams(vmem_limit_bytes=4 * 2**20),
        name="sort_blocks",
    )(*blocks)


def finish_kernel(chips, keep_ref, first_ref, second_ref, *out_refs):
    chip, _ = own_place()
    rows = out_refs[0].shape[0]
    for offset in range(chips):
        here = block_at(chip ^ offset, rows)
        total = keep_ref[here, :].astype(F32) + first_ref[0, here, :].astype(F32) + second_ref[here, :].astype(F32)
        out_refs[offset][...] = total.astype(BF16)


def finish(keep, first, second, chips):
    rows, columns = keep.shape
    return pl.pallas_call(
        functools.partial(finish_kernel, chips),
        in_specs=[WHOLE] * 3,
        out_specs=[WHOLE] * chips,
        out_shape=[jax.ShapeDtypeStruct((rows // chips, columns), BF16)] * chips,
        cost_estimate=CHEAP,
        compiler_params=pltpu.CompilerParams(vmem_limit_bytes=4 * 2**20),
        name="finish",
    )(keep, first, second)


def join_kernel(chips, keep_ref, first_ref, second_ref, *refs):
    in_refs, out_ref = refs[:chips], refs[chips]
    chip, _ = own_place()
    share = in_refs[0].shape[1]
    for offset in range(chips):
        out_ref[:, block_at(chip ^ offset, share)] = in_refs[offset][...]
    total = keep_ref[...].astype(F32) + first_ref[0].astype(F32) + second_ref[...].astype(F32)
    out_ref[:, pl.ds(chips * share, total.shape[1])] = total.astype(BF16)


def join(keep, first, second, blocks):
    chips = len(blocks)
    rows, share = blocks[0].shape
    return pl.pallas_call(
        functools.partial(join_kernel, chips),
        in_specs=[WHOLE] * (3 + chips),
        out_specs=WHOLE,
        out_shape=jax.ShapeDtypeStruct((rows, chips * share + keep.shape[1]), BF16),
        cost_estimate=CHEAP,
        compiler_params=pltpu.CompilerParams(vmem_limit_bytes=4 * 2**20),
        name="join",
    )(keep, first, second, *blocks)


def swapped(value, axis, offset):
    if not offset:
        return value
    return lax.ppermute(value, axis, [(source, source ^ offset) for source in range(lax.axis_size(axis))])


def to_chips(blocks):
    return [swapped(block, "seq", 2 * offset) for offset, block in enumerate(blocks)]


def after(value, *others):
    return lax.optimization_barrier((value, *others))[0]


def over_layers(passed, send):
    first = swapped(send, "chan", 1)
    passed = (passed.astype(F32) + first[1].astype(F32)).astype(BF16)
    return first, swapped(passed, "chan", 2)


def shards_direct(values_in, gate_values, filter_spectrum, skip_gain, out_weight):
    parts = lax.axis_size("seq")
    chips = parts // 2
    rows, width = values_in.shape
    tables = small_tables(parts, rows)

    first = pack_signals(values_in, filter_spectrum.reshape(4, rows, width), chips, tuple(range(chips)))
    other_weight = swapped(out_weight, "seq", 1)
    moved = pack_moved(after(gate_values, first[0]), out_weight, other_weight, chips)
    first = to_chips(first)
    own = [after(block, moved[0])[4] for block in first]
    own = [jnp.stack(own[: chips // 2]), jnp.stack(own[chips // 2 :])]
    moved = to_chips(moved)
    spectrum = forward(own, [swapped(half, "seq", 1) for half in own], tables)
    keep, *send = backward(spectrum, first, tables)
    gated = gate(skip_gain[None, :], keep, [swapped(half, "seq", 1) for half in send], first, moved)
    own_moved = collect([after(block, gated) for block in moved], out_weight.shape[0] // 2)
    gathered = to_chips([gated] * chips)

    keep, passed, send = project_moved(own_moved, swapped(own_moved, "seq", 1), gathered)
    blocks = to_chips(finish(keep, *over_layers(passed, send), chips))
    keep, passed, send = sort_blocks(to_chips(project_still(out_weight, other_weight, gathered)))
    return join(keep, *over_layers(passed, send), blocks)


def shards(values_in, gate_values, filter_spectrum, skip_gain, out_weight):
    parts, layers = lax.axis_size("seq"), lax.axis_size("chan")
    rows, width = values_in.shape
    share = out_weight.shape[1] // layers
    aligned = width // parts % 128 == 0 and share % 128 == 0 and rows % 32 == 0
    run = shards_direct if aligned and layers == 4 and parts == 8 else shards_general
    return run(values_in, gate_values, filter_spectrum, skip_gain, out_weight)


def solution(mesh):
    in_specs = (
        P("seq", "chan"),
        P("seq", "chan"),
        P(None, "seq", None, "chan"),
        P("chan"),
        P("chan", "seq"),
    )
    out_specs = P("seq", "chan")
    return jax.shard_map(shards, mesh=mesh, in_specs=in_specs, out_specs=out_specs, check_vma=False)
```

```python
import functools

import jax
import jax.numpy as jnp
import numpy as np
from jax import lax
from jax.experimental import pallas as pl
from jax.experimental.pallas import tpu as pltpu
from jax.sharding import PartitionSpec as P

BF16 = jnp.bfloat16
F32 = jnp.float32


def bit_reversed(number, width_bits):
    flipped = 0
    for bit_place in range(width_bits):
        flipped |= (number >> bit_place & 1) << (width_bits - 1 - bit_place)
    return flipped


def filter_row(residue, width_bits):
    return 2 * bit_reversed(residue // 2, width_bits) + residue % 2


def dft_tables(parts, rows):
    total = 2 * parts * rows
    residue = np.arange(2 * parts)[:, None, None]
    column = np.arange(rows)[None, :, None]
    position = np.arange(rows)[None, None, :]
    phase = 2.0 * np.pi * (position * (residue + 2 * parts * column) % total) / total
    cos, sin = np.cos(phase), np.sin(phase)
    forward = np.concatenate(
        [np.concatenate([cos, sin], axis=2), np.concatenate([-sin, cos], axis=2)], axis=1
    )
    inverse = np.transpose(forward, (0, 2, 1)) / total
    return forward.astype(BF16), inverse.astype(BF16)


def convolve_kernel(parts, rows, moved_ref, skip_ref, forward_ref, inverse_ref, out_ref, waves_ref, back_ref):
    width_bits = parts.bit_length() - 1
    chunk = 16

    def cosine(residue, block):
        return float(np.cos(np.pi * residue * block / parts))

    def sine(residue, block):
        return float(np.sin(np.pi * residue * block / parts))

    def spread(index, carry):
        here = pl.ds(index * chunk, chunk)
        there = pl.ds(rows + index * chunk, chunk)
        blocks = [moved_ref[block, here, :].astype(F32) for block in range(parts)]
        for residue in range(parts + 1):
            real = blocks[0]
            imag = jnp.zeros_like(real)
            for block in range(1, parts):
                real = real + cosine(residue, block) * blocks[block]
                imag = imag - sine(residue, block) * blocks[block]
            waves_ref[residue, here, :] = real.astype(BF16)
            waves_ref[residue, there, :] = imag.astype(BF16)
            if 0 < residue < parts:
                waves_ref[2 * parts - residue, here, :] = real.astype(BF16)
                waves_ref[2 * parts - residue, there, :] = (-imag).astype(BF16)
        return carry

    lax.fori_loop(0, rows // chunk, spread, 0)

    def through(residue):
        wave = jnp.dot(forward_ref[residue], waves_ref[residue], preferred_element_type=F32)
        source, odd = divmod(filter_row(residue, width_bits), 2)
        filter_real = moved_ref[source, pl.ds((2 + odd) * rows, rows), :].astype(F32)
        filter_imag = moved_ref[source, pl.ds((4 + odd) * rows, rows), :].astype(F32)
        real, imag = wave[:rows], wave[rows:]
        product = jnp.concatenate(
            [real * filter_real - imag * filter_imag, real * filter_imag + imag * filter_real], axis=0
        )
        return jnp.dot(inverse_ref[residue], product.astype(BF16), preferred_element_type=F32)

    for residue in range(parts + 1):
        back = through(residue)
        if 0 < residue < parts:
            other = through(2 * parts - residue)
            back_ref[residue, pl.ds(0, rows), :] = back[:rows] + other[:rows]
            back_ref[residue, pl.ds(rows, rows), :] = back[rows:] - other[rows:]
        else:
            back_ref[residue] = back

    skip = skip_ref[...]

    def gather(index, carry):
        here = pl.ds(index * chunk, chunk)
        there = pl.ds(rows + index * chunk, chunk)
        reals = [back_ref[residue, here, :] for residue in range(parts + 1)]
        imags = [back_ref[residue, there, :] for residue in range(parts + 1)]
        for block in range(parts):
            total = reals[0]
            for residue in range(1, parts + 1):
                total = total + cosine(residue, block) * reals[residue]
                if residue < parts and block:
                    total = total - sine(residue, block) * imags[residue]
            signal = moved_ref[block, here, :].astype(F32)
            gate = moved_ref[block, pl.ds(rows + index * chunk, chunk), :].astype(F32)
            out_ref[block, here, :] = (gate * (total + skip * signal)).astype(BF16)
        return carry

    lax.fori_loop(0, rows // chunk, gather, 0)


def convolve(moved, skip):
    parts, stacked, width = moved.shape
    rows = stacked // 6
    forward, inverse = dft_tables(parts, rows)
    whole = pl.BlockSpec(memory_space=pltpu.VMEM)
    return pl.pallas_call(
        functools.partial(convolve_kernel, parts, rows),
        out_shape=jax.ShapeDtypeStruct((parts, rows, width), BF16),
        in_specs=[whole] * 4,
        out_specs=whole,
        scratch_shapes=[
            pltpu.VMEM((2 * parts, 2 * rows, width), BF16),
            pltpu.VMEM((parts + 1, 2 * rows, width), F32),
        ],
        compiler_params=pltpu.CompilerParams(vmem_limit_bytes=40 * 2**20),
    )(moved, skip[None, :], forward, inverse)


def shards_general(values_in, gate_values, filter_spectrum, skip_gain, out_weight):
    parts = lax.axis_size("seq")
    layers = lax.axis_size("chan")
    rows, width = values_in.shape
    lanes = width // parts
    device = lax.axis_index("seq")

    def by_channel(array):
        return jnp.transpose(array.reshape(array.shape[0], parts, lanes), (1, 0, 2))

    filters = filter_spectrum.astype(BF16).reshape(4 * rows, width)
    packed = jnp.concatenate([by_channel(values_in), by_channel(gate_values), by_channel(filters)], axis=1)
    moved = lax.all_to_all(packed, "seq", 0, 0)
    skip = lax.dynamic_slice_in_dim(skip_gain, device * lanes, lanes)
    gated = convolve(moved, skip)
    gathered = lax.all_gather(gated.reshape(parts * rows, lanes), "seq", axis=1, tiled=True)

    own_cols = out_weight.shape[1]
    share = own_cols * parts // layers // parts
    per_block = parts // layers
    pieces = own_cols // share
    group = device % per_block
    member = device // per_block
    weight = jnp.zeros_like(out_weight)
    for step in range(pieces):
        piece = (member + step) % pieces
        sent = lax.dynamic_slice_in_dim(out_weight, piece * share, share, 1)
        pairs = [
            (source, source % per_block * pieces + (source // per_block + step) % pieces) for source in range(parts)
        ]
        arrived = lax.ppermute(sent, "seq", pairs)
        block = (device % pieces - step) % pieces
        weight = lax.dynamic_update_slice_in_dim(weight, arrived, block * share, 1)
    partials = jnp.dot(gathered, weight, preferred_element_type=F32).astype(BF16)
    mixed = lax.psum_scatter(partials, "chan", scatter_dimension=1, tiled=True)
    return lax.all_to_all(mixed, "seq", 0, 1, tiled=True)


WHOLE = pl.BlockSpec(memory_space=pltpu.VMEM)
CHEAP = pl.CostEstimate(flops=0, transcendentals=0, bytes_accessed=0)


def small_tables(parts, rows):
    total = 2 * parts * rows
    index = np.arange(rows)
    phase = 2.0 * np.pi * (index[:, None] * index[None, :] % rows) / rows
    cos, sin = np.cos(phase), np.sin(phase)
    forward = np.block([[cos, sin], [-sin, cos]])
    residue = np.arange(2 * parts).reshape(2, 1, parts)
    turn = 2.0 * np.pi * index[None, :, None] * residue / total
    return forward.astype(BF16), forward.T.astype(BF16), np.cos(turn).astype(F32), np.sin(turn).astype(F32)


def cosine(parts, residue, block):
    return float(np.cos(np.pi * residue * block / parts))


def sine(parts, residue, block):
    return float(np.sin(np.pi * residue * block / parts))


def weighted(terms):
    total = None
    for factor, term in terms:
        if abs(factor) < 1e-12:
            continue
        part = term if factor == 1.0 else factor * term
        total = part if total is None else total + part
    return total


def plus(left, right):
    return left if right is None else right if left is None else left + right


def minus(left, right):
    return left if right is None else -right if left is None else left - right


def own_place():
    device = lax.axis_index("seq")
    return device // 2, device % 2


def block_at(index, size):
    return pl.ds(pl.multiple_of(index * size, size), size)


def pack_signals_kernel(chips, values_ref, filter_ref, *refs):
    out_refs, (plane_ref, arrived) = refs[:chips], refs[chips:]
    chip, _ = own_place()
    planes, rows, _ = filter_ref.shape
    lanes = out_refs[0].shape[1]
    copies, work = [], []
    for offset in range(chips):
        here = block_at(chip ^ offset, lanes)
        for plane in range(planes):
            copies.append(
                pltpu.make_async_copy(filter_ref.at[plane, :, here], plane_ref.at[offset, plane], arrived.at[offset, plane])
            )
            work.append((offset, plane))
        values = out_refs[offset].at[pl.ds(planes * rows, rows)]
        copies.append(pltpu.make_async_copy(values_ref.at[:, here], values, arrived.at[offset, planes]))
        work.append(None)
    for copy in copies:
        copy.start()
    for copy, task in zip(copies, work):
        copy.wait()
        if task:
            offset, plane = task
            out_refs[offset][pl.ds(plane * rows, rows), :] = plane_ref[offset, plane].astype(BF16)
    used = (planes + 1) * rows
    for out_ref in out_refs:
        if out_ref.shape[0] > used:
            out_ref[pl.ds(used, out_ref.shape[0] - used), :] = out_ref[pl.ds(0, out_ref.shape[0] - used), :]


def pack_signals(values_in, filters, chips, spare):
    planes, rows, width = filters.shape
    lanes = width // chips
    return pl.pallas_call(
        functools.partial(pack_signals_kernel, chips),
        in_specs=[pl.BlockSpec(memory_space=pltpu.HBM)] * 2,
        out_specs=[WHOLE] * chips,
        out_shape=[jax.ShapeDtypeStruct(((planes + 1) * rows + more, lanes), BF16) for more in spare],
        scratch_shapes=[
            pltpu.VMEM((chips, planes, rows, lanes), F32),
            pltpu.SemaphoreType.DMA((chips, planes + 1)),
        ],
        cost_estimate=CHEAP,
        compiler_params=pltpu.CompilerParams(vmem_limit_bytes=8 * 2**20),
        name="pack_signals",
    )(*(pltpu.with_memory_space_constraint(array, pltpu.HBM) for array in (values_in, filters)))


def pack_moved_kernel(chips, gate_ref, own_ref, other_ref, *refs):
    out_refs, (mine_ref, arrived) = refs[:chips], refs[chips:]
    chip, core = own_place()
    rows = gate_ref.shape[0]
    depth, held = own_ref.shape
    quarter, share = depth // 4, held // chips

    def copies_from(weight_ref):
        copies = [pltpu.make_async_copy(weight_ref.at[:, block_at(chip, share)], mine_ref, arrived.at[0, 0])]
        for offset in range(chips):
            out_ref, target = out_refs[offset], chip ^ offset
            gates = gate_ref.at[:, block_at(target, out_ref.shape[1])]
            copies.append(pltpu.make_async_copy(gates, out_ref.at[pl.ds(0, rows)], arrived.at[offset, 2]))
            for part in range(2 if offset else 0):
                source = weight_ref.at[block_at(2 * core + part, quarter), block_at(target, share)]
                sink = out_ref.at[pl.ds(rows, quarter), pl.ds(part * share, share)]
                copies.append(pltpu.make_async_copy(source, sink, arrived.at[offset, part]))
        for copy in copies:
            copy.start()
        for copy in copies:
            copy.wait()

    @pl.when(core == 0)
    def _():
        copies_from(own_ref)

    @pl.when(core == 1)
    def _():
        copies_from(other_ref)


def pack_moved(gate_values, own, other, chips):
    rows, width = gate_values.shape
    depth, held = own.shape
    share = held // chips
    return pl.pallas_call(
        functools.partial(pack_moved_kernel, chips),
        in_specs=[pl.BlockSpec(memory_space=pltpu.HBM)] * 2 + [pl.BlockSpec(memory_space=pl.ANY)],
        out_specs=[WHOLE] * (chips + 1),
        out_shape=[
            *(jax.ShapeDtypeStruct((rows + (depth // 4 if offset else 0), 2 * share), BF16) for offset in range(chips)),
            jax.ShapeDtypeStruct((depth, share), BF16),
        ],
        scratch_shapes=[pltpu.SemaphoreType.DMA((chips, 3))],
        cost_estimate=CHEAP,
        compiler_params=pltpu.CompilerParams(vmem_limit_bytes=8 * 2**20),
        name="pack_moved",
    )(*(pltpu.with_memory_space_constraint(array, pltpu.HBM) for array in (gate_values, own)), other)


def pick_values_kernel(chips, start, *refs):
    in_refs, out_refs = refs[:chips], refs[chips:]
    for offset in range(chips):
        part, place = divmod(offset, chips // 2)
        out_refs[part][place] = in_refs[offset][pl.ds(start, out_refs[part].shape[1]), :]


def pick_values(first, rows, start):
    chips = len(first)
    half = jax.ShapeDtypeStruct((chips // 2, rows, first[0].shape[1]), BF16)
    return pl.pallas_call(
        functools.partial(pick_values_kernel, chips, start),
        in_specs=[WHOLE] * chips,
        out_specs=[WHOLE] * 2,
        out_shape=[half, half],
        cost_estimate=CHEAP,
        compiler_params=pltpu.CompilerParams(vmem_limit_bytes=4 * 2**20),
        name="pick_values",
    )(*first)


def forward_kernel(chips, cos_ref, sin_ref, table_ref, *refs):
    own_refs, other_refs, (out_ref, signal_ref, waves_ref) = refs[:2], refs[2:4], refs[4:]
    chip, core = own_place()
    parts = 2 * chips
    rows, lanes = own_refs[0].shape[1:]
    chunk, width = 16, 128
    for offset in range(chips):
        part, place = divmod(offset, chips // 2)
        signal_ref[2 * (chip ^ offset) + core] = own_refs[part][place]
        signal_ref[2 * (chip ^ offset) + 1 - core] = other_refs[part][place]
    sign = (1 - 2 * core).astype(F32)

    def spread(index, carry):
        here = block_at(index, chunk)
        there = pl.ds(pl.multiple_of(rows + index * chunk, chunk), chunk)
        cos_all, sin_all = cos_ref[core, here, :], sin_ref[core, here, :]
        for start in range(0, lanes, width):
            blocks = [signal_ref[block, here, pl.ds(start, width)].astype(F32) for block in range(parts)]
            blocks = [block * sign if place % 2 else block for place, block in enumerate(blocks)]

            def store(residue, real, imag):
                cos, sin = cos_all[:, residue : residue + 1], sin_all[:, residue : residue + 1]
                if imag is None:
                    real, imag = real * cos, -(real * sin)
                else:
                    real, imag = real * cos + imag * sin, imag * cos - real * sin
                columns = pl.ds(residue * lanes + start, width)
                waves_ref[here, columns] = real.astype(BF16)
                waves_ref[there, columns] = imag.astype(BF16)

            for residue in range(parts // 2 + 1):
                even, odd = range(0, parts, 2), range(1, parts, 2)
                cos_even = weighted([(cosine(parts, residue, block), blocks[block]) for block in even])
                cos_odd = weighted([(cosine(parts, residue, block), blocks[block]) for block in odd])
                sin_even = weighted([(sine(parts, residue, block), blocks[block]) for block in even])
                sin_odd = weighted([(sine(parts, residue, block), blocks[block]) for block in odd])
                sin_sum = plus(sin_even, sin_odd)
                store(residue, plus(cos_even, cos_odd), None if sin_sum is None else -sin_sum)
                if 0 < residue and 2 * residue != parts:
                    store(parts - residue, minus(cos_even, cos_odd), minus(sin_even, sin_odd))
        return carry

    lax.fori_loop(0, rows // chunk, spread, 0)
    for residue in range(parts):
        columns = pl.ds(residue * lanes, lanes)
        out_ref[:, columns] = jnp.dot(table_ref[...], waves_ref[:, columns], preferred_element_type=F32)


def forward(own, other, tables):
    chips, (_, rows, lanes) = 2 * own[0].shape[0], own[0].shape
    table, _, cos, sin = tables
    spectrum = (2 * rows, 2 * chips * lanes)
    return pl.pallas_call(
        functools.partial(forward_kernel, chips),
        in_specs=[WHOLE] * 7,
        out_specs=WHOLE,
        out_shape=jax.ShapeDtypeStruct(spectrum, F32),
        scratch_shapes=[pltpu.VMEM((2 * chips, rows, lanes), BF16), pltpu.VMEM(spectrum, BF16)],
        cost_estimate=CHEAP,
        compiler_params=pltpu.CompilerParams(vmem_limit_bytes=32 * 2**20),
        name="forward",
    )(cos, sin, table, *own, *other)


def backward_kernel(chips, cos_ref, sin_ref, table_ref, spectrum_ref, *refs):
    filter_refs, (keep_ref, *send_refs, filter_ref, product_ref, back_ref) = refs[:chips], refs[chips:]
    chip, core = own_place()
    parts = 2 * chips
    rows, lanes = keep_ref.shape[1:]
    chip_bits = chips.bit_length() - 1
    chunk, width = 16, 128
    for offset in range(chips):
        for plane in range(filter_ref.shape[1]):
            filter_ref[chip ^ offset, plane] = filter_refs[offset][pl.ds(plane * rows, rows), :]

    for residue in range(parts):
        source, odd = bit_reversed(residue // 2, chip_bits), residue % 2
        columns = pl.ds(residue * lanes, lanes)
        filter_real = filter_ref[source, odd].astype(F32)
        filter_imag = filter_ref[source, 2 + odd].astype(F32)
        real = spectrum_ref[pl.ds(0, rows), columns]
        imag = spectrum_ref[pl.ds(rows, rows), columns]
        product_ref[pl.ds(0, rows), columns] = (real * filter_real - imag * filter_imag).astype(BF16)
        product_ref[pl.ds(rows, rows), columns] = (real * filter_imag + imag * filter_real).astype(BF16)
        back_ref[:, columns] = jnp.dot(table_ref[...], product_ref[:, columns], preferred_element_type=F32)

    scale = 1.0 / (2 * parts * rows)
    sign = (1 - 2 * core).astype(F32)
    upper = core == 1

    def gather(index, carry):
        here = block_at(index, chunk)
        there = pl.ds(pl.multiple_of(rows + index * chunk, chunk), chunk)
        cos_all, sin_all = cos_ref[core, here, :] * scale, sin_ref[core, here, :] * scale
        for start in range(0, lanes, width):
            reals, imags = [], []
            for residue in range(parts):
                columns = pl.ds(residue * lanes + start, width)
                real, imag = back_ref[here, columns], back_ref[there, columns]
                cos, sin = cos_all[:, residue : residue + 1], sin_all[:, residue : residue + 1]
                reals.append(real * cos - imag * sin)
                imags.append(real * sin + imag * cos)
            totals = [None] * parts
            for block in range(parts // 2 + 1):
                even, odd = range(0, parts, 2), range(1, parts, 2)
                cos_even = weighted([(cosine(parts, residue, block), reals[residue]) for residue in even])
                cos_odd = weighted([(cosine(parts, residue, block), reals[residue]) for residue in odd])
                sin_even = weighted([(sine(parts, residue, block), imags[residue]) for residue in even])
                sin_odd = weighted([(sine(parts, residue, block), imags[residue]) for residue in odd])
                totals[block] = minus(plus(cos_even, cos_odd), plus(sin_even, sin_odd))
                if 0 < block and 2 * block != parts:
                    totals[parts - block] = plus(minus(cos_even, cos_odd), minus(sin_even, sin_odd))
            lane = pl.ds(start, width)
            for pair in range(chips):
                low, high = totals[2 * pair], totals[2 * pair + 1] * sign
                keep_ref[pair, here, lane] = jnp.where(upper, high, low)
                part, place = divmod(pair, chips // 2)
                send_refs[part][place, here, lane] = jnp.where(upper, low, high).astype(BF16)
        return carry

    lax.fori_loop(0, rows // chunk, gather, 0)


def backward(spectrum, first, tables):
    chips = len(first)
    rows, lanes = spectrum.shape[0] // 2, first[0].shape[1]
    _, table, cos, sin = tables
    half = jax.ShapeDtypeStruct((chips // 2, rows, lanes), BF16)
    return pl.pallas_call(
        functools.partial(backward_kernel, chips),
        in_specs=[WHOLE] * (4 + chips),
        out_specs=[WHOLE] * 3,
        out_shape=[jax.ShapeDtypeStruct((chips, rows, lanes), F32), half, half],
        scratch_shapes=[
            pltpu.VMEM((chips, 4, rows, lanes), BF16),
            pltpu.VMEM(spectrum.shape, BF16),
            pltpu.VMEM(spectrum.shape, F32),
        ],
        cost_estimate=CHEAP,
        compiler_params=pltpu.CompilerParams(vmem_limit_bytes=32 * 2**20),
        name="backward",
    )(cos, sin, table, spectrum, *first)


def gate_kernel(chips, skip_ref, keep_ref, low_ref, high_ref, *refs):
    signal_refs, gate_refs = refs[:chips], refs[chips : 2 * chips]
    out_ref, longer_ref, arrived_ref = refs[2 * chips :]
    chip, _ = own_place()
    rows, lanes = keep_ref.shape[1:]
    skip = skip_ref[:, block_at(chip, lanes)]
    arrived_ref[pl.ds(0, chips // 2)] = low_ref[...]
    arrived_ref[pl.ds(chips // 2, chips // 2)] = high_ref[...]
    for offset in range(chips):
        block = chip ^ offset
        convolved = keep_ref[block] + arrived_ref[block].astype(F32)
        signal = signal_refs[offset][pl.ds(4 * rows, rows), :].astype(F32)
        gate = gate_refs[offset][pl.ds(0, rows), :].astype(F32)
        gated = (gate * (convolved + skip * signal)).astype(BF16)
        out_ref[block_at(block, rows), :] = gated
        longer_ref[block_at(block, rows), :] = gated
    end = chips * rows
    longer_ref[pl.ds(end, longer_ref.shape[0] - end), :] = longer_ref[pl.ds(0, longer_ref.shape[0] - end), :]


def gate(skip, keep, arrived, first, gates, spare):
    chips, rows, lanes = keep.shape
    return pl.pallas_call(
        functools.partial(gate_kernel, chips),
        in_specs=[WHOLE] * (4 + 2 * chips),
        out_specs=[WHOLE] * 2,
        out_shape=[
            jax.ShapeDtypeStruct((chips * rows, lanes), BF16),
            jax.ShapeDtypeStruct((chips * rows + spare, lanes), BF16),
        ],
        scratch_shapes=[pltpu.VMEM((chips, rows, lanes), BF16)],
        cost_estimate=CHEAP,
        compiler_params=pltpu.CompilerParams(vmem_limit_bytes=6 * 2**20),
        name="gate",
    )(skip, keep, *arrived, *first, *gates)


def piece_of(ref, half, part):
    quarter, share = half // 2, ref.shape[1] // 2
    return ref[pl.ds(ref.shape[0] - quarter, quarter), pl.ds(part * share, share)]


def collect_kernel(in_refs, out_refs):
    rows = out_refs[0].shape[0]
    quarter = len(out_refs) * rows // (2 * len(in_refs))
    for place in range(2 * len(in_refs)):
        index, start = divmod(place * quarter, rows)
        out_refs[index][pl.ds(start, quarter), :] = piece_of(in_refs[place // 2], 2 * quarter, place % 2)


def collect(moved, half):
    count = len(moved)
    shape = (count * half // 2, moved[0].shape[1] // 2)
    return pl.pallas_call(
        lambda *refs: collect_kernel(refs[:count], refs[count:]),
        in_specs=[WHOLE] * count,
        out_specs=[WHOLE] * 2,
        out_shape=[jax.ShapeDtypeStruct(shape, BF16)] * 2,
        cost_estimate=CHEAP,
        compiler_params=pltpu.CompilerParams(vmem_limit_bytes=4 * 2**20),
        name="collect_weights",
    )(*moved)


def arrange_kernel(chips, mine_ref, *refs):
    moved_refs, (*other_refs, out_ref) = refs[: chips - 1], refs[chips - 1 :]
    chip, core = own_place()
    layer = lax.axis_index("chan")
    depth, share = mine_ref.shape
    quarter = depth // 4
    out_ref[:, block_at(chip ^ layer, share)] = mine_ref[...]
    for place in range(2 * (chips - 1)):
        offset, part = place // 2 + 1, place % 2
        columns = block_at(chip ^ layer ^ offset, share)
        index, start = divmod(place * quarter, other_refs[0].shape[0])
        out_ref[block_at(2 * core + part, quarter), columns] = piece_of(moved_refs[offset - 1], 2 * quarter, part)
        out_ref[block_at(2 * (1 - core) + part, quarter), columns] = other_refs[index][pl.ds(start, quarter), :]


def arrange(mine, moved, others):
    chips = len(moved) + 1
    depth, share = mine.shape
    return pl.pallas_call(
        functools.partial(arrange_kernel, chips),
        in_specs=[WHOLE] * (chips + len(others)),
        out_specs=WHOLE,
        out_shape=jax.ShapeDtypeStruct((depth, chips * share), BF16),
        cost_estimate=CHEAP,
        compiler_params=pltpu.CompilerParams(vmem_limit_bytes=8 * 2**20),
        name="arrange_weights",
    )(mine, *moved, *others)


def join_channels(chips, gated_refs, joined_ref):
    chip, _ = own_place()
    lanes = gated_refs[0].shape[1]
    for offset in range(chips):
        joined_ref[:, block_at(chip ^ offset, lanes)] = gated_refs[offset][pl.ds(0, joined_ref.shape[0]), :]


def project_moved_kernel(chips, weight_ref, *refs):
    gated_refs, (keep_ref, pass_ref, send_ref, joined_ref) = refs[:chips], refs[chips:]
    share = keep_ref.shape[1]
    join_channels(chips, gated_refs, joined_ref)
    partial = jnp.dot(joined_ref[...], weight_ref[...], preferred_element_type=F32).astype(BF16)
    keep_ref[...] = partial[:, :share]
    send_ref[0] = partial[:, share : 2 * share]
    pass_ref[...] = partial[:, 2 * share : 3 * share]
    send_ref[1] = partial[:, 3 * share :]


def project_moved(weight, gated):
    chips = len(gated)
    depth, columns = weight.shape
    rows = gated[0].shape[0]
    block = jax.ShapeDtypeStruct((rows, columns // chips), BF16)
    return pl.pallas_call(
        functools.partial(project_moved_kernel, chips),
        in_specs=[WHOLE] * (1 + chips),
        out_specs=[WHOLE] * 3,
        out_shape=[block, block, jax.ShapeDtypeStruct((2, rows, columns // chips), BF16)],
        scratch_shapes=[pltpu.VMEM((rows, depth), BF16)],
        cost_estimate=CHEAP,
        compiler_params=pltpu.CompilerParams(vmem_limit_bytes=8 * 2**20),
        name="project_moved",
    )(weight, *gated)


def project_still_kernel(chips, own_ref, other_ref, *refs):
    gated_refs, out_refs, joined_ref = refs[:chips], refs[chips : 2 * chips], refs[2 * chips]
    chip, core = own_place()
    rows = out_refs[0].shape[0]
    join_channels(chips, gated_refs, joined_ref)

    def project_with(weight_ref):
        for offset in range(chips):
            gated = joined_ref[block_at(chip ^ offset, rows), :]
            out_refs[offset][...] = jnp.dot(gated, weight_ref[...], preferred_element_type=F32).astype(BF16)

    @pl.when(core == 0)
    def _():
        project_with(other_ref)

    @pl.when(core == 1)
    def _():
        project_with(own_ref)


def project_still(own, other, gated):
    chips = len(gated)
    depth, held = own.shape
    rows = gated[0].shape[0] // chips
    return pl.pallas_call(
        functools.partial(project_still_kernel, chips),
        in_specs=[WHOLE] * (2 + chips),
        out_specs=[WHOLE] * chips,
        out_shape=[jax.ShapeDtypeStruct((rows, held), BF16)] * chips,
        scratch_shapes=[pltpu.VMEM((rows * chips, depth), BF16)],
        cost_estimate=CHEAP,
        compiler_params=pltpu.CompilerParams(vmem_limit_bytes=12 * 2**20),
        name="project_still",
    )(own, other, *gated)


def sort_kernel(chips, *refs):
    in_refs, (keep_ref, pass_ref, send_ref, sorted_ref) = refs[:chips], refs[chips:]
    chip, _ = own_place()
    layer = lax.axis_index("chan")
    for offset in range(chips):
        sorted_ref[chip ^ layer ^ offset] = in_refs[offset][...]
    keep_ref[...] = sorted_ref[0]
    send_ref[0] = sorted_ref[1]
    pass_ref[...] = sorted_ref[2]
    send_ref[1] = sorted_ref[3]


def sort_blocks(blocks):
    chips = len(blocks)
    block = jax.ShapeDtypeStruct(blocks[0].shape, BF16)
    return pl.pallas_call(
        functools.partial(sort_kernel, chips),
        in_specs=[WHOLE] * chips,
        out_specs=[WHOLE] * 3,
        out_shape=[block, block, jax.ShapeDtypeStruct((2, *block.shape), BF16)],
        scratch_shapes=[pltpu.VMEM((chips, *block.shape), BF16)],
        cost_estimate=CHEAP,
        compiler_params=pltpu.CompilerParams(vmem_limit_bytes=4 * 2**20),
        name="sort_blocks",
    )(*blocks)


def finish_kernel(chips, keep_ref, first_ref, second_ref, *out_refs):
    chip, _ = own_place()
    rows = out_refs[0].shape[0]
    for offset in range(chips):
        here = block_at(chip ^ offset, rows)
        total = keep_ref[here, :].astype(F32) + first_ref[0, here, :].astype(F32) + second_ref[here, :].astype(F32)
        out_refs[offset][...] = total.astype(BF16)


def finish(keep, first, second, chips):
    rows, columns = keep.shape
    return pl.pallas_call(
        functools.partial(finish_kernel, chips),
        in_specs=[WHOLE] * 3,
        out_specs=[WHOLE] * chips,
        out_shape=[jax.ShapeDtypeStruct((rows // chips, columns), BF16)] * chips,
        cost_estimate=CHEAP,
        compiler_params=pltpu.CompilerParams(vmem_limit_bytes=4 * 2**20),
        name="finish",
    )(keep, first, second)


def join_kernel(chips, keep_ref, first_ref, second_ref, *refs):
    in_refs, out_ref = refs[:chips], refs[chips]
    chip, _ = own_place()
    share = in_refs[0].shape[1]
    for offset in range(chips):
        out_ref[:, block_at(chip ^ offset, share)] = in_refs[offset][...]
    total = keep_ref[...].astype(F32) + first_ref[0].astype(F32) + second_ref[...].astype(F32)
    out_ref[:, pl.ds(chips * share, total.shape[1])] = total.astype(BF16)


def join(keep, first, second, blocks):
    chips = len(blocks)
    rows, share = blocks[0].shape
    return pl.pallas_call(
        functools.partial(join_kernel, chips),
        in_specs=[WHOLE] * (3 + chips),
        out_specs=WHOLE,
        out_shape=jax.ShapeDtypeStruct((rows, chips * share + keep.shape[1]), BF16),
        cost_estimate=CHEAP,
        compiler_params=pltpu.CompilerParams(vmem_limit_bytes=4 * 2**20),
        name="join",
    )(keep, first, second, *blocks)


def swapped(value, axis, offset):
    if not offset:
        return value
    return lax.ppermute(value, axis, [(source, source ^ offset) for source in range(lax.axis_size(axis))])


def to_chips(blocks):
    return [swapped(block, "seq", 2 * offset) for offset, block in enumerate(blocks)]


def after(value, *others):
    return lax.optimization_barrier((value, *others))[0]


def over_layers(passed, send):
    first = swapped(send, "chan", 1)
    passed = (passed.astype(F32) + first[1].astype(F32)).astype(BF16)
    return first, swapped(passed, "chan", 2)


def shards_direct(values_in, gate_values, filter_spectrum, skip_gain, out_weight):
    parts = lax.axis_size("seq")
    chips = parts // 2
    rows, width = values_in.shape
    tables = small_tables(parts, rows)

    first = pack_signals(values_in, filter_spectrum.reshape(4, rows, width), chips, (0, 16, 16, 0))
    other_weight = swapped(out_weight, "seq", 1)
    *moved, mine = pack_moved(after(gate_values, first[0]), out_weight, other_weight, chips)
    first = to_chips(first)
    own = pick_values([after(block, moved[0]) for block in first], rows, 4 * rows)
    moved = to_chips(moved)
    spectrum = forward(own, [swapped(part, "seq", 1) for part in own], tables)
    keep, *send = backward(spectrum, first, tables)
    gated, longer = gate(skip_gain[None, :], keep, [swapped(part, "seq", 1) for part in send], first, moved, 16)
    gathered = to_chips([gated, longer, longer, gated])

    others = [swapped(part, "seq", 1) for part in collect([after(block, gated) for block in moved[1:]], out_weight.shape[0] // 2)]
    keep, passed, send = project_moved(arrange(mine, moved[1:], others), gathered)
    blocks = to_chips(finish(keep, *over_layers(passed, send), chips))
    keep, passed, send = sort_blocks(to_chips(project_still(out_weight, other_weight, gathered)))
    return join(keep, *over_layers(passed, send), blocks)


def shards(values_in, gate_values, filter_spectrum, skip_gain, out_weight):
    parts, layers = lax.axis_size("seq"), lax.axis_size("chan")
    rows, width = values_in.shape
    share = out_weight.shape[1] // layers
    aligned = width // parts % 128 == 0 and share % 128 == 0 and rows % 32 == 0
    run = shards_direct if aligned and layers == 4 and parts == 8 else shards_general
    return run(values_in, gate_values, filter_spectrum, skip_gain, out_weight)


def solution(mesh):
    in_specs = (
        P("seq", "chan"),
        P("seq", "chan"),
        P(None, "seq", None, "chan"),
        P("chan"),
        P("chan", "seq"),
    )
    out_specs = P("seq", "chan")
    return jax.shard_map(shards, mesh=mesh, in_specs=in_specs, out_specs=out_specs, check_vma=False)
```

```python
import functools

import jax
import jax.numpy as jnp
import numpy as np
from jax import lax
from jax.experimental import pallas as pl
from jax.experimental.pallas import tpu as pltpu
from jax.sharding import PartitionSpec as P

BF16 = jnp.bfloat16
F32 = jnp.float32


def bit_reversed(number, width_bits):
    flipped = 0
    for bit_place in range(width_bits):
        flipped |= (number >> bit_place & 1) << (width_bits - 1 - bit_place)
    return flipped


def filter_row(residue, width_bits):
    return 2 * bit_reversed(residue // 2, width_bits) + residue % 2


def dft_tables(parts, rows):
    total = 2 * parts * rows
    residue = np.arange(2 * parts)[:, None, None]
    column = np.arange(rows)[None, :, None]
    position = np.arange(rows)[None, None, :]
    phase = 2.0 * np.pi * (position * (residue + 2 * parts * column) % total) / total
    cos, sin = np.cos(phase), np.sin(phase)
    forward = np.concatenate(
        [np.concatenate([cos, sin], axis=2), np.concatenate([-sin, cos], axis=2)], axis=1
    )
    inverse = np.transpose(forward, (0, 2, 1)) / total
    return forward.astype(BF16), inverse.astype(BF16)


def convolve_kernel(parts, rows, moved_ref, skip_ref, forward_ref, inverse_ref, out_ref, waves_ref, back_ref):
    width_bits = parts.bit_length() - 1
    chunk = 16

    def cosine(residue, block):
        return float(np.cos(np.pi * residue * block / parts))

    def sine(residue, block):
        return float(np.sin(np.pi * residue * block / parts))

    def spread(index, carry):
        here = pl.ds(index * chunk, chunk)
        there = pl.ds(rows + index * chunk, chunk)
        blocks = [moved_ref[block, here, :].astype(F32) for block in range(parts)]
        for residue in range(parts + 1):
            real = blocks[0]
            imag = jnp.zeros_like(real)
            for block in range(1, parts):
                real = real + cosine(residue, block) * blocks[block]
                imag = imag - sine(residue, block) * blocks[block]
            waves_ref[residue, here, :] = real.astype(BF16)
            waves_ref[residue, there, :] = imag.astype(BF16)
            if 0 < residue < parts:
                waves_ref[2 * parts - residue, here, :] = real.astype(BF16)
                waves_ref[2 * parts - residue, there, :] = (-imag).astype(BF16)
        return carry

    lax.fori_loop(0, rows // chunk, spread, 0)

    def through(residue):
        wave = jnp.dot(forward_ref[residue], waves_ref[residue], preferred_element_type=F32)
        source, odd = divmod(filter_row(residue, width_bits), 2)
        filter_real = moved_ref[source, pl.ds((2 + odd) * rows, rows), :].astype(F32)
        filter_imag = moved_ref[source, pl.ds((4 + odd) * rows, rows), :].astype(F32)
        real, imag = wave[:rows], wave[rows:]
        product = jnp.concatenate(
            [real * filter_real - imag * filter_imag, real * filter_imag + imag * filter_real], axis=0
        )
        return jnp.dot(inverse_ref[residue], product.astype(BF16), preferred_element_type=F32)

    for residue in range(parts + 1):
        back = through(residue)
        if 0 < residue < parts:
            other = through(2 * parts - residue)
            back_ref[residue, pl.ds(0, rows), :] = back[:rows] + other[:rows]
            back_ref[residue, pl.ds(rows, rows), :] = back[rows:] - other[rows:]
        else:
            back_ref[residue] = back

    skip = skip_ref[...]

    def gather(index, carry):
        here = pl.ds(index * chunk, chunk)
        there = pl.ds(rows + index * chunk, chunk)
        reals = [back_ref[residue, here, :] for residue in range(parts + 1)]
        imags = [back_ref[residue, there, :] for residue in range(parts + 1)]
        for block in range(parts):
            total = reals[0]
            for residue in range(1, parts + 1):
                total = total + cosine(residue, block) * reals[residue]
                if residue < parts and block:
                    total = total - sine(residue, block) * imags[residue]
            signal = moved_ref[block, here, :].astype(F32)
            gate = moved_ref[block, pl.ds(rows + index * chunk, chunk), :].astype(F32)
            out_ref[block, here, :] = (gate * (total + skip * signal)).astype(BF16)
        return carry

    lax.fori_loop(0, rows // chunk, gather, 0)


def convolve(moved, skip):
    parts, stacked, width = moved.shape
    rows = stacked // 6
    forward, inverse = dft_tables(parts, rows)
    whole = pl.BlockSpec(memory_space=pltpu.VMEM)
    return pl.pallas_call(
        functools.partial(convolve_kernel, parts, rows),
        out_shape=jax.ShapeDtypeStruct((parts, rows, width), BF16),
        in_specs=[whole] * 4,
        out_specs=whole,
        scratch_shapes=[
            pltpu.VMEM((2 * parts, 2 * rows, width), BF16),
            pltpu.VMEM((parts + 1, 2 * rows, width), F32),
        ],
        compiler_params=pltpu.CompilerParams(vmem_limit_bytes=40 * 2**20),
    )(moved, skip[None, :], forward, inverse)


def shards_general(values_in, gate_values, filter_spectrum, skip_gain, out_weight):
    parts = lax.axis_size("seq")
    layers = lax.axis_size("chan")
    rows, width = values_in.shape
    lanes = width // parts
    device = lax.axis_index("seq")

    def by_channel(array):
        return jnp.transpose(array.reshape(array.shape[0], parts, lanes), (1, 0, 2))

    filters = filter_spectrum.astype(BF16).reshape(4 * rows, width)
    packed = jnp.concatenate([by_channel(values_in), by_channel(gate_values), by_channel(filters)], axis=1)
    moved = lax.all_to_all(packed, "seq", 0, 0)
    skip = lax.dynamic_slice_in_dim(skip_gain, device * lanes, lanes)
    gated = convolve(moved, skip)
    gathered = lax.all_gather(gated.reshape(parts * rows, lanes), "seq", axis=1, tiled=True)

    own_cols = out_weight.shape[1]
    share = own_cols * parts // layers // parts
    per_block = parts // layers
    pieces = own_cols // share
    group = device % per_block
    member = device // per_block
    weight = jnp.zeros_like(out_weight)
    for step in range(pieces):
        piece = (member + step) % pieces
        sent = lax.dynamic_slice_in_dim(out_weight, piece * share, share, 1)
        pairs = [
            (source, source % per_block * pieces + (source // per_block + step) % pieces) for source in range(parts)
        ]
        arrived = lax.ppermute(sent, "seq", pairs)
        block = (device % pieces - step) % pieces
        weight = lax.dynamic_update_slice_in_dim(weight, arrived, block * share, 1)
    partials = jnp.dot(gathered, weight, preferred_element_type=F32).astype(BF16)
    mixed = lax.psum_scatter(partials, "chan", scatter_dimension=1, tiled=True)
    return lax.all_to_all(mixed, "seq", 0, 1, tiled=True)


WHOLE = pl.BlockSpec(memory_space=pltpu.VMEM)
CHEAP = pl.CostEstimate(flops=0, transcendentals=0, bytes_accessed=0)


def small_tables(parts, rows):
    total = 2 * parts * rows
    index = np.arange(rows)
    phase = 2.0 * np.pi * (index[:, None] * index[None, :] % rows) / rows
    cos, sin = np.cos(phase), np.sin(phase)
    forward = np.block([[cos, sin], [-sin, cos]])
    residue = np.arange(2 * parts).reshape(2, 1, parts)
    turn = 2.0 * np.pi * index[None, :, None] * residue / total
    return forward.astype(BF16), forward.T.astype(BF16), np.cos(turn).astype(F32), np.sin(turn).astype(F32)


def cosine(parts, residue, block):
    return float(np.cos(np.pi * residue * block / parts))


def sine(parts, residue, block):
    return float(np.sin(np.pi * residue * block / parts))


def weighted(terms):
    total = None
    for factor, term in terms:
        if abs(factor) < 1e-12:
            continue
        part = term if factor == 1.0 else factor * term
        total = part if total is None else total + part
    return total


def plus(left, right):
    return left if right is None else right if left is None else left + right


def minus(left, right):
    return left if right is None else -right if left is None else left - right


def own_place():
    device = lax.axis_index("seq")
    return device // 2, device % 2


def block_at(index, size):
    return pl.ds(pl.multiple_of(index * size, size), size)


def pack_signals_kernel(offsets, values_ref, filter_ref, *refs):
    out_refs, (plane_ref, arrived) = refs[: len(offsets)], refs[len(offsets) :]
    chip, _ = own_place()
    planes, rows, _ = filter_ref.shape
    lanes = out_refs[0].shape[1]
    copies, work = [], []
    for place, offset in enumerate(offsets):
        here = block_at(chip ^ offset, lanes)
        for plane in range(planes):
            copies.append(
                pltpu.make_async_copy(filter_ref.at[plane, :, here], plane_ref.at[place, plane], arrived.at[place, plane])
            )
            work.append((place, plane))
        values = out_refs[place].at[pl.ds(planes * rows, rows)]
        copies.append(pltpu.make_async_copy(values_ref.at[:, here], values, arrived.at[place, planes]))
        work.append(None)
    for copy in copies:
        copy.start()
    for copy, task in zip(copies, work):
        copy.wait()
        if task:
            place, plane = task
            out_refs[place][pl.ds(plane * rows, rows), :] = plane_ref[place, plane].astype(BF16)
    used = (planes + 1) * rows
    for out_ref in out_refs:
        if out_ref.shape[0] > used:
            out_ref[pl.ds(used, out_ref.shape[0] - used), :] = out_ref[pl.ds(0, out_ref.shape[0] - used), :]


def pack_signals(values_in, filters, chips, offsets, spare):
    planes, rows, width = filters.shape
    lanes = width // chips
    return pl.pallas_call(
        functools.partial(pack_signals_kernel, offsets),
        in_specs=[pl.BlockSpec(memory_space=pltpu.HBM)] * 2,
        out_specs=[WHOLE] * len(offsets),
        out_shape=[jax.ShapeDtypeStruct(((planes + 1) * rows + spare, lanes), BF16)] * len(offsets),
        scratch_shapes=[
            pltpu.VMEM((len(offsets), planes, rows, lanes), F32),
            pltpu.SemaphoreType.DMA((len(offsets), planes + 1)),
        ],
        cost_estimate=CHEAP,
        compiler_params=pltpu.CompilerParams(vmem_limit_bytes=8 * 2**20),
        name="pack_signals",
    )(*(pltpu.with_memory_space_constraint(array, pltpu.HBM) for array in (values_in, filters)))


def pack_moved_kernel(chips, gate_ref, own_ref, other_ref, *refs):
    out_refs, (mine_ref, arrived) = refs[:chips], refs[chips:]
    chip, core = own_place()
    rows = gate_ref.shape[0]
    depth, held = own_ref.shape
    quarter, share = depth // 4, held // chips

    def copies_from(weight_ref):
        copies = [pltpu.make_async_copy(weight_ref.at[:, block_at(chip, share)], mine_ref, arrived.at[0, 0])]
        for offset in range(chips):
            out_ref, target = out_refs[offset], chip ^ offset
            gates = gate_ref.at[:, block_at(target, out_ref.shape[1])]
            copies.append(pltpu.make_async_copy(gates, out_ref.at[pl.ds(0, rows)], arrived.at[offset, 2]))
            for part in range(2 if offset else 0):
                source = weight_ref.at[block_at(2 * core + part, quarter), block_at(target, share)]
                sink = out_ref.at[pl.ds(rows, quarter), pl.ds(part * share, share)]
                copies.append(pltpu.make_async_copy(source, sink, arrived.at[offset, part]))
        for copy in copies:
            copy.start()
        for copy in copies:
            copy.wait()

    @pl.when(core == 0)
    def _():
        copies_from(own_ref)

    @pl.when(core == 1)
    def _():
        copies_from(other_ref)


def pack_moved(gate_values, own, other, chips):
    rows, width = gate_values.shape
    depth, held = own.shape
    share = held // chips
    return pl.pallas_call(
        functools.partial(pack_moved_kernel, chips),
        in_specs=[pl.BlockSpec(memory_space=pltpu.HBM)] * 2 + [pl.BlockSpec(memory_space=pl.ANY)],
        out_specs=[WHOLE] * (chips + 1),
        out_shape=[
            *(jax.ShapeDtypeStruct((rows + (depth // 4 if offset else 0), 2 * share), BF16) for offset in range(chips)),
            jax.ShapeDtypeStruct((depth, share), BF16),
        ],
        scratch_shapes=[pltpu.SemaphoreType.DMA((chips, 3))],
        cost_estimate=CHEAP,
        compiler_params=pltpu.CompilerParams(vmem_limit_bytes=8 * 2**20),
        name="pack_moved",
    )(*(pltpu.with_memory_space_constraint(array, pltpu.HBM) for array in (gate_values, own)), other)


def pick_values_kernel(chips, start, *refs):
    in_refs, out_refs = refs[:chips], refs[chips:]
    for offset in range(chips):
        part, place = divmod(offset, chips // 2)
        out_refs[part][place] = in_refs[offset][pl.ds(start, out_refs[part].shape[1]), :]


def pick_values(first, rows, start):
    chips = len(first)
    half = jax.ShapeDtypeStruct((chips // 2, rows, first[0].shape[1]), BF16)
    return pl.pallas_call(
        functools.partial(pick_values_kernel, chips, start),
        in_specs=[WHOLE] * chips,
        out_specs=[WHOLE] * 2,
        out_shape=[half, half],
        cost_estimate=CHEAP,
        compiler_params=pltpu.CompilerParams(vmem_limit_bytes=4 * 2**20),
        name="pick_values",
    )(*first)


def forward_kernel(chips, cos_ref, sin_ref, table_ref, *refs):
    own_refs, other_refs, (out_ref, signal_ref, waves_ref) = refs[:2], refs[2:4], refs[4:]
    chip, core = own_place()
    parts = 2 * chips
    rows, lanes = own_refs[0].shape[1:]
    chunk, width = 16, 128
    for offset in range(chips):
        part, place = divmod(offset, chips // 2)
        signal_ref[2 * (chip ^ offset) + core] = own_refs[part][place]
        signal_ref[2 * (chip ^ offset) + 1 - core] = other_refs[part][place]
    sign = (1 - 2 * core).astype(F32)

    def spread(index, carry):
        here = block_at(index, chunk)
        there = pl.ds(pl.multiple_of(rows + index * chunk, chunk), chunk)
        cos_all, sin_all = cos_ref[core, here, :], sin_ref[core, here, :]
        for start in range(0, lanes, width):
            blocks = [signal_ref[block, here, pl.ds(start, width)].astype(F32) for block in range(parts)]
            blocks = [block * sign if place % 2 else block for place, block in enumerate(blocks)]

            def store(residue, real, imag):
                cos, sin = cos_all[:, residue : residue + 1], sin_all[:, residue : residue + 1]
                if imag is None:
                    real, imag = real * cos, -(real * sin)
                else:
                    real, imag = real * cos + imag * sin, imag * cos - real * sin
                columns = pl.ds(residue * lanes + start, width)
                waves_ref[here, columns] = real.astype(BF16)
                waves_ref[there, columns] = imag.astype(BF16)

            for residue in range(parts // 2 + 1):
                even, odd = range(0, parts, 2), range(1, parts, 2)
                cos_even = weighted([(cosine(parts, residue, block), blocks[block]) for block in even])
                cos_odd = weighted([(cosine(parts, residue, block), blocks[block]) for block in odd])
                sin_even = weighted([(sine(parts, residue, block), blocks[block]) for block in even])
                sin_odd = weighted([(sine(parts, residue, block), blocks[block]) for block in odd])
                sin_sum = plus(sin_even, sin_odd)
                store(residue, plus(cos_even, cos_odd), None if sin_sum is None else -sin_sum)
                if 0 < residue and 2 * residue != parts:
                    store(parts - residue, minus(cos_even, cos_odd), minus(sin_even, sin_odd))
        return carry

    lax.fori_loop(0, rows // chunk, spread, 0)
    for residue in range(parts):
        columns = pl.ds(residue * lanes, lanes)
        out_ref[:, columns] = jnp.dot(table_ref[...], waves_ref[:, columns], preferred_element_type=F32)


def forward(own, other, tables):
    chips, (_, rows, lanes) = 2 * own[0].shape[0], own[0].shape
    table, _, cos, sin = tables
    spectrum = (2 * rows, 2 * chips * lanes)
    return pl.pallas_call(
        functools.partial(forward_kernel, chips),
        in_specs=[WHOLE] * 7,
        out_specs=WHOLE,
        out_shape=jax.ShapeDtypeStruct(spectrum, F32),
        scratch_shapes=[pltpu.VMEM((2 * chips, rows, lanes), BF16), pltpu.VMEM(spectrum, BF16)],
        cost_estimate=CHEAP,
        compiler_params=pltpu.CompilerParams(vmem_limit_bytes=32 * 2**20),
        name="forward",
    )(cos, sin, table, *own, *other)


def backward_kernel(chips, cos_ref, sin_ref, table_ref, spectrum_ref, *refs):
    filter_refs, (keep_ref, *send_refs, filter_ref, product_ref, back_ref) = refs[:chips], refs[chips:]
    chip, core = own_place()
    parts = 2 * chips
    rows, lanes = keep_ref.shape[1:]
    chip_bits = chips.bit_length() - 1
    chunk, width = 16, 128
    for offset in range(chips):
        for plane in range(filter_ref.shape[1]):
            filter_ref[chip ^ offset, plane] = filter_refs[offset][pl.ds(plane * rows, rows), :]

    for residue in range(parts):
        source, odd = bit_reversed(residue // 2, chip_bits), residue % 2
        columns = pl.ds(residue * lanes, lanes)
        filter_real = filter_ref[source, odd].astype(F32)
        filter_imag = filter_ref[source, 2 + odd].astype(F32)
        real = spectrum_ref[pl.ds(0, rows), columns]
        imag = spectrum_ref[pl.ds(rows, rows), columns]
        product_ref[pl.ds(0, rows), columns] = (real * filter_real - imag * filter_imag).astype(BF16)
        product_ref[pl.ds(rows, rows), columns] = (real * filter_imag + imag * filter_real).astype(BF16)
        back_ref[:, columns] = jnp.dot(table_ref[...], product_ref[:, columns], preferred_element_type=F32)

    scale = 1.0 / (2 * parts * rows)
    sign = (1 - 2 * core).astype(F32)
    upper = core == 1

    def gather(index, carry):
        here = block_at(index, chunk)
        there = pl.ds(pl.multiple_of(rows + index * chunk, chunk), chunk)
        cos_all, sin_all = cos_ref[core, here, :] * scale, sin_ref[core, here, :] * scale
        for start in range(0, lanes, width):
            reals, imags = [], []
            for residue in range(parts):
                columns = pl.ds(residue * lanes + start, width)
                real, imag = back_ref[here, columns], back_ref[there, columns]
                cos, sin = cos_all[:, residue : residue + 1], sin_all[:, residue : residue + 1]
                reals.append(real * cos - imag * sin)
                imags.append(real * sin + imag * cos)
            totals = [None] * parts
            for block in range(parts // 2 + 1):
                even, odd = range(0, parts, 2), range(1, parts, 2)
                cos_even = weighted([(cosine(parts, residue, block), reals[residue]) for residue in even])
                cos_odd = weighted([(cosine(parts, residue, block), reals[residue]) for residue in odd])
                sin_even = weighted([(sine(parts, residue, block), imags[residue]) for residue in even])
                sin_odd = weighted([(sine(parts, residue, block), imags[residue]) for residue in odd])
                totals[block] = minus(plus(cos_even, cos_odd), plus(sin_even, sin_odd))
                if 0 < block and 2 * block != parts:
                    totals[parts - block] = plus(minus(cos_even, cos_odd), minus(sin_even, sin_odd))
            lane = pl.ds(start, width)
            for pair in range(chips):
                low, high = totals[2 * pair], totals[2 * pair + 1] * sign
                keep_ref[pair, here, lane] = jnp.where(upper, high, low)
                part, place = divmod(pair, chips // 2)
                send_refs[part][place, here, lane] = jnp.where(upper, low, high).astype(BF16)
        return carry

    lax.fori_loop(0, rows // chunk, gather, 0)


def backward(spectrum, first, tables):
    chips = len(first)
    rows, lanes = spectrum.shape[0] // 2, first[0].shape[1]
    _, table, cos, sin = tables
    half = jax.ShapeDtypeStruct((chips // 2, rows, lanes), BF16)
    return pl.pallas_call(
        functools.partial(backward_kernel, chips),
        in_specs=[WHOLE] * (4 + chips),
        out_specs=[WHOLE] * 3,
        out_shape=[jax.ShapeDtypeStruct((chips, rows, lanes), F32), half, half],
        scratch_shapes=[
            pltpu.VMEM((chips, 4, rows, lanes), BF16),
            pltpu.VMEM(spectrum.shape, BF16),
            pltpu.VMEM(spectrum.shape, F32),
        ],
        cost_estimate=CHEAP,
        compiler_params=pltpu.CompilerParams(vmem_limit_bytes=32 * 2**20),
        name="backward",
    )(cos, sin, table, spectrum, *first)


def gate_kernel(chips, skip_ref, keep_ref, low_ref, high_ref, *refs):
    signal_refs, gate_refs = refs[:chips], refs[chips : 2 * chips]
    out_ref, longer_ref, arrived_ref = refs[2 * chips :]
    chip, _ = own_place()
    rows, lanes = keep_ref.shape[1:]
    skip = skip_ref[:, block_at(chip, lanes)]
    arrived_ref[pl.ds(0, chips // 2)] = low_ref[...]
    arrived_ref[pl.ds(chips // 2, chips // 2)] = high_ref[...]
    for offset in range(chips):
        block = chip ^ offset
        convolved = keep_ref[block] + arrived_ref[block].astype(F32)
        signal = signal_refs[offset][pl.ds(4 * rows, rows), :].astype(F32)
        gate = gate_refs[offset][pl.ds(0, rows), :].astype(F32)
        gated = (gate * (convolved + skip * signal)).astype(BF16)
        out_ref[block_at(block, rows), :] = gated
        longer_ref[block_at(block, rows), :] = gated
    end = chips * rows
    longer_ref[pl.ds(end, longer_ref.shape[0] - end), :] = longer_ref[pl.ds(0, longer_ref.shape[0] - end), :]


def gate(skip, keep, arrived, first, gates, spare):
    chips, rows, lanes = keep.shape
    return pl.pallas_call(
        functools.partial(gate_kernel, chips),
        in_specs=[WHOLE] * (4 + 2 * chips),
        out_specs=[WHOLE] * 2,
        out_shape=[
            jax.ShapeDtypeStruct((chips * rows, lanes), BF16),
            jax.ShapeDtypeStruct((chips * rows + spare, lanes), BF16),
        ],
        scratch_shapes=[pltpu.VMEM((chips, rows, lanes), BF16)],
        cost_estimate=CHEAP,
        compiler_params=pltpu.CompilerParams(vmem_limit_bytes=6 * 2**20),
        name="gate",
    )(skip, keep, *arrived, *first, *gates)


def piece_of(ref, half, part):
    quarter, share = half // 2, ref.shape[1] // 2
    return ref[pl.ds(ref.shape[0] - quarter, quarter), pl.ds(part * share, share)]


def collect_kernel(in_refs, out_refs):
    rows = out_refs[0].shape[0]
    quarter = len(out_refs) * rows // (2 * len(in_refs))
    for place in range(2 * len(in_refs)):
        index, start = divmod(place * quarter, rows)
        out_refs[index][pl.ds(start, quarter), :] = piece_of(in_refs[place // 2], 2 * quarter, place % 2)


def collect(moved, half):
    count = len(moved)
    shape = (count * half // 2, moved[0].shape[1] // 2)
    return pl.pallas_call(
        lambda *refs: collect_kernel(refs[:count], refs[count:]),
        in_specs=[WHOLE] * count,
        out_specs=[WHOLE] * 2,
        out_shape=[jax.ShapeDtypeStruct(shape, BF16)] * 2,
        cost_estimate=CHEAP,
        compiler_params=pltpu.CompilerParams(vmem_limit_bytes=4 * 2**20),
        name="collect_weights",
    )(*moved)


def arrange_kernel(chips, mine_ref, *refs):
    moved_refs, (*other_refs, out_ref) = refs[: chips - 1], refs[chips - 1 :]
    chip, core = own_place()
    layer = lax.axis_index("chan")
    depth, share = mine_ref.shape
    quarter = depth // 4
    out_ref[:, block_at(chip ^ layer, share)] = mine_ref[...]
    for place in range(2 * (chips - 1)):
        offset, part = place // 2 + 1, place % 2
        columns = block_at(chip ^ layer ^ offset, share)
        index, start = divmod(place * quarter, other_refs[0].shape[0])
        out_ref[block_at(2 * core + part, quarter), columns] = piece_of(moved_refs[offset - 1], 2 * quarter, part)
        out_ref[block_at(2 * (1 - core) + part, quarter), columns] = other_refs[index][pl.ds(start, quarter), :]


def arrange(mine, moved, others):
    chips = len(moved) + 1
    depth, share = mine.shape
    return pl.pallas_call(
        functools.partial(arrange_kernel, chips),
        in_specs=[WHOLE] * (chips + len(others)),
        out_specs=WHOLE,
        out_shape=jax.ShapeDtypeStruct((depth, chips * share), BF16),
        cost_estimate=CHEAP,
        compiler_params=pltpu.CompilerParams(vmem_limit_bytes=8 * 2**20),
        name="arrange_weights",
    )(mine, *moved, *others)


def join_channels(chips, gated_refs, joined_ref):
    chip, _ = own_place()
    lanes = gated_refs[0].shape[1]
    for offset in range(chips):
        joined_ref[:, block_at(chip ^ offset, lanes)] = gated_refs[offset][pl.ds(0, joined_ref.shape[0]), :]


def project_moved_kernel(chips, weight_ref, *refs):
    gated_refs, (*out_refs, joined_ref) = refs[:chips], refs[chips:]
    share = out_refs[0].shape[1]
    join_channels(chips, gated_refs, joined_ref)
    partial = jnp.dot(joined_ref[...], weight_ref[...], preferred_element_type=F32).astype(BF16)
    for target, out_ref in enumerate(out_refs):
        out_ref[...] = partial[:, target * share : (target + 1) * share]


def project_moved(weight, gated):
    chips = len(gated)
    depth, columns = weight.shape
    rows = gated[0].shape[0]
    block = jax.ShapeDtypeStruct((rows, columns // chips), BF16)
    return pl.pallas_call(
        functools.partial(project_moved_kernel, chips),
        in_specs=[WHOLE] * (1 + chips),
        out_specs=[WHOLE] * chips,
        out_shape=[block] * chips,
        scratch_shapes=[pltpu.VMEM((rows, depth), BF16)],
        cost_estimate=CHEAP,
        compiler_params=pltpu.CompilerParams(vmem_limit_bytes=8 * 2**20),
        name="project_moved",
    )(weight, *gated)


def project_still_kernel(chips, own_ref, other_ref, *refs):
    gated_refs, out_refs, joined_ref = refs[:chips], refs[chips : 2 * chips], refs[2 * chips]
    chip, core = own_place()
    rows = out_refs[0].shape[0]
    join_channels(chips, gated_refs, joined_ref)

    def project_with(weight_ref):
        for offset in range(chips):
            gated = joined_ref[block_at(chip ^ offset, rows), :]
            partial = jnp.dot(gated, weight_ref[...], preferred_element_type=F32).astype(BF16)
            out_refs[offset][pl.ds(0, rows), :] = partial
            more = out_refs[offset].shape[0] - rows
            if more:
                out_refs[offset][pl.ds(rows, more), :] = partial[:more]

    @pl.when(core == 0)
    def _():
        project_with(other_ref)

    @pl.when(core == 1)
    def _():
        project_with(own_ref)


def project_still(own, other, gated, spare):
    chips = len(gated)
    depth, held = own.shape
    rows = gated[0].shape[0] // chips
    return pl.pallas_call(
        functools.partial(project_still_kernel, chips),
        in_specs=[WHOLE] * (2 + chips),
        out_specs=[WHOLE] * chips,
        out_shape=[jax.ShapeDtypeStruct((rows + (spare if offset else 0), held), BF16) for offset in range(chips)],
        scratch_shapes=[pltpu.VMEM((rows * chips, depth), BF16)],
        cost_estimate=CHEAP,
        compiler_params=pltpu.CompilerParams(vmem_limit_bytes=12 * 2**20),
        name="project_still",
    )(own, other, *gated)


def sort_kernel(chips, *refs):
    in_refs, (keep_ref, pass_ref, send_ref, sorted_ref) = refs[:chips], refs[chips:]
    chip, _ = own_place()
    layer = lax.axis_index("chan")
    for offset in range(chips):
        sorted_ref[chip ^ layer ^ offset] = in_refs[offset][pl.ds(0, sorted_ref.shape[1]), :]
    keep_ref[...] = sorted_ref[0]
    send_ref[0] = sorted_ref[1]
    pass_ref[...] = sorted_ref[2]
    send_ref[1] = sorted_ref[3]


def sort_blocks(blocks, rows):
    chips = len(blocks)
    block = jax.ShapeDtypeStruct((rows, blocks[0].shape[1]), BF16)
    return pl.pallas_call(
        functools.partial(sort_kernel, chips),
        in_specs=[WHOLE] * chips,
        out_specs=[WHOLE] * 3,
        out_shape=[block, block, jax.ShapeDtypeStruct((2, *block.shape), BF16)],
        scratch_shapes=[pltpu.VMEM((chips, *block.shape), BF16)],
        cost_estimate=CHEAP,
        compiler_params=pltpu.CompilerParams(vmem_limit_bytes=4 * 2**20),
        name="sort_blocks",
    )(*blocks)


def finish_kernel(chips, keep_ref, first_ref, second_ref, *out_refs):
    chip, _ = own_place()
    rows = out_refs[0].shape[0]
    for offset in range(chips):
        here = block_at(chip ^ offset, rows)
        total = keep_ref[here, :].astype(F32) + first_ref[here, :].astype(F32) + second_ref[here, :].astype(F32)
        out_refs[offset][...] = total.astype(BF16)


def finish(keep, first, second, chips):
    rows, columns = keep.shape
    return pl.pallas_call(
        functools.partial(finish_kernel, chips),
        in_specs=[WHOLE] * 3,
        out_specs=[WHOLE] * chips,
        out_shape=[jax.ShapeDtypeStruct((rows // chips, columns), BF16)] * chips,
        cost_estimate=CHEAP,
        compiler_params=pltpu.CompilerParams(vmem_limit_bytes=4 * 2**20),
        name="finish",
    )(keep, first, second)


def join_kernel(chips, keep_ref, first_ref, second_ref, *refs):
    in_refs, out_ref = refs[:chips], refs[chips]
    chip, _ = own_place()
    share = in_refs[0].shape[1]
    for offset in range(chips):
        out_ref[:, block_at(chip ^ offset, share)] = in_refs[offset][...]
    total = keep_ref[...].astype(F32) + first_ref[0].astype(F32) + second_ref[...].astype(F32)
    out_ref[:, pl.ds(chips * share, total.shape[1])] = total.astype(BF16)


def join(keep, first, second, blocks):
    chips = len(blocks)
    rows, share = blocks[0].shape
    return pl.pallas_call(
        functools.partial(join_kernel, chips),
        in_specs=[WHOLE] * (3 + chips),
        out_specs=WHOLE,
        out_shape=jax.ShapeDtypeStruct((rows, chips * share + keep.shape[1]), BF16),
        cost_estimate=CHEAP,
        compiler_params=pltpu.CompilerParams(vmem_limit_bytes=4 * 2**20),
        name="join",
    )(keep, first, second, *blocks)


def swapped(value, axis, offset):
    if not offset:
        return value
    return lax.ppermute(value, axis, [(source, source ^ offset) for source in range(lax.axis_size(axis))])


def to_chips(blocks):
    return [swapped(block, "seq", 2 * offset) for offset, block in enumerate(blocks)]


def after(value, *others):
    return lax.optimization_barrier((value, *others))[0]


def added(left, right):
    return (left.astype(F32) + right.astype(F32)).astype(BF16)


def shards_direct(values_in, gate_values, filter_spectrum, skip_gain, out_weight):
    parts = lax.axis_size("seq")
    chips = parts // 2
    rows, width = values_in.shape
    tables = small_tables(parts, rows)

    flat_filters = filter_spectrum.reshape(4, rows, width)
    near = pack_signals(values_in, flat_filters, chips, (1, 2), 16)
    own, far = pack_signals(after(values_in, near[0]), flat_filters, chips, (0, 3), 0)
    first = [own, *near, far]
    other_weight = swapped(out_weight, "seq", 1)
    *moved, mine = pack_moved(after(gate_values, first[0]), out_weight, other_weight, chips)
    first = to_chips(first)
    own = pick_values([after(block, moved[0]) for block in first], rows, 4 * rows)
    moved = to_chips(moved)
    spectrum = forward(own, [swapped(part, "seq", 1) for part in own], tables)
    keep, *send = backward(spectrum, first, tables)
    gated, longer = gate(skip_gain[None, :], keep, [swapped(part, "seq", 1) for part in send], first, moved, 16)
    gathered = to_chips([gated, longer, longer, gated])

    still = project_still(out_weight, other_weight, gathered, 16)
    others = [swapped(part, "seq", 1) for part in collect([after(block, gated) for block in moved[1:]], out_weight.shape[0] // 2)]
    moved_weight = arrange(mine, moved[1:], others)
    keep, near, passed, far = project_moved(moved_weight, [after(gated, still[0]), *gathered[1:]])
    first, other = swapped(near, "chan", 1), swapped(far, "chan", 1)
    blocks = to_chips(finish(keep, first, swapped(added(after(passed, first), other), "chan", 2), chips))
    keep, passed, send = sort_blocks(to_chips(still), rows)
    first = swapped(send, "chan", 1)
    return join(keep, first, swapped(added(passed, first[1]), "chan", 2), blocks)


def shards(values_in, gate_values, filter_spectrum, skip_gain, out_weight):
    parts, layers = lax.axis_size("seq"), lax.axis_size("chan")
    rows, width = values_in.shape
    share = out_weight.shape[1] // layers
    aligned = width // parts % 128 == 0 and share % 128 == 0 and rows % 32 == 0
    run = shards_direct if aligned and layers == 4 and parts == 8 else shards_general
    return run(values_in, gate_values, filter_spectrum, skip_gain, out_weight)


def solution(mesh):
    in_specs = (
        P("seq", "chan"),
        P("seq", "chan"),
        P(None, "seq", None, "chan"),
        P("chan"),
        P("chan", "seq"),
    )
    out_specs = P("seq", "chan")
    return jax.shard_map(shards, mesh=mesh, in_specs=in_specs, out_specs=out_specs, check_vma=False)
```

```python
import functools

import jax
import jax.numpy as jnp
import numpy as np
from jax import lax
from jax.experimental import pallas as pl
from jax.experimental.pallas import tpu as pltpu
from jax.sharding import PartitionSpec as P

BF16 = jnp.bfloat16
F32 = jnp.float32


def bit_reversed(number, width_bits):
    flipped = 0
    for bit_place in range(width_bits):
        flipped |= (number >> bit_place & 1) << (width_bits - 1 - bit_place)
    return flipped


def filter_row(residue, width_bits):
    return 2 * bit_reversed(residue // 2, width_bits) + residue % 2


def dft_tables(parts, rows):
    total = 2 * parts * rows
    residue = np.arange(2 * parts)[:, None, None]
    column = np.arange(rows)[None, :, None]
    position = np.arange(rows)[None, None, :]
    phase = 2.0 * np.pi * (position * (residue + 2 * parts * column) % total) / total
    cos, sin = np.cos(phase), np.sin(phase)
    forward = np.concatenate(
        [np.concatenate([cos, sin], axis=2), np.concatenate([-sin, cos], axis=2)], axis=1
    )
    inverse = np.transpose(forward, (0, 2, 1)) / total
    return forward.astype(BF16), inverse.astype(BF16)


def convolve_kernel(parts, rows, moved_ref, skip_ref, forward_ref, inverse_ref, out_ref, waves_ref, back_ref):
    width_bits = parts.bit_length() - 1
    chunk = 16

    def cosine(residue, block):
        return float(np.cos(np.pi * residue * block / parts))

    def sine(residue, block):
        return float(np.sin(np.pi * residue * block / parts))

    def spread(index, carry):
        here = pl.ds(index * chunk, chunk)
        there = pl.ds(rows + index * chunk, chunk)
        blocks = [moved_ref[block, here, :].astype(F32) for block in range(parts)]
        for residue in range(parts + 1):
            real = blocks[0]
            imag = jnp.zeros_like(real)
            for block in range(1, parts):
                real = real + cosine(residue, block) * blocks[block]
                imag = imag - sine(residue, block) * blocks[block]
            waves_ref[residue, here, :] = real.astype(BF16)
            waves_ref[residue, there, :] = imag.astype(BF16)
            if 0 < residue < parts:
                waves_ref[2 * parts - residue, here, :] = real.astype(BF16)
                waves_ref[2 * parts - residue, there, :] = (-imag).astype(BF16)
        return carry

    lax.fori_loop(0, rows // chunk, spread, 0)

    def through(residue):
        wave = jnp.dot(forward_ref[residue], waves_ref[residue], preferred_element_type=F32)
        source, odd = divmod(filter_row(residue, width_bits), 2)
        filter_real = moved_ref[source, pl.ds((2 + odd) * rows, rows), :].astype(F32)
        filter_imag = moved_ref[source, pl.ds((4 + odd) * rows, rows), :].astype(F32)
        real, imag = wave[:rows], wave[rows:]
        product = jnp.concatenate(
            [real * filter_real - imag * filter_imag, real * filter_imag + imag * filter_real], axis=0
        )
        return jnp.dot(inverse_ref[residue], product.astype(BF16), preferred_element_type=F32)

    for residue in range(parts + 1):
        back = through(residue)
        if 0 < residue < parts:
            other = through(2 * parts - residue)
            back_ref[residue, pl.ds(0, rows), :] = back[:rows] + other[:rows]
            back_ref[residue, pl.ds(rows, rows), :] = back[rows:] - other[rows:]
        else:
            back_ref[residue] = back

    skip = skip_ref[...]

    def gather(index, carry):
        here = pl.ds(index * chunk, chunk)
        there = pl.ds(rows + index * chunk, chunk)
        reals = [back_ref[residue, here, :] for residue in range(parts + 1)]
        imags = [back_ref[residue, there, :] for residue in range(parts + 1)]
        for block in range(parts):
            total = reals[0]
            for residue in range(1, parts + 1):
                total = total + cosine(residue, block) * reals[residue]
                if residue < parts and block:
                    total = total - sine(residue, block) * imags[residue]
            signal = moved_ref[block, here, :].astype(F32)
            gate = moved_ref[block, pl.ds(rows + index * chunk, chunk), :].astype(F32)
            out_ref[block, here, :] = (gate * (total + skip * signal)).astype(BF16)
        return carry

    lax.fori_loop(0, rows // chunk, gather, 0)


def convolve(moved, skip):
    parts, stacked, width = moved.shape
    rows = stacked // 6
    forward, inverse = dft_tables(parts, rows)
    whole = pl.BlockSpec(memory_space=pltpu.VMEM)
    return pl.pallas_call(
        functools.partial(convolve_kernel, parts, rows),
        out_shape=jax.ShapeDtypeStruct((parts, rows, width), BF16),
        in_specs=[whole] * 4,
        out_specs=whole,
        scratch_shapes=[
            pltpu.VMEM((2 * parts, 2 * rows, width), BF16),
            pltpu.VMEM((parts + 1, 2 * rows, width), F32),
        ],
        compiler_params=pltpu.CompilerParams(vmem_limit_bytes=40 * 2**20),
    )(moved, skip[None, :], forward, inverse)


def shards_general(values_in, gate_values, filter_spectrum, skip_gain, out_weight):
    parts = lax.axis_size("seq")
    layers = lax.axis_size("chan")
    rows, width = values_in.shape
    lanes = width // parts
    device = lax.axis_index("seq")

    def by_channel(array):
        return jnp.transpose(array.reshape(array.shape[0], parts, lanes), (1, 0, 2))

    filters = filter_spectrum.astype(BF16).reshape(4 * rows, width)
    packed = jnp.concatenate([by_channel(values_in), by_channel(gate_values), by_channel(filters)], axis=1)
    moved = lax.all_to_all(packed, "seq", 0, 0)
    skip = lax.dynamic_slice_in_dim(skip_gain, device * lanes, lanes)
    gated = convolve(moved, skip)
    gathered = lax.all_gather(gated.reshape(parts * rows, lanes), "seq", axis=1, tiled=True)

    own_cols = out_weight.shape[1]
    share = own_cols * parts // layers // parts
    per_block = parts // layers
    pieces = own_cols // share
    group = device % per_block
    member = device // per_block
    weight = jnp.zeros_like(out_weight)
    for step in range(pieces):
        piece = (member + step) % pieces
        sent = lax.dynamic_slice_in_dim(out_weight, piece * share, share, 1)
        pairs = [
            (source, source % per_block * pieces + (source // per_block + step) % pieces) for source in range(parts)
        ]
        arrived = lax.ppermute(sent, "seq", pairs)
        block = (device % pieces - step) % pieces
        weight = lax.dynamic_update_slice_in_dim(weight, arrived, block * share, 1)
    partials = jnp.dot(gathered, weight, preferred_element_type=F32).astype(BF16)
    mixed = lax.psum_scatter(partials, "chan", scatter_dimension=1, tiled=True)
    return lax.all_to_all(mixed, "seq", 0, 1, tiled=True)


WHOLE = pl.BlockSpec(memory_space=pltpu.VMEM)
CHEAP = pl.CostEstimate(flops=0, transcendentals=0, bytes_accessed=0)


def small_tables(parts, rows):
    total = 2 * parts * rows
    index = np.arange(rows)
    phase = 2.0 * np.pi * (index[:, None] * index[None, :] % rows) / rows
    cos, sin = np.cos(phase), np.sin(phase)
    forward = np.block([[cos, sin], [-sin, cos]])
    residue = np.arange(2 * parts).reshape(2, 1, parts)
    turn = 2.0 * np.pi * index[None, :, None] * residue / total
    return forward.astype(BF16), forward.T.astype(BF16), np.cos(turn).astype(F32), np.sin(turn).astype(F32)


def cosine(parts, residue, block):
    return float(np.cos(np.pi * residue * block / parts))


def sine(parts, residue, block):
    return float(np.sin(np.pi * residue * block / parts))


def weighted(terms):
    total = None
    for factor, term in terms:
        if abs(factor) < 1e-12:
            continue
        part = term if factor == 1.0 else factor * term
        total = part if total is None else total + part
    return total


def plus(left, right):
    return left if right is None else right if left is None else left + right


def minus(left, right):
    return left if right is None else -right if left is None else left - right


def own_place():
    device = lax.axis_index("seq")
    return device // 2, device % 2


def block_at(index, size):
    return pl.ds(pl.multiple_of(index * size, size), size)


def pack_filters_kernel(offsets, filter_ref, *refs):
    out_refs, (plane_ref, arrived) = refs[: len(offsets)], refs[len(offsets) :]
    chip, _ = own_place()
    planes, rows, _ = filter_ref.shape
    lanes = out_refs[0].shape[1]
    copies = []
    for place, offset in enumerate(offsets):
        here = block_at(chip ^ offset, lanes)
        for plane in range(planes):
            copies.append(
                pltpu.make_async_copy(filter_ref.at[plane, :, here], plane_ref.at[place, plane], arrived.at[place, plane])
            )
    for copy in copies:
        copy.start()
    for index, copy in enumerate(copies):
        copy.wait()
        place, plane = divmod(index, planes)
        out_refs[place][pl.ds(plane * rows, rows), :] = plane_ref[place, plane].astype(BF16)
    used = planes * rows
    for out_ref in out_refs:
        if out_ref.shape[0] > used:
            out_ref[pl.ds(used, out_ref.shape[0] - used), :] = out_ref[pl.ds(0, out_ref.shape[0] - used), :]


def pack_filters(filters, chips, offsets, spare):
    planes, rows, width = filters.shape
    lanes = width // chips
    return pl.pallas_call(
        functools.partial(pack_filters_kernel, offsets),
        in_specs=[pl.BlockSpec(memory_space=pltpu.HBM)],
        out_specs=[WHOLE] * len(offsets),
        out_shape=[jax.ShapeDtypeStruct((planes * rows + spare, lanes), BF16)] * len(offsets),
        scratch_shapes=[
            pltpu.VMEM((len(offsets), planes, rows, lanes), F32),
            pltpu.SemaphoreType.DMA((len(offsets), planes)),
        ],
        cost_estimate=CHEAP,
        compiler_params=pltpu.CompilerParams(vmem_limit_bytes=8 * 2**20),
        name="pack_filters",
    )(pltpu.with_memory_space_constraint(filters, pltpu.HBM))


def pack_values_kernel(chips, values_ref, *refs):
    out_refs, arrived = refs[:chips], refs[chips]
    rows = values_ref.shape[0]
    chip, _ = own_place()
    copies = []
    for offset, out_ref in enumerate(out_refs):
        values = values_ref.at[:, block_at(chip ^ offset, out_ref.shape[1])]
        copies.append(pltpu.make_async_copy(values, out_ref.at[pl.ds(0, rows)], arrived.at[offset]))
    for copy in copies:
        copy.start()
    for copy in copies:
        copy.wait()


def pack_values(values_in, chips, spare):
    rows, width = values_in.shape
    return pl.pallas_call(
        functools.partial(pack_values_kernel, chips),
        in_specs=[pl.BlockSpec(memory_space=pltpu.HBM)],
        out_specs=[WHOLE] * chips,
        out_shape=[jax.ShapeDtypeStruct((rows + spare, width // chips), BF16)] * chips,
        scratch_shapes=[pltpu.SemaphoreType.DMA((chips,))],
        cost_estimate=CHEAP,
        compiler_params=pltpu.CompilerParams(vmem_limit_bytes=4 * 2**20),
        name="pack_values",
    )(pltpu.with_memory_space_constraint(values_in, pltpu.HBM))


def pack_moved_kernel(chips, gate_ref, own_ref, other_ref, *refs):
    out_refs, (mine_ref, arrived) = refs[:chips], refs[chips:]
    chip, core = own_place()
    rows = gate_ref.shape[0]
    depth, held = own_ref.shape
    quarter, share = depth // 4, held // chips

    def copies_from(weight_ref):
        copies = [pltpu.make_async_copy(weight_ref.at[:, block_at(chip, share)], mine_ref, arrived.at[0, 0])]
        for offset in range(chips):
            out_ref, target = out_refs[offset], chip ^ offset
            gates = gate_ref.at[:, block_at(target, out_ref.shape[1])]
            copies.append(pltpu.make_async_copy(gates, out_ref.at[pl.ds(0, rows)], arrived.at[offset, 2]))
            for part in range(2 if offset else 0):
                source = weight_ref.at[block_at(2 * core + part, quarter), block_at(target, share)]
                sink = out_ref.at[pl.ds(rows, quarter), pl.ds(part * share, share)]
                copies.append(pltpu.make_async_copy(source, sink, arrived.at[offset, part]))
        for copy in copies:
            copy.start()
        for copy in copies:
            copy.wait()

    @pl.when(core == 0)
    def _():
        copies_from(own_ref)

    @pl.when(core == 1)
    def _():
        copies_from(other_ref)


def pack_moved(gate_values, own, other, chips):
    rows, width = gate_values.shape
    depth, held = own.shape
    share = held // chips
    return pl.pallas_call(
        functools.partial(pack_moved_kernel, chips),
        in_specs=[pl.BlockSpec(memory_space=pltpu.HBM)] * 2 + [pl.BlockSpec(memory_space=pl.ANY)],
        out_specs=[WHOLE] * (chips + 1),
        out_shape=[
            *(jax.ShapeDtypeStruct((rows + (depth // 4 if offset else 0), 2 * share), BF16) for offset in range(chips)),
            jax.ShapeDtypeStruct((depth, share), BF16),
        ],
        scratch_shapes=[pltpu.SemaphoreType.DMA((chips, 3))],
        cost_estimate=CHEAP,
        compiler_params=pltpu.CompilerParams(vmem_limit_bytes=8 * 2**20),
        name="pack_moved",
    )(*(pltpu.with_memory_space_constraint(array, pltpu.HBM) for array in (gate_values, own)), other)


def stack_kernel(chips, *refs):
    in_refs, out_refs = refs[:chips], refs[chips:]
    for offset, in_ref in enumerate(in_refs):
        part, place = divmod(offset, chips // 2)
        out_refs[part][place] = in_ref[pl.ds(0, out_refs[part].shape[1]), :]


def stack(blocks, rows):
    chips = len(blocks)
    half = jax.ShapeDtypeStruct((chips // 2, rows, blocks[0].shape[1]), BF16)
    return pl.pallas_call(
        functools.partial(stack_kernel, chips),
        in_specs=[WHOLE] * chips,
        out_specs=[WHOLE] * 2,
        out_shape=[half, half],
        cost_estimate=CHEAP,
        compiler_params=pltpu.CompilerParams(vmem_limit_bytes=4 * 2**20),
        name="stack",
    )(*blocks)


def forward_kernel(chips, cos_ref, sin_ref, table_ref, *refs):
    own_refs, other_refs, (out_ref, signal_ref, waves_ref) = refs[:2], refs[2:4], refs[4:]
    chip, core = own_place()
    parts = 2 * chips
    rows, lanes = own_refs[0].shape[1:]
    chunk, width = 16, 128
    for offset in range(chips):
        part, place = divmod(offset, chips // 2)
        signal_ref[2 * (chip ^ offset) + core] = own_refs[part][place]
        signal_ref[2 * (chip ^ offset) + 1 - core] = other_refs[part][place]
    sign = (1 - 2 * core).astype(F32)

    def spread(index, carry):
        here = block_at(index, chunk)
        there = pl.ds(pl.multiple_of(rows + index * chunk, chunk), chunk)
        cos_all, sin_all = cos_ref[core, here, :], sin_ref[core, here, :]
        for start in range(0, lanes, width):
            blocks = [signal_ref[block, here, pl.ds(start, width)].astype(F32) for block in range(parts)]
            blocks = [block * sign if place % 2 else block for place, block in enumerate(blocks)]

            def store(residue, real, imag):
                cos, sin = cos_all[:, residue : residue + 1], sin_all[:, residue : residue + 1]
                if imag is None:
                    real, imag = real * cos, -(real * sin)
                else:
                    real, imag = real * cos + imag * sin, imag * cos - real * sin
                columns = pl.ds(residue * lanes + start, width)
                waves_ref[here, columns] = real.astype(BF16)
                waves_ref[there, columns] = imag.astype(BF16)

            for residue in range(parts // 2 + 1):
                even, odd = range(0, parts, 2), range(1, parts, 2)
                cos_even = weighted([(cosine(parts, residue, block), blocks[block]) for block in even])
                cos_odd = weighted([(cosine(parts, residue, block), blocks[block]) for block in odd])
                sin_even = weighted([(sine(parts, residue, block), blocks[block]) for block in even])
                sin_odd = weighted([(sine(parts, residue, block), blocks[block]) for block in odd])
                sin_sum = plus(sin_even, sin_odd)
                store(residue, plus(cos_even, cos_odd), None if sin_sum is None else -sin_sum)
                if 0 < residue and 2 * residue != parts:
                    store(parts - residue, minus(cos_even, cos_odd), minus(sin_even, sin_odd))
        return carry

    lax.fori_loop(0, rows // chunk, spread, 0)
    for residue in range(parts):
        columns = pl.ds(residue * lanes, lanes)
        out_ref[:, columns] = jnp.dot(table_ref[...], waves_ref[:, columns], preferred_element_type=F32)


def forward(own, other, tables):
    chips, (_, rows, lanes) = 2 * own[0].shape[0], own[0].shape
    table, _, cos, sin = tables
    spectrum = (2 * rows, 2 * chips * lanes)
    return pl.pallas_call(
        functools.partial(forward_kernel, chips),
        in_specs=[WHOLE] * 7,
        out_specs=WHOLE,
        out_shape=jax.ShapeDtypeStruct(spectrum, F32),
        scratch_shapes=[pltpu.VMEM((2 * chips, rows, lanes), BF16), pltpu.VMEM(spectrum, BF16)],
        cost_estimate=CHEAP,
        compiler_params=pltpu.CompilerParams(vmem_limit_bytes=32 * 2**20),
        name="forward",
    )(cos, sin, table, *own, *other)


def backward_kernel(chips, cos_ref, sin_ref, table_ref, spectrum_ref, *refs):
    filter_refs, (keep_ref, *send_refs, filter_ref, product_ref, back_ref) = refs[:chips], refs[chips:]
    chip, core = own_place()
    parts = 2 * chips
    rows, lanes = keep_ref.shape[1:]
    chip_bits = chips.bit_length() - 1
    chunk, width = 16, 128
    for offset in range(chips):
        for plane in range(filter_ref.shape[1]):
            filter_ref[chip ^ offset, plane] = filter_refs[offset][pl.ds(plane * rows, rows), :]

    for residue in range(parts):
        source, odd = bit_reversed(residue // 2, chip_bits), residue % 2
        columns = pl.ds(residue * lanes, lanes)
        filter_real = filter_ref[source, odd].astype(F32)
        filter_imag = filter_ref[source, 2 + odd].astype(F32)
        real = spectrum_ref[pl.ds(0, rows), columns]
        imag = spectrum_ref[pl.ds(rows, rows), columns]
        product_ref[pl.ds(0, rows), columns] = (real * filter_real - imag * filter_imag).astype(BF16)
        product_ref[pl.ds(rows, rows), columns] = (real * filter_imag + imag * filter_real).astype(BF16)
        back_ref[:, columns] = jnp.dot(table_ref[...], product_ref[:, columns], preferred_element_type=F32)

    scale = 1.0 / (2 * parts * rows)
    sign = (1 - 2 * core).astype(F32)
    upper = core == 1

    def gather(index, carry):
        here = block_at(index, chunk)
        there = pl.ds(pl.multiple_of(rows + index * chunk, chunk), chunk)
        cos_all, sin_all = cos_ref[core, here, :] * scale, sin_ref[core, here, :] * scale
        for start in range(0, lanes, width):
            reals, imags = [], []
            for residue in range(parts):
                columns = pl.ds(residue * lanes + start, width)
                real, imag = back_ref[here, columns], back_ref[there, columns]
                cos, sin = cos_all[:, residue : residue + 1], sin_all[:, residue : residue + 1]
                reals.append(real * cos - imag * sin)
                imags.append(real * sin + imag * cos)
            totals = [None] * parts
            for block in range(parts // 2 + 1):
                even, odd = range(0, parts, 2), range(1, parts, 2)
                cos_even = weighted([(cosine(parts, residue, block), reals[residue]) for residue in even])
                cos_odd = weighted([(cosine(parts, residue, block), reals[residue]) for residue in odd])
                sin_even = weighted([(sine(parts, residue, block), imags[residue]) for residue in even])
                sin_odd = weighted([(sine(parts, residue, block), imags[residue]) for residue in odd])
                totals[block] = minus(plus(cos_even, cos_odd), plus(sin_even, sin_odd))
                if 0 < block and 2 * block != parts:
                    totals[parts - block] = plus(minus(cos_even, cos_odd), minus(sin_even, sin_odd))
            lane = pl.ds(start, width)
            for pair in range(chips):
                low, high = totals[2 * pair], totals[2 * pair + 1] * sign
                keep_ref[pair, here, lane] = jnp.where(upper, high, low)
                part, place = divmod(pair, chips // 2)
                send_refs[part][place, here, lane] = jnp.where(upper, low, high).astype(BF16)
        return carry

    lax.fori_loop(0, rows // chunk, gather, 0)


def backward(spectrum, first, tables):
    chips = len(first)
    rows, lanes = spectrum.shape[0] // 2, first[0].shape[1]
    _, table, cos, sin = tables
    half = jax.ShapeDtypeStruct((chips // 2, rows, lanes), BF16)
    return pl.pallas_call(
        functools.partial(backward_kernel, chips),
        in_specs=[WHOLE] * (4 + chips),
        out_specs=[WHOLE] * 3,
        out_shape=[jax.ShapeDtypeStruct((chips, rows, lanes), F32), half, half],
        scratch_shapes=[
            pltpu.VMEM((chips, 4, rows, lanes), BF16),
            pltpu.VMEM(spectrum.shape, BF16),
            pltpu.VMEM(spectrum.shape, F32),
        ],
        cost_estimate=CHEAP,
        compiler_params=pltpu.CompilerParams(vmem_limit_bytes=32 * 2**20),
        name="backward",
    )(cos, sin, table, spectrum, *first)


def gate_kernel(chips, skip_ref, keep_ref, low_ref, high_ref, *refs):
    signal_refs, gate_refs = refs[:chips], refs[chips : 2 * chips]
    out_ref, longer_ref, arrived_ref = refs[2 * chips :]
    chip, _ = own_place()
    rows, lanes = keep_ref.shape[1:]
    skip = skip_ref[:, block_at(chip, lanes)]
    arrived_ref[pl.ds(0, chips // 2)] = low_ref[...]
    arrived_ref[pl.ds(chips // 2, chips // 2)] = high_ref[...]
    for offset in range(chips):
        block = chip ^ offset
        convolved = keep_ref[block] + arrived_ref[block].astype(F32)
        signal = signal_refs[offset][pl.ds(0, rows), :].astype(F32)
        gate = gate_refs[offset][pl.ds(0, rows), :].astype(F32)
        gated = (gate * (convolved + skip * signal)).astype(BF16)
        out_ref[block_at(block, rows), :] = gated
        longer_ref[block_at(block, rows), :] = gated
    end = chips * rows
    longer_ref[pl.ds(end, longer_ref.shape[0] - end), :] = longer_ref[pl.ds(0, longer_ref.shape[0] - end), :]


def gate(skip, keep, arrived, first, gates, spare):
    chips, rows, lanes = keep.shape
    return pl.pallas_call(
        functools.partial(gate_kernel, chips),
        in_specs=[WHOLE] * (4 + 2 * chips),
        out_specs=[WHOLE] * 2,
        out_shape=[
            jax.ShapeDtypeStruct((chips * rows, lanes), BF16),
            jax.ShapeDtypeStruct((chips * rows + spare, lanes), BF16),
        ],
        scratch_shapes=[pltpu.VMEM((chips, rows, lanes), BF16)],
        cost_estimate=CHEAP,
        compiler_params=pltpu.CompilerParams(vmem_limit_bytes=6 * 2**20),
        name="gate",
    )(skip, keep, *arrived, *first, *gates)


def piece_of(ref, half, part):
    quarter, share = half // 2, ref.shape[1] // 2
    return ref[pl.ds(ref.shape[0] - quarter, quarter), pl.ds(part * share, share)]


def collect_kernel(in_refs, out_refs):
    rows = out_refs[0].shape[0]
    quarter = len(out_refs) * rows // (2 * len(in_refs))
    for place in range(2 * len(in_refs)):
        index, start = divmod(place * quarter, rows)
        out_refs[index][pl.ds(start, quarter), :] = piece_of(in_refs[place // 2], 2 * quarter, place % 2)


def collect(moved, half):
    count = len(moved)
    shape = (count * half // 2, moved[0].shape[1] // 2)
    return pl.pallas_call(
        lambda *refs: collect_kernel(refs[:count], refs[count:]),
        in_specs=[WHOLE] * count,
        out_specs=[WHOLE] * 2,
        out_shape=[jax.ShapeDtypeStruct(shape, BF16)] * 2,
        cost_estimate=CHEAP,
        compiler_params=pltpu.CompilerParams(vmem_limit_bytes=4 * 2**20),
        name="collect_weights",
    )(*moved)


def arrange_kernel(chips, mine_ref, *refs):
    moved_refs, (*other_refs, out_ref) = refs[: chips - 1], refs[chips - 1 :]
    chip, core = own_place()
    layer = lax.axis_index("chan")
    depth, share = mine_ref.shape
    quarter = depth // 4
    out_ref[:, block_at(chip ^ layer, share)] = mine_ref[...]
    for place in range(2 * (chips - 1)):
        offset, part = place // 2 + 1, place % 2
        columns = block_at(chip ^ layer ^ offset, share)
        index, start = divmod(place * quarter, other_refs[0].shape[0])
        out_ref[block_at(2 * core + part, quarter), columns] = piece_of(moved_refs[offset - 1], 2 * quarter, part)
        out_ref[block_at(2 * (1 - core) + part, quarter), columns] = other_refs[index][pl.ds(start, quarter), :]


def arrange(mine, moved, others):
    chips = len(moved) + 1
    depth, share = mine.shape
    return pl.pallas_call(
        functools.partial(arrange_kernel, chips),
        in_specs=[WHOLE] * (chips + len(others)),
        out_specs=WHOLE,
        out_shape=jax.ShapeDtypeStruct((depth, chips * share), BF16),
        cost_estimate=CHEAP,
        compiler_params=pltpu.CompilerParams(vmem_limit_bytes=8 * 2**20),
        name="arrange_weights",
    )(mine, *moved, *others)


def join_channels(chips, gated_refs, joined_ref):
    chip, _ = own_place()
    lanes = gated_refs[0].shape[1]
    for offset in range(chips):
        joined_ref[:, block_at(chip ^ offset, lanes)] = gated_refs[offset][pl.ds(0, joined_ref.shape[0]), :]


def project_moved_kernel(chips, weight_ref, *refs):
    gated_refs, (keep_ref, pass_ref, send_ref, joined_ref) = refs[:chips], refs[chips:]
    share = keep_ref.shape[1]
    join_channels(chips, gated_refs, joined_ref)
    partial = jnp.dot(joined_ref[...], weight_ref[...], preferred_element_type=F32).astype(BF16)
    keep_ref[...] = partial[:, :share]
    send_ref[0] = partial[:, share : 2 * share]
    pass_ref[...] = partial[:, 2 * share : 3 * share]
    send_ref[1] = partial[:, 3 * share :]


def project_moved(weight, gated):
    chips = len(gated)
    depth, columns = weight.shape
    rows = gated[0].shape[0]
    block = jax.ShapeDtypeStruct((rows, columns // chips), BF16)
    return pl.pallas_call(
        functools.partial(project_moved_kernel, chips),
        in_specs=[WHOLE] * (1 + chips),
        out_specs=[WHOLE] * 3,
        out_shape=[block, block, jax.ShapeDtypeStruct((2, rows, columns // chips), BF16)],
        scratch_shapes=[pltpu.VMEM((rows, depth), BF16)],
        cost_estimate=CHEAP,
        compiler_params=pltpu.CompilerParams(vmem_limit_bytes=8 * 2**20),
        name="project_moved",
    )(weight, *gated)


def project_still_kernel(chips, own_ref, other_ref, *refs):
    gated_refs, out_refs, joined_ref = refs[:chips], refs[chips : 2 * chips], refs[2 * chips]
    chip, core = own_place()
    rows = out_refs[0].shape[0]
    join_channels(chips, gated_refs, joined_ref)

    def project_with(weight_ref):
        for offset in range(chips):
            gated = joined_ref[block_at(chip ^ offset, rows), :]
            out_refs[offset][...] = jnp.dot(gated, weight_ref[...], preferred_element_type=F32).astype(BF16)

    @pl.when(core == 0)
    def _():
        project_with(other_ref)

    @pl.when(core == 1)
    def _():
        project_with(own_ref)


def project_still(own, other, gated):
    chips = len(gated)
    depth, held = own.shape
    rows = gated[0].shape[0] // chips
    return pl.pallas_call(
        functools.partial(project_still_kernel, chips),
        in_specs=[WHOLE] * (2 + chips),
        out_specs=[WHOLE] * chips,
        out_shape=[jax.ShapeDtypeStruct((rows, held), BF16)] * chips,
        scratch_shapes=[pltpu.VMEM((rows * chips, depth), BF16)],
        cost_estimate=CHEAP,
        compiler_params=pltpu.CompilerParams(vmem_limit_bytes=12 * 2**20),
        name="project_still",
    )(own, other, *gated)


def sort_kernel(chips, *refs):
    in_refs, (keep_ref, pass_ref, send_ref, sorted_ref) = refs[:chips], refs[chips:]
    chip, _ = own_place()
    layer = lax.axis_index("chan")
    for offset in range(chips):
        sorted_ref[chip ^ layer ^ offset] = in_refs[offset][...]
    keep_ref[...] = sorted_ref[0]
    send_ref[0] = sorted_ref[1]
    pass_ref[...] = sorted_ref[2]
    send_ref[1] = sorted_ref[3]


def sort_blocks(blocks):
    chips = len(blocks)
    block = jax.ShapeDtypeStruct(blocks[0].shape, BF16)
    return pl.pallas_call(
        functools.partial(sort_kernel, chips),
        in_specs=[WHOLE] * chips,
        out_specs=[WHOLE] * 3,
        out_shape=[block, block, jax.ShapeDtypeStruct((2, *block.shape), BF16)],
        scratch_shapes=[pltpu.VMEM((chips, *block.shape), BF16)],
        cost_estimate=CHEAP,
        compiler_params=pltpu.CompilerParams(vmem_limit_bytes=4 * 2**20),
        name="sort_blocks",
    )(*blocks)


def finish_kernel(chips, keep_ref, first_ref, second_ref, *out_refs):
    chip, _ = own_place()
    rows = out_refs[0].shape[0]
    for offset in range(chips):
        here = block_at(chip ^ offset, rows)
        total = keep_ref[here, :].astype(F32) + first_ref[0, here, :].astype(F32) + second_ref[here, :].astype(F32)
        out_refs[offset][...] = total.astype(BF16)


def finish(keep, first, second, chips):
    rows, columns = keep.shape
    return pl.pallas_call(
        functools.partial(finish_kernel, chips),
        in_specs=[WHOLE] * 3,
        out_specs=[WHOLE] * chips,
        out_shape=[jax.ShapeDtypeStruct((rows // chips, columns), BF16)] * chips,
        cost_estimate=CHEAP,
        compiler_params=pltpu.CompilerParams(vmem_limit_bytes=4 * 2**20),
        name="finish",
    )(keep, first, second)


def join_kernel(chips, keep_ref, first_ref, second_ref, *refs):
    in_refs, out_ref = refs[:chips], refs[chips]
    chip, _ = own_place()
    share = in_refs[0].shape[1]
    for offset in range(chips):
        out_ref[:, block_at(chip ^ offset, share)] = in_refs[offset][...]
    total = keep_ref[...].astype(F32) + first_ref[0].astype(F32) + second_ref[...].astype(F32)
    out_ref[:, pl.ds(chips * share, total.shape[1])] = total.astype(BF16)


def join(keep, first, second, blocks):
    chips = len(blocks)
    rows, share = blocks[0].shape
    return pl.pallas_call(
        functools.partial(join_kernel, chips),
        in_specs=[WHOLE] * (3 + chips),
        out_specs=WHOLE,
        out_shape=jax.ShapeDtypeStruct((rows, chips * share + keep.shape[1]), BF16),
        cost_estimate=CHEAP,
        compiler_params=pltpu.CompilerParams(vmem_limit_bytes=4 * 2**20),
        name="join",
    )(keep, first, second, *blocks)


def swapped(value, axis, offset):
    if not offset:
        return value
    return lax.ppermute(value, axis, [(source, source ^ offset) for source in range(lax.axis_size(axis))])


def to_chips(blocks):
    return [swapped(block, "seq", 2 * offset) for offset, block in enumerate(blocks)]


def after(value, *others):
    return lax.optimization_barrier((value, *others))[0]


def over_layers(passed, send):
    first = swapped(send, "chan", 1)
    passed = (passed.astype(F32) + first[1].astype(F32)).astype(BF16)
    return first, swapped(passed, "chan", 2)


def shards_direct(values_in, gate_values, filter_spectrum, skip_gain, out_weight):
    parts = lax.axis_size("seq")
    chips = parts // 2
    rows, width = values_in.shape
    tables = small_tables(parts, rows)

    values = pack_values(values_in, chips, 0)
    flat_filters = filter_spectrum.reshape(4, rows, width)
    near = pack_filters(after(flat_filters, values[0]), chips, (1, 2), 0)
    other_weight = swapped(out_weight, "seq", 1)
    *moved, mine = pack_moved(after(gate_values, near[0]), out_weight, other_weight, chips)
    own, far = pack_filters(after(flat_filters, moved[0]), chips, (0, 3), 0)
    values, filters = to_chips(values), to_chips([own, *near, far])
    own = stack([after(block, far) for block in values], rows)
    spectrum = forward(own, [swapped(part, "seq", 1) for part in own], tables)
    moved = to_chips([after(block, spectrum) for block in moved])
    keep, *send = backward(spectrum, filters, tables)
    gated, longer = gate(skip_gain[None, :], keep, [swapped(part, "seq", 1) for part in send], values, moved, 16)
    gathered = to_chips([gated, longer, longer, gated])

    others = [swapped(part, "seq", 1) for part in collect([after(block, gated) for block in moved[1:]], out_weight.shape[0] // 2)]
    keep, passed, send = project_moved(arrange(mine, moved[1:], others), gathered)
    blocks = to_chips(finish(keep, *over_layers(passed, send), chips))
    keep, passed, send = sort_blocks(to_chips(project_still(out_weight, other_weight, gathered)))
    return join(keep, *over_layers(passed, send), blocks)


def shards(values_in, gate_values, filter_spectrum, skip_gain, out_weight):
    parts, layers = lax.axis_size("seq"), lax.axis_size("chan")
    rows, width = values_in.shape
    share = out_weight.shape[1] // layers
    aligned = width // parts % 128 == 0 and share % 128 == 0 and rows % 32 == 0
    run = shards_direct if aligned and layers == 4 and parts == 8 else shards_general
    return run(values_in, gate_values, filter_spectrum, skip_gain, out_weight)


def solution(mesh):
    in_specs = (
        P("seq", "chan"),
        P("seq", "chan"),
        P(None, "seq", None, "chan"),
        P("chan"),
        P("chan", "seq"),
    )
    out_specs = P("seq", "chan")
    return jax.shard_map(shards, mesh=mesh, in_specs=in_specs, out_specs=out_specs, check_vma=False)
```

```python
import functools

import jax
import jax.numpy as jnp
import numpy as np
from jax import lax
from jax.experimental import pallas as pl
from jax.experimental.pallas import tpu as pltpu
from jax.sharding import PartitionSpec as P

BF16 = jnp.bfloat16
F32 = jnp.float32


def bit_reversed(number, width_bits):
    flipped = 0
    for bit_place in range(width_bits):
        flipped |= (number >> bit_place & 1) << (width_bits - 1 - bit_place)
    return flipped


def filter_row(residue, width_bits):
    return 2 * bit_reversed(residue // 2, width_bits) + residue % 2


def dft_tables(parts, rows):
    total = 2 * parts * rows
    residue = np.arange(2 * parts)[:, None, None]
    column = np.arange(rows)[None, :, None]
    position = np.arange(rows)[None, None, :]
    phase = 2.0 * np.pi * (position * (residue + 2 * parts * column) % total) / total
    cos, sin = np.cos(phase), np.sin(phase)
    forward = np.concatenate(
        [np.concatenate([cos, sin], axis=2), np.concatenate([-sin, cos], axis=2)], axis=1
    )
    inverse = np.transpose(forward, (0, 2, 1)) / total
    return forward.astype(BF16), inverse.astype(BF16)


def convolve_kernel(parts, rows, moved_ref, skip_ref, forward_ref, inverse_ref, out_ref, waves_ref, back_ref):
    width_bits = parts.bit_length() - 1
    chunk = 16

    def cosine(residue, block):
        return float(np.cos(np.pi * residue * block / parts))

    def sine(residue, block):
        return float(np.sin(np.pi * residue * block / parts))

    def spread(index, carry):
        here = pl.ds(index * chunk, chunk)
        there = pl.ds(rows + index * chunk, chunk)
        blocks = [moved_ref[block, here, :].astype(F32) for block in range(parts)]
        for residue in range(parts + 1):
            real = blocks[0]
            imag = jnp.zeros_like(real)
            for block in range(1, parts):
                real = real + cosine(residue, block) * blocks[block]
                imag = imag - sine(residue, block) * blocks[block]
            waves_ref[residue, here, :] = real.astype(BF16)
            waves_ref[residue, there, :] = imag.astype(BF16)
            if 0 < residue < parts:
                waves_ref[2 * parts - residue, here, :] = real.astype(BF16)
                waves_ref[2 * parts - residue, there, :] = (-imag).astype(BF16)
        return carry

    lax.fori_loop(0, rows // chunk, spread, 0)

    def through(residue):
        wave = jnp.dot(forward_ref[residue], waves_ref[residue], preferred_element_type=F32)
        source, odd = divmod(filter_row(residue, width_bits), 2)
        filter_real = moved_ref[source, pl.ds((2 + odd) * rows, rows), :].astype(F32)
        filter_imag = moved_ref[source, pl.ds((4 + odd) * rows, rows), :].astype(F32)
        real, imag = wave[:rows], wave[rows:]
        product = jnp.concatenate(
            [real * filter_real - imag * filter_imag, real * filter_imag + imag * filter_real], axis=0
        )
        return jnp.dot(inverse_ref[residue], product.astype(BF16), preferred_element_type=F32)

    for residue in range(parts + 1):
        back = through(residue)
        if 0 < residue < parts:
            other = through(2 * parts - residue)
            back_ref[residue, pl.ds(0, rows), :] = back[:rows] + other[:rows]
            back_ref[residue, pl.ds(rows, rows), :] = back[rows:] - other[rows:]
        else:
            back_ref[residue] = back

    skip = skip_ref[...]

    def gather(index, carry):
        here = pl.ds(index * chunk, chunk)
        there = pl.ds(rows + index * chunk, chunk)
        reals = [back_ref[residue, here, :] for residue in range(parts + 1)]
        imags = [back_ref[residue, there, :] for residue in range(parts + 1)]
        for block in range(parts):
            total = reals[0]
            for residue in range(1, parts + 1):
                total = total + cosine(residue, block) * reals[residue]
                if residue < parts and block:
                    total = total - sine(residue, block) * imags[residue]
            signal = moved_ref[block, here, :].astype(F32)
            gate = moved_ref[block, pl.ds(rows + index * chunk, chunk), :].astype(F32)
            out_ref[block, here, :] = (gate * (total + skip * signal)).astype(BF16)
        return carry

    lax.fori_loop(0, rows // chunk, gather, 0)


def convolve(moved, skip):
    parts, stacked, width = moved.shape
    rows = stacked // 6
    forward, inverse = dft_tables(parts, rows)
    whole = pl.BlockSpec(memory_space=pltpu.VMEM)
    return pl.pallas_call(
        functools.partial(convolve_kernel, parts, rows),
        out_shape=jax.ShapeDtypeStruct((parts, rows, width), BF16),
        in_specs=[whole] * 4,
        out_specs=whole,
        scratch_shapes=[
            pltpu.VMEM((2 * parts, 2 * rows, width), BF16),
            pltpu.VMEM((parts + 1, 2 * rows, width), F32),
        ],
        compiler_params=pltpu.CompilerParams(vmem_limit_bytes=40 * 2**20),
    )(moved, skip[None, :], forward, inverse)


def shards_general(values_in, gate_values, filter_spectrum, skip_gain, out_weight):
    parts = lax.axis_size("seq")
    layers = lax.axis_size("chan")
    rows, width = values_in.shape
    lanes = width // parts
    device = lax.axis_index("seq")

    def by_channel(array):
        return jnp.transpose(array.reshape(array.shape[0], parts, lanes), (1, 0, 2))

    filters = filter_spectrum.astype(BF16).reshape(4 * rows, width)
    packed = jnp.concatenate([by_channel(values_in), by_channel(gate_values), by_channel(filters)], axis=1)
    moved = lax.all_to_all(packed, "seq", 0, 0)
    skip = lax.dynamic_slice_in_dim(skip_gain, device * lanes, lanes)
    gated = convolve(moved, skip)
    gathered = lax.all_gather(gated.reshape(parts * rows, lanes), "seq", axis=1, tiled=True)

    own_cols = out_weight.shape[1]
    share = own_cols * parts // layers // parts
    per_block = parts // layers
    pieces = own_cols // share
    group = device % per_block
    member = device // per_block
    weight = jnp.zeros_like(out_weight)
    for step in range(pieces):
        piece = (member + step) % pieces
        sent = lax.dynamic_slice_in_dim(out_weight, piece * share, share, 1)
        pairs = [
            (source, source % per_block * pieces + (source // per_block + step) % pieces) for source in range(parts)
        ]
        arrived = lax.ppermute(sent, "seq", pairs)
        block = (device % pieces - step) % pieces
        weight = lax.dynamic_update_slice_in_dim(weight, arrived, block * share, 1)
    partials = jnp.dot(gathered, weight, preferred_element_type=F32).astype(BF16)
    mixed = lax.psum_scatter(partials, "chan", scatter_dimension=1, tiled=True)
    return lax.all_to_all(mixed, "seq", 0, 1, tiled=True)


WHOLE = pl.BlockSpec(memory_space=pltpu.VMEM)
CHEAP = pl.CostEstimate(flops=0, transcendentals=0, bytes_accessed=0)


def small_tables(parts, rows):
    total = 2 * parts * rows
    index = np.arange(rows)
    phase = 2.0 * np.pi * (index[:, None] * index[None, :] % rows) / rows
    cos, sin = np.cos(phase), np.sin(phase)
    forward = np.block([[cos, sin], [-sin, cos]])
    residue = np.arange(2 * parts).reshape(2, 1, parts)
    turn = 2.0 * np.pi * index[None, :, None] * residue / total
    return forward.astype(BF16), forward.T.astype(BF16), np.cos(turn).astype(F32), np.sin(turn).astype(F32)


def cosine(parts, residue, block):
    return float(np.cos(np.pi * residue * block / parts))


def sine(parts, residue, block):
    return float(np.sin(np.pi * residue * block / parts))


def weighted(terms):
    total = None
    for factor, term in terms:
        if abs(factor) < 1e-12:
            continue
        part = term if factor == 1.0 else factor * term
        total = part if total is None else total + part
    return total


def plus(left, right):
    return left if right is None else right if left is None else left + right


def minus(left, right):
    return left if right is None else -right if left is None else left - right


def own_place():
    device = lax.axis_index("seq")
    return device // 2, device % 2


def block_at(index, size):
    return pl.ds(pl.multiple_of(index * size, size), size)


def pack_filters_kernel(offsets, filter_ref, *refs):
    out_refs, (plane_ref, arrived) = refs[: len(offsets)], refs[len(offsets) :]
    chip, _ = own_place()
    planes, rows, _ = filter_ref.shape
    lanes = out_refs[0].shape[1]
    copies = []
    for place, offset in enumerate(offsets):
        here = block_at(chip ^ offset, lanes)
        for plane in range(planes):
            copies.append(
                pltpu.make_async_copy(filter_ref.at[plane, :, here], plane_ref.at[place, plane], arrived.at[place, plane])
            )
    for copy in copies:
        copy.start()
    for index, copy in enumerate(copies):
        copy.wait()
        place, plane = divmod(index, planes)
        out_refs[place][pl.ds(plane * rows, rows), :] = plane_ref[place, plane].astype(BF16)
    used = planes * rows
    for out_ref in out_refs:
        if out_ref.shape[0] > used:
            out_ref[pl.ds(used, out_ref.shape[0] - used), :] = out_ref[pl.ds(0, out_ref.shape[0] - used), :]


def pack_filters(filters, chips, offsets, spare):
    planes, rows, width = filters.shape
    lanes = width // chips
    return pl.pallas_call(
        functools.partial(pack_filters_kernel, offsets),
        in_specs=[pl.BlockSpec(memory_space=pltpu.HBM)],
        out_specs=[WHOLE] * len(offsets),
        out_shape=[jax.ShapeDtypeStruct((planes * rows + spare, lanes), BF16)] * len(offsets),
        scratch_shapes=[
            pltpu.VMEM((len(offsets), planes, rows, lanes), F32),
            pltpu.SemaphoreType.DMA((len(offsets), planes)),
        ],
        cost_estimate=CHEAP,
        compiler_params=pltpu.CompilerParams(vmem_limit_bytes=8 * 2**20),
        name="pack_filters",
    )(pltpu.with_memory_space_constraint(filters, pltpu.HBM))


def pack_values_kernel(chips, values_ref, *refs):
    out_refs, arrived = refs[:chips], refs[chips]
    rows = values_ref.shape[0]
    chip, _ = own_place()
    copies = []
    for offset, out_ref in enumerate(out_refs):
        values = values_ref.at[:, block_at(chip ^ offset, out_ref.shape[1])]
        copies.append(pltpu.make_async_copy(values, out_ref.at[pl.ds(0, rows)], arrived.at[offset]))
    for copy in copies:
        copy.start()
    for copy in copies:
        copy.wait()


def pack_values(values_in, chips, spare):
    rows, width = values_in.shape
    return pl.pallas_call(
        functools.partial(pack_values_kernel, chips),
        in_specs=[pl.BlockSpec(memory_space=pltpu.HBM)],
        out_specs=[WHOLE] * chips,
        out_shape=[jax.ShapeDtypeStruct((rows + spare, width // chips), BF16)] * chips,
        scratch_shapes=[pltpu.SemaphoreType.DMA((chips,))],
        cost_estimate=CHEAP,
        compiler_params=pltpu.CompilerParams(vmem_limit_bytes=4 * 2**20),
        name="pack_values",
    )(pltpu.with_memory_space_constraint(values_in, pltpu.HBM))


def pack_moved_kernel(chips, gate_ref, own_ref, other_ref, *refs):
    out_refs, (mine_ref, arrived) = refs[:chips], refs[chips:]
    chip, core = own_place()
    rows = gate_ref.shape[0]
    depth, held = own_ref.shape
    quarter, share = depth // 4, held // chips

    def copies_from(weight_ref):
        copies = [pltpu.make_async_copy(weight_ref.at[:, block_at(chip, share)], mine_ref, arrived.at[0, 0])]
        for offset in range(chips):
            out_ref, target = out_refs[offset], chip ^ offset
            gates = gate_ref.at[:, block_at(target, out_ref.shape[1])]
            copies.append(pltpu.make_async_copy(gates, out_ref.at[pl.ds(0, rows)], arrived.at[offset, 2]))
            for part in range(2 if offset else 0):
                source = weight_ref.at[block_at(2 * core + part, quarter), block_at(target, share)]
                sink = out_ref.at[pl.ds(rows, quarter), pl.ds(part * share, share)]
                copies.append(pltpu.make_async_copy(source, sink, arrived.at[offset, part]))
        for copy in copies:
            copy.start()
        for copy in copies:
            copy.wait()

    @pl.when(core == 0)
    def _():
        copies_from(own_ref)

    @pl.when(core == 1)
    def _():
        copies_from(other_ref)


def pack_moved(gate_values, own, other, chips):
    rows, width = gate_values.shape
    depth, held = own.shape
    share = held // chips
    return pl.pallas_call(
        functools.partial(pack_moved_kernel, chips),
        in_specs=[pl.BlockSpec(memory_space=pltpu.HBM)] * 2 + [pl.BlockSpec(memory_space=pl.ANY)],
        out_specs=[WHOLE] * (chips + 1),
        out_shape=[
            *(jax.ShapeDtypeStruct((rows + (depth // 4 if offset else 0), 2 * share), BF16) for offset in range(chips)),
            jax.ShapeDtypeStruct((depth, share), BF16),
        ],
        scratch_shapes=[pltpu.SemaphoreType.DMA((chips, 3))],
        cost_estimate=CHEAP,
        compiler_params=pltpu.CompilerParams(vmem_limit_bytes=8 * 2**20),
        name="pack_moved",
    )(*(pltpu.with_memory_space_constraint(array, pltpu.HBM) for array in (gate_values, own)), other)


def stack_kernel(chips, *refs):
    in_refs, out_refs = refs[:chips], refs[chips:]
    for offset, in_ref in enumerate(in_refs):
        part, place = divmod(offset, chips // 2)
        out_refs[part][place] = in_ref[pl.ds(0, out_refs[part].shape[1]), :]


def stack(blocks, rows):
    chips = len(blocks)
    half = jax.ShapeDtypeStruct((chips // 2, rows, blocks[0].shape[1]), BF16)
    return pl.pallas_call(
        functools.partial(stack_kernel, chips),
        in_specs=[WHOLE] * chips,
        out_specs=[WHOLE] * 2,
        out_shape=[half, half],
        cost_estimate=CHEAP,
        compiler_params=pltpu.CompilerParams(vmem_limit_bytes=4 * 2**20),
        name="stack",
    )(*blocks)


def forward_kernel(chips, cos_ref, sin_ref, table_ref, *refs):
    own_refs, other_refs, (out_ref, signal_ref, waves_ref) = refs[:2], refs[2:4], refs[4:]
    chip, core = own_place()
    parts = 2 * chips
    rows, lanes = own_refs[0].shape[1:]
    chunk, width = 16, 128
    for offset in range(chips):
        part, place = divmod(offset, chips // 2)
        signal_ref[2 * (chip ^ offset) + core] = own_refs[part][place]
        signal_ref[2 * (chip ^ offset) + 1 - core] = other_refs[part][place]
    sign = (1 - 2 * core).astype(F32)

    def spread(index, carry):
        here = block_at(index, chunk)
        there = pl.ds(pl.multiple_of(rows + index * chunk, chunk), chunk)
        cos_all, sin_all = cos_ref[core, here, :], sin_ref[core, here, :]
        for start in range(0, lanes, width):
            blocks = [signal_ref[block, here, pl.ds(start, width)].astype(F32) for block in range(parts)]
            blocks = [block * sign if place % 2 else block for place, block in enumerate(blocks)]

            def store(residue, real, imag):
                cos, sin = cos_all[:, residue : residue + 1], sin_all[:, residue : residue + 1]
                if imag is None:
                    real, imag = real * cos, -(real * sin)
                else:
                    real, imag = real * cos + imag * sin, imag * cos - real * sin
                columns = pl.ds(residue * lanes + start, width)
                waves_ref[here, columns] = real.astype(BF16)
                waves_ref[there, columns] = imag.astype(BF16)

            for residue in range(parts // 2 + 1):
                even, odd = range(0, parts, 2), range(1, parts, 2)
                cos_even = weighted([(cosine(parts, residue, block), blocks[block]) for block in even])
                cos_odd = weighted([(cosine(parts, residue, block), blocks[block]) for block in odd])
                sin_even = weighted([(sine(parts, residue, block), blocks[block]) for block in even])
                sin_odd = weighted([(sine(parts, residue, block), blocks[block]) for block in odd])
                sin_sum = plus(sin_even, sin_odd)
                store(residue, plus(cos_even, cos_odd), None if sin_sum is None else -sin_sum)
                if 0 < residue and 2 * residue != parts:
                    store(parts - residue, minus(cos_even, cos_odd), minus(sin_even, sin_odd))
        return carry

    lax.fori_loop(0, rows // chunk, spread, 0)
    for residue in range(parts):
        columns = pl.ds(residue * lanes, lanes)
        out_ref[:, columns] = jnp.dot(table_ref[...], waves_ref[:, columns], preferred_element_type=F32)


def forward(own, other, tables):
    chips, (_, rows, lanes) = 2 * own[0].shape[0], own[0].shape
    table, _, cos, sin = tables
    spectrum = (2 * rows, 2 * chips * lanes)
    return pl.pallas_call(
        functools.partial(forward_kernel, chips),
        in_specs=[WHOLE] * 7,
        out_specs=WHOLE,
        out_shape=jax.ShapeDtypeStruct(spectrum, F32),
        scratch_shapes=[pltpu.VMEM((2 * chips, rows, lanes), BF16), pltpu.VMEM(spectrum, BF16)],
        cost_estimate=CHEAP,
        compiler_params=pltpu.CompilerParams(vmem_limit_bytes=32 * 2**20),
        name="forward",
    )(cos, sin, table, *own, *other)


def backward_kernel(chips, cos_ref, sin_ref, table_ref, spectrum_ref, *refs):
    filter_refs, (keep_ref, *send_refs, filter_ref, product_ref, back_ref) = refs[:chips], refs[chips:]
    chip, core = own_place()
    parts = 2 * chips
    rows, lanes = keep_ref.shape[1:]
    chip_bits = chips.bit_length() - 1
    chunk, width = 16, 128
    for offset in range(chips):
        for plane in range(filter_ref.shape[1]):
            filter_ref[chip ^ offset, plane] = filter_refs[offset][pl.ds(plane * rows, rows), :]

    for residue in range(parts):
        source, odd = bit_reversed(residue // 2, chip_bits), residue % 2
        columns = pl.ds(residue * lanes, lanes)
        filter_real = filter_ref[source, odd].astype(F32)
        filter_imag = filter_ref[source, 2 + odd].astype(F32)
        real = spectrum_ref[pl.ds(0, rows), columns]
        imag = spectrum_ref[pl.ds(rows, rows), columns]
        product_ref[pl.ds(0, rows), columns] = (real * filter_real - imag * filter_imag).astype(BF16)
        product_ref[pl.ds(rows, rows), columns] = (real * filter_imag + imag * filter_real).astype(BF16)
        back_ref[:, columns] = jnp.dot(table_ref[...], product_ref[:, columns], preferred_element_type=F32)

    scale = 1.0 / (2 * parts * rows)
    sign = (1 - 2 * core).astype(F32)
    upper = core == 1

    def gather(index, carry):
        here = block_at(index, chunk)
        there = pl.ds(pl.multiple_of(rows + index * chunk, chunk), chunk)
        cos_all, sin_all = cos_ref[core, here, :] * scale, sin_ref[core, here, :] * scale
        for start in range(0, lanes, width):
            reals, imags = [], []
            for residue in range(parts):
                columns = pl.ds(residue * lanes + start, width)
                real, imag = back_ref[here, columns], back_ref[there, columns]
                cos, sin = cos_all[:, residue : residue + 1], sin_all[:, residue : residue + 1]
                reals.append(real * cos - imag * sin)
                imags.append(real * sin + imag * cos)
            totals = [None] * parts
            for block in range(parts // 2 + 1):
                even, odd = range(0, parts, 2), range(1, parts, 2)
                cos_even = weighted([(cosine(parts, residue, block), reals[residue]) for residue in even])
                cos_odd = weighted([(cosine(parts, residue, block), reals[residue]) for residue in odd])
                sin_even = weighted([(sine(parts, residue, block), imags[residue]) for residue in even])
                sin_odd = weighted([(sine(parts, residue, block), imags[residue]) for residue in odd])
                totals[block] = minus(plus(cos_even, cos_odd), plus(sin_even, sin_odd))
                if 0 < block and 2 * block != parts:
                    totals[parts - block] = plus(minus(cos_even, cos_odd), minus(sin_even, sin_odd))
            lane = pl.ds(start, width)
            for pair in range(chips):
                low, high = totals[2 * pair], totals[2 * pair + 1] * sign
                keep_ref[pair, here, lane] = jnp.where(upper, high, low)
                part, place = divmod(pair, chips // 2)
                send_refs[part][place, here, lane] = jnp.where(upper, low, high).astype(BF16)
        return carry

    lax.fori_loop(0, rows // chunk, gather, 0)


def backward(spectrum, first, tables):
    chips = len(first)
    rows, lanes = spectrum.shape[0] // 2, first[0].shape[1]
    _, table, cos, sin = tables
    half = jax.ShapeDtypeStruct((chips // 2, rows, lanes), BF16)
    return pl.pallas_call(
        functools.partial(backward_kernel, chips),
        in_specs=[WHOLE] * (4 + chips),
        out_specs=[WHOLE] * 3,
        out_shape=[jax.ShapeDtypeStruct((chips, rows, lanes), F32), half, half],
        scratch_shapes=[
            pltpu.VMEM((chips, 4, rows, lanes), BF16),
            pltpu.VMEM(spectrum.shape, BF16),
            pltpu.VMEM(spectrum.shape, F32),
        ],
        cost_estimate=CHEAP,
        compiler_params=pltpu.CompilerParams(vmem_limit_bytes=32 * 2**20),
        name="backward",
    )(cos, sin, table, spectrum, *first)


def gate_kernel(chips, skip_ref, keep_ref, low_ref, high_ref, *refs):
    signal_refs, gate_refs = refs[:chips], refs[chips : 2 * chips]
    out_ref, longer_ref, arrived_ref = refs[2 * chips :]
    chip, _ = own_place()
    rows, lanes = keep_ref.shape[1:]
    skip = skip_ref[:, block_at(chip, lanes)]
    arrived_ref[pl.ds(0, chips // 2)] = low_ref[...]
    arrived_ref[pl.ds(chips // 2, chips // 2)] = high_ref[...]
    for offset in range(chips):
        block = chip ^ offset
        convolved = keep_ref[block] + arrived_ref[block].astype(F32)
        signal = signal_refs[offset][pl.ds(0, rows), :].astype(F32)
        gate = gate_refs[offset][pl.ds(0, rows), :].astype(F32)
        gated = (gate * (convolved + skip * signal)).astype(BF16)
        out_ref[block_at(block, rows), :] = gated
        longer_ref[block_at(block, rows), :] = gated
    end = chips * rows
    longer_ref[pl.ds(end, longer_ref.shape[0] - end), :] = longer_ref[pl.ds(0, longer_ref.shape[0] - end), :]


def gate(skip, keep, arrived, first, gates, spare):
    chips, rows, lanes = keep.shape
    return pl.pallas_call(
        functools.partial(gate_kernel, chips),
        in_specs=[WHOLE] * (4 + 2 * chips),
        out_specs=[WHOLE] * 2,
        out_shape=[
            jax.ShapeDtypeStruct((chips * rows, lanes), BF16),
            jax.ShapeDtypeStruct((chips * rows + spare, lanes), BF16),
        ],
        scratch_shapes=[pltpu.VMEM((chips, rows, lanes), BF16)],
        cost_estimate=CHEAP,
        compiler_params=pltpu.CompilerParams(vmem_limit_bytes=6 * 2**20),
        name="gate",
    )(skip, keep, *arrived, *first, *gates)


def piece_of(ref, half, part):
    quarter, share = half // 2, ref.shape[1] // 2
    return ref[pl.ds(ref.shape[0] - quarter, quarter), pl.ds(part * share, share)]


def collect_kernel(in_refs, out_refs):
    rows = out_refs[0].shape[0]
    quarter = len(out_refs) * rows // (2 * len(in_refs))
    for place in range(2 * len(in_refs)):
        index, start = divmod(place * quarter, rows)
        out_refs[index][pl.ds(start, quarter), :] = piece_of(in_refs[place // 2], 2 * quarter, place % 2)


def collect(moved, half):
    count = len(moved)
    shape = (count * half // 2, moved[0].shape[1] // 2)
    return pl.pallas_call(
        lambda *refs: collect_kernel(refs[:count], refs[count:]),
        in_specs=[WHOLE] * count,
        out_specs=[WHOLE] * 2,
        out_shape=[jax.ShapeDtypeStruct(shape, BF16)] * 2,
        cost_estimate=CHEAP,
        compiler_params=pltpu.CompilerParams(vmem_limit_bytes=4 * 2**20),
        name="collect_weights",
    )(*moved)


def arrange_kernel(chips, mine_ref, *refs):
    moved_refs, (*other_refs, out_ref) = refs[: chips - 1], refs[chips - 1 :]
    chip, core = own_place()
    layer = lax.axis_index("chan")
    depth, share = mine_ref.shape
    quarter = depth // 4
    out_ref[:, block_at(chip ^ layer, share)] = mine_ref[...]
    for place in range(2 * (chips - 1)):
        offset, part = place // 2 + 1, place % 2
        columns = block_at(chip ^ layer ^ offset, share)
        index, start = divmod(place * quarter, other_refs[0].shape[0])
        out_ref[block_at(2 * core + part, quarter), columns] = piece_of(moved_refs[offset - 1], 2 * quarter, part)
        out_ref[block_at(2 * (1 - core) + part, quarter), columns] = other_refs[index][pl.ds(start, quarter), :]


def arrange(mine, moved, others):
    chips = len(moved) + 1
    depth, share = mine.shape
    return pl.pallas_call(
        functools.partial(arrange_kernel, chips),
        in_specs=[WHOLE] * (chips + len(others)),
        out_specs=WHOLE,
        out_shape=jax.ShapeDtypeStruct((depth, chips * share), BF16),
        cost_estimate=CHEAP,
        compiler_params=pltpu.CompilerParams(vmem_limit_bytes=8 * 2**20),
        name="arrange_weights",
    )(mine, *moved, *others)


def join_channels(chips, gated_refs, joined_ref):
    chip, _ = own_place()
    lanes = gated_refs[0].shape[1]
    for offset in range(chips):
        joined_ref[:, block_at(chip ^ offset, lanes)] = gated_refs[offset][pl.ds(0, joined_ref.shape[0]), :]


def project_moved_kernel(chips, weight_ref, *refs):
    gated_refs, (keep_ref, pass_ref, send_ref, joined_ref) = refs[:chips], refs[chips:]
    share = keep_ref.shape[1]
    join_channels(chips, gated_refs, joined_ref)
    partial = jnp.dot(joined_ref[...], weight_ref[...], preferred_element_type=F32).astype(BF16)
    keep_ref[...] = partial[:, :share]
    send_ref[0] = partial[:, share : 2 * share]
    pass_ref[...] = partial[:, 2 * share : 3 * share]
    send_ref[1] = partial[:, 3 * share :]


def project_moved(weight, gated):
    chips = len(gated)
    depth, columns = weight.shape
    rows = gated[0].shape[0]
    block = jax.ShapeDtypeStruct((rows, columns // chips), BF16)
    return pl.pallas_call(
        functools.partial(project_moved_kernel, chips),
        in_specs=[WHOLE] * (1 + chips),
        out_specs=[WHOLE] * 3,
        out_shape=[block, block, jax.ShapeDtypeStruct((2, rows, columns // chips), BF16)],
        scratch_shapes=[pltpu.VMEM((rows, depth), BF16)],
        cost_estimate=CHEAP,
        compiler_params=pltpu.CompilerParams(vmem_limit_bytes=8 * 2**20),
        name="project_moved",
    )(weight, *gated)


def project_still_kernel(chips, own_ref, other_ref, *refs):
    gated_refs, out_refs, joined_ref = refs[:chips], refs[chips : 2 * chips], refs[2 * chips]
    chip, core = own_place()
    rows = out_refs[0].shape[0]
    join_channels(chips, gated_refs, joined_ref)

    def project_with(weight_ref):
        for offset in range(chips):
            gated = joined_ref[block_at(chip ^ offset, rows), :]
            out_refs[offset][...] = jnp.dot(gated, weight_ref[...], preferred_element_type=F32).astype(BF16)

    @pl.when(core == 0)
    def _():
        project_with(other_ref)

    @pl.when(core == 1)
    def _():
        project_with(own_ref)


def project_still(own, other, gated):
    chips = len(gated)
    depth, held = own.shape
    rows = gated[0].shape[0] // chips
    return pl.pallas_call(
        functools.partial(project_still_kernel, chips),
        in_specs=[WHOLE] * (2 + chips),
        out_specs=[WHOLE] * chips,
        out_shape=[jax.ShapeDtypeStruct((rows, held), BF16)] * chips,
        scratch_shapes=[pltpu.VMEM((rows * chips, depth), BF16)],
        cost_estimate=CHEAP,
        compiler_params=pltpu.CompilerParams(vmem_limit_bytes=12 * 2**20),
        name="project_still",
    )(own, other, *gated)


def sort_kernel(chips, *refs):
    in_refs, (keep_ref, pass_ref, send_ref, sorted_ref) = refs[:chips], refs[chips:]
    chip, _ = own_place()
    layer = lax.axis_index("chan")
    for offset in range(chips):
        sorted_ref[chip ^ layer ^ offset] = in_refs[offset][...]
    keep_ref[...] = sorted_ref[0]
    send_ref[0] = sorted_ref[1]
    pass_ref[...] = sorted_ref[2]
    send_ref[1] = sorted_ref[3]


def sort_blocks(blocks):
    chips = len(blocks)
    block = jax.ShapeDtypeStruct(blocks[0].shape, BF16)
    return pl.pallas_call(
        functools.partial(sort_kernel, chips),
        in_specs=[WHOLE] * chips,
        out_specs=[WHOLE] * 3,
        out_shape=[block, block, jax.ShapeDtypeStruct((2, *block.shape), BF16)],
        scratch_shapes=[pltpu.VMEM((chips, *block.shape), BF16)],
        cost_estimate=CHEAP,
        compiler_params=pltpu.CompilerParams(vmem_limit_bytes=4 * 2**20),
        name="sort_blocks",
    )(*blocks)


def finish_kernel(keep_ref, first_ref, second_ref, own_ref, beside_ref, above_ref):
    chip, _ = own_place()
    rows = own_ref.shape[0]

    def block_of(target):
        here = block_at(target, rows)
        total = keep_ref[here, :].astype(F32) + first_ref[0, here, :].astype(F32) + second_ref[here, :].astype(F32)
        return total.astype(BF16)

    own_ref[...] = block_of(chip)
    beside_ref[pl.ds(0, rows), :] = block_of(chip ^ 1)
    beside_ref[pl.ds(rows, rows), :] = block_of(chip ^ 3)
    more = beside_ref.shape[0] - 2 * rows
    beside_ref[pl.ds(2 * rows, more), :] = beside_ref[pl.ds(0, more), :]
    above_ref[...] = block_of(chip ^ 2)


def finish(keep, first, second, rows, spare):
    columns = keep.shape[1]
    block = jax.ShapeDtypeStruct((rows, columns), BF16)
    return pl.pallas_call(
        finish_kernel,
        in_specs=[WHOLE] * 3,
        out_specs=[WHOLE] * 3,
        out_shape=[block, jax.ShapeDtypeStruct((2 * rows + spare, columns), BF16), block],
        cost_estimate=CHEAP,
        compiler_params=pltpu.CompilerParams(vmem_limit_bytes=4 * 2**20),
        name="finish",
    )(keep, first, second)


def relay_kernel(own_ref, arrived_ref, out_ref):
    rows = own_ref.shape[0]
    out_ref[pl.ds(0, rows), :] = own_ref[...]
    out_ref[pl.ds(rows, out_ref.shape[0] - rows), :] = arrived_ref[pl.ds(rows, out_ref.shape[0] - rows), :]


def relay(own, arrived):
    return pl.pallas_call(
        relay_kernel,
        in_specs=[WHOLE] * 2,
        out_specs=WHOLE,
        out_shape=jax.ShapeDtypeStruct(arrived.shape, BF16),
        cost_estimate=CHEAP,
        compiler_params=pltpu.CompilerParams(vmem_limit_bytes=4 * 2**20),
        name="relay",
    )(own, arrived)


def join_kernel(chips, keep_ref, first_ref, second_ref, own_ref, beside_ref, above_ref, out_ref):
    chip, _ = own_place()
    rows, share = own_ref.shape
    for offset, (ref, part) in enumerate(((own_ref, 0), (beside_ref, 0), (above_ref, 0), (above_ref, 1))):
        out_ref[:, block_at(chip ^ offset, share)] = ref[pl.ds(part * rows, rows), :]
    total = keep_ref[...].astype(F32) + first_ref[0].astype(F32) + second_ref[...].astype(F32)
    out_ref[:, pl.ds(chips * share, total.shape[1])] = total.astype(BF16)


def join(keep, first, second, blocks, chips):
    rows, share = blocks[0].shape
    return pl.pallas_call(
        functools.partial(join_kernel, chips),
        in_specs=[WHOLE] * (3 + len(blocks)),
        out_specs=WHOLE,
        out_shape=jax.ShapeDtypeStruct((rows, chips * share + keep.shape[1]), BF16),
        cost_estimate=CHEAP,
        compiler_params=pltpu.CompilerParams(vmem_limit_bytes=4 * 2**20),
        name="join",
    )(keep, first, second, *blocks)


def swapped(value, axis, offset):
    if not offset:
        return value
    return lax.ppermute(value, axis, [(source, source ^ offset) for source in range(lax.axis_size(axis))])


def to_chips(blocks):
    return [swapped(block, "seq", 2 * offset) for offset, block in enumerate(blocks)]


def after(value, *others):
    return lax.optimization_barrier((value, *others))[0]


def added(left, right):
    return (left.astype(F32) + right.astype(F32)).astype(BF16)


def after(value, *others):
    return lax.optimization_barrier((value, *others))[0]


def over_layers(passed, send):
    first = swapped(send, "chan", 1)
    passed = (passed.astype(F32) + first[1].astype(F32)).astype(BF16)
    return first, swapped(passed, "chan", 2)


def shards_direct(values_in, gate_values, filter_spectrum, skip_gain, out_weight):
    parts = lax.axis_size("seq")
    chips = parts // 2
    rows, width = values_in.shape
    tables = small_tables(parts, rows)

    values = pack_values(values_in, chips, 0)
    flat_filters = filter_spectrum.reshape(4, rows, width)
    near = pack_filters(after(flat_filters, values[0]), chips, (1, 2), 0)
    other_weight = swapped(out_weight, "seq", 1)
    own, far = pack_filters(after(flat_filters, near[0], other_weight), chips, (0, 3), 0)
    *moved, mine = pack_moved(after(gate_values, far), out_weight, other_weight, chips)
    values, filters = to_chips(values), to_chips([own, *near, far])
    own = stack([after(block, moved[0]) for block in values], rows)
    spectrum = forward(own, [swapped(part, "seq", 1) for part in own], tables)
    moved = to_chips([after(block, spectrum) for block in moved])
    keep, *send = backward(spectrum, filters, tables)
    gated, longer = gate(skip_gain[None, :], keep, [swapped(part, "seq", 1) for part in send], values, moved, 16)
    gathered = to_chips([gated, longer, longer, gated])

    others = [swapped(part, "seq", 1) for part in collect([after(block, gated) for block in moved[1:]], out_weight.shape[0] // 2)]
    keep, passed, send = project_moved(arrange(mine, moved[1:], others), gathered)
    first = swapped(send, "chan", 1)
    own, beside, above = finish(keep, first, swapped(added(passed, first[1]), "chan", 2), rows, 16)
    beside = swapped(beside, "seq", 2)
    above = swapped(relay(above, beside), "seq", 4)
    keep, passed, send = sort_blocks(to_chips(project_still(out_weight, other_weight, gathered)))
    first = swapped(send, "chan", 1)
    passed = added(after(passed, above), first[1])
    return join(keep, first, swapped(passed, "chan", 2), (own, beside, above), chips)


def shards(values_in, gate_values, filter_spectrum, skip_gain, out_weight):
    parts, layers = lax.axis_size("seq"), lax.axis_size("chan")
    rows, width = values_in.shape
    share = out_weight.shape[1] // layers
    aligned = width // parts % 128 == 0 and share % 128 == 0 and rows % 32 == 0
    run = shards_direct if aligned and layers == 4 and parts == 8 else shards_general
    return run(values_in, gate_values, filter_spectrum, skip_gain, out_weight)


def solution(mesh):
    in_specs = (
        P("seq", "chan"),
        P("seq", "chan"),
        P(None, "seq", None, "chan"),
        P("chan"),
        P("chan", "seq"),
    )
    out_specs = P("seq", "chan")
    return jax.shard_map(shards, mesh=mesh, in_specs=in_specs, out_specs=out_specs, check_vma=False)
```

```python
import functools

import jax
import jax.numpy as jnp
import numpy as np
from jax import lax
from jax.experimental import pallas as pl
from jax.experimental.pallas import tpu as pltpu
from jax.sharding import PartitionSpec as P

BF16 = jnp.bfloat16
F32 = jnp.float32


def bit_reversed(number, width_bits):
    flipped = 0
    for bit_place in range(width_bits):
        flipped |= (number >> bit_place & 1) << (width_bits - 1 - bit_place)
    return flipped


def filter_row(residue, width_bits):
    return 2 * bit_reversed(residue // 2, width_bits) + residue % 2


def dft_tables(parts, rows):
    total = 2 * parts * rows
    residue = np.arange(2 * parts)[:, None, None]
    column = np.arange(rows)[None, :, None]
    position = np.arange(rows)[None, None, :]
    phase = 2.0 * np.pi * (position * (residue + 2 * parts * column) % total) / total
    cos, sin = np.cos(phase), np.sin(phase)
    forward = np.concatenate(
        [np.concatenate([cos, sin], axis=2), np.concatenate([-sin, cos], axis=2)], axis=1
    )
    inverse = np.transpose(forward, (0, 2, 1)) / total
    return forward.astype(BF16), inverse.astype(BF16)


def convolve_kernel(parts, rows, moved_ref, skip_ref, forward_ref, inverse_ref, out_ref, waves_ref, back_ref):
    width_bits = parts.bit_length() - 1
    chunk = 16

    def cosine(residue, block):
        return float(np.cos(np.pi * residue * block / parts))

    def sine(residue, block):
        return float(np.sin(np.pi * residue * block / parts))

    def spread(index, carry):
        here = pl.ds(index * chunk, chunk)
        there = pl.ds(rows + index * chunk, chunk)
        blocks = [moved_ref[block, here, :].astype(F32) for block in range(parts)]
        for residue in range(parts + 1):
            real = blocks[0]
            imag = jnp.zeros_like(real)
            for block in range(1, parts):
                real = real + cosine(residue, block) * blocks[block]
                imag = imag - sine(residue, block) * blocks[block]
            waves_ref[residue, here, :] = real.astype(BF16)
            waves_ref[residue, there, :] = imag.astype(BF16)
            if 0 < residue < parts:
                waves_ref[2 * parts - residue, here, :] = real.astype(BF16)
                waves_ref[2 * parts - residue, there, :] = (-imag).astype(BF16)
        return carry

    lax.fori_loop(0, rows // chunk, spread, 0)

    def through(residue):
        wave = jnp.dot(forward_ref[residue], waves_ref[residue], preferred_element_type=F32)
        source, odd = divmod(filter_row(residue, width_bits), 2)
        filter_real = moved_ref[source, pl.ds((2 + odd) * rows, rows), :].astype(F32)
        filter_imag = moved_ref[source, pl.ds((4 + odd) * rows, rows), :].astype(F32)
        real, imag = wave[:rows], wave[rows:]
        product = jnp.concatenate(
            [real * filter_real - imag * filter_imag, real * filter_imag + imag * filter_real], axis=0
        )
        return jnp.dot(inverse_ref[residue], product.astype(BF16), preferred_element_type=F32)

    for residue in range(parts + 1):
        back = through(residue)
        if 0 < residue < parts:
            other = through(2 * parts - residue)
            back_ref[residue, pl.ds(0, rows), :] = back[:rows] + other[:rows]
            back_ref[residue, pl.ds(rows, rows), :] = back[rows:] - other[rows:]
        else:
            back_ref[residue] = back

    skip = skip_ref[...]

    def gather(index, carry):
        here = pl.ds(index * chunk, chunk)
        there = pl.ds(rows + index * chunk, chunk)
        reals = [back_ref[residue, here, :] for residue in range(parts + 1)]
        imags = [back_ref[residue, there, :] for residue in range(parts + 1)]
        for block in range(parts):
            total = reals[0]
            for residue in range(1, parts + 1):
                total = total + cosine(residue, block) * reals[residue]
                if residue < parts and block:
                    total = total - sine(residue, block) * imags[residue]
            signal = moved_ref[block, here, :].astype(F32)
            gate = moved_ref[block, pl.ds(rows + index * chunk, chunk), :].astype(F32)
            out_ref[block, here, :] = (gate * (total + skip * signal)).astype(BF16)
        return carry

    lax.fori_loop(0, rows // chunk, gather, 0)


def convolve(moved, skip):
    parts, stacked, width = moved.shape
    rows = stacked // 6
    forward, inverse = dft_tables(parts, rows)
    whole = pl.BlockSpec(memory_space=pltpu.VMEM)
    return pl.pallas_call(
        functools.partial(convolve_kernel, parts, rows),
        out_shape=jax.ShapeDtypeStruct((parts, rows, width), BF16),
        in_specs=[whole] * 4,
        out_specs=whole,
        scratch_shapes=[
            pltpu.VMEM((2 * parts, 2 * rows, width), BF16),
            pltpu.VMEM((parts + 1, 2 * rows, width), F32),
        ],
        compiler_params=pltpu.CompilerParams(vmem_limit_bytes=40 * 2**20),
    )(moved, skip[None, :], forward, inverse)


def shards_general(values_in, gate_values, filter_spectrum, skip_gain, out_weight):
    parts = lax.axis_size("seq")
    layers = lax.axis_size("chan")
    rows, width = values_in.shape
    lanes = width // parts
    device = lax.axis_index("seq")

    def by_channel(array):
        return jnp.transpose(array.reshape(array.shape[0], parts, lanes), (1, 0, 2))

    filters = filter_spectrum.astype(BF16).reshape(4 * rows, width)
    packed = jnp.concatenate([by_channel(values_in), by_channel(gate_values), by_channel(filters)], axis=1)
    moved = lax.all_to_all(packed, "seq", 0, 0)
    skip = lax.dynamic_slice_in_dim(skip_gain, device * lanes, lanes)
    gated = convolve(moved, skip)
    gathered = lax.all_gather(gated.reshape(parts * rows, lanes), "seq", axis=1, tiled=True)

    own_cols = out_weight.shape[1]
    share = own_cols * parts // layers // parts
    per_block = parts // layers
    pieces = own_cols // share
    group = device % per_block
    member = device // per_block
    weight = jnp.zeros_like(out_weight)
    for step in range(pieces):
        piece = (member + step) % pieces
        sent = lax.dynamic_slice_in_dim(out_weight, piece * share, share, 1)
        pairs = [
            (source, source % per_block * pieces + (source // per_block + step) % pieces) for source in range(parts)
        ]
        arrived = lax.ppermute(sent, "seq", pairs)
        block = (device % pieces - step) % pieces
        weight = lax.dynamic_update_slice_in_dim(weight, arrived, block * share, 1)
    partials = jnp.dot(gathered, weight, preferred_element_type=F32).astype(BF16)
    mixed = lax.psum_scatter(partials, "chan", scatter_dimension=1, tiled=True)
    return lax.all_to_all(mixed, "seq", 0, 1, tiled=True)


WHOLE = pl.BlockSpec(memory_space=pltpu.VMEM)
CHEAP = pl.CostEstimate(flops=0, transcendentals=0, bytes_accessed=0)


def small_tables(parts, rows):
    total = 2 * parts * rows
    index = np.arange(rows)
    phase = 2.0 * np.pi * (index[:, None] * index[None, :] % rows) / rows
    cos, sin = np.cos(phase), np.sin(phase)
    forward = np.block([[cos, sin], [-sin, cos]])
    residue = np.arange(2 * parts).reshape(2, 1, parts)
    turn = 2.0 * np.pi * index[None, :, None] * residue / total
    return forward.astype(BF16), forward.T.astype(BF16), np.cos(turn).astype(F32), np.sin(turn).astype(F32)


def cosine(parts, residue, block):
    return float(np.cos(np.pi * residue * block / parts))


def sine(parts, residue, block):
    return float(np.sin(np.pi * residue * block / parts))


def weighted(terms):
    total = None
    for factor, term in terms:
        if abs(factor) < 1e-12:
            continue
        part = term if factor == 1.0 else factor * term
        total = part if total is None else total + part
    return total


def plus(left, right):
    return left if right is None else right if left is None else left + right


def minus(left, right):
    return left if right is None else -right if left is None else left - right


def own_place():
    device = lax.axis_index("seq")
    return device // 2, device % 2


def block_at(index, size):
    return pl.ds(pl.multiple_of(index * size, size), size)


def pack_filters_kernel(offsets, filter_ref, *refs):
    out_refs, (plane_ref, arrived) = refs[: len(offsets)], refs[len(offsets) :]
    chip, _ = own_place()
    planes, rows, _ = filter_ref.shape
    lanes = out_refs[0].shape[1]
    copies = []
    for place, offset in enumerate(offsets):
        here = block_at(chip ^ offset, lanes)
        for plane in range(planes):
            copies.append(
                pltpu.make_async_copy(filter_ref.at[plane, :, here], plane_ref.at[place, plane], arrived.at[place, plane])
            )
    for copy in copies:
        copy.start()
    for index, copy in enumerate(copies):
        copy.wait()
        place, plane = divmod(index, planes)
        out_refs[place][pl.ds(plane * rows, rows), :] = plane_ref[place, plane].astype(BF16)
    used = planes * rows
    for out_ref in out_refs:
        if out_ref.shape[0] > used:
            out_ref[pl.ds(used, out_ref.shape[0] - used), :] = out_ref[pl.ds(0, out_ref.shape[0] - used), :]


def pack_filters(filters, chips, offsets, spare):
    planes, rows, width = filters.shape
    lanes = width // chips
    return pl.pallas_call(
        functools.partial(pack_filters_kernel, offsets),
        in_specs=[pl.BlockSpec(memory_space=pltpu.HBM)],
        out_specs=[WHOLE] * len(offsets),
        out_shape=[jax.ShapeDtypeStruct((planes * rows + spare, lanes), BF16)] * len(offsets),
        scratch_shapes=[
            pltpu.VMEM((len(offsets), planes, rows, lanes), F32),
            pltpu.SemaphoreType.DMA((len(offsets), planes)),
        ],
        cost_estimate=CHEAP,
        compiler_params=pltpu.CompilerParams(vmem_limit_bytes=8 * 2**20),
        name="pack_filters",
    )(pltpu.with_memory_space_constraint(filters, pltpu.HBM))


def pack_values_kernel(chips, values_ref, *refs):
    out_refs, arrived = refs[:chips], refs[chips]
    chip, _ = own_place()
    rows = values_ref.shape[0]
    copies = []
    for offset, out_ref in enumerate(out_refs):
        values = values_ref.at[:, block_at(chip ^ offset, out_ref.shape[1])]
        copies.append(pltpu.make_async_copy(values, out_ref.at[pl.ds(0, rows)], arrived.at[offset]))
    for copy in copies:
        copy.start()
    for copy in copies:
        copy.wait()
    for out_ref in out_refs:
        more = out_ref.shape[0] - rows
        if more:
            out_ref[pl.ds(rows, more), :] = out_ref[pl.ds(0, more), :]


def pack_values(values_in, chips, spare):
    rows, width = values_in.shape
    return pl.pallas_call(
        functools.partial(pack_values_kernel, chips),
        in_specs=[pl.BlockSpec(memory_space=pltpu.HBM)],
        out_specs=[WHOLE] * chips,
        out_shape=[jax.ShapeDtypeStruct((rows + more, width // chips), BF16) for more in spare],
        scratch_shapes=[pltpu.SemaphoreType.DMA((chips,))],
        cost_estimate=CHEAP,
        compiler_params=pltpu.CompilerParams(vmem_limit_bytes=4 * 2**20),
        name="pack_values",
    )(pltpu.with_memory_space_constraint(values_in, pltpu.HBM))


def pack_moved_kernel(chips, gate_ref, own_ref, other_ref, *refs):
    out_refs, (mine_ref, arrived) = refs[:chips], refs[chips:]
    chip, core = own_place()
    rows = gate_ref.shape[0]
    depth, held = own_ref.shape
    quarter, share = depth // 4, held // chips

    def copies_from(weight_ref):
        copies = [pltpu.make_async_copy(weight_ref.at[:, block_at(chip, share)], mine_ref, arrived.at[0, 0])]
        for offset in range(chips):
            out_ref, target = out_refs[offset], chip ^ offset
            gates = gate_ref.at[:, block_at(target, out_ref.shape[1])]
            copies.append(pltpu.make_async_copy(gates, out_ref.at[pl.ds(0, rows)], arrived.at[offset, 2]))
            for part in range(2 if offset else 0):
                source = weight_ref.at[block_at(2 * core + part, quarter), block_at(target, share)]
                sink = out_ref.at[pl.ds(rows, quarter), pl.ds(part * share, share)]
                copies.append(pltpu.make_async_copy(source, sink, arrived.at[offset, part]))
        for copy in copies:
            copy.start()
        for copy in copies:
            copy.wait()

    @pl.when(core == 0)
    def _():
        copies_from(own_ref)

    @pl.when(core == 1)
    def _():
        copies_from(other_ref)


def pack_moved(gate_values, own, other, chips):
    rows, width = gate_values.shape
    depth, held = own.shape
    share = held // chips
    return pl.pallas_call(
        functools.partial(pack_moved_kernel, chips),
        in_specs=[pl.BlockSpec(memory_space=pltpu.HBM)] * 2 + [pl.BlockSpec(memory_space=pl.ANY)],
        out_specs=[WHOLE] * (chips + 1),
        out_shape=[
            *(jax.ShapeDtypeStruct((rows + (depth // 4 if offset else 0), 2 * share), BF16) for offset in range(chips)),
            jax.ShapeDtypeStruct((depth, share), BF16),
        ],
        scratch_shapes=[pltpu.SemaphoreType.DMA((chips, 3))],
        cost_estimate=CHEAP,
        compiler_params=pltpu.CompilerParams(vmem_limit_bytes=8 * 2**20),
        name="pack_moved",
    )(*(pltpu.with_memory_space_constraint(array, pltpu.HBM) for array in (gate_values, own)), other)


def stack_kernel(chips, *refs):
    in_refs, out_refs = refs[:chips], refs[chips:]
    for offset, in_ref in enumerate(reversed(in_refs)):
        part, place = divmod(offset, chips // 2)
        out_refs[part][place] = in_ref[pl.ds(0, out_refs[part].shape[1]), :]


def stack(blocks, rows):
    chips = len(blocks)
    half = jax.ShapeDtypeStruct((chips // 2, rows, blocks[0].shape[1]), BF16)
    return pl.pallas_call(
        functools.partial(stack_kernel, chips),
        in_specs=[WHOLE] * chips,
        out_specs=[WHOLE] * 2,
        out_shape=[half, half],
        cost_estimate=CHEAP,
        compiler_params=pltpu.CompilerParams(vmem_limit_bytes=4 * 2**20),
        name="stack",
    )(*reversed(blocks))


def forward_kernel(chips, cos_ref, sin_ref, table_ref, *refs):
    own_refs, other_refs, (out_ref, signal_ref, waves_ref) = refs[:2], refs[2:4], refs[4:]
    chip, core = own_place()
    parts = 2 * chips
    rows, lanes = own_refs[0].shape[1:]
    chunk, width = 16, 128
    for offset in range(chips):
        part, place = divmod(offset, chips // 2)
        signal_ref[2 * (chip ^ offset) + core] = own_refs[part][place]
        signal_ref[2 * (chip ^ offset) + 1 - core] = other_refs[part][place]
    sign = (1 - 2 * core).astype(F32)

    def spread(index, carry):
        here = block_at(index, chunk)
        there = pl.ds(pl.multiple_of(rows + index * chunk, chunk), chunk)
        cos_all, sin_all = cos_ref[core, here, :], sin_ref[core, here, :]
        for start in range(0, lanes, width):
            blocks = [signal_ref[block, here, pl.ds(start, width)].astype(F32) for block in range(parts)]
            blocks = [block * sign if place % 2 else block for place, block in enumerate(blocks)]

            def store(residue, real, imag):
                cos, sin = cos_all[:, residue : residue + 1], sin_all[:, residue : residue + 1]
                if imag is None:
                    real, imag = real * cos, -(real * sin)
                else:
                    real, imag = real * cos + imag * sin, imag * cos - real * sin
                columns = pl.ds(residue * lanes + start, width)
                waves_ref[here, columns] = real.astype(BF16)
                waves_ref[there, columns] = imag.astype(BF16)

            for residue in range(parts // 2 + 1):
                even, odd = range(0, parts, 2), range(1, parts, 2)
                cos_even = weighted([(cosine(parts, residue, block), blocks[block]) for block in even])
                cos_odd = weighted([(cosine(parts, residue, block), blocks[block]) for block in odd])
                sin_even = weighted([(sine(parts, residue, block), blocks[block]) for block in even])
                sin_odd = weighted([(sine(parts, residue, block), blocks[block]) for block in odd])
                sin_sum = plus(sin_even, sin_odd)
                store(residue, plus(cos_even, cos_odd), None if sin_sum is None else -sin_sum)
                if 0 < residue and 2 * residue != parts:
                    store(parts - residue, minus(cos_even, cos_odd), minus(sin_even, sin_odd))
        return carry

    lax.fori_loop(0, rows // chunk, spread, 0)
    for residue in range(parts):
        columns = pl.ds(residue * lanes, lanes)
        out_ref[:, columns] = jnp.dot(table_ref[...], waves_ref[:, columns], preferred_element_type=F32)


def forward(own, other, tables):
    chips, (_, rows, lanes) = 2 * own[0].shape[0], own[0].shape
    table, _, cos, sin = tables
    spectrum = (2 * rows, 2 * chips * lanes)
    return pl.pallas_call(
        functools.partial(forward_kernel, chips),
        in_specs=[WHOLE] * 7,
        out_specs=WHOLE,
        out_shape=jax.ShapeDtypeStruct(spectrum, F32),
        scratch_shapes=[pltpu.VMEM((2 * chips, rows, lanes), BF16), pltpu.VMEM(spectrum, BF16)],
        cost_estimate=CHEAP,
        compiler_params=pltpu.CompilerParams(vmem_limit_bytes=32 * 2**20),
        name="forward",
    )(cos, sin, table, *own, *other)


def backward_kernel(chips, cos_ref, sin_ref, table_ref, spectrum_ref, *refs):
    filter_refs, (keep_ref, *send_refs, filter_ref, product_ref, back_ref) = refs[:chips], refs[chips:]
    chip, core = own_place()
    parts = 2 * chips
    rows, lanes = keep_ref.shape[1:]
    chip_bits = chips.bit_length() - 1
    chunk, width = 16, 128
    for offset in range(chips):
        for plane in range(filter_ref.shape[1]):
            filter_ref[chip ^ offset, plane] = filter_refs[offset][pl.ds(plane * rows, rows), :]

    for residue in range(parts):
        source, odd = bit_reversed(residue // 2, chip_bits), residue % 2
        columns = pl.ds(residue * lanes, lanes)
        filter_real = filter_ref[source, odd].astype(F32)
        filter_imag = filter_ref[source, 2 + odd].astype(F32)
        real = spectrum_ref[pl.ds(0, rows), columns]
        imag = spectrum_ref[pl.ds(rows, rows), columns]
        product_ref[pl.ds(0, rows), columns] = (real * filter_real - imag * filter_imag).astype(BF16)
        product_ref[pl.ds(rows, rows), columns] = (real * filter_imag + imag * filter_real).astype(BF16)
        back_ref[:, columns] = jnp.dot(table_ref[...], product_ref[:, columns], preferred_element_type=F32)

    scale = 1.0 / (2 * parts * rows)
    sign = (1 - 2 * core).astype(F32)
    upper = core == 1

    def gather(index, carry):
        here = block_at(index, chunk)
        there = pl.ds(pl.multiple_of(rows + index * chunk, chunk), chunk)
        cos_all, sin_all = cos_ref[core, here, :] * scale, sin_ref[core, here, :] * scale
        for start in range(0, lanes, width):
            reals, imags = [], []
            for residue in range(parts):
                columns = pl.ds(residue * lanes + start, width)
                real, imag = back_ref[here, columns], back_ref[there, columns]
                cos, sin = cos_all[:, residue : residue + 1], sin_all[:, residue : residue + 1]
                reals.append(real * cos - imag * sin)
                imags.append(real * sin + imag * cos)
            totals = [None] * parts
            for block in range(parts // 2 + 1):
                even, odd = range(0, parts, 2), range(1, parts, 2)
                cos_even = weighted([(cosine(parts, residue, block), reals[residue]) for residue in even])
                cos_odd = weighted([(cosine(parts, residue, block), reals[residue]) for residue in odd])
                sin_even = weighted([(sine(parts, residue, block), imags[residue]) for residue in even])
                sin_odd = weighted([(sine(parts, residue, block), imags[residue]) for residue in odd])
                totals[block] = minus(plus(cos_even, cos_odd), plus(sin_even, sin_odd))
                if 0 < block and 2 * block != parts:
                    totals[parts - block] = plus(minus(cos_even, cos_odd), minus(sin_even, sin_odd))
            lane = pl.ds(start, width)
            for pair in range(chips):
                low, high = totals[2 * pair], totals[2 * pair + 1] * sign
                keep_ref[pair, here, lane] = jnp.where(upper, high, low)
                part, place = divmod(pair, chips // 2)
                send_refs[part][place, here, lane] = jnp.where(upper, low, high).astype(BF16)
        return carry

    lax.fori_loop(0, rows // chunk, gather, 0)


def backward(spectrum, first, tables):
    chips = len(first)
    rows, lanes = spectrum.shape[0] // 2, first[0].shape[1]
    _, table, cos, sin = tables
    half = jax.ShapeDtypeStruct((chips // 2, rows, lanes), BF16)
    return pl.pallas_call(
        functools.partial(backward_kernel, chips),
        in_specs=[WHOLE] * (4 + chips),
        out_specs=[WHOLE] * 3,
        out_shape=[jax.ShapeDtypeStruct((chips, rows, lanes), F32), half, half],
        scratch_shapes=[
            pltpu.VMEM((chips, 4, rows, lanes), BF16),
            pltpu.VMEM(spectrum.shape, BF16),
            pltpu.VMEM(spectrum.shape, F32),
        ],
        cost_estimate=CHEAP,
        compiler_params=pltpu.CompilerParams(vmem_limit_bytes=32 * 2**20),
        name="backward",
    )(cos, sin, table, spectrum, *first)


def gate_kernel(chips, skip_ref, keep_ref, low_ref, high_ref, *refs):
    signal_refs, gate_refs = refs[:chips], refs[chips : 2 * chips]
    out_ref, longer_ref, arrived_ref = refs[2 * chips :]
    chip, _ = own_place()
    rows, lanes = keep_ref.shape[1:]
    skip = skip_ref[:, block_at(chip, lanes)]
    arrived_ref[pl.ds(0, chips // 2)] = low_ref[...]
    arrived_ref[pl.ds(chips // 2, chips // 2)] = high_ref[...]
    for offset in range(chips):
        block = chip ^ offset
        convolved = keep_ref[block] + arrived_ref[block].astype(F32)
        signal = signal_refs[offset][pl.ds(0, rows), :].astype(F32)
        gate = gate_refs[offset][pl.ds(0, rows), :].astype(F32)
        gated = (gate * (convolved + skip * signal)).astype(BF16)
        out_ref[block_at(block, rows), :] = gated
        longer_ref[block_at(block, rows), :] = gated
    end = chips * rows
    longer_ref[pl.ds(end, longer_ref.shape[0] - end), :] = longer_ref[pl.ds(0, longer_ref.shape[0] - end), :]


def gate(skip, keep, arrived, first, gates, spare):
    chips, rows, lanes = keep.shape
    return pl.pallas_call(
        functools.partial(gate_kernel, chips),
        in_specs=[WHOLE] * (4 + 2 * chips),
        out_specs=[WHOLE] * 2,
        out_shape=[
            jax.ShapeDtypeStruct((chips * rows, lanes), BF16),
            jax.ShapeDtypeStruct((chips * rows + spare, lanes), BF16),
        ],
        scratch_shapes=[pltpu.VMEM((chips, rows, lanes), BF16)],
        cost_estimate=CHEAP,
        compiler_params=pltpu.CompilerParams(vmem_limit_bytes=6 * 2**20),
        name="gate",
    )(skip, keep, *arrived, *first, *gates)


def piece_of(ref, half, part):
    quarter, share = half // 2, ref.shape[1] // 2
    return ref[pl.ds(ref.shape[0] - quarter, quarter), pl.ds(part * share, share)]


def collect_kernel(in_refs, out_refs):
    rows = out_refs[0].shape[0]
    quarter = len(out_refs) * rows // (2 * len(in_refs))
    for place in range(2 * len(in_refs)):
        index, start = divmod(place * quarter, rows)
        out_refs[index][pl.ds(start, quarter), :] = piece_of(in_refs[place // 2], 2 * quarter, place % 2)


def collect(moved, half):
    count = len(moved)
    shape = (count * half // 2, moved[0].shape[1] // 2)
    return pl.pallas_call(
        lambda *refs: collect_kernel(refs[:count], refs[count:]),
        in_specs=[WHOLE] * count,
        out_specs=[WHOLE] * 2,
        out_shape=[jax.ShapeDtypeStruct(shape, BF16)] * 2,
        cost_estimate=CHEAP,
        compiler_params=pltpu.CompilerParams(vmem_limit_bytes=4 * 2**20),
        name="collect_weights",
    )(*moved)


def arrange_kernel(chips, mine_ref, *refs):
    moved_refs, (*other_refs, out_ref) = refs[: chips - 1], refs[chips - 1 :]
    chip, core = own_place()
    layer = lax.axis_index("chan")
    depth, share = mine_ref.shape
    quarter = depth // 4
    out_ref[:, block_at(chip ^ layer, share)] = mine_ref[...]
    for place in range(2 * (chips - 1)):
        offset, part = place // 2 + 1, place % 2
        columns = block_at(chip ^ layer ^ offset, share)
        index, start = divmod(place * quarter, other_refs[0].shape[0])
        out_ref[block_at(2 * core + part, quarter), columns] = piece_of(moved_refs[offset - 1], 2 * quarter, part)
        out_ref[block_at(2 * (1 - core) + part, quarter), columns] = other_refs[index][pl.ds(start, quarter), :]


def arrange(mine, moved, others):
    chips = len(moved) + 1
    depth, share = mine.shape
    return pl.pallas_call(
        functools.partial(arrange_kernel, chips),
        in_specs=[WHOLE] * (chips + len(others)),
        out_specs=WHOLE,
        out_shape=jax.ShapeDtypeStruct((depth, chips * share), BF16),
        cost_estimate=CHEAP,
        compiler_params=pltpu.CompilerParams(vmem_limit_bytes=8 * 2**20),
        name="arrange_weights",
    )(mine, *moved, *others)


def join_channels(chips, gated_refs, joined_ref):
    chip, _ = own_place()
    lanes = gated_refs[0].shape[1]
    for offset in range(chips):
        joined_ref[:, block_at(chip ^ offset, lanes)] = gated_refs[offset][pl.ds(0, joined_ref.shape[0]), :]


def project_moved_kernel(chips, weight_ref, *refs):
    gated_refs, (keep_ref, pass_ref, send_ref, joined_ref) = refs[:chips], refs[chips:]
    share = keep_ref.shape[1]
    join_channels(chips, gated_refs, joined_ref)
    partial = jnp.dot(joined_ref[...], weight_ref[...], preferred_element_type=F32).astype(BF16)
    keep_ref[...] = partial[:, :share]
    send_ref[0] = partial[:, share : 2 * share]
    pass_ref[...] = partial[:, 2 * share : 3 * share]
    send_ref[1] = partial[:, 3 * share :]


def project_moved(weight, gated):
    chips = len(gated)
    depth, columns = weight.shape
    rows = gated[0].shape[0]
    block = jax.ShapeDtypeStruct((rows, columns // chips), BF16)
    return pl.pallas_call(
        functools.partial(project_moved_kernel, chips),
        in_specs=[WHOLE] * (1 + chips),
        out_specs=[WHOLE] * 3,
        out_shape=[block, block, jax.ShapeDtypeStruct((2, rows, columns // chips), BF16)],
        scratch_shapes=[pltpu.VMEM((rows, depth), BF16)],
        cost_estimate=CHEAP,
        compiler_params=pltpu.CompilerParams(vmem_limit_bytes=8 * 2**20),
        name="project_moved",
    )(weight, *gated)


def project_still_kernel(chips, own_ref, other_ref, *refs):
    gated_refs, out_refs, joined_ref = refs[:chips], refs[chips : 2 * chips], refs[2 * chips]
    chip, core = own_place()
    rows = out_refs[0].shape[0]
    join_channels(chips, gated_refs, joined_ref)

    def project_with(weight_ref):
        for offset in range(chips):
            gated = joined_ref[block_at(chip ^ offset, rows), :]
            out_refs[offset][...] = jnp.dot(gated, weight_ref[...], preferred_element_type=F32).astype(BF16)

    @pl.when(core == 0)
    def _():
        project_with(other_ref)

    @pl.when(core == 1)
    def _():
        project_with(own_ref)


def project_still(own, other, gated):
    chips = len(gated)
    depth, held = own.shape
    rows = gated[0].shape[0] // chips
    return pl.pallas_call(
        functools.partial(project_still_kernel, chips),
        in_specs=[WHOLE] * (2 + chips),
        out_specs=[WHOLE] * chips,
        out_shape=[jax.ShapeDtypeStruct((rows, held), BF16)] * chips,
        scratch_shapes=[pltpu.VMEM((rows * chips, depth), BF16)],
        cost_estimate=CHEAP,
        compiler_params=pltpu.CompilerParams(vmem_limit_bytes=12 * 2**20),
        name="project_still",
    )(own, other, *gated)


def sort_kernel(chips, *refs):
    in_refs, (keep_ref, pass_ref, send_ref, sorted_ref) = refs[:chips], refs[chips:]
    chip, _ = own_place()
    layer = lax.axis_index("chan")
    for offset in range(chips):
        sorted_ref[chip ^ layer ^ offset] = in_refs[offset][...]
    keep_ref[...] = sorted_ref[0]
    send_ref[0] = sorted_ref[1]
    pass_ref[...] = sorted_ref[2]
    send_ref[1] = sorted_ref[3]


def sort_blocks(blocks):
    chips = len(blocks)
    block = jax.ShapeDtypeStruct(blocks[0].shape, BF16)
    return pl.pallas_call(
        functools.partial(sort_kernel, chips),
        in_specs=[WHOLE] * chips,
        out_specs=[WHOLE] * 3,
        out_shape=[block, block, jax.ShapeDtypeStruct((2, *block.shape), BF16)],
        scratch_shapes=[pltpu.VMEM((chips, *block.shape), BF16)],
        cost_estimate=CHEAP,
        compiler_params=pltpu.CompilerParams(vmem_limit_bytes=4 * 2**20),
        name="sort_blocks",
    )(*blocks)


def finish_kernel(keep_ref, first_ref, second_ref, own_ref, beside_ref, above_ref):
    chip, _ = own_place()
    rows = own_ref.shape[0]

    def block_of(target):
        here = block_at(target, rows)
        total = keep_ref[here, :].astype(F32) + first_ref[0, here, :].astype(F32) + second_ref[here, :].astype(F32)
        return total.astype(BF16)

    own_ref[...] = block_of(chip)
    beside_ref[pl.ds(0, rows), :] = block_of(chip ^ 1)
    beside_ref[pl.ds(rows, rows), :] = block_of(chip ^ 3)
    more = beside_ref.shape[0] - 2 * rows
    beside_ref[pl.ds(2 * rows, more), :] = beside_ref[pl.ds(0, more), :]
    above_ref[...] = block_of(chip ^ 2)


def finish(keep, first, second, rows, spare):
    columns = keep.shape[1]
    block = jax.ShapeDtypeStruct((rows, columns), BF16)
    return pl.pallas_call(
        finish_kernel,
        in_specs=[WHOLE] * 3,
        out_specs=[WHOLE] * 3,
        out_shape=[block, jax.ShapeDtypeStruct((2 * rows + spare, columns), BF16), block],
        cost_estimate=CHEAP,
        compiler_params=pltpu.CompilerParams(vmem_limit_bytes=4 * 2**20),
        name="finish",
    )(keep, first, second)


def relay_kernel(own_ref, arrived_ref, out_ref):
    rows = own_ref.shape[0]
    out_ref[pl.ds(0, rows), :] = own_ref[...]
    out_ref[pl.ds(rows, out_ref.shape[0] - rows), :] = arrived_ref[pl.ds(rows, out_ref.shape[0] - rows), :]


def relay(own, arrived):
    return pl.pallas_call(
        relay_kernel,
        in_specs=[WHOLE] * 2,
        out_specs=WHOLE,
        out_shape=jax.ShapeDtypeStruct(arrived.shape, BF16),
        cost_estimate=CHEAP,
        compiler_params=pltpu.CompilerParams(vmem_limit_bytes=4 * 2**20),
        name="relay",
    )(own, arrived)


def join_kernel(chips, keep_ref, first_ref, second_ref, own_ref, beside_ref, above_ref, out_ref):
    chip, _ = own_place()
    rows, share = own_ref.shape
    for offset, (ref, part) in enumerate(((own_ref, 0), (beside_ref, 0), (above_ref, 0), (above_ref, 1))):
        out_ref[:, block_at(chip ^ offset, share)] = ref[pl.ds(part * rows, rows), :]
    total = keep_ref[...].astype(F32) + first_ref[0].astype(F32) + second_ref[...].astype(F32)
    out_ref[:, pl.ds(chips * share, total.shape[1])] = total.astype(BF16)


def join(keep, first, second, blocks, chips):
    rows, share = blocks[0].shape
    return pl.pallas_call(
        functools.partial(join_kernel, chips),
        in_specs=[WHOLE] * (3 + len(blocks)),
        out_specs=WHOLE,
        out_shape=jax.ShapeDtypeStruct((rows, chips * share + keep.shape[1]), BF16),
        cost_estimate=CHEAP,
        compiler_params=pltpu.CompilerParams(vmem_limit_bytes=4 * 2**20),
        name="join",
    )(keep, first, second, *blocks)


def swapped(value, axis, offset):
    if not offset:
        return value
    return lax.ppermute(value, axis, [(source, source ^ offset) for source in range(lax.axis_size(axis))])


def to_chips(blocks):
    return [swapped(block, "seq", 2 * offset) for offset, block in enumerate(blocks)]


def after(value, *others):
    return lax.optimization_barrier((value, *others))[0]


def added(left, right):
    return (left.astype(F32) + right.astype(F32)).astype(BF16)


def after(value, *others):
    return lax.optimization_barrier((value, *others))[0]


def over_layers(passed, send):
    first = swapped(send, "chan", 1)
    passed = (passed.astype(F32) + first[1].astype(F32)).astype(BF16)
    return first, swapped(passed, "chan", 2)


def shards_direct(values_in, gate_values, filter_spectrum, skip_gain, out_weight):
    parts = lax.axis_size("seq")
    chips = parts // 2
    rows, width = values_in.shape
    tables = small_tables(parts, rows)

    values = pack_values(values_in, chips, (0, 0, 0, 0))
    flat_filters = filter_spectrum.reshape(4, rows, width)
    near = pack_filters(after(flat_filters, values[0]), chips, (1, 2), 0)
    other_weight = swapped(out_weight, "seq", 1)
    own, far = pack_filters(after(flat_filters, near[0], other_weight), chips, (0, 3), 0)
    *moved, mine = pack_moved(after(gate_values, far), out_weight, other_weight, chips)
    values, filters = to_chips(values), to_chips([own, *near, far])
    own = stack([after(block, moved[0]) for block in values], rows)
    spectrum = forward(own, [swapped(part, "seq", 1) for part in own], tables)
    moved = to_chips([after(block, spectrum) for block in moved])
    keep, *send = backward(spectrum, filters, tables)
    gated, longer = gate(skip_gain[None, :], keep, [swapped(part, "seq", 1) for part in send], values, moved, 16)
    gathered = to_chips([gated, longer, longer, gated])

    others = [swapped(part, "seq", 1) for part in collect([after(block, gated) for block in moved[1:]], out_weight.shape[0] // 2)]
    keep, passed, send = project_moved(arrange(mine, moved[1:], others), gathered)
    first = swapped(send, "chan", 1)
    own, beside, above = finish(keep, first, swapped(added(passed, first[1]), "chan", 2), rows, 16)
    beside = swapped(beside, "seq", 2)
    above = swapped(relay(above, beside), "seq", 4)
    keep, passed, send = sort_blocks(to_chips(project_still(out_weight, other_weight, gathered)))
    first = swapped(send, "chan", 1)
    passed = added(passed, first[1])
    return join(keep, first, swapped(passed, "chan", 2), (own, beside, above), chips)


def shards(values_in, gate_values, filter_spectrum, skip_gain, out_weight):
    parts, layers = lax.axis_size("seq"), lax.axis_size("chan")
    rows, width = values_in.shape
    share = out_weight.shape[1] // layers
    aligned = width // parts % 128 == 0 and share % 128 == 0 and rows % 32 == 0
    run = shards_direct if aligned and layers == 4 and parts == 8 else shards_general
    return run(values_in, gate_values, filter_spectrum, skip_gain, out_weight)


def solution(mesh):
    in_specs = (
        P("seq", "chan"),
        P("seq", "chan"),
        P(None, "seq", None, "chan"),
        P("chan"),
        P("chan", "seq"),
    )
    out_specs = P("seq", "chan")
    return jax.shard_map(shards, mesh=mesh, in_specs=in_specs, out_specs=out_specs, check_vma=False)
```

```python
import functools

import jax
import jax.numpy as jnp
import numpy as np
from jax import lax
from jax.experimental import pallas as pl
from jax.experimental.pallas import tpu as pltpu
from jax.sharding import PartitionSpec as P

BF16 = jnp.bfloat16
F32 = jnp.float32


def bit_reversed(number, width_bits):
    flipped = 0
    for bit_place in range(width_bits):
        flipped |= (number >> bit_place & 1) << (width_bits - 1 - bit_place)
    return flipped


def filter_row(residue, width_bits):
    return 2 * bit_reversed(residue // 2, width_bits) + residue % 2


def dft_tables(parts, rows):
    total = 2 * parts * rows
    residue = np.arange(2 * parts)[:, None, None]
    column = np.arange(rows)[None, :, None]
    position = np.arange(rows)[None, None, :]
    phase = 2.0 * np.pi * (position * (residue + 2 * parts * column) % total) / total
    cos, sin = np.cos(phase), np.sin(phase)
    forward = np.concatenate(
        [np.concatenate([cos, sin], axis=2), np.concatenate([-sin, cos], axis=2)], axis=1
    )
    inverse = np.transpose(forward, (0, 2, 1)) / total
    return forward.astype(BF16), inverse.astype(BF16)


def convolve_kernel(parts, rows, moved_ref, skip_ref, forward_ref, inverse_ref, out_ref, waves_ref, back_ref):
    width_bits = parts.bit_length() - 1
    chunk = 16

    def cosine(residue, block):
        return float(np.cos(np.pi * residue * block / parts))

    def sine(residue, block):
        return float(np.sin(np.pi * residue * block / parts))

    def spread(index, carry):
        here = pl.ds(index * chunk, chunk)
        there = pl.ds(rows + index * chunk, chunk)
        blocks = [moved_ref[block, here, :].astype(F32) for block in range(parts)]
        for residue in range(parts + 1):
            real = blocks[0]
            imag = jnp.zeros_like(real)
            for block in range(1, parts):
                real = real + cosine(residue, block) * blocks[block]
                imag = imag - sine(residue, block) * blocks[block]
            waves_ref[residue, here, :] = real.astype(BF16)
            waves_ref[residue, there, :] = imag.astype(BF16)
            if 0 < residue < parts:
                waves_ref[2 * parts - residue, here, :] = real.astype(BF16)
                waves_ref[2 * parts - residue, there, :] = (-imag).astype(BF16)
        return carry

    lax.fori_loop(0, rows // chunk, spread, 0)

    def through(residue):
        wave = jnp.dot(forward_ref[residue], waves_ref[residue], preferred_element_type=F32)
        source, odd = divmod(filter_row(residue, width_bits), 2)
        filter_real = moved_ref[source, pl.ds((2 + odd) * rows, rows), :].astype(F32)
        filter_imag = moved_ref[source, pl.ds((4 + odd) * rows, rows), :].astype(F32)
        real, imag = wave[:rows], wave[rows:]
        product = jnp.concatenate(
            [real * filter_real - imag * filter_imag, real * filter_imag + imag * filter_real], axis=0
        )
        return jnp.dot(inverse_ref[residue], product.astype(BF16), preferred_element_type=F32)

    for residue in range(parts + 1):
        back = through(residue)
        if 0 < residue < parts:
            other = through(2 * parts - residue)
            back_ref[residue, pl.ds(0, rows), :] = back[:rows] + other[:rows]
            back_ref[residue, pl.ds(rows, rows), :] = back[rows:] - other[rows:]
        else:
            back_ref[residue] = back

    skip = skip_ref[...]

    def gather(index, carry):
        here = pl.ds(index * chunk, chunk)
        there = pl.ds(rows + index * chunk, chunk)
        reals = [back_ref[residue, here, :] for residue in range(parts + 1)]
        imags = [back_ref[residue, there, :] for residue in range(parts + 1)]
        for block in range(parts):
            total = reals[0]
            for residue in range(1, parts + 1):
                total = total + cosine(residue, block) * reals[residue]
                if residue < parts and block:
                    total = total - sine(residue, block) * imags[residue]
            signal = moved_ref[block, here, :].astype(F32)
            gate = moved_ref[block, pl.ds(rows + index * chunk, chunk), :].astype(F32)
            out_ref[block, here, :] = (gate * (total + skip * signal)).astype(BF16)
        return carry

    lax.fori_loop(0, rows // chunk, gather, 0)


def convolve(moved, skip):
    parts, stacked, width = moved.shape
    rows = stacked // 6
    forward, inverse = dft_tables(parts, rows)
    whole = pl.BlockSpec(memory_space=pltpu.VMEM)
    return pl.pallas_call(
        functools.partial(convolve_kernel, parts, rows),
        out_shape=jax.ShapeDtypeStruct((parts, rows, width), BF16),
        in_specs=[whole] * 4,
        out_specs=whole,
        scratch_shapes=[
            pltpu.VMEM((2 * parts, 2 * rows, width), BF16),
            pltpu.VMEM((parts + 1, 2 * rows, width), F32),
        ],
        compiler_params=pltpu.CompilerParams(vmem_limit_bytes=40 * 2**20),
    )(moved, skip[None, :], forward, inverse)


def shards_general(values_in, gate_values, filter_spectrum, skip_gain, out_weight):
    parts = lax.axis_size("seq")
    layers = lax.axis_size("chan")
    rows, width = values_in.shape
    lanes = width // parts
    device = lax.axis_index("seq")

    def by_channel(array):
        return jnp.transpose(array.reshape(array.shape[0], parts, lanes), (1, 0, 2))

    filters = filter_spectrum.astype(BF16).reshape(4 * rows, width)
    packed = jnp.concatenate([by_channel(values_in), by_channel(gate_values), by_channel(filters)], axis=1)
    moved = lax.all_to_all(packed, "seq", 0, 0)
    skip = lax.dynamic_slice_in_dim(skip_gain, device * lanes, lanes)
    gated = convolve(moved, skip)
    gathered = lax.all_gather(gated.reshape(parts * rows, lanes), "seq", axis=1, tiled=True)

    own_cols = out_weight.shape[1]
    share = own_cols * parts // layers // parts
    per_block = parts // layers
    pieces = own_cols // share
    group = device % per_block
    member = device // per_block
    weight = jnp.zeros_like(out_weight)
    for step in range(pieces):
        piece = (member + step) % pieces
        sent = lax.dynamic_slice_in_dim(out_weight, piece * share, share, 1)
        pairs = [
            (source, source % per_block * pieces + (source // per_block + step) % pieces) for source in range(parts)
        ]
        arrived = lax.ppermute(sent, "seq", pairs)
        block = (device % pieces - step) % pieces
        weight = lax.dynamic_update_slice_in_dim(weight, arrived, block * share, 1)
    partials = jnp.dot(gathered, weight, preferred_element_type=F32).astype(BF16)
    mixed = lax.psum_scatter(partials, "chan", scatter_dimension=1, tiled=True)
    return lax.all_to_all(mixed, "seq", 0, 1, tiled=True)


WHOLE = pl.BlockSpec(memory_space=pltpu.VMEM)
CHEAP = pl.CostEstimate(flops=0, transcendentals=0, bytes_accessed=0)


def small_tables(parts, rows):
    total = 2 * parts * rows
    index = np.arange(rows)
    phase = 2.0 * np.pi * (index[:, None] * index[None, :] % rows) / rows
    cos, sin = np.cos(phase), np.sin(phase)
    forward = np.block([[cos, sin], [-sin, cos]])
    residue = np.arange(2 * parts).reshape(2, 1, parts)
    turn = 2.0 * np.pi * index[None, :, None] * residue / total
    return forward.astype(BF16), forward.T.astype(BF16), np.cos(turn).astype(F32), np.sin(turn).astype(F32)


def cosine(parts, residue, block):
    return float(np.cos(np.pi * residue * block / parts))


def sine(parts, residue, block):
    return float(np.sin(np.pi * residue * block / parts))


def weighted(terms):
    total = None
    for factor, term in terms:
        if abs(factor) < 1e-12:
            continue
        part = term if factor == 1.0 else factor * term
        total = part if total is None else total + part
    return total


def plus(left, right):
    return left if right is None else right if left is None else left + right


def minus(left, right):
    return left if right is None else -right if left is None else left - right


def own_place():
    device = lax.axis_index("seq")
    return device // 2, device % 2


def block_at(index, size):
    return pl.ds(pl.multiple_of(index * size, size), size)


def pack_filters_kernel(offsets, filter_ref, *refs):
    out_refs, (plane_ref, arrived) = refs[: len(offsets)], refs[len(offsets) :]
    chip, _ = own_place()
    planes, rows, _ = filter_ref.shape
    lanes = out_refs[0].shape[1]
    copies = []
    for place, offset in enumerate(offsets):
        here = block_at(chip ^ offset, lanes)
        for plane in range(planes):
            copies.append(
                pltpu.make_async_copy(filter_ref.at[plane, :, here], plane_ref.at[place, plane], arrived.at[place, plane])
            )
    for copy in copies:
        copy.start()
    for index, copy in enumerate(copies):
        copy.wait()
        place, plane = divmod(index, planes)
        out_refs[place][pl.ds(plane * rows, rows), :] = plane_ref[place, plane].astype(BF16)
    used = planes * rows
    for out_ref in out_refs:
        if out_ref.shape[0] > used:
            out_ref[pl.ds(used, out_ref.shape[0] - used), :] = out_ref[pl.ds(0, out_ref.shape[0] - used), :]


def pack_filters(filters, chips, offsets, spare):
    planes, rows, width = filters.shape
    lanes = width // chips
    return pl.pallas_call(
        functools.partial(pack_filters_kernel, offsets),
        in_specs=[pl.BlockSpec(memory_space=pltpu.HBM)],
        out_specs=[WHOLE] * len(offsets),
        out_shape=[jax.ShapeDtypeStruct((planes * rows + spare, lanes), BF16)] * len(offsets),
        scratch_shapes=[
            pltpu.VMEM((len(offsets), planes, rows, lanes), F32),
            pltpu.SemaphoreType.DMA((len(offsets), planes)),
        ],
        cost_estimate=CHEAP,
        compiler_params=pltpu.CompilerParams(vmem_limit_bytes=8 * 2**20),
        name="pack_filters",
    )(pltpu.with_memory_space_constraint(filters, pltpu.HBM))


def pack_values_kernel(chips, values_ref, *refs):
    out_refs, arrived = refs[:chips], refs[chips]
    chip, _ = own_place()
    rows = values_ref.shape[0]
    copies = []
    for offset, out_ref in enumerate(out_refs):
        values = values_ref.at[:, block_at(chip ^ offset, out_ref.shape[1])]
        copies.append(pltpu.make_async_copy(values, out_ref.at[pl.ds(0, rows)], arrived.at[offset]))
    for copy in copies:
        copy.start()
    for copy in copies:
        copy.wait()
    for out_ref in out_refs:
        more = out_ref.shape[0] - rows
        if more:
            out_ref[pl.ds(rows, more), :] = out_ref[pl.ds(0, more), :]


def pack_values(values_in, chips, spare):
    rows, width = values_in.shape
    return pl.pallas_call(
        functools.partial(pack_values_kernel, chips),
        in_specs=[pl.BlockSpec(memory_space=pltpu.HBM)],
        out_specs=[WHOLE] * chips,
        out_shape=[jax.ShapeDtypeStruct((rows + more, width // chips), BF16) for more in spare],
        scratch_shapes=[pltpu.SemaphoreType.DMA((chips,))],
        cost_estimate=CHEAP,
        compiler_params=pltpu.CompilerParams(vmem_limit_bytes=4 * 2**20),
        name="pack_values",
    )(pltpu.with_memory_space_constraint(values_in, pltpu.HBM))


def pack_moved_kernel(chips, gate_ref, own_ref, other_ref, *refs):
    out_refs, (mine_ref, arrived) = refs[:chips], refs[chips:]
    chip, core = own_place()
    rows = gate_ref.shape[0]
    depth, held = own_ref.shape
    quarter, share = depth // 4, held // chips

    def copies_from(weight_ref):
        copies = [pltpu.make_async_copy(weight_ref.at[:, block_at(chip, share)], mine_ref, arrived.at[0, 0])]
        for offset in range(chips):
            out_ref, target = out_refs[offset], chip ^ offset
            gates = gate_ref.at[:, block_at(target, out_ref.shape[1])]
            copies.append(pltpu.make_async_copy(gates, out_ref.at[pl.ds(0, rows)], arrived.at[offset, 2]))
            for part in range(2 if offset else 0):
                source = weight_ref.at[block_at(2 * core + part, quarter), block_at(target, share)]
                sink = out_ref.at[pl.ds(rows, quarter), pl.ds(part * share, share)]
                copies.append(pltpu.make_async_copy(source, sink, arrived.at[offset, part]))
        for copy in copies:
            copy.start()
        for copy in copies:
            copy.wait()

    @pl.when(core == 0)
    def _():
        copies_from(own_ref)

    @pl.when(core == 1)
    def _():
        copies_from(other_ref)


def pack_moved(gate_values, own, other, chips):
    rows, width = gate_values.shape
    depth, held = own.shape
    share = held // chips
    return pl.pallas_call(
        functools.partial(pack_moved_kernel, chips),
        in_specs=[pl.BlockSpec(memory_space=pltpu.HBM)] * 2 + [pl.BlockSpec(memory_space=pl.ANY)],
        out_specs=[WHOLE] * (chips + 1),
        out_shape=[
            *(jax.ShapeDtypeStruct((rows + (depth // 4 if offset else 0), 2 * share), BF16) for offset in range(chips)),
            jax.ShapeDtypeStruct((depth, share), BF16),
        ],
        scratch_shapes=[pltpu.SemaphoreType.DMA((chips, 3))],
        cost_estimate=CHEAP,
        compiler_params=pltpu.CompilerParams(vmem_limit_bytes=8 * 2**20),
        name="pack_moved",
    )(*(pltpu.with_memory_space_constraint(array, pltpu.HBM) for array in (gate_values, own)), other)


def stack_kernel(chips, *refs):
    in_refs, out_refs = refs[:chips], refs[chips:]
    for offset, in_ref in enumerate(in_refs):
        part, place = divmod(offset, chips // 2)
        out_refs[part][place] = in_ref[pl.ds(0, out_refs[part].shape[1]), :]


def stack(blocks, rows):
    chips = len(blocks)
    half = jax.ShapeDtypeStruct((chips // 2, rows, blocks[0].shape[1]), BF16)
    return pl.pallas_call(
        functools.partial(stack_kernel, chips),
        in_specs=[WHOLE] * chips,
        out_specs=[WHOLE] * 2,
        out_shape=[half, half],
        cost_estimate=CHEAP,
        compiler_params=pltpu.CompilerParams(vmem_limit_bytes=4 * 2**20),
        name="stack",
    )(*blocks)


def forward_kernel(chips, cos_ref, sin_ref, table_ref, *refs):
    own_refs, other_refs, (out_ref, signal_ref, waves_ref) = refs[:2], refs[2:4], refs[4:]
    chip, core = own_place()
    parts = 2 * chips
    rows, lanes = own_refs[0].shape[1:]
    chunk, width = 16, 128
    for offset in range(chips):
        part, place = divmod(offset, chips // 2)
        signal_ref[2 * (chip ^ offset) + core] = own_refs[part][place]
        signal_ref[2 * (chip ^ offset) + 1 - core] = other_refs[part][place]
    sign = (1 - 2 * core).astype(F32)

    def spread(index, carry):
        here = block_at(index, chunk)
        there = pl.ds(pl.multiple_of(rows + index * chunk, chunk), chunk)
        cos_all, sin_all = cos_ref[core, here, :], sin_ref[core, here, :]
        for start in range(0, lanes, width):
            blocks = [signal_ref[block, here, pl.ds(start, width)].astype(F32) for block in range(parts)]
            blocks = [block * sign if place % 2 else block for place, block in enumerate(blocks)]

            def store(residue, real, imag):
                cos, sin = cos_all[:, residue : residue + 1], sin_all[:, residue : residue + 1]
                if imag is None:
                    real, imag = real * cos, -(real * sin)
                else:
                    real, imag = real * cos + imag * sin, imag * cos - real * sin
                columns = pl.ds(residue * lanes + start, width)
                waves_ref[here, columns] = real.astype(BF16)
                waves_ref[there, columns] = imag.astype(BF16)

            for residue in range(parts // 2 + 1):
                even, odd = range(0, parts, 2), range(1, parts, 2)
                cos_even = weighted([(cosine(parts, residue, block), blocks[block]) for block in even])
                cos_odd = weighted([(cosine(parts, residue, block), blocks[block]) for block in odd])
                sin_even = weighted([(sine(parts, residue, block), blocks[block]) for block in even])
                sin_odd = weighted([(sine(parts, residue, block), blocks[block]) for block in odd])
                sin_sum = plus(sin_even, sin_odd)
                store(residue, plus(cos_even, cos_odd), None if sin_sum is None else -sin_sum)
                if 0 < residue and 2 * residue != parts:
                    store(parts - residue, minus(cos_even, cos_odd), minus(sin_even, sin_odd))
        return carry

    lax.fori_loop(0, rows // chunk, spread, 0)
    for residue in range(parts):
        columns = pl.ds(residue * lanes, lanes)
        out_ref[:, columns] = jnp.dot(table_ref[...], waves_ref[:, columns], preferred_element_type=F32)


def forward(own, other, tables):
    chips, (_, rows, lanes) = 2 * own[0].shape[0], own[0].shape
    table, _, cos, sin = tables
    spectrum = (2 * rows, 2 * chips * lanes)
    return pl.pallas_call(
        functools.partial(forward_kernel, chips),
        in_specs=[WHOLE] * 7,
        out_specs=WHOLE,
        out_shape=jax.ShapeDtypeStruct(spectrum, F32),
        scratch_shapes=[pltpu.VMEM((2 * chips, rows, lanes), BF16), pltpu.VMEM(spectrum, BF16)],
        cost_estimate=CHEAP,
        compiler_params=pltpu.CompilerParams(vmem_limit_bytes=32 * 2**20),
        name="forward",
    )(cos, sin, table, *own, *other)


def backward_kernel(chips, cos_ref, sin_ref, table_ref, spectrum_ref, *refs):
    filter_refs, (keep_ref, *send_refs, filter_ref, product_ref, back_ref) = refs[:chips], refs[chips:]
    chip, core = own_place()
    parts = 2 * chips
    rows, lanes = keep_ref.shape[1:]
    chip_bits = chips.bit_length() - 1
    chunk, width = 16, 128
    for offset in range(chips):
        for plane in range(filter_ref.shape[1]):
            filter_ref[chip ^ offset, plane] = filter_refs[offset][pl.ds(plane * rows, rows), :]

    for residue in range(parts):
        source, odd = bit_reversed(residue // 2, chip_bits), residue % 2
        columns = pl.ds(residue * lanes, lanes)
        filter_real = filter_ref[source, odd].astype(F32)
        filter_imag = filter_ref[source, 2 + odd].astype(F32)
        real = spectrum_ref[pl.ds(0, rows), columns]
        imag = spectrum_ref[pl.ds(rows, rows), columns]
        product_ref[pl.ds(0, rows), columns] = (real * filter_real - imag * filter_imag).astype(BF16)
        product_ref[pl.ds(rows, rows), columns] = (real * filter_imag + imag * filter_real).astype(BF16)
        back_ref[:, columns] = jnp.dot(table_ref[...], product_ref[:, columns], preferred_element_type=F32)

    scale = 1.0 / (2 * parts * rows)
    sign = (1 - 2 * core).astype(F32)
    upper = core == 1

    def gather(index, carry):
        here = block_at(index, chunk)
        there = pl.ds(pl.multiple_of(rows + index * chunk, chunk), chunk)
        cos_all, sin_all = cos_ref[core, here, :] * scale, sin_ref[core, here, :] * scale
        for start in range(0, lanes, width):
            reals, imags = [], []
            for residue in range(parts):
                columns = pl.ds(residue * lanes + start, width)
                real, imag = back_ref[here, columns], back_ref[there, columns]
                cos, sin = cos_all[:, residue : residue + 1], sin_all[:, residue : residue + 1]
                reals.append(real * cos - imag * sin)
                imags.append(real * sin + imag * cos)
            totals = [None] * parts
            for block in range(parts // 2 + 1):
                even, odd = range(0, parts, 2), range(1, parts, 2)
                cos_even = weighted([(cosine(parts, residue, block), reals[residue]) for residue in even])
                cos_odd = weighted([(cosine(parts, residue, block), reals[residue]) for residue in odd])
                sin_even = weighted([(sine(parts, residue, block), imags[residue]) for residue in even])
                sin_odd = weighted([(sine(parts, residue, block), imags[residue]) for residue in odd])
                totals[block] = minus(plus(cos_even, cos_odd), plus(sin_even, sin_odd))
                if 0 < block and 2 * block != parts:
                    totals[parts - block] = plus(minus(cos_even, cos_odd), minus(sin_even, sin_odd))
            lane = pl.ds(start, width)
            for pair in range(chips):
                low, high = totals[2 * pair], totals[2 * pair + 1] * sign
                keep_ref[pair, here, lane] = jnp.where(upper, high, low)
                part, place = divmod(pair, chips // 2)
                send_refs[part][place, here, lane] = jnp.where(upper, low, high).astype(BF16)
        return carry

    lax.fori_loop(0, rows // chunk, gather, 0)


def backward(spectrum, first, tables):
    chips = len(first)
    rows, lanes = spectrum.shape[0] // 2, first[0].shape[1]
    _, table, cos, sin = tables
    half = jax.ShapeDtypeStruct((chips // 2, rows, lanes), BF16)
    return pl.pallas_call(
        functools.partial(backward_kernel, chips),
        in_specs=[WHOLE] * (4 + chips),
        out_specs=[WHOLE] * 3,
        out_shape=[jax.ShapeDtypeStruct((chips, rows, lanes), F32), half, half],
        scratch_shapes=[
            pltpu.VMEM((chips, 4, rows, lanes), BF16),
            pltpu.VMEM(spectrum.shape, BF16),
            pltpu.VMEM(spectrum.shape, F32),
        ],
        cost_estimate=CHEAP,
        compiler_params=pltpu.CompilerParams(vmem_limit_bytes=32 * 2**20),
        name="backward",
    )(cos, sin, table, spectrum, *first)


def gate_kernel(chips, skip_ref, keep_ref, low_ref, high_ref, *refs):
    signal_refs, gate_refs = refs[:chips], refs[chips : 2 * chips]
    out_ref, longer_ref, arrived_ref = refs[2 * chips :]
    chip, _ = own_place()
    rows, lanes = keep_ref.shape[1:]
    skip = skip_ref[:, block_at(chip, lanes)]
    arrived_ref[pl.ds(0, chips // 2)] = low_ref[...]
    arrived_ref[pl.ds(chips // 2, chips // 2)] = high_ref[...]
    for offset in range(chips):
        block = chip ^ offset
        convolved = keep_ref[block] + arrived_ref[block].astype(F32)
        signal = signal_refs[offset][pl.ds(0, rows), :].astype(F32)
        gate = gate_refs[offset][pl.ds(0, rows), :].astype(F32)
        gated = (gate * (convolved + skip * signal)).astype(BF16)
        out_ref[block_at(block, rows), :] = gated
        longer_ref[block_at(block, rows), :] = gated
    end = chips * rows
    longer_ref[pl.ds(end, longer_ref.shape[0] - end), :] = longer_ref[pl.ds(0, longer_ref.shape[0] - end), :]


def gate(skip, keep, arrived, first, gates, spare):
    chips, rows, lanes = keep.shape
    return pl.pallas_call(
        functools.partial(gate_kernel, chips),
        in_specs=[WHOLE] * (4 + 2 * chips),
        out_specs=[WHOLE] * 2,
        out_shape=[
            jax.ShapeDtypeStruct((chips * rows, lanes), BF16),
            jax.ShapeDtypeStruct((chips * rows + spare, lanes), BF16),
        ],
        scratch_shapes=[pltpu.VMEM((chips, rows, lanes), BF16)],
        cost_estimate=CHEAP,
        compiler_params=pltpu.CompilerParams(vmem_limit_bytes=6 * 2**20),
        name="gate",
    )(skip, keep, *arrived, *first, *gates)


def piece_of(ref, half, part):
    quarter, share = half // 2, ref.shape[1] // 2
    return ref[pl.ds(ref.shape[0] - quarter, quarter), pl.ds(part * share, share)]


def collect_kernel(in_refs, out_refs):
    rows = out_refs[0].shape[0]
    quarter = len(out_refs) * rows // (2 * len(in_refs))
    for place in range(2 * len(in_refs)):
        index, start = divmod(place * quarter, rows)
        out_refs[index][pl.ds(start, quarter), :] = piece_of(in_refs[place // 2], 2 * quarter, place % 2)


def collect(moved, half):
    count = len(moved)
    shape = (count * half // 2, moved[0].shape[1] // 2)
    return pl.pallas_call(
        lambda *refs: collect_kernel(refs[:count], refs[count:]),
        in_specs=[WHOLE] * count,
        out_specs=[WHOLE] * 2,
        out_shape=[jax.ShapeDtypeStruct(shape, BF16)] * 2,
        cost_estimate=CHEAP,
        compiler_params=pltpu.CompilerParams(vmem_limit_bytes=4 * 2**20),
        name="collect_weights",
    )(*moved)


def arrange_kernel(chips, mine_ref, *refs):
    moved_refs, (*other_refs, out_ref) = refs[: chips - 1], refs[chips - 1 :]
    chip, core = own_place()
    layer = lax.axis_index("chan")
    depth, share = mine_ref.shape
    quarter = depth // 4
    out_ref[:, block_at(chip ^ layer, share)] = mine_ref[...]
    for place in range(2 * (chips - 1)):
        offset, part = place // 2 + 1, place % 2
        columns = block_at(chip ^ layer ^ offset, share)
        index, start = divmod(place * quarter, other_refs[0].shape[0])
        out_ref[block_at(2 * core + part, quarter), columns] = piece_of(moved_refs[offset - 1], 2 * quarter, part)
        out_ref[block_at(2 * (1 - core) + part, quarter), columns] = other_refs[index][pl.ds(start, quarter), :]


def arrange(mine, moved, others):
    chips = len(moved) + 1
    depth, share = mine.shape
    return pl.pallas_call(
        functools.partial(arrange_kernel, chips),
        in_specs=[WHOLE] * (chips + len(others)),
        out_specs=WHOLE,
        out_shape=jax.ShapeDtypeStruct((depth, chips * share), BF16),
        cost_estimate=CHEAP,
        compiler_params=pltpu.CompilerParams(vmem_limit_bytes=8 * 2**20),
        name="arrange_weights",
    )(mine, *moved, *others)


def join_channels(chips, gated_refs, joined_ref):
    chip, _ = own_place()
    lanes = gated_refs[0].shape[1]
    for offset in range(chips):
        joined_ref[:, block_at(chip ^ offset, lanes)] = gated_refs[offset][pl.ds(0, joined_ref.shape[0]), :]


def project_moved_kernel(chips, weight_ref, *refs):
    gated_refs, (keep_ref, pass_ref, send_ref, joined_ref) = refs[:chips], refs[chips:]
    share = keep_ref.shape[1]
    join_channels(chips, gated_refs, joined_ref)
    partial = jnp.dot(joined_ref[...], weight_ref[...], preferred_element_type=F32).astype(BF16)
    keep_ref[...] = partial[:, :share]
    send_ref[0] = partial[:, share : 2 * share]
    pass_ref[...] = partial[:, 2 * share : 3 * share]
    send_ref[1] = partial[:, 3 * share :]


def project_moved(weight, gated):
    chips = len(gated)
    depth, columns = weight.shape
    rows = gated[0].shape[0]
    block = jax.ShapeDtypeStruct((rows, columns // chips), BF16)
    return pl.pallas_call(
        functools.partial(project_moved_kernel, chips),
        in_specs=[WHOLE] * (1 + chips),
        out_specs=[WHOLE] * 3,
        out_shape=[block, block, jax.ShapeDtypeStruct((2, rows, columns // chips), BF16)],
        scratch_shapes=[pltpu.VMEM((rows, depth), BF16)],
        cost_estimate=CHEAP,
        compiler_params=pltpu.CompilerParams(vmem_limit_bytes=8 * 2**20),
        name="project_moved",
    )(weight, *gated)


def project_still_kernel(chips, own_ref, other_ref, *refs):
    gated_refs, out_refs, joined_ref = refs[:chips], refs[chips : 2 * chips], refs[2 * chips]
    chip, core = own_place()
    rows = out_refs[0].shape[0]
    join_channels(chips, gated_refs, joined_ref)

    def project_with(weight_ref):
        for offset in range(chips):
            gated = joined_ref[block_at(chip ^ offset, rows), :]
            out_refs[offset][...] = jnp.dot(gated, weight_ref[...], preferred_element_type=F32).astype(BF16)

    @pl.when(core == 0)
    def _():
        project_with(other_ref)

    @pl.when(core == 1)
    def _():
        project_with(own_ref)


def project_still(own, other, gated):
    chips = len(gated)
    depth, held = own.shape
    rows = gated[0].shape[0] // chips
    return pl.pallas_call(
        functools.partial(project_still_kernel, chips),
        in_specs=[WHOLE] * (2 + chips),
        out_specs=[WHOLE] * chips,
        out_shape=[jax.ShapeDtypeStruct((rows, held), BF16)] * chips,
        scratch_shapes=[pltpu.VMEM((rows * chips, depth), BF16)],
        cost_estimate=CHEAP,
        compiler_params=pltpu.CompilerParams(vmem_limit_bytes=12 * 2**20),
        name="project_still",
    )(own, other, *gated)


def sort_kernel(chips, *refs):
    in_refs, (keep_ref, pass_ref, send_ref, sorted_ref) = refs[:chips], refs[chips:]
    chip, _ = own_place()
    layer = lax.axis_index("chan")
    for offset in range(chips):
        sorted_ref[chip ^ layer ^ offset] = in_refs[offset][...]
    keep_ref[...] = sorted_ref[0]
    send_ref[0] = sorted_ref[1]
    pass_ref[...] = sorted_ref[2]
    send_ref[1] = sorted_ref[3]


def sort_blocks(blocks):
    chips = len(blocks)
    block = jax.ShapeDtypeStruct(blocks[0].shape, BF16)
    return pl.pallas_call(
        functools.partial(sort_kernel, chips),
        in_specs=[WHOLE] * chips,
        out_specs=[WHOLE] * 3,
        out_shape=[block, block, jax.ShapeDtypeStruct((2, *block.shape), BF16)],
        scratch_shapes=[pltpu.VMEM((chips, *block.shape), BF16)],
        cost_estimate=CHEAP,
        compiler_params=pltpu.CompilerParams(vmem_limit_bytes=4 * 2**20),
        name="sort_blocks",
    )(*blocks)


def finish_kernel(keep_ref, first_ref, second_ref, own_ref, beside_ref, above_ref):
    chip, _ = own_place()
    rows = own_ref.shape[0]

    def block_of(target):
        here = block_at(target, rows)
        total = keep_ref[here, :].astype(F32) + first_ref[0, here, :].astype(F32) + second_ref[here, :].astype(F32)
        return total.astype(BF16)

    own_ref[...] = block_of(chip)
    beside_ref[pl.ds(0, rows), :] = block_of(chip ^ 1)
    beside_ref[pl.ds(rows, rows), :] = block_of(chip ^ 3)
    more = beside_ref.shape[0] - 2 * rows
    beside_ref[pl.ds(2 * rows, more), :] = beside_ref[pl.ds(0, more), :]
    above_ref[...] = block_of(chip ^ 2)


def finish(keep, first, second, rows, spare):
    columns = keep.shape[1]
    block = jax.ShapeDtypeStruct((rows, columns), BF16)
    return pl.pallas_call(
        finish_kernel,
        in_specs=[WHOLE] * 3,
        out_specs=[WHOLE] * 3,
        out_shape=[block, jax.ShapeDtypeStruct((2 * rows + spare, columns), BF16), block],
        cost_estimate=CHEAP,
        compiler_params=pltpu.CompilerParams(vmem_limit_bytes=4 * 2**20),
        name="finish",
    )(keep, first, second)


def relay_kernel(own_ref, arrived_ref, out_ref):
    rows = own_ref.shape[0]
    out_ref[pl.ds(0, rows), :] = own_ref[...]
    out_ref[pl.ds(rows, out_ref.shape[0] - rows), :] = arrived_ref[pl.ds(rows, out_ref.shape[0] - rows), :]


def relay(own, arrived):
    return pl.pallas_call(
        relay_kernel,
        in_specs=[WHOLE] * 2,
        out_specs=WHOLE,
        out_shape=jax.ShapeDtypeStruct(arrived.shape, BF16),
        cost_estimate=CHEAP,
        compiler_params=pltpu.CompilerParams(vmem_limit_bytes=4 * 2**20),
        name="relay",
    )(own, arrived)


def join_kernel(chips, keep_ref, first_ref, second_ref, own_ref, beside_ref, above_ref, out_ref):
    chip, _ = own_place()
    rows, share = own_ref.shape
    for offset, (ref, part) in enumerate(((own_ref, 0), (beside_ref, 0), (above_ref, 0), (above_ref, 1))):
        out_ref[:, block_at(chip ^ offset, share)] = ref[pl.ds(part * rows, rows), :]
    total = keep_ref[...].astype(F32) + first_ref[0].astype(F32) + second_ref[...].astype(F32)
    out_ref[:, pl.ds(chips * share, total.shape[1])] = total.astype(BF16)


def join(keep, first, second, blocks, chips):
    rows, share = blocks[0].shape
    return pl.pallas_call(
        functools.partial(join_kernel, chips),
        in_specs=[WHOLE] * (3 + len(blocks)),
        out_specs=WHOLE,
        out_shape=jax.ShapeDtypeStruct((rows, chips * share + keep.shape[1]), BF16),
        cost_estimate=CHEAP,
        compiler_params=pltpu.CompilerParams(vmem_limit_bytes=4 * 2**20),
        name="join",
    )(keep, first, second, *blocks)


def swapped(value, axis, offset):
    if not offset:
        return value
    return lax.ppermute(value, axis, [(source, source ^ offset) for source in range(lax.axis_size(axis))])


def to_chips(blocks):
    return [swapped(block, "seq", 2 * offset) for offset, block in enumerate(blocks)]


def after(value, *others):
    return lax.optimization_barrier((value, *others))[0]


def added(left, right):
    return (left.astype(F32) + right.astype(F32)).astype(BF16)


def after(value, *others):
    return lax.optimization_barrier((value, *others))[0]


def over_layers(passed, send):
    first = swapped(send, "chan", 1)
    passed = (passed.astype(F32) + first[1].astype(F32)).astype(BF16)
    return first, swapped(passed, "chan", 2)


def shards_direct(values_in, gate_values, filter_spectrum, skip_gain, out_weight):
    parts = lax.axis_size("seq")
    chips = parts // 2
    rows, width = values_in.shape
    tables = small_tables(parts, rows)

    values = pack_values(values_in, chips, (0, 0, 0, 0))
    flat_filters = filter_spectrum.reshape(4, rows, width)
    near = pack_filters(after(flat_filters, values[0]), chips, (1, 2), 0)
    other_weight = swapped(out_weight, "seq", 1)
    own, far = pack_filters(after(flat_filters, near[0], other_weight), chips, (0, 3), 0)
    *moved, mine = pack_moved(after(gate_values, far), out_weight, other_weight, chips)
    values, filters = to_chips(values), to_chips([own, *near, far])
    own = stack([after(block, moved[0]) for block in values], rows)
    spectrum = forward(own, [swapped(part, "seq", 1) for part in own], tables)
    moved = to_chips([after(block, spectrum) for block in moved])
    keep, *send = backward(spectrum, filters, tables)
    gated, longer = gate(skip_gain[None, :], keep, [swapped(part, "seq", 1) for part in send], values, moved, 16)
    gathered = to_chips([gated, longer, longer, gated])

    others = [swapped(part, "seq", 1) for part in collect([after(block, gated) for block in moved[1:]], out_weight.shape[0] // 2)]
    keep, passed, send = project_moved(arrange(mine, moved[1:], others), gathered)
    first = swapped(send, "chan", 1)
    own, beside, above = finish(keep, first, swapped(added(passed, first[1]), "chan", 2), rows, 16)
    beside = swapped(beside, "seq", 2)
    above = swapped(relay(above, beside), "seq", 4)
    keep, passed, send = sort_blocks(to_chips(project_still(out_weight, other_weight, gathered)))
    first = swapped(send, "chan", 1)
    passed = added(passed, first[1])
    return join(keep, first, swapped(passed, "chan", 2), (own, beside, above), chips)


def shards(values_in, gate_values, filter_spectrum, skip_gain, out_weight):
    parts, layers = lax.axis_size("seq"), lax.axis_size("chan")
    rows, width = values_in.shape
    share = out_weight.shape[1] // layers
    aligned = width // parts % 128 == 0 and share % 128 == 0 and rows % 32 == 0
    run = shards_direct if aligned and layers == 4 and parts == 8 else shards_general
    return run(values_in, gate_values, filter_spectrum, skip_gain, out_weight)


def solution(mesh):
    in_specs = (
        P("seq", "chan"),
        P("seq", "chan"),
        P(None, "seq", None, "chan"),
        P("chan"),
        P("chan", "seq"),
    )
    out_specs = P("seq", "chan")
    return jax.shard_map(shards, mesh=mesh, in_specs=in_specs, out_specs=out_specs, check_vma=False)
```

```python
import functools

import jax
import jax.numpy as jnp
import numpy as np
from jax import lax
from jax.experimental import pallas as pl
from jax.experimental.pallas import tpu as pltpu
from jax.sharding import PartitionSpec as P

BF16 = jnp.bfloat16
F32 = jnp.float32


def bit_reversed(number, width_bits):
    flipped = 0
    for bit_place in range(width_bits):
        flipped |= (number >> bit_place & 1) << (width_bits - 1 - bit_place)
    return flipped


def filter_row(residue, width_bits):
    return 2 * bit_reversed(residue // 2, width_bits) + residue % 2


def dft_tables(parts, rows):
    total = 2 * parts * rows
    residue = np.arange(2 * parts)[:, None, None]
    column = np.arange(rows)[None, :, None]
    position = np.arange(rows)[None, None, :]
    phase = 2.0 * np.pi * (position * (residue + 2 * parts * column) % total) / total
    cos, sin = np.cos(phase), np.sin(phase)
    forward = np.concatenate(
        [np.concatenate([cos, sin], axis=2), np.concatenate([-sin, cos], axis=2)], axis=1
    )
    inverse = np.transpose(forward, (0, 2, 1)) / total
    return forward.astype(BF16), inverse.astype(BF16)


def convolve_kernel(parts, rows, moved_ref, skip_ref, forward_ref, inverse_ref, out_ref, waves_ref, back_ref):
    width_bits = parts.bit_length() - 1
    chunk = 16

    def cosine(residue, block):
        return float(np.cos(np.pi * residue * block / parts))

    def sine(residue, block):
        return float(np.sin(np.pi * residue * block / parts))

    def spread(index, carry):
        here = pl.ds(index * chunk, chunk)
        there = pl.ds(rows + index * chunk, chunk)
        blocks = [moved_ref[block, here, :].astype(F32) for block in range(parts)]
        for residue in range(parts + 1):
            real = blocks[0]
            imag = jnp.zeros_like(real)
            for block in range(1, parts):
                real = real + cosine(residue, block) * blocks[block]
                imag = imag - sine(residue, block) * blocks[block]
            waves_ref[residue, here, :] = real.astype(BF16)
            waves_ref[residue, there, :] = imag.astype(BF16)
            if 0 < residue < parts:
                waves_ref[2 * parts - residue, here, :] = real.astype(BF16)
                waves_ref[2 * parts - residue, there, :] = (-imag).astype(BF16)
        return carry

    lax.fori_loop(0, rows // chunk, spread, 0)

    def through(residue):
        wave = jnp.dot(forward_ref[residue], waves_ref[residue], preferred_element_type=F32)
        source, odd = divmod(filter_row(residue, width_bits), 2)
        filter_real = moved_ref[source, pl.ds((2 + odd) * rows, rows), :].astype(F32)
        filter_imag = moved_ref[source, pl.ds((4 + odd) * rows, rows), :].astype(F32)
        real, imag = wave[:rows], wave[rows:]
        product = jnp.concatenate(
            [real * filter_real - imag * filter_imag, real * filter_imag + imag * filter_real], axis=0
        )
        return jnp.dot(inverse_ref[residue], product.astype(BF16), preferred_element_type=F32)

    for residue in range(parts + 1):
        back = through(residue)
        if 0 < residue < parts:
            other = through(2 * parts - residue)
            back_ref[residue, pl.ds(0, rows), :] = back[:rows] + other[:rows]
            back_ref[residue, pl.ds(rows, rows), :] = back[rows:] - other[rows:]
        else:
            back_ref[residue] = back

    skip = skip_ref[...]

    def gather(index, carry):
        here = pl.ds(index * chunk, chunk)
        there = pl.ds(rows + index * chunk, chunk)
        reals = [back_ref[residue, here, :] for residue in range(parts + 1)]
        imags = [back_ref[residue, there, :] for residue in range(parts + 1)]
        for block in range(parts):
            total = reals[0]
            for residue in range(1, parts + 1):
                total = total + cosine(residue, block) * reals[residue]
                if residue < parts and block:
                    total = total - sine(residue, block) * imags[residue]
            signal = moved_ref[block, here, :].astype(F32)
            gate = moved_ref[block, pl.ds(rows + index * chunk, chunk), :].astype(F32)
            out_ref[block, here, :] = (gate * (total + skip * signal)).astype(BF16)
        return carry

    lax.fori_loop(0, rows // chunk, gather, 0)


def convolve(moved, skip):
    parts, stacked, width = moved.shape
    rows = stacked // 6
    forward, inverse = dft_tables(parts, rows)
    whole = pl.BlockSpec(memory_space=pltpu.VMEM)
    return pl.pallas_call(
        functools.partial(convolve_kernel, parts, rows),
        out_shape=jax.ShapeDtypeStruct((parts, rows, width), BF16),
        in_specs=[whole] * 4,
        out_specs=whole,
        scratch_shapes=[
            pltpu.VMEM((2 * parts, 2 * rows, width), BF16),
            pltpu.VMEM((parts + 1, 2 * rows, width), F32),
        ],
        compiler_params=pltpu.CompilerParams(vmem_limit_bytes=40 * 2**20),
    )(moved, skip[None, :], forward, inverse)


def shards_general(values_in, gate_values, filter_spectrum, skip_gain, out_weight):
    parts = lax.axis_size("seq")
    layers = lax.axis_size("chan")
    rows, width = values_in.shape
    lanes = width // parts
    device = lax.axis_index("seq")

    def by_channel(array):
        return jnp.transpose(array.reshape(array.shape[0], parts, lanes), (1, 0, 2))

    filters = filter_spectrum.astype(BF16).reshape(4 * rows, width)
    packed = jnp.concatenate([by_channel(values_in), by_channel(gate_values), by_channel(filters)], axis=1)
    moved = lax.all_to_all(packed, "seq", 0, 0)
    skip = lax.dynamic_slice_in_dim(skip_gain, device * lanes, lanes)
    gated = convolve(moved, skip)
    gathered = lax.all_gather(gated.reshape(parts * rows, lanes), "seq", axis=1, tiled=True)

    own_cols = out_weight.shape[1]
    share = own_cols * parts // layers // parts
    per_block = parts // layers
    pieces = own_cols // share
    group = device % per_block
    member = device // per_block
    weight = jnp.zeros_like(out_weight)
    for step in range(pieces):
        piece = (member + step) % pieces
        sent = lax.dynamic_slice_in_dim(out_weight, piece * share, share, 1)
        pairs = [
            (source, source % per_block * pieces + (source // per_block + step) % pieces) for source in range(parts)
        ]
        arrived = lax.ppermute(sent, "seq", pairs)
        block = (device % pieces - step) % pieces
        weight = lax.dynamic_update_slice_in_dim(weight, arrived, block * share, 1)
    partials = jnp.dot(gathered, weight, preferred_element_type=F32).astype(BF16)
    mixed = lax.psum_scatter(partials, "chan", scatter_dimension=1, tiled=True)
    return lax.all_to_all(mixed, "seq", 0, 1, tiled=True)


WHOLE = pl.BlockSpec(memory_space=pltpu.VMEM)
CHEAP = pl.CostEstimate(flops=0, transcendentals=0, bytes_accessed=0)


def small_tables(parts, rows):
    total = 2 * parts * rows
    index = np.arange(rows)
    phase = 2.0 * np.pi * (index[:, None] * index[None, :] % rows) / rows
    cos, sin = np.cos(phase), np.sin(phase)
    forward = np.block([[cos, sin], [-sin, cos]])
    residue = np.arange(2 * parts).reshape(2, 1, parts)
    turn = 2.0 * np.pi * index[None, :, None] * residue / total
    return forward.astype(BF16), forward.T.astype(BF16), np.cos(turn).astype(F32), np.sin(turn).astype(F32)


def cosine(parts, residue, block):
    return float(np.cos(np.pi * residue * block / parts))


def sine(parts, residue, block):
    return float(np.sin(np.pi * residue * block / parts))


def weighted(terms):
    total = None
    for factor, term in terms:
        if abs(factor) < 1e-12:
            continue
        part = term if factor == 1.0 else factor * term
        total = part if total is None else total + part
    return total


def plus(left, right):
    return left if right is None else right if left is None else left + right


def minus(left, right):
    return left if right is None else -right if left is None else left - right


def own_place():
    device = lax.axis_index("seq")
    return device // 2, device % 2


def block_at(index, size):
    return pl.ds(pl.multiple_of(index * size, size), size)


def pack_filters_kernel(offsets, filter_ref, *refs):
    out_refs, (plane_ref, arrived) = refs[: len(offsets)], refs[len(offsets) :]
    chip, _ = own_place()
    planes, rows, _ = filter_ref.shape
    lanes = out_refs[0].shape[1]
    copies = []
    for place, offset in enumerate(offsets):
        here = block_at(chip ^ offset, lanes)
        for plane in range(planes):
            copies.append(
                pltpu.make_async_copy(filter_ref.at[plane, :, here], plane_ref.at[place, plane], arrived.at[place, plane])
            )
    for copy in copies:
        copy.start()
    for index, copy in enumerate(copies):
        copy.wait()
        place, plane = divmod(index, planes)
        out_refs[place][pl.ds(plane * rows, rows), :] = plane_ref[place, plane].astype(BF16)
    used = planes * rows
    for out_ref in out_refs:
        if out_ref.shape[0] > used:
            out_ref[pl.ds(used, out_ref.shape[0] - used), :] = out_ref[pl.ds(0, out_ref.shape[0] - used), :]


def pack_filters(filters, chips, offsets, spare):
    planes, rows, width = filters.shape
    lanes = width // chips
    return pl.pallas_call(
        functools.partial(pack_filters_kernel, offsets),
        in_specs=[pl.BlockSpec(memory_space=pltpu.HBM)],
        out_specs=[WHOLE] * len(offsets),
        out_shape=[jax.ShapeDtypeStruct((planes * rows + spare, lanes), BF16)] * len(offsets),
        scratch_shapes=[
            pltpu.VMEM((len(offsets), planes, rows, lanes), F32),
            pltpu.SemaphoreType.DMA((len(offsets), planes)),
        ],
        cost_estimate=CHEAP,
        compiler_params=pltpu.CompilerParams(vmem_limit_bytes=8 * 2**20),
        name="pack_filters",
    )(pltpu.with_memory_space_constraint(filters, pltpu.HBM))


def pack_values_kernel(chips, values_ref, *refs):
    out_refs, arrived = refs[:chips], refs[chips]
    rows = values_ref.shape[0]
    chip, _ = own_place()
    copies = []
    for offset, out_ref in enumerate(out_refs):
        values = values_ref.at[:, block_at(chip ^ offset, out_ref.shape[1])]
        copies.append(pltpu.make_async_copy(values, out_ref.at[pl.ds(0, rows)], arrived.at[offset]))
    for copy in copies:
        copy.start()
    for copy in copies:
        copy.wait()


def pack_values(values_in, chips, spare):
    rows, width = values_in.shape
    return pl.pallas_call(
        functools.partial(pack_values_kernel, chips),
        in_specs=[pl.BlockSpec(memory_space=pltpu.HBM)],
        out_specs=[WHOLE] * chips,
        out_shape=[jax.ShapeDtypeStruct((rows + spare, width // chips), BF16)] * chips,
        scratch_shapes=[pltpu.SemaphoreType.DMA((chips,))],
        cost_estimate=CHEAP,
        compiler_params=pltpu.CompilerParams(vmem_limit_bytes=4 * 2**20),
        name="pack_values",
    )(pltpu.with_memory_space_constraint(values_in, pltpu.HBM))


def pack_moved_kernel(chips, gate_ref, own_ref, other_ref, *refs):
    out_refs, (mine_ref, arrived) = refs[:chips], refs[chips:]
    chip, core = own_place()
    rows = gate_ref.shape[0]
    depth, held = own_ref.shape
    quarter, share = depth // 4, held // chips

    def copies_from(weight_ref):
        copies = [pltpu.make_async_copy(weight_ref.at[:, block_at(chip, share)], mine_ref, arrived.at[0, 0])]
        for offset in range(chips):
            out_ref, target = out_refs[offset], chip ^ offset
            gates = gate_ref.at[:, block_at(target, out_ref.shape[1])]
            copies.append(pltpu.make_async_copy(gates, out_ref.at[pl.ds(0, rows)], arrived.at[offset, 2]))
            for part in range(2 if offset else 0):
                source = weight_ref.at[block_at(2 * core + part, quarter), block_at(target, share)]
                sink = out_ref.at[pl.ds(rows, quarter), pl.ds(part * share, share)]
                copies.append(pltpu.make_async_copy(source, sink, arrived.at[offset, part]))
        for copy in copies:
            copy.start()
        for copy in copies:
            copy.wait()

    @pl.when(core == 0)
    def _():
        copies_from(own_ref)

    @pl.when(core == 1)
    def _():
        copies_from(other_ref)


def pack_moved(gate_values, own, other, chips):
    rows, width = gate_values.shape
    depth, held = own.shape
    share = held // chips
    return pl.pallas_call(
        functools.partial(pack_moved_kernel, chips),
        in_specs=[pl.BlockSpec(memory_space=pltpu.HBM)] * 2 + [pl.BlockSpec(memory_space=pl.ANY)],
        out_specs=[WHOLE] * (chips + 1),
        out_shape=[
            *(jax.ShapeDtypeStruct((rows + (depth // 4 if offset else 0), 2 * share), BF16) for offset in range(chips)),
            jax.ShapeDtypeStruct((depth, share), BF16),
        ],
        scratch_shapes=[pltpu.SemaphoreType.DMA((chips, 3))],
        cost_estimate=CHEAP,
        compiler_params=pltpu.CompilerParams(vmem_limit_bytes=8 * 2**20),
        name="pack_moved",
    )(*(pltpu.with_memory_space_constraint(array, pltpu.HBM) for array in (gate_values, own)), other)


def stack_kernel(chips, *refs):
    in_refs, out_refs = refs[:chips], refs[chips:]
    for offset, in_ref in enumerate(in_refs):
        part, place = divmod(offset, chips // 2)
        out_refs[part][place] = in_ref[pl.ds(0, out_refs[part].shape[1]), :]


def stack(blocks, rows):
    chips = len(blocks)
    half = jax.ShapeDtypeStruct((chips // 2, rows, blocks[0].shape[1]), BF16)
    return pl.pallas_call(
        functools.partial(stack_kernel, chips),
        in_specs=[WHOLE] * chips,
        out_specs=[WHOLE] * 2,
        out_shape=[half, half],
        cost_estimate=CHEAP,
        compiler_params=pltpu.CompilerParams(vmem_limit_bytes=4 * 2**20),
        name="stack",
    )(*blocks)


def forward_kernel(chips, cos_ref, sin_ref, table_ref, *refs):
    own_refs, other_refs, (out_ref, signal_ref, waves_ref) = refs[:2], refs[2:4], refs[4:]
    chip, core = own_place()
    parts = 2 * chips
    rows, lanes = own_refs[0].shape[1:]
    chunk, width = 16, 128
    for offset in range(chips):
        part, place = divmod(offset, chips // 2)
        signal_ref[2 * (chip ^ offset) + core] = own_refs[part][place]
        signal_ref[2 * (chip ^ offset) + 1 - core] = other_refs[part][place]
    sign = (1 - 2 * core).astype(F32)

    def spread(index, carry):
        here = block_at(index, chunk)
        there = pl.ds(pl.multiple_of(rows + index * chunk, chunk), chunk)
        cos_all, sin_all = cos_ref[core, here, :], sin_ref[core, here, :]
        for start in range(0, lanes, width):
            blocks = [signal_ref[block, here, pl.ds(start, width)].astype(F32) for block in range(parts)]
            blocks = [block * sign if place % 2 else block for place, block in enumerate(blocks)]

            def store(residue, real, imag):
                cos, sin = cos_all[:, residue : residue + 1], sin_all[:, residue : residue + 1]
                if imag is None:
                    real, imag = real * cos, -(real * sin)
                else:
                    real, imag = real * cos + imag * sin, imag * cos - real * sin
                columns = pl.ds(residue * lanes + start, width)
                waves_ref[here, columns] = real.astype(BF16)
                waves_ref[there, columns] = imag.astype(BF16)

            for residue in range(parts // 2 + 1):
                even, odd = range(0, parts, 2), range(1, parts, 2)
                cos_even = weighted([(cosine(parts, residue, block), blocks[block]) for block in even])
                cos_odd = weighted([(cosine(parts, residue, block), blocks[block]) for block in odd])
                sin_even = weighted([(sine(parts, residue, block), blocks[block]) for block in even])
                sin_odd = weighted([(sine(parts, residue, block), blocks[block]) for block in odd])
                sin_sum = plus(sin_even, sin_odd)
                store(residue, plus(cos_even, cos_odd), None if sin_sum is None else -sin_sum)
                if 0 < residue and 2 * residue != parts:
                    store(parts - residue, minus(cos_even, cos_odd), minus(sin_even, sin_odd))
        return carry

    lax.fori_loop(0, rows // chunk, spread, 0)
    for residue in range(parts):
        columns = pl.ds(residue * lanes, lanes)
        out_ref[:, columns] = jnp.dot(table_ref[...], waves_ref[:, columns], preferred_element_type=F32)


def forward(own, other, tables):
    chips, (_, rows, lanes) = 2 * own[0].shape[0], own[0].shape
    table, _, cos, sin = tables
    spectrum = (2 * rows, 2 * chips * lanes)
    return pl.pallas_call(
        functools.partial(forward_kernel, chips),
        in_specs=[WHOLE] * 7,
        out_specs=WHOLE,
        out_shape=jax.ShapeDtypeStruct(spectrum, F32),
        scratch_shapes=[pltpu.VMEM((2 * chips, rows, lanes), BF16), pltpu.VMEM(spectrum, BF16)],
        cost_estimate=CHEAP,
        compiler_params=pltpu.CompilerParams(vmem_limit_bytes=32 * 2**20),
        name="forward",
    )(cos, sin, table, *own, *other)


def backward_kernel(chips, offsets, cos_ref, sin_ref, table_ref, spectrum_ref, *refs):
    filter_refs, (keep_ref, *send_refs, filter_ref, product_ref, back_ref) = refs[:chips], refs[chips:]
    chip, core = own_place()
    parts = 2 * chips
    rows, lanes = keep_ref.shape[1:]
    chip_bits = chips.bit_length() - 1
    chunk, width = 16, 128
    for offset, ref in zip(offsets, filter_refs):
        for plane in range(filter_ref.shape[1]):
            filter_ref[chip ^ offset, plane] = ref[pl.ds(plane * rows, rows), :]

    for residue in range(parts):
        source, odd = bit_reversed(residue // 2, chip_bits), residue % 2
        columns = pl.ds(residue * lanes, lanes)
        filter_real = filter_ref[source, odd].astype(F32)
        filter_imag = filter_ref[source, 2 + odd].astype(F32)
        real = spectrum_ref[pl.ds(0, rows), columns]
        imag = spectrum_ref[pl.ds(rows, rows), columns]
        product_ref[pl.ds(0, rows), columns] = (real * filter_real - imag * filter_imag).astype(BF16)
        product_ref[pl.ds(rows, rows), columns] = (real * filter_imag + imag * filter_real).astype(BF16)
        back_ref[:, columns] = jnp.dot(table_ref[...], product_ref[:, columns], preferred_element_type=F32)

    scale = 1.0 / (2 * parts * rows)
    sign = (1 - 2 * core).astype(F32)
    upper = core == 1

    def gather(index, carry):
        here = block_at(index, chunk)
        there = pl.ds(pl.multiple_of(rows + index * chunk, chunk), chunk)
        cos_all, sin_all = cos_ref[core, here, :] * scale, sin_ref[core, here, :] * scale
        for start in range(0, lanes, width):
            reals, imags = [], []
            for residue in range(parts):
                columns = pl.ds(residue * lanes + start, width)
                real, imag = back_ref[here, columns], back_ref[there, columns]
                cos, sin = cos_all[:, residue : residue + 1], sin_all[:, residue : residue + 1]
                reals.append(real * cos - imag * sin)
                imags.append(real * sin + imag * cos)
            totals = [None] * parts
            for block in range(parts // 2 + 1):
                even, odd = range(0, parts, 2), range(1, parts, 2)
                cos_even = weighted([(cosine(parts, residue, block), reals[residue]) for residue in even])
                cos_odd = weighted([(cosine(parts, residue, block), reals[residue]) for residue in odd])
                sin_even = weighted([(sine(parts, residue, block), imags[residue]) for residue in even])
                sin_odd = weighted([(sine(parts, residue, block), imags[residue]) for residue in odd])
                totals[block] = minus(plus(cos_even, cos_odd), plus(sin_even, sin_odd))
                if 0 < block and 2 * block != parts:
                    totals[parts - block] = plus(minus(cos_even, cos_odd), minus(sin_even, sin_odd))
            lane = pl.ds(start, width)
            for pair in range(chips):
                low, high = totals[2 * pair], totals[2 * pair + 1] * sign
                keep_ref[pair, here, lane] = jnp.where(upper, high, low)
                part, place = divmod(pair, chips // 2)
                send_refs[part][place, here, lane] = jnp.where(upper, low, high).astype(BF16)
        return carry

    lax.fori_loop(0, rows // chunk, gather, 0)


def backward(spectrum, filters, offsets, tables):
    chips = len(filters)
    first = [filters[offset] for offset in offsets]
    rows, lanes = spectrum.shape[0] // 2, first[0].shape[1]
    _, table, cos, sin = tables
    half = jax.ShapeDtypeStruct((chips // 2, rows, lanes), BF16)
    return pl.pallas_call(
        functools.partial(backward_kernel, chips, offsets),
        in_specs=[WHOLE] * (4 + chips),
        out_specs=[WHOLE] * 3,
        out_shape=[jax.ShapeDtypeStruct((chips, rows, lanes), F32), half, half],
        scratch_shapes=[
            pltpu.VMEM((chips, 4, rows, lanes), BF16),
            pltpu.VMEM(spectrum.shape, BF16),
            pltpu.VMEM(spectrum.shape, F32),
        ],
        cost_estimate=CHEAP,
        compiler_params=pltpu.CompilerParams(vmem_limit_bytes=32 * 2**20),
        name="backward",
    )(cos, sin, table, spectrum, *first)


def gate_kernel(chips, skip_ref, keep_ref, low_ref, high_ref, *refs):
    signal_refs, gate_refs = refs[:chips], refs[chips : 2 * chips]
    out_ref, longer_ref, arrived_ref = refs[2 * chips :]
    chip, _ = own_place()
    rows, lanes = keep_ref.shape[1:]
    skip = skip_ref[:, block_at(chip, lanes)]
    arrived_ref[pl.ds(0, chips // 2)] = low_ref[...]
    arrived_ref[pl.ds(chips // 2, chips // 2)] = high_ref[...]
    for offset in range(chips):
        block = chip ^ offset
        convolved = keep_ref[block] + arrived_ref[block].astype(F32)
        signal = signal_refs[offset][pl.ds(0, rows), :].astype(F32)
        gate = gate_refs[offset][pl.ds(0, rows), :].astype(F32)
        gated = (gate * (convolved + skip * signal)).astype(BF16)
        out_ref[block_at(block, rows), :] = gated
        longer_ref[block_at(block, rows), :] = gated
    end = chips * rows
    longer_ref[pl.ds(end, longer_ref.shape[0] - end), :] = longer_ref[pl.ds(0, longer_ref.shape[0] - end), :]


def gate(skip, keep, arrived, first, gates, spare):
    chips, rows, lanes = keep.shape
    return pl.pallas_call(
        functools.partial(gate_kernel, chips),
        in_specs=[WHOLE] * (4 + 2 * chips),
        out_specs=[WHOLE] * 2,
        out_shape=[
            jax.ShapeDtypeStruct((chips * rows, lanes), BF16),
            jax.ShapeDtypeStruct((chips * rows + spare, lanes), BF16),
        ],
        scratch_shapes=[pltpu.VMEM((chips, rows, lanes), BF16)],
        cost_estimate=CHEAP,
        compiler_params=pltpu.CompilerParams(vmem_limit_bytes=6 * 2**20),
        name="gate",
    )(skip, keep, *arrived, *first, *gates)


def piece_of(ref, half, part):
    quarter, share = half // 2, ref.shape[1] // 2
    return ref[pl.ds(ref.shape[0] - quarter, quarter), pl.ds(part * share, share)]


def collect_kernel(in_refs, out_refs):
    rows = out_refs[0].shape[0]
    quarter = len(out_refs) * rows // (2 * len(in_refs))
    for place in range(2 * len(in_refs)):
        index, start = divmod(place * quarter, rows)
        out_refs[index][pl.ds(start, quarter), :] = piece_of(in_refs[place // 2], 2 * quarter, place % 2)


def collect(moved, half):
    count = len(moved)
    shape = (count * half // 2, moved[0].shape[1] // 2)
    return pl.pallas_call(
        lambda *refs: collect_kernel(refs[:count], refs[count:]),
        in_specs=[WHOLE] * count,
        out_specs=[WHOLE] * 2,
        out_shape=[jax.ShapeDtypeStruct(shape, BF16)] * 2,
        cost_estimate=CHEAP,
        compiler_params=pltpu.CompilerParams(vmem_limit_bytes=4 * 2**20),
        name="collect_weights",
    )(*moved)


def arrange_kernel(chips, mine_ref, *refs):
    moved_refs, (*other_refs, out_ref) = refs[: chips - 1], refs[chips - 1 :]
    chip, core = own_place()
    layer = lax.axis_index("chan")
    depth, share = mine_ref.shape
    quarter = depth // 4
    out_ref[:, block_at(chip ^ layer, share)] = mine_ref[...]
    for place in range(2 * (chips - 1)):
        offset, part = place // 2 + 1, place % 2
        columns = block_at(chip ^ layer ^ offset, share)
        index, start = divmod(place * quarter, other_refs[0].shape[0])
        out_ref[block_at(2 * core + part, quarter), columns] = piece_of(moved_refs[offset - 1], 2 * quarter, part)
        out_ref[block_at(2 * (1 - core) + part, quarter), columns] = other_refs[index][pl.ds(start, quarter), :]


def arrange(mine, moved, others):
    chips = len(moved) + 1
    depth, share = mine.shape
    return pl.pallas_call(
        functools.partial(arrange_kernel, chips),
        in_specs=[WHOLE] * (chips + len(others)),
        out_specs=WHOLE,
        out_shape=jax.ShapeDtypeStruct((depth, chips * share), BF16),
        cost_estimate=CHEAP,
        compiler_params=pltpu.CompilerParams(vmem_limit_bytes=8 * 2**20),
        name="arrange_weights",
    )(mine, *moved, *others)


def join_channels(chips, gated_refs, joined_ref):
    chip, _ = own_place()
    lanes = gated_refs[0].shape[1]
    for offset in range(chips):
        joined_ref[:, block_at(chip ^ offset, lanes)] = gated_refs[offset][pl.ds(0, joined_ref.shape[0]), :]


def project_moved_kernel(chips, weight_ref, *refs):
    gated_refs, (keep_ref, pass_ref, send_ref, joined_ref) = refs[:chips], refs[chips:]
    share = keep_ref.shape[1]
    join_channels(chips, gated_refs, joined_ref)
    partial = jnp.dot(joined_ref[...], weight_ref[...], preferred_element_type=F32).astype(BF16)
    keep_ref[...] = partial[:, :share]
    send_ref[0] = partial[:, share : 2 * share]
    pass_ref[...] = partial[:, 2 * share : 3 * share]
    send_ref[1] = partial[:, 3 * share :]


def project_moved(weight, gated):
    chips = len(gated)
    depth, columns = weight.shape
    rows = gated[0].shape[0]
    block = jax.ShapeDtypeStruct((rows, columns // chips), BF16)
    return pl.pallas_call(
        functools.partial(project_moved_kernel, chips),
        in_specs=[WHOLE] * (1 + chips),
        out_specs=[WHOLE] * 3,
        out_shape=[block, block, jax.ShapeDtypeStruct((2, rows, columns // chips), BF16)],
        scratch_shapes=[pltpu.VMEM((rows, depth), BF16)],
        cost_estimate=CHEAP,
        compiler_params=pltpu.CompilerParams(vmem_limit_bytes=8 * 2**20),
        name="project_moved",
    )(weight, *gated)


def project_still_kernel(chips, own_ref, other_ref, *refs):
    gated_refs, out_refs, joined_ref = refs[:chips], refs[chips : 2 * chips], refs[2 * chips]
    chip, core = own_place()
    rows = out_refs[0].shape[0]
    join_channels(chips, gated_refs, joined_ref)

    def project_with(weight_ref):
        for offset in range(chips):
            gated = joined_ref[block_at(chip ^ offset, rows), :]
            out_refs[offset][...] = jnp.dot(gated, weight_ref[...], preferred_element_type=F32).astype(BF16)

    @pl.when(core == 0)
    def _():
        project_with(other_ref)

    @pl.when(core == 1)
    def _():
        project_with(own_ref)


def project_still(own, other, gated):
    chips = len(gated)
    depth, held = own.shape
    rows = gated[0].shape[0] // chips
    return pl.pallas_call(
        functools.partial(project_still_kernel, chips),
        in_specs=[WHOLE] * (2 + chips),
        out_specs=[WHOLE] * chips,
        out_shape=[jax.ShapeDtypeStruct((rows, held), BF16)] * chips,
        scratch_shapes=[pltpu.VMEM((rows * chips, depth), BF16)],
        cost_estimate=CHEAP,
        compiler_params=pltpu.CompilerParams(vmem_limit_bytes=12 * 2**20),
        name="project_still",
    )(own, other, *gated)


def sort_kernel(chips, *refs):
    in_refs, (keep_ref, pass_ref, send_ref, sorted_ref) = refs[:chips], refs[chips:]
    chip, _ = own_place()
    layer = lax.axis_index("chan")
    for offset in range(chips):
        sorted_ref[chip ^ layer ^ offset] = in_refs[offset][...]
    keep_ref[...] = sorted_ref[0]
    send_ref[0] = sorted_ref[1]
    pass_ref[...] = sorted_ref[2]
    send_ref[1] = sorted_ref[3]


def sort_blocks(blocks):
    chips = len(blocks)
    block = jax.ShapeDtypeStruct(blocks[0].shape, BF16)
    return pl.pallas_call(
        functools.partial(sort_kernel, chips),
        in_specs=[WHOLE] * chips,
        out_specs=[WHOLE] * 3,
        out_shape=[block, block, jax.ShapeDtypeStruct((2, *block.shape), BF16)],
        scratch_shapes=[pltpu.VMEM((chips, *block.shape), BF16)],
        cost_estimate=CHEAP,
        compiler_params=pltpu.CompilerParams(vmem_limit_bytes=4 * 2**20),
        name="sort_blocks",
    )(*blocks)


def finish_kernel(chips, keep_ref, first_ref, second_ref, *out_refs):
    chip, _ = own_place()
    rows = out_refs[0].shape[0]
    for offset in range(chips):
        here = block_at(chip ^ offset, rows)
        total = keep_ref[here, :].astype(F32) + first_ref[0, here, :].astype(F32) + second_ref[here, :].astype(F32)
        out_refs[offset][...] = total.astype(BF16)


def finish(keep, first, second, chips):
    rows, columns = keep.shape
    return pl.pallas_call(
        functools.partial(finish_kernel, chips),
        in_specs=[WHOLE] * 3,
        out_specs=[WHOLE] * chips,
        out_shape=[jax.ShapeDtypeStruct((rows // chips, columns), BF16)] * chips,
        cost_estimate=CHEAP,
        compiler_params=pltpu.CompilerParams(vmem_limit_bytes=4 * 2**20),
        name="finish",
    )(keep, first, second)


def join_kernel(chips, keep_ref, first_ref, second_ref, *refs):
    in_refs, out_ref = refs[:chips], refs[chips]
    chip, _ = own_place()
    share = in_refs[0].shape[1]
    for offset in range(chips):
        out_ref[:, block_at(chip ^ offset, share)] = in_refs[offset][...]
    total = keep_ref[...].astype(F32) + first_ref[0].astype(F32) + second_ref[...].astype(F32)
    out_ref[:, pl.ds(chips * share, total.shape[1])] = total.astype(BF16)


def join(keep, first, second, blocks):
    chips = len(blocks)
    rows, share = blocks[0].shape
    return pl.pallas_call(
        functools.partial(join_kernel, chips),
        in_specs=[WHOLE] * (3 + chips),
        out_specs=WHOLE,
        out_shape=jax.ShapeDtypeStruct((rows, chips * share + keep.shape[1]), BF16),
        cost_estimate=CHEAP,
        compiler_params=pltpu.CompilerParams(vmem_limit_bytes=4 * 2**20),
        name="join",
    )(keep, first, second, *blocks)


def swapped(value, axis, offset):
    if not offset:
        return value
    return lax.ppermute(value, axis, [(source, source ^ offset) for source in range(lax.axis_size(axis))])


def to_chips(blocks):
    return [swapped(block, "seq", 2 * offset) for offset, block in enumerate(blocks)]


def after(value, *others):
    return lax.optimization_barrier((value, *others))[0]


def over_layers(passed, send):
    first = swapped(send, "chan", 1)
    passed = (passed.astype(F32) + first[1].astype(F32)).astype(BF16)
    return first, swapped(passed, "chan", 2)


def shards_direct(values_in, gate_values, filter_spectrum, skip_gain, out_weight):
    parts = lax.axis_size("seq")
    chips = parts // 2
    rows, width = values_in.shape
    tables = small_tables(parts, rows)

    values = pack_values(values_in, chips, 0)
    flat_filters = filter_spectrum.reshape(4, rows, width)
    early = pack_filters(after(flat_filters, values[0]), chips, (3,), 0)
    other_weight = swapped(out_weight, "seq", 1)
    late = pack_filters(after(flat_filters, early[0], other_weight), chips, (1, 2), 0)
    packed = dict(zip((3, 1, 2), (*early, *late)))
    *moved, mine = pack_moved(after(gate_values, late[0]), out_weight, other_weight, chips)
    (packed[0],) = pack_filters(after(flat_filters, moved[0]), chips, (0,), 0)
    values, filters = to_chips(values), to_chips([packed[offset] for offset in range(chips)])
    own = stack([after(block, packed[0]) for block in values], rows)
    spectrum = forward(own, [swapped(part, "seq", 1) for part in own], tables)
    moved = to_chips([after(block, spectrum) for block in moved])
    keep, *send = backward(spectrum, filters, (0, 1, 3, 2), tables)
    gated, longer = gate(skip_gain[None, :], keep, [swapped(part, "seq", 1) for part in send], values, moved, 16)
    gathered = to_chips([gated, longer, longer, gated])

    others = [swapped(part, "seq", 1) for part in collect([after(block, gated) for block in moved[1:]], out_weight.shape[0] // 2)]
    keep, passed, send = project_moved(arrange(mine, moved[1:], others), gathered)
    blocks = to_chips(finish(keep, *over_layers(passed, send), chips))
    keep, passed, send = sort_blocks(to_chips(project_still(out_weight, other_weight, gathered)))
    return join(keep, *over_layers(passed, send), blocks)


def shards(values_in, gate_values, filter_spectrum, skip_gain, out_weight):
    parts, layers = lax.axis_size("seq"), lax.axis_size("chan")
    rows, width = values_in.shape
    share = out_weight.shape[1] // layers
    aligned = width // parts % 128 == 0 and share % 128 == 0 and rows % 32 == 0
    run = shards_direct if aligned and layers == 4 and parts == 8 else shards_general
    return run(values_in, gate_values, filter_spectrum, skip_gain, out_weight)


def solution(mesh):
    in_specs = (
        P("seq", "chan"),
        P("seq", "chan"),
        P(None, "seq", None, "chan"),
        P("chan"),
        P("chan", "seq"),
    )
    out_specs = P("seq", "chan")
    return jax.shard_map(shards, mesh=mesh, in_specs=in_specs, out_specs=out_specs, check_vma=False)
```

```python
import functools

import jax
import jax.numpy as jnp
import numpy as np
from jax import lax
from jax.experimental import pallas as pl
from jax.experimental.pallas import tpu as pltpu
from jax.sharding import PartitionSpec as P

BF16 = jnp.bfloat16
F32 = jnp.float32


def bit_reversed(number, width_bits):
    flipped = 0
    for bit_place in range(width_bits):
        flipped |= (number >> bit_place & 1) << (width_bits - 1 - bit_place)
    return flipped


def filter_row(residue, width_bits):
    return 2 * bit_reversed(residue // 2, width_bits) + residue % 2


def dft_tables(parts, rows):
    total = 2 * parts * rows
    residue = np.arange(2 * parts)[:, None, None]
    column = np.arange(rows)[None, :, None]
    position = np.arange(rows)[None, None, :]
    phase = 2.0 * np.pi * (position * (residue + 2 * parts * column) % total) / total
    cos, sin = np.cos(phase), np.sin(phase)
    forward = np.concatenate(
        [np.concatenate([cos, sin], axis=2), np.concatenate([-sin, cos], axis=2)], axis=1
    )
    inverse = np.transpose(forward, (0, 2, 1)) / total
    return forward.astype(BF16), inverse.astype(BF16)


def convolve_kernel(parts, rows, moved_ref, skip_ref, forward_ref, inverse_ref, out_ref, waves_ref, back_ref):
    width_bits = parts.bit_length() - 1
    chunk = 16

    def cosine(residue, block):
        return float(np.cos(np.pi * residue * block / parts))

    def sine(residue, block):
        return float(np.sin(np.pi * residue * block / parts))

    def spread(index, carry):
        here = pl.ds(index * chunk, chunk)
        there = pl.ds(rows + index * chunk, chunk)
        blocks = [moved_ref[block, here, :].astype(F32) for block in range(parts)]
        for residue in range(parts + 1):
            real = blocks[0]
            imag = jnp.zeros_like(real)
            for block in range(1, parts):
                real = real + cosine(residue, block) * blocks[block]
                imag = imag - sine(residue, block) * blocks[block]
            waves_ref[residue, here, :] = real.astype(BF16)
            waves_ref[residue, there, :] = imag.astype(BF16)
            if 0 < residue < parts:
                waves_ref[2 * parts - residue, here, :] = real.astype(BF16)
                waves_ref[2 * parts - residue, there, :] = (-imag).astype(BF16)
        return carry

    lax.fori_loop(0, rows // chunk, spread, 0)

    def through(residue):
        wave = jnp.dot(forward_ref[residue], waves_ref[residue], preferred_element_type=F32)
        source, odd = divmod(filter_row(residue, width_bits), 2)
        filter_real = moved_ref[source, pl.ds((2 + odd) * rows, rows), :].astype(F32)
        filter_imag = moved_ref[source, pl.ds((4 + odd) * rows, rows), :].astype(F32)
        real, imag = wave[:rows], wave[rows:]
        product = jnp.concatenate(
            [real * filter_real - imag * filter_imag, real * filter_imag + imag * filter_real], axis=0
        )
        return jnp.dot(inverse_ref[residue], product.astype(BF16), preferred_element_type=F32)

    for residue in range(parts + 1):
        back = through(residue)
        if 0 < residue < parts:
            other = through(2 * parts - residue)
            back_ref[residue, pl.ds(0, rows), :] = back[:rows] + other[:rows]
            back_ref[residue, pl.ds(rows, rows), :] = back[rows:] - other[rows:]
        else:
            back_ref[residue] = back

    skip = skip_ref[...]

    def gather(index, carry):
        here = pl.ds(index * chunk, chunk)
        there = pl.ds(rows + index * chunk, chunk)
        reals = [back_ref[residue, here, :] for residue in range(parts + 1)]
        imags = [back_ref[residue, there, :] for residue in range(parts + 1)]
        for block in range(parts):
            total = reals[0]
            for residue in range(1, parts + 1):
                total = total + cosine(residue, block) * reals[residue]
                if residue < parts and block:
                    total = total - sine(residue, block) * imags[residue]
            signal = moved_ref[block, here, :].astype(F32)
            gate = moved_ref[block, pl.ds(rows + index * chunk, chunk), :].astype(F32)
            out_ref[block, here, :] = (gate * (total + skip * signal)).astype(BF16)
        return carry

    lax.fori_loop(0, rows // chunk, gather, 0)


def convolve(moved, skip):
    parts, stacked, width = moved.shape
    rows = stacked // 6
    forward, inverse = dft_tables(parts, rows)
    whole = pl.BlockSpec(memory_space=pltpu.VMEM)
    return pl.pallas_call(
        functools.partial(convolve_kernel, parts, rows),
        out_shape=jax.ShapeDtypeStruct((parts, rows, width), BF16),
        in_specs=[whole] * 4,
        out_specs=whole,
        scratch_shapes=[
            pltpu.VMEM((2 * parts, 2 * rows, width), BF16),
            pltpu.VMEM((parts + 1, 2 * rows, width), F32),
        ],
        compiler_params=pltpu.CompilerParams(vmem_limit_bytes=40 * 2**20),
    )(moved, skip[None, :], forward, inverse)


def shards_general(values_in, gate_values, filter_spectrum, skip_gain, out_weight):
    parts = lax.axis_size("seq")
    layers = lax.axis_size("chan")
    rows, width = values_in.shape
    lanes = width // parts
    device = lax.axis_index("seq")

    def by_channel(array):
        return jnp.transpose(array.reshape(array.shape[0], parts, lanes), (1, 0, 2))

    filters = filter_spectrum.astype(BF16).reshape(4 * rows, width)
    packed = jnp.concatenate([by_channel(values_in), by_channel(gate_values), by_channel(filters)], axis=1)
    moved = lax.all_to_all(packed, "seq", 0, 0)
    skip = lax.dynamic_slice_in_dim(skip_gain, device * lanes, lanes)
    gated = convolve(moved, skip)
    gathered = lax.all_gather(gated.reshape(parts * rows, lanes), "seq", axis=1, tiled=True)

    own_cols = out_weight.shape[1]
    share = own_cols * parts // layers // parts
    per_block = parts // layers
    pieces = own_cols // share
    group = device % per_block
    member = device // per_block
    weight = jnp.zeros_like(out_weight)
    for step in range(pieces):
        piece = (member + step) % pieces
        sent = lax.dynamic_slice_in_dim(out_weight, piece * share, share, 1)
        pairs = [
            (source, source % per_block * pieces + (source // per_block + step) % pieces) for source in range(parts)
        ]
        arrived = lax.ppermute(sent, "seq", pairs)
        block = (device % pieces - step) % pieces
        weight = lax.dynamic_update_slice_in_dim(weight, arrived, block * share, 1)
    partials = jnp.dot(gathered, weight, preferred_element_type=F32).astype(BF16)
    mixed = lax.psum_scatter(partials, "chan", scatter_dimension=1, tiled=True)
    return lax.all_to_all(mixed, "seq", 0, 1, tiled=True)


WHOLE = pl.BlockSpec(memory_space=pltpu.VMEM)
CHEAP = pl.CostEstimate(flops=0, transcendentals=0, bytes_accessed=0)


def small_tables(parts, rows):
    total = 2 * parts * rows
    index = np.arange(rows)
    phase = 2.0 * np.pi * (index[:, None] * index[None, :] % rows) / rows
    cos, sin = np.cos(phase), np.sin(phase)
    forward = np.block([[cos, sin], [-sin, cos]])
    residue = np.arange(2 * parts).reshape(2, 1, parts)
    turn = 2.0 * np.pi * index[None, :, None] * residue / total
    return forward.astype(BF16), forward.T.astype(BF16), np.cos(turn).astype(F32), np.sin(turn).astype(F32)


def cosine(parts, residue, block):
    return float(np.cos(np.pi * residue * block / parts))


def sine(parts, residue, block):
    return float(np.sin(np.pi * residue * block / parts))


def weighted(terms):
    total = None
    for factor, term in terms:
        if abs(factor) < 1e-12:
            continue
        part = term if factor == 1.0 else factor * term
        total = part if total is None else total + part
    return total


def plus(left, right):
    return left if right is None else right if left is None else left + right


def minus(left, right):
    return left if right is None else -right if left is None else left - right


def own_place():
    device = lax.axis_index("seq")
    return device // 2, device % 2


def block_at(index, size):
    return pl.ds(pl.multiple_of(index * size, size), size)


def pack_filters_kernel(offsets, filter_ref, *refs):
    out_refs, (plane_ref, arrived) = refs[: len(offsets)], refs[len(offsets) :]
    chip, _ = own_place()
    planes, rows, _ = filter_ref.shape
    lanes = out_refs[0].shape[1]
    copies = []
    for place, offset in enumerate(offsets):
        here = block_at(chip ^ offset, lanes)
        for plane in range(planes):
            copies.append(
                pltpu.make_async_copy(filter_ref.at[plane, :, here], plane_ref.at[place, plane], arrived.at[place, plane])
            )
    for copy in copies:
        copy.start()
    for index, copy in enumerate(copies):
        copy.wait()
        place, plane = divmod(index, planes)
        out_refs[place][pl.ds(plane * rows, rows), :] = plane_ref[place, plane].astype(BF16)
    used = planes * rows
    for out_ref in out_refs:
        if out_ref.shape[0] > used:
            out_ref[pl.ds(used, out_ref.shape[0] - used), :] = out_ref[pl.ds(0, out_ref.shape[0] - used), :]


def pack_filters(filters, chips, offsets, spare):
    planes, rows, width = filters.shape
    lanes = width // chips
    return pl.pallas_call(
        functools.partial(pack_filters_kernel, offsets),
        in_specs=[pl.BlockSpec(memory_space=pltpu.HBM)],
        out_specs=[WHOLE] * len(offsets),
        out_shape=[jax.ShapeDtypeStruct((planes * rows + spare, lanes), BF16)] * len(offsets),
        scratch_shapes=[
            pltpu.VMEM((len(offsets), planes, rows, lanes), F32),
            pltpu.SemaphoreType.DMA((len(offsets), planes)),
        ],
        cost_estimate=CHEAP,
        compiler_params=pltpu.CompilerParams(vmem_limit_bytes=8 * 2**20),
        name="pack_filters",
    )(pltpu.with_memory_space_constraint(filters, pltpu.HBM))


def pack_values_kernel(chips, values_ref, *refs):
    out_refs, arrived = refs[:chips], refs[chips]
    rows = values_ref.shape[0]
    chip, _ = own_place()
    copies = []
    for offset, out_ref in enumerate(out_refs):
        values = values_ref.at[:, block_at(chip ^ offset, out_ref.shape[1])]
        copies.append(pltpu.make_async_copy(values, out_ref.at[pl.ds(0, rows)], arrived.at[offset]))
    for copy in copies:
        copy.start()
    for copy in copies:
        copy.wait()


def pack_values(values_in, chips, spare):
    rows, width = values_in.shape
    return pl.pallas_call(
        functools.partial(pack_values_kernel, chips),
        in_specs=[pl.BlockSpec(memory_space=pltpu.HBM)],
        out_specs=[WHOLE] * chips,
        out_shape=[jax.ShapeDtypeStruct((rows + spare, width // chips), BF16)] * chips,
        scratch_shapes=[pltpu.SemaphoreType.DMA((chips,))],
        cost_estimate=CHEAP,
        compiler_params=pltpu.CompilerParams(vmem_limit_bytes=4 * 2**20),
        name="pack_values",
    )(pltpu.with_memory_space_constraint(values_in, pltpu.HBM))


def pack_moved_kernel(chips, gate_ref, own_ref, other_ref, *refs):
    out_refs, (mine_ref, arrived) = refs[:chips], refs[chips:]
    chip, core = own_place()
    rows = gate_ref.shape[0]
    depth, held = own_ref.shape
    quarter, share = depth // 4, held // chips

    def copies_from(weight_ref):
        copies = [pltpu.make_async_copy(weight_ref.at[:, block_at(chip, share)], mine_ref, arrived.at[0, 0])]
        for offset in range(chips):
            out_ref, target = out_refs[offset], chip ^ offset
            gates = gate_ref.at[:, block_at(target, out_ref.shape[1])]
            copies.append(pltpu.make_async_copy(gates, out_ref.at[pl.ds(0, rows)], arrived.at[offset, 2]))
            for part in range(2 if offset else 0):
                source = weight_ref.at[block_at(2 * core + part, quarter), block_at(target, share)]
                sink = out_ref.at[pl.ds(rows, quarter), pl.ds(part * share, share)]
                copies.append(pltpu.make_async_copy(source, sink, arrived.at[offset, part]))
        for copy in copies:
            copy.start()
        for copy in copies:
            copy.wait()

    @pl.when(core == 0)
    def _():
        copies_from(own_ref)

    @pl.when(core == 1)
    def _():
        copies_from(other_ref)


def pack_moved(gate_values, own, other, chips):
    rows, width = gate_values.shape
    depth, held = own.shape
    share = held // chips
    return pl.pallas_call(
        functools.partial(pack_moved_kernel, chips),
        in_specs=[pl.BlockSpec(memory_space=pltpu.HBM)] * 2 + [pl.BlockSpec(memory_space=pl.ANY)],
        out_specs=[WHOLE] * (chips + 1),
        out_shape=[
            *(jax.ShapeDtypeStruct((rows + (depth // 4 if offset else 0), 2 * share), BF16) for offset in range(chips)),
            jax.ShapeDtypeStruct((depth, share), BF16),
        ],
        scratch_shapes=[pltpu.SemaphoreType.DMA((chips, 3))],
        cost_estimate=CHEAP,
        compiler_params=pltpu.CompilerParams(vmem_limit_bytes=8 * 2**20),
        name="pack_moved",
    )(*(pltpu.with_memory_space_constraint(array, pltpu.HBM) for array in (gate_values, own)), other)


def stack_kernel(chips, *refs):
    in_refs, out_refs = refs[:chips], refs[chips:]
    for offset, in_ref in enumerate(in_refs):
        part, place = divmod(offset, chips // 2)
        out_refs[part][place] = in_ref[pl.ds(0, out_refs[part].shape[1]), :]


def stack(blocks, rows):
    chips = len(blocks)
    half = jax.ShapeDtypeStruct((chips // 2, rows, blocks[0].shape[1]), BF16)
    return pl.pallas_call(
        functools.partial(stack_kernel, chips),
        in_specs=[WHOLE] * chips,
        out_specs=[WHOLE] * 2,
        out_shape=[half, half],
        cost_estimate=CHEAP,
        compiler_params=pltpu.CompilerParams(vmem_limit_bytes=4 * 2**20),
        name="stack",
    )(*blocks)


def forward_kernel(chips, cos_ref, sin_ref, table_ref, *refs):
    own_refs, other_refs, (out_ref, signal_ref, waves_ref) = refs[:2], refs[2:4], refs[4:]
    chip, core = own_place()
    parts = 2 * chips
    rows, lanes = own_refs[0].shape[1:]
    chunk, width = 16, 128
    for offset in range(chips):
        part, place = divmod(offset, chips // 2)
        signal_ref[2 * (chip ^ offset) + core] = own_refs[part][place]
        signal_ref[2 * (chip ^ offset) + 1 - core] = other_refs[part][place]
    sign = (1 - 2 * core).astype(F32)

    def spread(index, carry):
        here = block_at(index, chunk)
        there = pl.ds(pl.multiple_of(rows + index * chunk, chunk), chunk)
        cos_all, sin_all = cos_ref[core, here, :], sin_ref[core, here, :]
        for start in range(0, lanes, width):
            blocks = [signal_ref[block, here, pl.ds(start, width)].astype(F32) for block in range(parts)]
            blocks = [block * sign if place % 2 else block for place, block in enumerate(blocks)]

            def store(residue, real, imag):
                cos, sin = cos_all[:, residue : residue + 1], sin_all[:, residue : residue + 1]
                if imag is None:
                    real, imag = real * cos, -(real * sin)
                else:
                    real, imag = real * cos + imag * sin, imag * cos - real * sin
                columns = pl.ds(residue * lanes + start, width)
                waves_ref[here, columns] = real.astype(BF16)
                waves_ref[there, columns] = imag.astype(BF16)

            for residue in range(parts // 2 + 1):
                even, odd = range(0, parts, 2), range(1, parts, 2)
                cos_even = weighted([(cosine(parts, residue, block), blocks[block]) for block in even])
                cos_odd = weighted([(cosine(parts, residue, block), blocks[block]) for block in odd])
                sin_even = weighted([(sine(parts, residue, block), blocks[block]) for block in even])
                sin_odd = weighted([(sine(parts, residue, block), blocks[block]) for block in odd])
                sin_sum = plus(sin_even, sin_odd)
                store(residue, plus(cos_even, cos_odd), None if sin_sum is None else -sin_sum)
                if 0 < residue and 2 * residue != parts:
                    store(parts - residue, minus(cos_even, cos_odd), minus(sin_even, sin_odd))
        return carry

    lax.fori_loop(0, rows // chunk, spread, 0)
    for residue in range(parts):
        columns = pl.ds(residue * lanes, lanes)
        out_ref[:, columns] = jnp.dot(table_ref[...], waves_ref[:, columns], preferred_element_type=F32)


def forward(own, other, tables):
    chips, (_, rows, lanes) = 2 * own[0].shape[0], own[0].shape
    table, _, cos, sin = tables
    spectrum = (2 * rows, 2 * chips * lanes)
    return pl.pallas_call(
        functools.partial(forward_kernel, chips),
        in_specs=[WHOLE] * 7,
        out_specs=WHOLE,
        out_shape=jax.ShapeDtypeStruct(spectrum, F32),
        scratch_shapes=[pltpu.VMEM((2 * chips, rows, lanes), BF16), pltpu.VMEM(spectrum, BF16)],
        cost_estimate=CHEAP,
        compiler_params=pltpu.CompilerParams(vmem_limit_bytes=32 * 2**20),
        name="forward",
    )(cos, sin, table, *own, *other)


def backward_kernel(chips, cos_ref, sin_ref, table_ref, spectrum_ref, *refs):
    filter_refs, (keep_ref, *send_refs, filter_ref, product_ref, back_ref) = refs[:chips], refs[chips:]
    chip, core = own_place()
    parts = 2 * chips
    rows, lanes = keep_ref.shape[1:]
    chip_bits = chips.bit_length() - 1
    chunk, width = 16, 128
    for offset in range(chips):
        for plane in range(filter_ref.shape[1]):
            filter_ref[chip ^ offset, plane] = filter_refs[offset][pl.ds(plane * rows, rows), :]

    for residue in range(parts):
        source, odd = bit_reversed(residue // 2, chip_bits), residue % 2
        columns = pl.ds(residue * lanes, lanes)
        filter_real = filter_ref[source, odd].astype(F32)
        filter_imag = filter_ref[source, 2 + odd].astype(F32)
        real = spectrum_ref[pl.ds(0, rows), columns]
        imag = spectrum_ref[pl.ds(rows, rows), columns]
        product_ref[pl.ds(0, rows), columns] = (real * filter_real - imag * filter_imag).astype(BF16)
        product_ref[pl.ds(rows, rows), columns] = (real * filter_imag + imag * filter_real).astype(BF16)
        back_ref[:, columns] = jnp.dot(table_ref[...], product_ref[:, columns], preferred_element_type=F32)

    scale = 1.0 / (2 * parts * rows)
    sign = (1 - 2 * core).astype(F32)
    upper = core == 1

    def gather(index, carry):
        here = block_at(index, chunk)
        there = pl.ds(pl.multiple_of(rows + index * chunk, chunk), chunk)
        cos_all, sin_all = cos_ref[core, here, :] * scale, sin_ref[core, here, :] * scale
        for start in range(0, lanes, width):
            reals, imags = [], []
            for residue in range(parts):
                columns = pl.ds(residue * lanes + start, width)
                real, imag = back_ref[here, columns], back_ref[there, columns]
                cos, sin = cos_all[:, residue : residue + 1], sin_all[:, residue : residue + 1]
                reals.append(real * cos - imag * sin)
                imags.append(real * sin + imag * cos)
            totals = [None] * parts
            for block in range(parts // 2 + 1):
                even, odd = range(0, parts, 2), range(1, parts, 2)
                cos_even = weighted([(cosine(parts, residue, block), reals[residue]) for residue in even])
                cos_odd = weighted([(cosine(parts, residue, block), reals[residue]) for residue in odd])
                sin_even = weighted([(sine(parts, residue, block), imags[residue]) for residue in even])
                sin_odd = weighted([(sine(parts, residue, block), imags[residue]) for residue in odd])
                totals[block] = minus(plus(cos_even, cos_odd), plus(sin_even, sin_odd))
                if 0 < block and 2 * block != parts:
                    totals[parts - block] = plus(minus(cos_even, cos_odd), minus(sin_even, sin_odd))
            lane = pl.ds(start, width)
            for pair in range(chips):
                low, high = totals[2 * pair], totals[2 * pair + 1] * sign
                keep_ref[pair, here, lane] = jnp.where(upper, high, low)
                part, place = divmod(pair, chips // 2)
                send_refs[part][place, here, lane] = jnp.where(upper, low, high).astype(BF16)
        return carry

    lax.fori_loop(0, rows // chunk, gather, 0)


def backward(spectrum, first, tables):
    chips = len(first)
    rows, lanes = spectrum.shape[0] // 2, first[0].shape[1]
    _, table, cos, sin = tables
    half = jax.ShapeDtypeStruct((chips // 2, rows, lanes), BF16)
    return pl.pallas_call(
        functools.partial(backward_kernel, chips),
        in_specs=[WHOLE] * (4 + chips),
        out_specs=[WHOLE] * 3,
        out_shape=[jax.ShapeDtypeStruct((chips, rows, lanes), F32), half, half],
        scratch_shapes=[
            pltpu.VMEM((chips, 4, rows, lanes), BF16),
            pltpu.VMEM(spectrum.shape, BF16),
            pltpu.VMEM(spectrum.shape, F32),
        ],
        cost_estimate=CHEAP,
        compiler_params=pltpu.CompilerParams(vmem_limit_bytes=32 * 2**20),
        name="backward",
    )(cos, sin, table, spectrum, *first)


def gate_kernel(chips, skip_ref, keep_ref, low_ref, high_ref, *refs):
    signal_refs, gate_refs = refs[:chips], refs[chips : 2 * chips]
    out_ref, longer_ref, arrived_ref = refs[2 * chips :]
    chip, _ = own_place()
    rows, lanes = keep_ref.shape[1:]
    skip = skip_ref[:, block_at(chip, lanes)]
    arrived_ref[pl.ds(0, chips // 2)] = low_ref[...]
    arrived_ref[pl.ds(chips // 2, chips // 2)] = high_ref[...]
    for offset in range(chips):
        block = chip ^ offset
        convolved = keep_ref[block] + arrived_ref[block].astype(F32)
        signal = signal_refs[offset][pl.ds(0, rows), :].astype(F32)
        gate = gate_refs[offset][pl.ds(0, rows), :].astype(F32)
        gated = (gate * (convolved + skip * signal)).astype(BF16)
        out_ref[block_at(block, rows), :] = gated
        longer_ref[block_at(block, rows), :] = gated
    end = chips * rows
    longer_ref[pl.ds(end, longer_ref.shape[0] - end), :] = longer_ref[pl.ds(0, longer_ref.shape[0] - end), :]


def gate(skip, keep, arrived, first, gates, spare):
    chips, rows, lanes = keep.shape
    return pl.pallas_call(
        functools.partial(gate_kernel, chips),
        in_specs=[WHOLE] * (4 + 2 * chips),
        out_specs=[WHOLE] * 2,
        out_shape=[
            jax.ShapeDtypeStruct((chips * rows, lanes), BF16),
            jax.ShapeDtypeStruct((chips * rows + spare, lanes), BF16),
        ],
        scratch_shapes=[pltpu.VMEM((chips, rows, lanes), BF16)],
        cost_estimate=CHEAP,
        compiler_params=pltpu.CompilerParams(vmem_limit_bytes=6 * 2**20),
        name="gate",
    )(skip, keep, *arrived, *first, *gates)


def piece_of(ref, half, part):
    quarter, share = half // 2, ref.shape[1] // 2
    return ref[pl.ds(ref.shape[0] - quarter, quarter), pl.ds(part * share, share)]


def collect_kernel(in_refs, out_refs):
    rows = out_refs[0].shape[0]
    quarter = len(out_refs) * rows // (2 * len(in_refs))
    for place in range(2 * len(in_refs)):
        index, start = divmod(place * quarter, rows)
        out_refs[index][pl.ds(start, quarter), :] = piece_of(in_refs[place // 2], 2 * quarter, place % 2)


def collect(moved, half):
    count = len(moved)
    shape = (count * half // 2, moved[0].shape[1] // 2)
    return pl.pallas_call(
        lambda *refs: collect_kernel(refs[:count], refs[count:]),
        in_specs=[WHOLE] * count,
        out_specs=[WHOLE] * 2,
        out_shape=[jax.ShapeDtypeStruct(shape, BF16)] * 2,
        cost_estimate=CHEAP,
        compiler_params=pltpu.CompilerParams(vmem_limit_bytes=4 * 2**20),
        name="collect_weights",
    )(*moved)


def arrange_kernel(chips, mine_ref, *refs):
    moved_refs, (*other_refs, out_ref) = refs[: chips - 1], refs[chips - 1 :]
    chip, core = own_place()
    layer = lax.axis_index("chan")
    depth, share = mine_ref.shape
    quarter = depth // 4
    out_ref[:, block_at(chip ^ layer, share)] = mine_ref[...]
    for place in range(2 * (chips - 1)):
        offset, part = place // 2 + 1, place % 2
        columns = block_at(chip ^ layer ^ offset, share)
        index, start = divmod(place * quarter, other_refs[0].shape[0])
        out_ref[block_at(2 * core + part, quarter), columns] = piece_of(moved_refs[offset - 1], 2 * quarter, part)
        out_ref[block_at(2 * (1 - core) + part, quarter), columns] = other_refs[index][pl.ds(start, quarter), :]


def arrange(mine, moved, others):
    chips = len(moved) + 1
    depth, share = mine.shape
    return pl.pallas_call(
        functools.partial(arrange_kernel, chips),
        in_specs=[WHOLE] * (chips + len(others)),
        out_specs=WHOLE,
        out_shape=jax.ShapeDtypeStruct((depth, chips * share), BF16),
        cost_estimate=CHEAP,
        compiler_params=pltpu.CompilerParams(vmem_limit_bytes=8 * 2**20),
        name="arrange_weights",
    )(mine, *moved, *others)


def join_channels(chips, gated_refs, joined_ref):
    chip, _ = own_place()
    lanes = gated_refs[0].shape[1]
    for offset in range(chips):
        joined_ref[:, block_at(chip ^ offset, lanes)] = gated_refs[offset][pl.ds(0, joined_ref.shape[0]), :]


def project_moved_kernel(chips, weight_ref, *refs):
    gated_refs, (keep_ref, pass_ref, send_ref, joined_ref) = refs[:chips], refs[chips:]
    share = keep_ref.shape[1]
    join_channels(chips, gated_refs, joined_ref)
    partial = jnp.dot(joined_ref[...], weight_ref[...], preferred_element_type=F32).astype(BF16)
    keep_ref[...] = partial[:, :share]
    send_ref[0] = partial[:, share : 2 * share]
    pass_ref[...] = partial[:, 2 * share : 3 * share]
    send_ref[1] = partial[:, 3 * share :]


def project_moved(weight, gated):
    chips = len(gated)
    depth, columns = weight.shape
    rows = gated[0].shape[0]
    block = jax.ShapeDtypeStruct((rows, columns // chips), BF16)
    return pl.pallas_call(
        functools.partial(project_moved_kernel, chips),
        in_specs=[WHOLE] * (1 + chips),
        out_specs=[WHOLE] * 3,
        out_shape=[block, block, jax.ShapeDtypeStruct((2, rows, columns // chips), BF16)],
        scratch_shapes=[pltpu.VMEM((rows, depth), BF16)],
        cost_estimate=CHEAP,
        compiler_params=pltpu.CompilerParams(vmem_limit_bytes=8 * 2**20),
        name="project_moved",
    )(weight, *gated)


def project_still_kernel(chips, own_ref, other_ref, *refs):
    gated_refs, out_refs, joined_ref = refs[:chips], refs[chips : 2 * chips], refs[2 * chips]
    chip, core = own_place()
    rows = out_refs[0].shape[0]
    join_channels(chips, gated_refs, joined_ref)

    def project_with(weight_ref):
        for offset in range(chips):
            gated = joined_ref[block_at(chip ^ offset, rows), :]
            out_refs[offset][...] = jnp.dot(gated, weight_ref[...], preferred_element_type=F32).astype(BF16)

    @pl.when(core == 0)
    def _():
        project_with(other_ref)

    @pl.when(core == 1)
    def _():
        project_with(own_ref)


def project_still(own, other, gated):
    chips = len(gated)
    depth, held = own.shape
    rows = gated[0].shape[0] // chips
    return pl.pallas_call(
        functools.partial(project_still_kernel, chips),
        in_specs=[WHOLE] * (2 + chips),
        out_specs=[WHOLE] * chips,
        out_shape=[jax.ShapeDtypeStruct((rows, held), BF16)] * chips,
        scratch_shapes=[pltpu.VMEM((rows * chips, depth), BF16)],
        cost_estimate=CHEAP,
        compiler_params=pltpu.CompilerParams(vmem_limit_bytes=12 * 2**20),
        name="project_still",
    )(own, other, *gated)


def sort_kernel(chips, *refs):
    in_refs, (*out_refs, sorted_ref) = refs[:chips], refs[chips:]
    chip, _ = own_place()
    layer = lax.axis_index("chan")
    for offset in range(chips):
        sorted_ref[chip ^ layer ^ offset] = in_refs[offset][...]
    for target, out_ref in enumerate(out_refs):
        out_ref[...] = sorted_ref[target]


def sort_blocks(blocks):
    chips = len(blocks)
    block = jax.ShapeDtypeStruct(blocks[0].shape, BF16)
    return pl.pallas_call(
        functools.partial(sort_kernel, chips),
        in_specs=[WHOLE] * chips,
        out_specs=[WHOLE] * chips,
        out_shape=[block] * chips,
        scratch_shapes=[pltpu.VMEM((chips, *block.shape), BF16)],
        cost_estimate=CHEAP,
        compiler_params=pltpu.CompilerParams(vmem_limit_bytes=4 * 2**20),
        name="sort_blocks",
    )(*blocks)


def add_kernel(left_ref, right_ref, out_ref):
    rows = left_ref.shape[0]
    total = (left_ref[...].astype(F32) + right_ref[...].astype(F32)).astype(BF16)
    out_ref[pl.ds(0, rows), :] = total
    more = out_ref.shape[0] - rows
    if more:
        out_ref[pl.ds(rows, more), :] = total[:more]


def add(left, right, spare):
    rows, columns = left.shape
    return pl.pallas_call(
        add_kernel,
        in_specs=[WHOLE] * 2,
        out_specs=WHOLE,
        out_shape=jax.ShapeDtypeStruct((rows + spare, columns), BF16),
        cost_estimate=CHEAP,
        compiler_params=pltpu.CompilerParams(vmem_limit_bytes=4 * 2**20),
        name="add",
    )(left, right)


def finish_kernel(chips, keep_ref, first_ref, second_ref, *out_refs):
    chip, _ = own_place()
    rows = out_refs[0].shape[0]
    for offset in range(chips):
        here = block_at(chip ^ offset, rows)
        total = keep_ref[here, :].astype(F32) + first_ref[0, here, :].astype(F32) + second_ref[here, :].astype(F32)
        out_refs[offset][...] = total.astype(BF16)


def finish(keep, first, second, chips):
    rows, columns = keep.shape
    return pl.pallas_call(
        functools.partial(finish_kernel, chips),
        in_specs=[WHOLE] * 3,
        out_specs=[WHOLE] * chips,
        out_shape=[jax.ShapeDtypeStruct((rows // chips, columns), BF16)] * chips,
        cost_estimate=CHEAP,
        compiler_params=pltpu.CompilerParams(vmem_limit_bytes=4 * 2**20),
        name="finish",
    )(keep, first, second)


def join_kernel(chips, keep_ref, first_ref, second_ref, *refs):
    in_refs, out_ref = refs[:chips], refs[chips]
    chip, _ = own_place()
    share = in_refs[0].shape[1]
    for offset in range(chips):
        out_ref[:, block_at(chip ^ offset, share)] = in_refs[offset][...]
    total = keep_ref[...].astype(F32) + first_ref[...].astype(F32)
    total = total + second_ref[pl.ds(0, total.shape[0]), :].astype(F32)
    out_ref[:, pl.ds(chips * share, total.shape[1])] = total.astype(BF16)


def join(keep, first, second, blocks):
    chips = len(blocks)
    rows, share = blocks[0].shape
    return pl.pallas_call(
        functools.partial(join_kernel, chips),
        in_specs=[WHOLE] * (3 + chips),
        out_specs=WHOLE,
        out_shape=jax.ShapeDtypeStruct((rows, chips * share + keep.shape[1]), BF16),
        cost_estimate=CHEAP,
        compiler_params=pltpu.CompilerParams(vmem_limit_bytes=4 * 2**20),
        name="join",
    )(keep, first, second, *blocks)


def swapped(value, axis, offset):
    if not offset:
        return value
    return lax.ppermute(value, axis, [(source, source ^ offset) for source in range(lax.axis_size(axis))])


def to_chips(blocks):
    return [swapped(block, "seq", 2 * offset) for offset, block in enumerate(blocks)]


def after(value, *others):
    return lax.optimization_barrier((value, *others))[0]


def over_layers(passed, send):
    first = swapped(send, "chan", 1)
    passed = (passed.astype(F32) + first[1].astype(F32)).astype(BF16)
    return first, swapped(passed, "chan", 2)


def shards_direct(values_in, gate_values, filter_spectrum, skip_gain, out_weight):
    parts = lax.axis_size("seq")
    chips = parts // 2
    rows, width = values_in.shape
    tables = small_tables(parts, rows)

    values = pack_values(values_in, chips, 0)
    flat_filters = filter_spectrum.reshape(4, rows, width)
    near = pack_filters(after(flat_filters, values[0]), chips, (1, 2), 0)
    other_weight = swapped(out_weight, "seq", 1)
    *moved, mine = pack_moved(after(gate_values, near[0]), out_weight, other_weight, chips)
    own, far = pack_filters(after(flat_filters, moved[0]), chips, (0, 3), 0)
    values, filters = to_chips(values), to_chips([own, *near, far])
    own = stack([after(block, far) for block in values], rows)
    spectrum = forward(own, [swapped(part, "seq", 1) for part in own], tables)
    moved = to_chips([after(block, spectrum) for block in moved])
    keep, *send = backward(spectrum, filters, tables)
    gated, longer = gate(skip_gain[None, :], keep, [swapped(part, "seq", 1) for part in send], values, moved, 16)
    gathered = to_chips([gated, longer, longer, gated])

    others = [swapped(part, "seq", 1) for part in collect([after(block, gated) for block in moved[1:]], out_weight.shape[0] // 2)]
    keep, passed, send = project_moved(arrange(mine, moved[1:], others), gathered)
    blocks = to_chips(finish(keep, *over_layers(passed, send), chips))
    keep, near, passed, far = sort_blocks(to_chips(project_still(out_weight, other_weight, gathered)))
    second = swapped(add(passed, swapped(far, "chan", 1), 0), "chan", 2)
    return join(keep, swapped(near, "chan", 1), second, blocks)


def shards(values_in, gate_values, filter_spectrum, skip_gain, out_weight):
    parts, layers = lax.axis_size("seq"), lax.axis_size("chan")
    rows, width = values_in.shape
    share = out_weight.shape[1] // layers
    aligned = width // parts % 128 == 0 and share % 128 == 0 and rows % 32 == 0
    run = shards_direct if aligned and layers == 4 and parts == 8 else shards_general
    return run(values_in, gate_values, filter_spectrum, skip_gain, out_weight)


def solution(mesh):
    in_specs = (
        P("seq", "chan"),
        P("seq", "chan"),
        P(None, "seq", None, "chan"),
        P("chan"),
        P("chan", "seq"),
    )
    out_specs = P("seq", "chan")
    return jax.shard_map(shards, mesh=mesh, in_specs=in_specs, out_specs=out_specs, check_vma=False)
```

```python
import functools

import jax
import jax.numpy as jnp
import numpy as np
from jax import lax
from jax.experimental import pallas as pl
from jax.experimental.pallas import tpu as pltpu
from jax.sharding import PartitionSpec as P

BF16 = jnp.bfloat16
F32 = jnp.float32


def bit_reversed(number, width_bits):
    flipped = 0
    for bit_place in range(width_bits):
        flipped |= (number >> bit_place & 1) << (width_bits - 1 - bit_place)
    return flipped


def filter_row(residue, width_bits):
    return 2 * bit_reversed(residue // 2, width_bits) + residue % 2


def dft_tables(parts, rows):
    total = 2 * parts * rows
    residue = np.arange(2 * parts)[:, None, None]
    column = np.arange(rows)[None, :, None]
    position = np.arange(rows)[None, None, :]
    phase = 2.0 * np.pi * (position * (residue + 2 * parts * column) % total) / total
    cos, sin = np.cos(phase), np.sin(phase)
    forward = np.concatenate(
        [np.concatenate([cos, sin], axis=2), np.concatenate([-sin, cos], axis=2)], axis=1
    )
    inverse = np.transpose(forward, (0, 2, 1)) / total
    return forward.astype(BF16), inverse.astype(BF16)


def convolve_kernel(parts, rows, moved_ref, skip_ref, forward_ref, inverse_ref, out_ref, waves_ref, back_ref):
    width_bits = parts.bit_length() - 1
    chunk = 16

    def cosine(residue, block):
        return float(np.cos(np.pi * residue * block / parts))

    def sine(residue, block):
        return float(np.sin(np.pi * residue * block / parts))

    def spread(index, carry):
        here = pl.ds(index * chunk, chunk)
        there = pl.ds(rows + index * chunk, chunk)
        blocks = [moved_ref[block, here, :].astype(F32) for block in range(parts)]
        for residue in range(parts + 1):
            real = blocks[0]
            imag = jnp.zeros_like(real)
            for block in range(1, parts):
                real = real + cosine(residue, block) * blocks[block]
                imag = imag - sine(residue, block) * blocks[block]
            waves_ref[residue, here, :] = real.astype(BF16)
            waves_ref[residue, there, :] = imag.astype(BF16)
            if 0 < residue < parts:
                waves_ref[2 * parts - residue, here, :] = real.astype(BF16)
                waves_ref[2 * parts - residue, there, :] = (-imag).astype(BF16)
        return carry

    lax.fori_loop(0, rows // chunk, spread, 0)

    def through(residue):
        wave = jnp.dot(forward_ref[residue], waves_ref[residue], preferred_element_type=F32)
        source, odd = divmod(filter_row(residue, width_bits), 2)
        filter_real = moved_ref[source, pl.ds((2 + odd) * rows, rows), :].astype(F32)
        filter_imag = moved_ref[source, pl.ds((4 + odd) * rows, rows), :].astype(F32)
        real, imag = wave[:rows], wave[rows:]
        product = jnp.concatenate(
            [real * filter_real - imag * filter_imag, real * filter_imag + imag * filter_real], axis=0
        )
        return jnp.dot(inverse_ref[residue], product.astype(BF16), preferred_element_type=F32)

    for residue in range(parts + 1):
        back = through(residue)
        if 0 < residue < parts:
            other = through(2 * parts - residue)
            back_ref[residue, pl.ds(0, rows), :] = back[:rows] + other[:rows]
            back_ref[residue, pl.ds(rows, rows), :] = back[rows:] - other[rows:]
        else:
            back_ref[residue] = back

    skip = skip_ref[...]

    def gather(index, carry):
        here = pl.ds(index * chunk, chunk)
        there = pl.ds(rows + index * chunk, chunk)
        reals = [back_ref[residue, here, :] for residue in range(parts + 1)]
        imags = [back_ref[residue, there, :] for residue in range(parts + 1)]
        for block in range(parts):
            total = reals[0]
            for residue in range(1, parts + 1):
                total = total + cosine(residue, block) * reals[residue]
                if residue < parts and block:
                    total = total - sine(residue, block) * imags[residue]
            signal = moved_ref[block, here, :].astype(F32)
            gate = moved_ref[block, pl.ds(rows + index * chunk, chunk), :].astype(F32)
            out_ref[block, here, :] = (gate * (total + skip * signal)).astype(BF16)
        return carry

    lax.fori_loop(0, rows // chunk, gather, 0)


def convolve(moved, skip):
    parts, stacked, width = moved.shape
    rows = stacked // 6
    forward, inverse = dft_tables(parts, rows)
    whole = pl.BlockSpec(memory_space=pltpu.VMEM)
    return pl.pallas_call(
        functools.partial(convolve_kernel, parts, rows),
        out_shape=jax.ShapeDtypeStruct((parts, rows, width), BF16),
        in_specs=[whole] * 4,
        out_specs=whole,
        scratch_shapes=[
            pltpu.VMEM((2 * parts, 2 * rows, width), BF16),
            pltpu.VMEM((parts + 1, 2 * rows, width), F32),
        ],
        compiler_params=pltpu.CompilerParams(vmem_limit_bytes=40 * 2**20),
    )(moved, skip[None, :], forward, inverse)


def shards_general(values_in, gate_values, filter_spectrum, skip_gain, out_weight):
    parts = lax.axis_size("seq")
    layers = lax.axis_size("chan")
    rows, width = values_in.shape
    lanes = width // parts
    device = lax.axis_index("seq")

    def by_channel(array):
        return jnp.transpose(array.reshape(array.shape[0], parts, lanes), (1, 0, 2))

    filters = filter_spectrum.astype(BF16).reshape(4 * rows, width)
    packed = jnp.concatenate([by_channel(values_in), by_channel(gate_values), by_channel(filters)], axis=1)
    moved = lax.all_to_all(packed, "seq", 0, 0)
    skip = lax.dynamic_slice_in_dim(skip_gain, device * lanes, lanes)
    gated = convolve(moved, skip)
    gathered = lax.all_gather(gated.reshape(parts * rows, lanes), "seq", axis=1, tiled=True)

    own_cols = out_weight.shape[1]
    share = own_cols * parts // layers // parts
    per_block = parts // layers
    pieces = own_cols // share
    group = device % per_block
    member = device // per_block
    weight = jnp.zeros_like(out_weight)
    for step in range(pieces):
        piece = (member + step) % pieces
        sent = lax.dynamic_slice_in_dim(out_weight, piece * share, share, 1)
        pairs = [
            (source, source % per_block * pieces + (source // per_block + step) % pieces) for source in range(parts)
        ]
        arrived = lax.ppermute(sent, "seq", pairs)
        block = (device % pieces - step) % pieces
        weight = lax.dynamic_update_slice_in_dim(weight, arrived, block * share, 1)
    partials = jnp.dot(gathered, weight, preferred_element_type=F32).astype(BF16)
    mixed = lax.psum_scatter(partials, "chan", scatter_dimension=1, tiled=True)
    return lax.all_to_all(mixed, "seq", 0, 1, tiled=True)


WHOLE = pl.BlockSpec(memory_space=pltpu.VMEM)
CHEAP = pl.CostEstimate(flops=0, transcendentals=0, bytes_accessed=0)


def small_tables(parts, rows):
    total = 2 * parts * rows
    index = np.arange(rows)
    phase = 2.0 * np.pi * (index[:, None] * index[None, :] % rows) / rows
    cos, sin = np.cos(phase), np.sin(phase)
    forward = np.block([[cos, sin], [-sin, cos]])
    residue = np.arange(2 * parts).reshape(2, 1, parts)
    turn = 2.0 * np.pi * index[None, :, None] * residue / total
    return forward.astype(BF16), forward.T.astype(BF16), np.cos(turn).astype(F32), np.sin(turn).astype(F32)


def cosine(parts, residue, block):
    return float(np.cos(np.pi * residue * block / parts))


def sine(parts, residue, block):
    return float(np.sin(np.pi * residue * block / parts))


def weighted(terms):
    total = None
    for factor, term in terms:
        if abs(factor) < 1e-12:
            continue
        part = term if factor == 1.0 else factor * term
        total = part if total is None else total + part
    return total


def plus(left, right):
    return left if right is None else right if left is None else left + right


def minus(left, right):
    return left if right is None else -right if left is None else left - right


def own_place():
    device = lax.axis_index("seq")
    return device // 2, device % 2


def block_at(index, size):
    return pl.ds(pl.multiple_of(index * size, size), size)


def pack_filters_kernel(offsets, filter_ref, *refs):
    out_refs, (plane_ref, arrived) = refs[: len(offsets)], refs[len(offsets) :]
    chip, _ = own_place()
    planes, rows, _ = filter_ref.shape
    lanes = out_refs[0].shape[1]
    copies = []
    for place, offset in enumerate(offsets):
        here = block_at(chip ^ offset, lanes)
        for plane in range(planes):
            copies.append(
                pltpu.make_async_copy(filter_ref.at[plane, :, here], plane_ref.at[place, plane], arrived.at[place, plane])
            )
    for copy in copies:
        copy.start()
    for index, copy in enumerate(copies):
        copy.wait()
        place, plane = divmod(index, planes)
        out_refs[place][pl.ds(plane * rows, rows), :] = plane_ref[place, plane].astype(BF16)
    used = planes * rows
    for out_ref in out_refs:
        if out_ref.shape[0] > used:
            out_ref[pl.ds(used, out_ref.shape[0] - used), :] = out_ref[pl.ds(0, out_ref.shape[0] - used), :]


def pack_filters(filters, chips, offsets, spare):
    planes, rows, width = filters.shape
    lanes = width // chips
    return pl.pallas_call(
        functools.partial(pack_filters_kernel, offsets),
        in_specs=[pl.BlockSpec(memory_space=pltpu.HBM)],
        out_specs=[WHOLE] * len(offsets),
        out_shape=[jax.ShapeDtypeStruct((planes * rows + spare, lanes), BF16)] * len(offsets),
        scratch_shapes=[
            pltpu.VMEM((len(offsets), planes, rows, lanes), F32),
            pltpu.SemaphoreType.DMA((len(offsets), planes)),
        ],
        cost_estimate=CHEAP,
        compiler_params=pltpu.CompilerParams(vmem_limit_bytes=8 * 2**20),
        name="pack_filters",
    )(pltpu.with_memory_space_constraint(filters, pltpu.HBM))


def pack_values_kernel(chips, values_ref, *refs):
    out_refs, arrived = refs[:chips], refs[chips]
    rows = values_ref.shape[0]
    chip, _ = own_place()
    copies = []
    for offset, out_ref in enumerate(out_refs):
        values = values_ref.at[:, block_at(chip ^ offset, out_ref.shape[1])]
        copies.append(pltpu.make_async_copy(values, out_ref.at[pl.ds(0, rows)], arrived.at[offset]))
    for copy in copies:
        copy.start()
    for copy in copies:
        copy.wait()


def pack_values(values_in, chips, spare):
    rows, width = values_in.shape
    return pl.pallas_call(
        functools.partial(pack_values_kernel, chips),
        in_specs=[pl.BlockSpec(memory_space=pltpu.HBM)],
        out_specs=[WHOLE] * chips,
        out_shape=[jax.ShapeDtypeStruct((rows + spare, width // chips), BF16)] * chips,
        scratch_shapes=[pltpu.SemaphoreType.DMA((chips,))],
        cost_estimate=CHEAP,
        compiler_params=pltpu.CompilerParams(vmem_limit_bytes=4 * 2**20),
        name="pack_values",
    )(pltpu.with_memory_space_constraint(values_in, pltpu.HBM))


def pack_moved_kernel(chips, gate_ref, own_ref, other_ref, *refs):
    out_refs, (mine_ref, arrived) = refs[:chips], refs[chips:]
    chip, core = own_place()
    rows = gate_ref.shape[0]
    depth, held = own_ref.shape
    quarter, share = depth // 4, held // chips

    def copies_from(weight_ref):
        copies = [pltpu.make_async_copy(weight_ref.at[:, block_at(chip, share)], mine_ref, arrived.at[0, 0])]
        for offset in range(chips):
            out_ref, target = out_refs[offset], chip ^ offset
            gates = gate_ref.at[:, block_at(target, out_ref.shape[1])]
            copies.append(pltpu.make_async_copy(gates, out_ref.at[pl.ds(0, rows)], arrived.at[offset, 2]))
            for part in range(2 if offset else 0):
                source = weight_ref.at[block_at(2 * core + part, quarter), block_at(target, share)]
                sink = out_ref.at[pl.ds(rows, quarter), pl.ds(part * share, share)]
                copies.append(pltpu.make_async_copy(source, sink, arrived.at[offset, part]))
        for copy in copies:
            copy.start()
        for copy in copies:
            copy.wait()

    @pl.when(core == 0)
    def _():
        copies_from(own_ref)

    @pl.when(core == 1)
    def _():
        copies_from(other_ref)


def pack_moved(gate_values, own, other, chips):
    rows, width = gate_values.shape
    depth, held = own.shape
    share = held // chips
    return pl.pallas_call(
        functools.partial(pack_moved_kernel, chips),
        in_specs=[pl.BlockSpec(memory_space=pltpu.HBM)] * 2 + [pl.BlockSpec(memory_space=pl.ANY)],
        out_specs=[WHOLE] * (chips + 1),
        out_shape=[
            *(jax.ShapeDtypeStruct((rows + (depth // 4 if offset else 0), 2 * share), BF16) for offset in range(chips)),
            jax.ShapeDtypeStruct((depth, share), BF16),
        ],
        scratch_shapes=[pltpu.SemaphoreType.DMA((chips, 3))],
        cost_estimate=CHEAP,
        compiler_params=pltpu.CompilerParams(vmem_limit_bytes=8 * 2**20),
        name="pack_moved",
    )(*(pltpu.with_memory_space_constraint(array, pltpu.HBM) for array in (gate_values, own)), other)


def stack_kernel(chips, *refs):
    in_refs, out_refs = refs[:chips], refs[chips:]
    for offset, in_ref in enumerate(in_refs):
        part, place = divmod(offset, chips // 2)
        out_refs[part][place] = in_ref[pl.ds(0, out_refs[part].shape[1]), :]


def stack(blocks, rows):
    chips = len(blocks)
    half = jax.ShapeDtypeStruct((chips // 2, rows, blocks[0].shape[1]), BF16)
    return pl.pallas_call(
        functools.partial(stack_kernel, chips),
        in_specs=[WHOLE] * chips,
        out_specs=[WHOLE] * 2,
        out_shape=[half, half],
        cost_estimate=CHEAP,
        compiler_params=pltpu.CompilerParams(vmem_limit_bytes=4 * 2**20),
        name="stack",
    )(*blocks)


def forward_kernel(chips, cos_ref, sin_ref, table_ref, *refs):
    own_refs, other_refs, (out_ref, signal_ref, waves_ref) = refs[:2], refs[2:4], refs[4:]
    chip, core = own_place()
    parts = 2 * chips
    rows, lanes = own_refs[0].shape[1:]
    chunk, width = 16, 128
    for offset in range(chips):
        part, place = divmod(offset, chips // 2)
        signal_ref[2 * (chip ^ offset) + core] = own_refs[part][place]
        signal_ref[2 * (chip ^ offset) + 1 - core] = other_refs[part][place]
    sign = (1 - 2 * core).astype(F32)

    def spread(index, carry):
        here = block_at(index, chunk)
        there = pl.ds(pl.multiple_of(rows + index * chunk, chunk), chunk)
        cos_all, sin_all = cos_ref[core, here, :], sin_ref[core, here, :]
        for start in range(0, lanes, width):
            blocks = [signal_ref[block, here, pl.ds(start, width)].astype(F32) for block in range(parts)]
            blocks = [block * sign if place % 2 else block for place, block in enumerate(blocks)]

            def store(residue, real, imag):
                cos, sin = cos_all[:, residue : residue + 1], sin_all[:, residue : residue + 1]
                if imag is None:
                    real, imag = real * cos, -(real * sin)
                else:
                    real, imag = real * cos + imag * sin, imag * cos - real * sin
                columns = pl.ds(residue * lanes + start, width)
                waves_ref[here, columns] = real.astype(BF16)
                waves_ref[there, columns] = imag.astype(BF16)

            for residue in range(parts // 2 + 1):
                even, odd = range(0, parts, 2), range(1, parts, 2)
                cos_even = weighted([(cosine(parts, residue, block), blocks[block]) for block in even])
                cos_odd = weighted([(cosine(parts, residue, block), blocks[block]) for block in odd])
                sin_even = weighted([(sine(parts, residue, block), blocks[block]) for block in even])
                sin_odd = weighted([(sine(parts, residue, block), blocks[block]) for block in odd])
                sin_sum = plus(sin_even, sin_odd)
                store(residue, plus(cos_even, cos_odd), None if sin_sum is None else -sin_sum)
                if 0 < residue and 2 * residue != parts:
                    store(parts - residue, minus(cos_even, cos_odd), minus(sin_even, sin_odd))
        return carry

    lax.fori_loop(0, rows // chunk, spread, 0)
    for residue in range(parts):
        columns = pl.ds(residue * lanes, lanes)
        out_ref[:, columns] = jnp.dot(table_ref[...], waves_ref[:, columns], preferred_element_type=F32)


def forward(own, other, tables):
    chips, (_, rows, lanes) = 2 * own[0].shape[0], own[0].shape
    table, _, cos, sin = tables
    spectrum = (2 * rows, 2 * chips * lanes)
    return pl.pallas_call(
        functools.partial(forward_kernel, chips),
        in_specs=[WHOLE] * 7,
        out_specs=WHOLE,
        out_shape=jax.ShapeDtypeStruct(spectrum, F32),
        scratch_shapes=[pltpu.VMEM((2 * chips, rows, lanes), BF16), pltpu.VMEM(spectrum, BF16)],
        cost_estimate=CHEAP,
        compiler_params=pltpu.CompilerParams(vmem_limit_bytes=32 * 2**20),
        name="forward",
    )(cos, sin, table, *own, *other)


def backward_kernel(chips, cos_ref, sin_ref, table_ref, spectrum_ref, *refs):
    filter_refs, (keep_ref, *send_refs, filter_ref, product_ref, back_ref) = refs[:chips], refs[chips:]
    chip, core = own_place()
    parts = 2 * chips
    rows, lanes = keep_ref.shape[1:]
    chip_bits = chips.bit_length() - 1
    chunk, width = 16, 128
    for offset in range(chips):
        for plane in range(filter_ref.shape[1]):
            filter_ref[chip ^ offset, plane] = filter_refs[offset][pl.ds(plane * rows, rows), :]

    for residue in range(parts):
        source, odd = bit_reversed(residue // 2, chip_bits), residue % 2
        columns = pl.ds(residue * lanes, lanes)
        filter_real = filter_ref[source, odd].astype(F32)
        filter_imag = filter_ref[source, 2 + odd].astype(F32)
        real = spectrum_ref[pl.ds(0, rows), columns]
        imag = spectrum_ref[pl.ds(rows, rows), columns]
        product_ref[pl.ds(0, rows), columns] = (real * filter_real - imag * filter_imag).astype(BF16)
        product_ref[pl.ds(rows, rows), columns] = (real * filter_imag + imag * filter_real).astype(BF16)
        back_ref[:, columns] = jnp.dot(table_ref[...], product_ref[:, columns], preferred_element_type=F32)

    scale = 1.0 / (2 * parts * rows)
    sign = (1 - 2 * core).astype(F32)
    upper = core == 1

    def gather(index, carry):
        here = block_at(index, chunk)
        there = pl.ds(pl.multiple_of(rows + index * chunk, chunk), chunk)
        cos_all, sin_all = cos_ref[core, here, :] * scale, sin_ref[core, here, :] * scale
        for start in range(0, lanes, width):
            reals, imags = [], []
            for residue in range(parts):
                columns = pl.ds(residue * lanes + start, width)
                real, imag = back_ref[here, columns], back_ref[there, columns]
                cos, sin = cos_all[:, residue : residue + 1], sin_all[:, residue : residue + 1]
                reals.append(real * cos - imag * sin)
                imags.append(real * sin + imag * cos)
            totals = [None] * parts
            for block in range(parts // 2 + 1):
                even, odd = range(0, parts, 2), range(1, parts, 2)
                cos_even = weighted([(cosine(parts, residue, block), reals[residue]) for residue in even])
                cos_odd = weighted([(cosine(parts, residue, block), reals[residue]) for residue in odd])
                sin_even = weighted([(sine(parts, residue, block), imags[residue]) for residue in even])
                sin_odd = weighted([(sine(parts, residue, block), imags[residue]) for residue in odd])
                totals[block] = minus(plus(cos_even, cos_odd), plus(sin_even, sin_odd))
                if 0 < block and 2 * block != parts:
                    totals[parts - block] = plus(minus(cos_even, cos_odd), minus(sin_even, sin_odd))
            lane = pl.ds(start, width)
            for pair in range(chips):
                low, high = totals[2 * pair], totals[2 * pair + 1] * sign
                keep_ref[pair, here, lane] = jnp.where(upper, high, low)
                part, place = divmod(pair, chips // 2)
                send_refs[part][place, here, lane] = jnp.where(upper, low, high).astype(BF16)
        return carry

    lax.fori_loop(0, rows // chunk, gather, 0)


def backward(spectrum, first, tables):
    chips = len(first)
    rows, lanes = spectrum.shape[0] // 2, first[0].shape[1]
    _, table, cos, sin = tables
    half = jax.ShapeDtypeStruct((chips // 2, rows, lanes), BF16)
    return pl.pallas_call(
        functools.partial(backward_kernel, chips),
        in_specs=[WHOLE] * (4 + chips),
        out_specs=[WHOLE] * 3,
        out_shape=[jax.ShapeDtypeStruct((chips, rows, lanes), F32), half, half],
        scratch_shapes=[
            pltpu.VMEM((chips, 4, rows, lanes), BF16),
            pltpu.VMEM(spectrum.shape, BF16),
            pltpu.VMEM(spectrum.shape, F32),
        ],
        cost_estimate=CHEAP,
        compiler_params=pltpu.CompilerParams(vmem_limit_bytes=32 * 2**20),
        name="backward",
    )(cos, sin, table, spectrum, *first)


def gate_kernel(chips, skip_ref, keep_ref, low_ref, high_ref, *refs):
    signal_refs, gate_refs = refs[:chips], refs[chips : 2 * chips]
    out_ref, longer_ref, arrived_ref = refs[2 * chips :]
    chip, _ = own_place()
    rows, lanes = keep_ref.shape[1:]
    skip = skip_ref[:, block_at(chip, lanes)]
    arrived_ref[pl.ds(0, chips // 2)] = low_ref[...]
    arrived_ref[pl.ds(chips // 2, chips // 2)] = high_ref[...]
    for offset in range(chips):
        block = chip ^ offset
        convolved = keep_ref[block] + arrived_ref[block].astype(F32)
        signal = signal_refs[offset][pl.ds(0, rows), :].astype(F32)
        gate = gate_refs[offset][pl.ds(0, rows), :].astype(F32)
        gated = (gate * (convolved + skip * signal)).astype(BF16)
        out_ref[block_at(block, rows), :] = gated
        longer_ref[block_at(block, rows), :] = gated
    end = chips * rows
    longer_ref[pl.ds(end, longer_ref.shape[0] - end), :] = longer_ref[pl.ds(0, longer_ref.shape[0] - end), :]


def gate(skip, keep, arrived, first, gates, spare):
    chips, rows, lanes = keep.shape
    return pl.pallas_call(
        functools.partial(gate_kernel, chips),
        in_specs=[WHOLE] * (4 + 2 * chips),
        out_specs=[WHOLE] * 2,
        out_shape=[
            jax.ShapeDtypeStruct((chips * rows, lanes), BF16),
            jax.ShapeDtypeStruct((chips * rows + spare, lanes), BF16),
        ],
        scratch_shapes=[pltpu.VMEM((chips, rows, lanes), BF16)],
        cost_estimate=CHEAP,
        compiler_params=pltpu.CompilerParams(vmem_limit_bytes=6 * 2**20),
        name="gate",
    )(skip, keep, *arrived, *first, *gates)


def piece_of(ref, half, part):
    quarter, share = half // 2, ref.shape[1] // 2
    return ref[pl.ds(ref.shape[0] - quarter, quarter), pl.ds(part * share, share)]


def collect_kernel(in_refs, out_refs):
    rows = out_refs[0].shape[0]
    quarter = len(out_refs) * rows // (2 * len(in_refs))
    for place in range(2 * len(in_refs)):
        index, start = divmod(place * quarter, rows)
        out_refs[index][pl.ds(start, quarter), :] = piece_of(in_refs[place // 2], 2 * quarter, place % 2)


def collect(moved, half):
    count = len(moved)
    shape = (count * half // 2, moved[0].shape[1] // 2)
    return pl.pallas_call(
        lambda *refs: collect_kernel(refs[:count], refs[count:]),
        in_specs=[WHOLE] * count,
        out_specs=[WHOLE] * 2,
        out_shape=[jax.ShapeDtypeStruct(shape, BF16)] * 2,
        cost_estimate=CHEAP,
        compiler_params=pltpu.CompilerParams(vmem_limit_bytes=4 * 2**20),
        name="collect_weights",
    )(*moved)


def arrange_kernel(chips, mine_ref, *refs):
    moved_refs, (*other_refs, out_ref) = refs[: chips - 1], refs[chips - 1 :]
    chip, core = own_place()
    layer = lax.axis_index("chan")
    depth, share = mine_ref.shape
    quarter = depth // 4
    out_ref[:, block_at(chip ^ layer, share)] = mine_ref[...]
    for place in range(2 * (chips - 1)):
        offset, part = place // 2 + 1, place % 2
        columns = block_at(chip ^ layer ^ offset, share)
        index, start = divmod(place * quarter, other_refs[0].shape[0])
        out_ref[block_at(2 * core + part, quarter), columns] = piece_of(moved_refs[offset - 1], 2 * quarter, part)
        out_ref[block_at(2 * (1 - core) + part, quarter), columns] = other_refs[index][pl.ds(start, quarter), :]


def arrange(mine, moved, others):
    chips = len(moved) + 1
    depth, share = mine.shape
    return pl.pallas_call(
        functools.partial(arrange_kernel, chips),
        in_specs=[WHOLE] * (chips + len(others)),
        out_specs=WHOLE,
        out_shape=jax.ShapeDtypeStruct((depth, chips * share), BF16),
        cost_estimate=CHEAP,
        compiler_params=pltpu.CompilerParams(vmem_limit_bytes=8 * 2**20),
        name="arrange_weights",
    )(mine, *moved, *others)


def join_channels(chips, gated_refs, joined_ref):
    chip, _ = own_place()
    lanes = gated_refs[0].shape[1]
    for offset in range(chips):
        joined_ref[:, block_at(chip ^ offset, lanes)] = gated_refs[offset][pl.ds(0, joined_ref.shape[0]), :]


def project_moved_kernel(chips, weight_ref, *refs):
    gated_refs, (keep_ref, pass_ref, send_ref, joined_ref) = refs[:chips], refs[chips:]
    share = keep_ref.shape[1]
    join_channels(chips, gated_refs, joined_ref)
    partial = jnp.dot(joined_ref[...], weight_ref[...], preferred_element_type=F32).astype(BF16)
    keep_ref[...] = partial[:, :share]
    send_ref[0] = partial[:, share : 2 * share]
    pass_ref[...] = partial[:, 2 * share : 3 * share]
    send_ref[1] = partial[:, 3 * share :]


def project_moved(weight, gated):
    chips = len(gated)
    depth, columns = weight.shape
    rows = gated[0].shape[0]
    block = jax.ShapeDtypeStruct((rows, columns // chips), BF16)
    return pl.pallas_call(
        functools.partial(project_moved_kernel, chips),
        in_specs=[WHOLE] * (1 + chips),
        out_specs=[WHOLE] * 3,
        out_shape=[block, block, jax.ShapeDtypeStruct((2, rows, columns // chips), BF16)],
        scratch_shapes=[pltpu.VMEM((rows, depth), BF16)],
        cost_estimate=CHEAP,
        compiler_params=pltpu.CompilerParams(vmem_limit_bytes=8 * 2**20),
        name="project_moved",
    )(weight, *gated)


def project_still_kernel(chips, own_ref, other_ref, *refs):
    gated_refs, out_refs, joined_ref = refs[:chips], refs[chips : 2 * chips], refs[2 * chips]
    chip, core = own_place()
    rows = out_refs[0].shape[0]
    join_channels(chips, gated_refs, joined_ref)

    def project_with(weight_ref):
        for offset in range(chips):
            gated = joined_ref[block_at(chip ^ offset, rows), :]
            out_refs[offset][...] = jnp.dot(gated, weight_ref[...], preferred_element_type=F32).astype(BF16)

    @pl.when(core == 0)
    def _():
        project_with(other_ref)

    @pl.when(core == 1)
    def _():
        project_with(own_ref)


def project_still(own, other, gated):
    chips = len(gated)
    depth, held = own.shape
    rows = gated[0].shape[0] // chips
    return pl.pallas_call(
        functools.partial(project_still_kernel, chips),
        in_specs=[WHOLE] * (2 + chips),
        out_specs=[WHOLE] * chips,
        out_shape=[jax.ShapeDtypeStruct((rows, held), BF16)] * chips,
        scratch_shapes=[pltpu.VMEM((rows * chips, depth), BF16)],
        cost_estimate=CHEAP,
        compiler_params=pltpu.CompilerParams(vmem_limit_bytes=12 * 2**20),
        name="project_still",
    )(own, other, *gated)


def sort_kernel(chips, *refs):
    in_refs, (*out_refs, sorted_ref) = refs[:chips], refs[chips:]
    chip, _ = own_place()
    layer = lax.axis_index("chan")
    for offset in range(chips):
        sorted_ref[chip ^ layer ^ offset] = in_refs[offset][...]
    for target, out_ref in enumerate(out_refs):
        out_ref[...] = sorted_ref[target]


def sort_blocks(blocks):
    chips = len(blocks)
    block = jax.ShapeDtypeStruct(blocks[0].shape, BF16)
    return pl.pallas_call(
        functools.partial(sort_kernel, chips),
        in_specs=[WHOLE] * chips,
        out_specs=[WHOLE] * chips,
        out_shape=[block] * chips,
        scratch_shapes=[pltpu.VMEM((chips, *block.shape), BF16)],
        cost_estimate=CHEAP,
        compiler_params=pltpu.CompilerParams(vmem_limit_bytes=4 * 2**20),
        name="sort_blocks",
    )(*blocks)


def add_kernel(left_ref, right_ref, out_ref):
    rows = left_ref.shape[0]
    total = (left_ref[...].astype(F32) + right_ref[...].astype(F32)).astype(BF16)
    out_ref[pl.ds(0, rows), :] = total
    more = out_ref.shape[0] - rows
    if more:
        out_ref[pl.ds(rows, more), :] = total[:more]


def add(left, right, spare):
    rows, columns = left.shape
    return pl.pallas_call(
        add_kernel,
        in_specs=[WHOLE] * 2,
        out_specs=WHOLE,
        out_shape=jax.ShapeDtypeStruct((rows + spare, columns), BF16),
        cost_estimate=CHEAP,
        compiler_params=pltpu.CompilerParams(vmem_limit_bytes=4 * 2**20),
        name="add",
    )(left, right)


def finish_kernel(chips, keep_ref, first_ref, second_ref, *out_refs):
    chip, _ = own_place()
    rows = out_refs[0].shape[0]
    for offset in range(chips):
        here = block_at(chip ^ offset, rows)
        total = keep_ref[here, :].astype(F32) + first_ref[0, here, :].astype(F32) + second_ref[here, :].astype(F32)
        out_refs[offset][...] = total.astype(BF16)


def finish(keep, first, second, chips):
    rows, columns = keep.shape
    return pl.pallas_call(
        functools.partial(finish_kernel, chips),
        in_specs=[WHOLE] * 3,
        out_specs=[WHOLE] * chips,
        out_shape=[jax.ShapeDtypeStruct((rows // chips, columns), BF16)] * chips,
        cost_estimate=CHEAP,
        compiler_params=pltpu.CompilerParams(vmem_limit_bytes=4 * 2**20),
        name="finish",
    )(keep, first, second)


def join_kernel(chips, keep_ref, first_ref, second_ref, *refs):
    in_refs, out_ref = refs[:chips], refs[chips]
    chip, _ = own_place()
    share = in_refs[0].shape[1]
    for offset in range(chips):
        out_ref[:, block_at(chip ^ offset, share)] = in_refs[offset][...]
    total = keep_ref[...].astype(F32) + first_ref[...].astype(F32)
    total = total + second_ref[pl.ds(0, total.shape[0]), :].astype(F32)
    out_ref[:, pl.ds(chips * share, total.shape[1])] = total.astype(BF16)


def join(keep, first, second, blocks):
    chips = len(blocks)
    rows, share = blocks[0].shape
    return pl.pallas_call(
        functools.partial(join_kernel, chips),
        in_specs=[WHOLE] * (3 + chips),
        out_specs=WHOLE,
        out_shape=jax.ShapeDtypeStruct((rows, chips * share + keep.shape[1]), BF16),
        cost_estimate=CHEAP,
        compiler_params=pltpu.CompilerParams(vmem_limit_bytes=4 * 2**20),
        name="join",
    )(keep, first, second, *blocks)


def swapped(value, axis, offset):
    if not offset:
        return value
    return lax.ppermute(value, axis, [(source, source ^ offset) for source in range(lax.axis_size(axis))])


def to_chips(blocks):
    return [swapped(block, "seq", 2 * offset) for offset, block in enumerate(blocks)]


def after(value, *others):
    return lax.optimization_barrier((value, *others))[0]


def over_layers(passed, send):
    first = swapped(send, "chan", 1)
    passed = (passed.astype(F32) + first[1].astype(F32)).astype(BF16)
    return first, swapped(passed, "chan", 2)


def shards_direct(values_in, gate_values, filter_spectrum, skip_gain, out_weight):
    parts = lax.axis_size("seq")
    chips = parts // 2
    rows, width = values_in.shape
    tables = small_tables(parts, rows)

    values = pack_values(values_in, chips, 0)
    flat_filters = filter_spectrum.reshape(4, rows, width)
    near = pack_filters(after(flat_filters, values[0]), chips, (1, 2), 0)
    other_weight = swapped(out_weight, "seq", 1)
    *moved, mine = pack_moved(after(gate_values, near[0]), out_weight, other_weight, chips)
    own, far = pack_filters(after(flat_filters, moved[0]), chips, (0, 3), 0)
    values, filters = to_chips(values), to_chips([own, *near, far])
    own = stack([after(block, far) for block in values], rows)
    spectrum = forward(own, [swapped(part, "seq", 1) for part in own], tables)
    moved = to_chips([after(block, spectrum) for block in moved])
    keep, *send = backward(spectrum, filters, tables)
    gated, longer = gate(skip_gain[None, :], keep, [swapped(part, "seq", 1) for part in send], values, moved, 16)
    gathered = to_chips([gated, longer, longer, gated])

    others = [swapped(part, "seq", 1) for part in collect([after(block, gated) for block in moved[1:]], out_weight.shape[0] // 2)]
    keep, passed, send = project_moved(arrange(mine, moved[1:], others), gathered)
    blocks = to_chips(finish(keep, *over_layers(passed, send), chips))
    keep, near, passed, far = sort_blocks(to_chips(project_still(out_weight, other_weight, gathered)))
    second = swapped(add(after(passed, blocks[1]), swapped(far, "chan", 1), 0), "chan", 2)
    return join(keep, swapped(near, "chan", 1), second, blocks)


def shards(values_in, gate_values, filter_spectrum, skip_gain, out_weight):
    parts, layers = lax.axis_size("seq"), lax.axis_size("chan")
    rows, width = values_in.shape
    share = out_weight.shape[1] // layers
    aligned = width // parts % 128 == 0 and share % 128 == 0 and rows % 32 == 0
    run = shards_direct if aligned and layers == 4 and parts == 8 else shards_general
    return run(values_in, gate_values, filter_spectrum, skip_gain, out_weight)


def solution(mesh):
    in_specs = (
        P("seq", "chan"),
        P("seq", "chan"),
        P(None, "seq", None, "chan"),
        P("chan"),
        P("chan", "seq"),
    )
    out_specs = P("seq", "chan")
    return jax.shard_map(shards, mesh=mesh, in_specs=in_specs, out_specs=out_specs, check_vma=False)
```

```python
import functools

import jax
import jax.numpy as jnp
import numpy as np
from jax import lax
from jax.experimental import pallas as pl
from jax.experimental.pallas import tpu as pltpu
from jax.sharding import PartitionSpec as P

BF16 = jnp.bfloat16
F32 = jnp.float32


def bit_reversed(number, width_bits):
    flipped = 0
    for bit_place in range(width_bits):
        flipped |= (number >> bit_place & 1) << (width_bits - 1 - bit_place)
    return flipped


def filter_row(residue, width_bits):
    return 2 * bit_reversed(residue // 2, width_bits) + residue % 2


def dft_tables(parts, rows):
    total = 2 * parts * rows
    residue = np.arange(2 * parts)[:, None, None]
    column = np.arange(rows)[None, :, None]
    position = np.arange(rows)[None, None, :]
    phase = 2.0 * np.pi * (position * (residue + 2 * parts * column) % total) / total
    cos, sin = np.cos(phase), np.sin(phase)
    forward = np.concatenate(
        [np.concatenate([cos, sin], axis=2), np.concatenate([-sin, cos], axis=2)], axis=1
    )
    inverse = np.transpose(forward, (0, 2, 1)) / total
    return forward.astype(BF16), inverse.astype(BF16)


def convolve_kernel(parts, rows, moved_ref, skip_ref, forward_ref, inverse_ref, out_ref, waves_ref, back_ref):
    width_bits = parts.bit_length() - 1
    chunk = 16

    def cosine(residue, block):
        return float(np.cos(np.pi * residue * block / parts))

    def sine(residue, block):
        return float(np.sin(np.pi * residue * block / parts))

    def spread(index, carry):
        here = pl.ds(index * chunk, chunk)
        there = pl.ds(rows + index * chunk, chunk)
        blocks = [moved_ref[block, here, :].astype(F32) for block in range(parts)]
        for residue in range(parts + 1):
            real = blocks[0]
            imag = jnp.zeros_like(real)
            for block in range(1, parts):
                real = real + cosine(residue, block) * blocks[block]
                imag = imag - sine(residue, block) * blocks[block]
            waves_ref[residue, here, :] = real.astype(BF16)
            waves_ref[residue, there, :] = imag.astype(BF16)
            if 0 < residue < parts:
                waves_ref[2 * parts - residue, here, :] = real.astype(BF16)
                waves_ref[2 * parts - residue, there, :] = (-imag).astype(BF16)
        return carry

    lax.fori_loop(0, rows // chunk, spread, 0)

    def through(residue):
        wave = jnp.dot(forward_ref[residue], waves_ref[residue], preferred_element_type=F32)
        source, odd = divmod(filter_row(residue, width_bits), 2)
        filter_real = moved_ref[source, pl.ds((2 + odd) * rows, rows), :].astype(F32)
        filter_imag = moved_ref[source, pl.ds((4 + odd) * rows, rows), :].astype(F32)
        real, imag = wave[:rows], wave[rows:]
        product = jnp.concatenate(
            [real * filter_real - imag * filter_imag, real * filter_imag + imag * filter_real], axis=0
        )
        return jnp.dot(inverse_ref[residue], product.astype(BF16), preferred_element_type=F32)

    for residue in range(parts + 1):
        back = through(residue)
        if 0 < residue < parts:
            other = through(2 * parts - residue)
            back_ref[residue, pl.ds(0, rows), :] = back[:rows] + other[:rows]
            back_ref[residue, pl.ds(rows, rows), :] = back[rows:] - other[rows:]
        else:
            back_ref[residue] = back

    skip = skip_ref[...]

    def gather(index, carry):
        here = pl.ds(index * chunk, chunk)
        there = pl.ds(rows + index * chunk, chunk)
        reals = [back_ref[residue, here, :] for residue in range(parts + 1)]
        imags = [back_ref[residue, there, :] for residue in range(parts + 1)]
        for block in range(parts):
            total = reals[0]
            for residue in range(1, parts + 1):
                total = total + cosine(residue, block) * reals[residue]
                if residue < parts and block:
                    total = total - sine(residue, block) * imags[residue]
            signal = moved_ref[block, here, :].astype(F32)
            gate = moved_ref[block, pl.ds(rows + index * chunk, chunk), :].astype(F32)
            out_ref[block, here, :] = (gate * (total + skip * signal)).astype(BF16)
        return carry

    lax.fori_loop(0, rows // chunk, gather, 0)


def convolve(moved, skip):
    parts, stacked, width = moved.shape
    rows = stacked // 6
    forward, inverse = dft_tables(parts, rows)
    whole = pl.BlockSpec(memory_space=pltpu.VMEM)
    return pl.pallas_call(
        functools.partial(convolve_kernel, parts, rows),
        out_shape=jax.ShapeDtypeStruct((parts, rows, width), BF16),
        in_specs=[whole] * 4,
        out_specs=whole,
        scratch_shapes=[
            pltpu.VMEM((2 * parts, 2 * rows, width), BF16),
            pltpu.VMEM((parts + 1, 2 * rows, width), F32),
        ],
        compiler_params=pltpu.CompilerParams(vmem_limit_bytes=40 * 2**20),
    )(moved, skip[None, :], forward, inverse)


def shards_general(values_in, gate_values, filter_spectrum, skip_gain, out_weight):
    parts = lax.axis_size("seq")
    layers = lax.axis_size("chan")
    rows, width = values_in.shape
    lanes = width // parts
    device = lax.axis_index("seq")

    def by_channel(array):
        return jnp.transpose(array.reshape(array.shape[0], parts, lanes), (1, 0, 2))

    filters = filter_spectrum.astype(BF16).reshape(4 * rows, width)
    packed = jnp.concatenate([by_channel(values_in), by_channel(gate_values), by_channel(filters)], axis=1)
    moved = lax.all_to_all(packed, "seq", 0, 0)
    skip = lax.dynamic_slice_in_dim(skip_gain, device * lanes, lanes)
    gated = convolve(moved, skip)
    gathered = lax.all_gather(gated.reshape(parts * rows, lanes), "seq", axis=1, tiled=True)

    own_cols = out_weight.shape[1]
    share = own_cols * parts // layers // parts
    per_block = parts // layers
    pieces = own_cols // share
    group = device % per_block
    member = device // per_block
    weight = jnp.zeros_like(out_weight)
    for step in range(pieces):
        piece = (member + step) % pieces
        sent = lax.dynamic_slice_in_dim(out_weight, piece * share, share, 1)
        pairs = [
            (source, source % per_block * pieces + (source // per_block + step) % pieces) for source in range(parts)
        ]
        arrived = lax.ppermute(sent, "seq", pairs)
        block = (device % pieces - step) % pieces
        weight = lax.dynamic_update_slice_in_dim(weight, arrived, block * share, 1)
    partials = jnp.dot(gathered, weight, preferred_element_type=F32).astype(BF16)
    mixed = lax.psum_scatter(partials, "chan", scatter_dimension=1, tiled=True)
    return lax.all_to_all(mixed, "seq", 0, 1, tiled=True)


WHOLE = pl.BlockSpec(memory_space=pltpu.VMEM)
CHEAP = pl.CostEstimate(flops=0, transcendentals=0, bytes_accessed=0)


def small_tables(parts, rows):
    total = 2 * parts * rows
    index = np.arange(rows)
    phase = 2.0 * np.pi * (index[:, None] * index[None, :] % rows) / rows
    cos, sin = np.cos(phase), np.sin(phase)
    forward = np.block([[cos, sin], [-sin, cos]])
    residue = np.arange(2 * parts).reshape(2, 1, parts)
    turn = 2.0 * np.pi * index[None, :, None] * residue / total
    return forward.astype(BF16), forward.T.astype(BF16), np.cos(turn).astype(F32), np.sin(turn).astype(F32)


def cosine(parts, residue, block):
    return float(np.cos(np.pi * residue * block / parts))


def sine(parts, residue, block):
    return float(np.sin(np.pi * residue * block / parts))


def weighted(terms):
    total = None
    for factor, term in terms:
        if abs(factor) < 1e-12:
            continue
        part = term if factor == 1.0 else factor * term
        total = part if total is None else total + part
    return total


def plus(left, right):
    return left if right is None else right if left is None else left + right


def minus(left, right):
    return left if right is None else -right if left is None else left - right


def own_place():
    device = lax.axis_index("seq")
    return device // 2, device % 2


def block_at(index, size):
    return pl.ds(pl.multiple_of(index * size, size), size)


def pack_filters_kernel(offsets, filter_ref, *refs):
    out_refs, (plane_ref, arrived) = refs[: len(offsets)], refs[len(offsets) :]
    chip, _ = own_place()
    planes, rows, _ = filter_ref.shape
    lanes = out_refs[0].shape[1]
    copies = []
    for place, offset in enumerate(offsets):
        here = block_at(chip ^ offset, lanes)
        for plane in range(planes):
            copies.append(
                pltpu.make_async_copy(filter_ref.at[plane, :, here], plane_ref.at[place, plane], arrived.at[place, plane])
            )
    for copy in copies:
        copy.start()
    for index, copy in enumerate(copies):
        copy.wait()
        place, plane = divmod(index, planes)
        out_refs[place][pl.ds(plane * rows, rows), :] = plane_ref[place, plane].astype(BF16)
    used = planes * rows
    for out_ref in out_refs:
        if out_ref.shape[0] > used:
            out_ref[pl.ds(used, out_ref.shape[0] - used), :] = out_ref[pl.ds(0, out_ref.shape[0] - used), :]


def pack_filters(filters, chips, offsets, spare):
    planes, rows, width = filters.shape
    lanes = width // chips
    return pl.pallas_call(
        functools.partial(pack_filters_kernel, offsets),
        in_specs=[pl.BlockSpec(memory_space=pltpu.HBM)],
        out_specs=[WHOLE] * len(offsets),
        out_shape=[jax.ShapeDtypeStruct((planes * rows + spare, lanes), BF16)] * len(offsets),
        scratch_shapes=[
            pltpu.VMEM((len(offsets), planes, rows, lanes), F32),
            pltpu.SemaphoreType.DMA((len(offsets), planes)),
        ],
        cost_estimate=CHEAP,
        compiler_params=pltpu.CompilerParams(vmem_limit_bytes=8 * 2**20),
        name="pack_filters",
    )(pltpu.with_memory_space_constraint(filters, pltpu.HBM))


def pack_values_kernel(chips, values_ref, *refs):
    out_refs, arrived = refs[:chips], refs[chips]
    rows = values_ref.shape[0]
    chip, _ = own_place()
    copies = []
    for offset, out_ref in enumerate(out_refs):
        values = values_ref.at[:, block_at(chip ^ offset, out_ref.shape[1])]
        copies.append(pltpu.make_async_copy(values, out_ref.at[pl.ds(0, rows)], arrived.at[offset]))
    for copy in copies:
        copy.start()
    for copy in copies:
        copy.wait()


def pack_values(values_in, chips, spare):
    rows, width = values_in.shape
    return pl.pallas_call(
        functools.partial(pack_values_kernel, chips),
        in_specs=[pl.BlockSpec(memory_space=pltpu.HBM)],
        out_specs=[WHOLE] * chips,
        out_shape=[jax.ShapeDtypeStruct((rows + spare, width // chips), BF16)] * chips,
        scratch_shapes=[pltpu.SemaphoreType.DMA((chips,))],
        cost_estimate=CHEAP,
        compiler_params=pltpu.CompilerParams(vmem_limit_bytes=4 * 2**20),
        name="pack_values",
    )(pltpu.with_memory_space_constraint(values_in, pltpu.HBM))


def pack_moved_kernel(chips, gate_ref, own_ref, other_ref, *refs):
    out_refs, (mine_ref, arrived) = refs[:chips], refs[chips:]
    chip, core = own_place()
    rows = gate_ref.shape[0]
    depth, held = own_ref.shape
    quarter, share = depth // 4, held // chips

    def copies_from(weight_ref):
        copies = [pltpu.make_async_copy(weight_ref.at[:, block_at(chip, share)], mine_ref, arrived.at[0, 0])]
        for offset in range(chips):
            out_ref, target = out_refs[offset], chip ^ offset
            gates = gate_ref.at[:, block_at(target, out_ref.shape[1])]
            copies.append(pltpu.make_async_copy(gates, out_ref.at[pl.ds(0, rows)], arrived.at[offset, 2]))
            for part in range(2 if offset else 0):
                source = weight_ref.at[block_at(2 * core + part, quarter), block_at(target, share)]
                sink = out_ref.at[pl.ds(rows, quarter), pl.ds(part * share, share)]
                copies.append(pltpu.make_async_copy(source, sink, arrived.at[offset, part]))
        for copy in copies:
            copy.start()
        for copy in copies:
            copy.wait()

    @pl.when(core == 0)
    def _():
        copies_from(own_ref)

    @pl.when(core == 1)
    def _():
        copies_from(other_ref)


def pack_moved(gate_values, own, other, chips):
    rows, width = gate_values.shape
    depth, held = own.shape
    share = held // chips
    return pl.pallas_call(
        functools.partial(pack_moved_kernel, chips),
        in_specs=[pl.BlockSpec(memory_space=pltpu.HBM)] * 2 + [pl.BlockSpec(memory_space=pl.ANY)],
        out_specs=[WHOLE] * (chips + 1),
        out_shape=[
            *(jax.ShapeDtypeStruct((rows + (depth // 4 if offset else 0), 2 * share), BF16) for offset in range(chips)),
            jax.ShapeDtypeStruct((depth, share), BF16),
        ],
        scratch_shapes=[pltpu.SemaphoreType.DMA((chips, 3))],
        cost_estimate=CHEAP,
        compiler_params=pltpu.CompilerParams(vmem_limit_bytes=8 * 2**20),
        name="pack_moved",
    )(*(pltpu.with_memory_space_constraint(array, pltpu.HBM) for array in (gate_values, own)), other)


def stack_kernel(chips, *refs):
    in_refs, out_refs = refs[:chips], refs[chips:]
    for offset, in_ref in enumerate(in_refs):
        part, place = divmod(offset, chips // 2)
        out_refs[part][place] = in_ref[pl.ds(0, out_refs[part].shape[1]), :]


def stack(blocks, rows):
    chips = len(blocks)
    half = jax.ShapeDtypeStruct((chips // 2, rows, blocks[0].shape[1]), BF16)
    return pl.pallas_call(
        functools.partial(stack_kernel, chips),
        in_specs=[WHOLE] * chips,
        out_specs=[WHOLE] * 2,
        out_shape=[half, half],
        cost_estimate=CHEAP,
        compiler_params=pltpu.CompilerParams(vmem_limit_bytes=4 * 2**20),
        name="stack",
    )(*blocks)


def forward_kernel(chips, cos_ref, sin_ref, table_ref, *refs):
    own_refs, other_refs, (out_ref, signal_ref, waves_ref) = refs[:2], refs[2:4], refs[4:]
    chip, core = own_place()
    parts = 2 * chips
    rows, lanes = own_refs[0].shape[1:]
    chunk, width = 16, 128
    for offset in range(chips):
        part, place = divmod(offset, chips // 2)
        signal_ref[2 * (chip ^ offset) + core] = own_refs[part][place]
        signal_ref[2 * (chip ^ offset) + 1 - core] = other_refs[part][place]
    sign = (1 - 2 * core).astype(F32)

    def spread(index, carry):
        here = block_at(index, chunk)
        there = pl.ds(pl.multiple_of(rows + index * chunk, chunk), chunk)
        cos_all, sin_all = cos_ref[core, here, :], sin_ref[core, here, :]
        for start in range(0, lanes, width):
            blocks = [signal_ref[block, here, pl.ds(start, width)].astype(F32) for block in range(parts)]
            blocks = [block * sign if place % 2 else block for place, block in enumerate(blocks)]

            def store(residue, real, imag):
                cos, sin = cos_all[:, residue : residue + 1], sin_all[:, residue : residue + 1]
                if imag is None:
                    real, imag = real * cos, -(real * sin)
                else:
                    real, imag = real * cos + imag * sin, imag * cos - real * sin
                columns = pl.ds(residue * lanes + start, width)
                waves_ref[here, columns] = real.astype(BF16)
                waves_ref[there, columns] = imag.astype(BF16)

            for residue in range(parts // 2 + 1):
                even, odd = range(0, parts, 2), range(1, parts, 2)
                cos_even = weighted([(cosine(parts, residue, block), blocks[block]) for block in even])
                cos_odd = weighted([(cosine(parts, residue, block), blocks[block]) for block in odd])
                sin_even = weighted([(sine(parts, residue, block), blocks[block]) for block in even])
                sin_odd = weighted([(sine(parts, residue, block), blocks[block]) for block in odd])
                sin_sum = plus(sin_even, sin_odd)
                store(residue, plus(cos_even, cos_odd), None if sin_sum is None else -sin_sum)
                if 0 < residue and 2 * residue != parts:
                    store(parts - residue, minus(cos_even, cos_odd), minus(sin_even, sin_odd))
        return carry

    lax.fori_loop(0, rows // chunk, spread, 0)
    for residue in range(parts):
        columns = pl.ds(residue * lanes, lanes)
        out_ref[:, columns] = jnp.dot(table_ref[...], waves_ref[:, columns], preferred_element_type=F32)


def forward(own, other, tables):
    chips, (_, rows, lanes) = 2 * own[0].shape[0], own[0].shape
    table, _, cos, sin = tables
    spectrum = (2 * rows, 2 * chips * lanes)
    return pl.pallas_call(
        functools.partial(forward_kernel, chips),
        in_specs=[WHOLE] * 7,
        out_specs=WHOLE,
        out_shape=jax.ShapeDtypeStruct(spectrum, F32),
        scratch_shapes=[pltpu.VMEM((2 * chips, rows, lanes), BF16), pltpu.VMEM(spectrum, BF16)],
        cost_estimate=CHEAP,
        compiler_params=pltpu.CompilerParams(vmem_limit_bytes=32 * 2**20),
        name="forward",
    )(cos, sin, table, *own, *other)


def backward_kernel(chips, cos_ref, sin_ref, table_ref, spectrum_ref, *refs):
    filter_refs, (keep_ref, *send_refs, filter_ref, product_ref, back_ref) = refs[:chips], refs[chips:]
    chip, core = own_place()
    parts = 2 * chips
    rows, lanes = keep_ref.shape[1:]
    chip_bits = chips.bit_length() - 1
    chunk, width = 16, 128
    for offset in range(chips):
        for plane in range(filter_ref.shape[1]):
            filter_ref[chip ^ offset, plane] = filter_refs[offset][pl.ds(plane * rows, rows), :]

    for residue in range(parts):
        source, odd = bit_reversed(residue // 2, chip_bits), residue % 2
        columns = pl.ds(residue * lanes, lanes)
        filter_real = filter_ref[source, odd].astype(F32)
        filter_imag = filter_ref[source, 2 + odd].astype(F32)
        real = spectrum_ref[pl.ds(0, rows), columns]
        imag = spectrum_ref[pl.ds(rows, rows), columns]
        product_ref[pl.ds(0, rows), columns] = (real * filter_real - imag * filter_imag).astype(BF16)
        product_ref[pl.ds(rows, rows), columns] = (real * filter_imag + imag * filter_real).astype(BF16)
        back_ref[:, columns] = jnp.dot(table_ref[...], product_ref[:, columns], preferred_element_type=F32)

    scale = 1.0 / (2 * parts * rows)
    sign = (1 - 2 * core).astype(F32)
    upper = core == 1

    def gather(index, carry):
        here = block_at(index, chunk)
        there = pl.ds(pl.multiple_of(rows + index * chunk, chunk), chunk)
        cos_all, sin_all = cos_ref[core, here, :] * scale, sin_ref[core, here, :] * scale
        for start in range(0, lanes, width):
            reals, imags = [], []
            for residue in range(parts):
                columns = pl.ds(residue * lanes + start, width)
                real, imag = back_ref[here, columns], back_ref[there, columns]
                cos, sin = cos_all[:, residue : residue + 1], sin_all[:, residue : residue + 1]
                reals.append(real * cos - imag * sin)
                imags.append(real * sin + imag * cos)
            totals = [None] * parts
            for block in range(parts // 2 + 1):
                even, odd = range(0, parts, 2), range(1, parts, 2)
                cos_even = weighted([(cosine(parts, residue, block), reals[residue]) for residue in even])
                cos_odd = weighted([(cosine(parts, residue, block), reals[residue]) for residue in odd])
                sin_even = weighted([(sine(parts, residue, block), imags[residue]) for residue in even])
                sin_odd = weighted([(sine(parts, residue, block), imags[residue]) for residue in odd])
                totals[block] = minus(plus(cos_even, cos_odd), plus(sin_even, sin_odd))
                if 0 < block and 2 * block != parts:
                    totals[parts - block] = plus(minus(cos_even, cos_odd), minus(sin_even, sin_odd))
            lane = pl.ds(start, width)
            for pair in range(chips):
                low, high = totals[2 * pair], totals[2 * pair + 1] * sign
                keep_ref[pair, here, lane] = jnp.where(upper, high, low)
                part, place = divmod(pair, chips // 2)
                send_refs[part][place, here, lane] = jnp.where(upper, low, high).astype(BF16)
        return carry

    lax.fori_loop(0, rows // chunk, gather, 0)


def backward(spectrum, first, tables):
    chips = len(first)
    rows, lanes = spectrum.shape[0] // 2, first[0].shape[1]
    _, table, cos, sin = tables
    half = jax.ShapeDtypeStruct((chips // 2, rows, lanes), BF16)
    return pl.pallas_call(
        functools.partial(backward_kernel, chips),
        in_specs=[WHOLE] * (4 + chips),
        out_specs=[WHOLE] * 3,
        out_shape=[jax.ShapeDtypeStruct((chips, rows, lanes), F32), half, half],
        scratch_shapes=[
            pltpu.VMEM((chips, 4, rows, lanes), BF16),
            pltpu.VMEM(spectrum.shape, BF16),
            pltpu.VMEM(spectrum.shape, F32),
        ],
        cost_estimate=CHEAP,
        compiler_params=pltpu.CompilerParams(vmem_limit_bytes=32 * 2**20),
        name="backward",
    )(cos, sin, table, spectrum, *first)


def gate_kernel(chips, skip_ref, keep_ref, low_ref, high_ref, *refs):
    signal_refs, gate_refs = refs[:chips], refs[chips : 2 * chips]
    out_ref, longer_ref, arrived_ref = refs[2 * chips :]
    chip, _ = own_place()
    rows, lanes = keep_ref.shape[1:]
    skip = skip_ref[:, block_at(chip, lanes)]
    arrived_ref[pl.ds(0, chips // 2)] = low_ref[...]
    arrived_ref[pl.ds(chips // 2, chips // 2)] = high_ref[...]
    for offset in range(chips):
        block = chip ^ offset
        convolved = keep_ref[block] + arrived_ref[block].astype(F32)
        signal = signal_refs[offset][pl.ds(0, rows), :].astype(F32)
        gate = gate_refs[offset][pl.ds(0, rows), :].astype(F32)
        gated = (gate * (convolved + skip * signal)).astype(BF16)
        out_ref[block_at(block, rows), :] = gated
        longer_ref[block_at(block, rows), :] = gated
    end = chips * rows
    longer_ref[pl.ds(end, longer_ref.shape[0] - end), :] = longer_ref[pl.ds(0, longer_ref.shape[0] - end), :]


def gate(skip, keep, arrived, first, gates, spare):
    chips, rows, lanes = keep.shape
    return pl.pallas_call(
        functools.partial(gate_kernel, chips),
        in_specs=[WHOLE] * (4 + 2 * chips),
        out_specs=[WHOLE] * 2,
        out_shape=[
            jax.ShapeDtypeStruct((chips * rows, lanes), BF16),
            jax.ShapeDtypeStruct((chips * rows + spare, lanes), BF16),
        ],
        scratch_shapes=[pltpu.VMEM((chips, rows, lanes), BF16)],
        cost_estimate=CHEAP,
        compiler_params=pltpu.CompilerParams(vmem_limit_bytes=6 * 2**20),
        name="gate",
    )(skip, keep, *arrived, *first, *gates)


def piece_of(ref, half, part):
    quarter, share = half // 2, ref.shape[1] // 2
    return ref[pl.ds(ref.shape[0] - quarter, quarter), pl.ds(part * share, share)]


def collect_kernel(in_refs, out_refs):
    rows = out_refs[0].shape[0]
    quarter = len(out_refs) * rows // (2 * len(in_refs))
    for place in range(2 * len(in_refs)):
        index, start = divmod(place * quarter, rows)
        out_refs[index][pl.ds(start, quarter), :] = piece_of(in_refs[place // 2], 2 * quarter, place % 2)


def collect(moved, half):
    count = len(moved)
    shape = (count * half // 2, moved[0].shape[1] // 2)
    return pl.pallas_call(
        lambda *refs: collect_kernel(refs[:count], refs[count:]),
        in_specs=[WHOLE] * count,
        out_specs=[WHOLE] * 2,
        out_shape=[jax.ShapeDtypeStruct(shape, BF16)] * 2,
        cost_estimate=CHEAP,
        compiler_params=pltpu.CompilerParams(vmem_limit_bytes=4 * 2**20),
        name="collect_weights",
    )(*moved)


def arrange_kernel(chips, mine_ref, *refs):
    moved_refs, (*other_refs, out_ref) = refs[: chips - 1], refs[chips - 1 :]
    chip, core = own_place()
    layer = lax.axis_index("chan")
    depth, share = mine_ref.shape
    quarter = depth // 4
    out_ref[:, block_at(chip ^ layer, share)] = mine_ref[...]
    for place in range(2 * (chips - 1)):
        offset, part = place // 2 + 1, place % 2
        columns = block_at(chip ^ layer ^ offset, share)
        index, start = divmod(place * quarter, other_refs[0].shape[0])
        out_ref[block_at(2 * core + part, quarter), columns] = piece_of(moved_refs[offset - 1], 2 * quarter, part)
        out_ref[block_at(2 * (1 - core) + part, quarter), columns] = other_refs[index][pl.ds(start, quarter), :]


def arrange(mine, moved, others):
    chips = len(moved) + 1
    depth, share = mine.shape
    return pl.pallas_call(
        functools.partial(arrange_kernel, chips),
        in_specs=[WHOLE] * (chips + len(others)),
        out_specs=WHOLE,
        out_shape=jax.ShapeDtypeStruct((depth, chips * share), BF16),
        cost_estimate=CHEAP,
        compiler_params=pltpu.CompilerParams(vmem_limit_bytes=8 * 2**20),
        name="arrange_weights",
    )(mine, *moved, *others)


def join_channels(chips, gated_refs, joined_ref):
    chip, _ = own_place()
    lanes = gated_refs[0].shape[1]
    for offset in range(chips):
        joined_ref[:, block_at(chip ^ offset, lanes)] = gated_refs[offset][pl.ds(0, joined_ref.shape[0]), :]


def project_moved_kernel(chips, weight_ref, *refs):
    gated_refs, (keep_ref, pass_ref, send_ref, joined_ref) = refs[:chips], refs[chips:]
    share = keep_ref.shape[1]
    join_channels(chips, gated_refs, joined_ref)
    partial = jnp.dot(joined_ref[...], weight_ref[...], preferred_element_type=F32).astype(BF16)
    keep_ref[...] = partial[:, :share]
    send_ref[0] = partial[:, share : 2 * share]
    pass_ref[...] = partial[:, 2 * share : 3 * share]
    send_ref[1] = partial[:, 3 * share :]


def project_moved(weight, gated):
    chips = len(gated)
    depth, columns = weight.shape
    rows = gated[0].shape[0]
    block = jax.ShapeDtypeStruct((rows, columns // chips), BF16)
    return pl.pallas_call(
        functools.partial(project_moved_kernel, chips),
        in_specs=[WHOLE] * (1 + chips),
        out_specs=[WHOLE] * 3,
        out_shape=[block, block, jax.ShapeDtypeStruct((2, rows, columns // chips), BF16)],
        scratch_shapes=[pltpu.VMEM((rows, depth), BF16)],
        cost_estimate=CHEAP,
        compiler_params=pltpu.CompilerParams(vmem_limit_bytes=8 * 2**20),
        name="project_moved",
    )(weight, *gated)


def project_still_kernel(chips, own_ref, other_ref, *refs):
    gated_refs, out_refs, joined_ref = refs[:chips], refs[chips : 2 * chips], refs[2 * chips]
    chip, core = own_place()
    rows = out_refs[0].shape[0]
    join_channels(chips, gated_refs, joined_ref)

    def project_with(weight_ref):
        for offset in range(chips):
            gated = joined_ref[block_at(chip ^ offset, rows), :]
            out_refs[offset][...] = jnp.dot(gated, weight_ref[...], preferred_element_type=F32).astype(BF16)

    @pl.when(core == 0)
    def _():
        project_with(other_ref)

    @pl.when(core == 1)
    def _():
        project_with(own_ref)


def project_still(own, other, gated):
    chips = len(gated)
    depth, held = own.shape
    rows = gated[0].shape[0] // chips
    return pl.pallas_call(
        functools.partial(project_still_kernel, chips),
        in_specs=[WHOLE] * (2 + chips),
        out_specs=[WHOLE] * chips,
        out_shape=[jax.ShapeDtypeStruct((rows, held), BF16)] * chips,
        scratch_shapes=[pltpu.VMEM((rows * chips, depth), BF16)],
        cost_estimate=CHEAP,
        compiler_params=pltpu.CompilerParams(vmem_limit_bytes=12 * 2**20),
        name="project_still",
    )(own, other, *gated)


def sort_kernel(chips, *refs):
    in_refs, (*out_refs, sorted_ref) = refs[:chips], refs[chips:]
    chip, _ = own_place()
    layer = lax.axis_index("chan")
    for offset in range(chips):
        sorted_ref[chip ^ layer ^ offset] = in_refs[offset][...]
    for target, out_ref in enumerate(out_refs):
        out_ref[...] = sorted_ref[target]


def sort_blocks(blocks):
    chips = len(blocks)
    block = jax.ShapeDtypeStruct(blocks[0].shape, BF16)
    return pl.pallas_call(
        functools.partial(sort_kernel, chips),
        in_specs=[WHOLE] * chips,
        out_specs=[WHOLE] * chips,
        out_shape=[block] * chips,
        scratch_shapes=[pltpu.VMEM((chips, *block.shape), BF16)],
        cost_estimate=CHEAP,
        compiler_params=pltpu.CompilerParams(vmem_limit_bytes=4 * 2**20),
        name="sort_blocks",
    )(*blocks)


def add_kernel(left_ref, right_ref, out_ref):
    rows = left_ref.shape[0]
    total = (left_ref[...].astype(F32) + right_ref[...].astype(F32)).astype(BF16)
    out_ref[pl.ds(0, rows), :] = total
    more = out_ref.shape[0] - rows
    if more:
        out_ref[pl.ds(rows, more), :] = total[:more]


def add(left, right, spare):
    rows, columns = left.shape
    return pl.pallas_call(
        add_kernel,
        in_specs=[WHOLE] * 2,
        out_specs=WHOLE,
        out_shape=jax.ShapeDtypeStruct((rows + spare, columns), BF16),
        cost_estimate=CHEAP,
        compiler_params=pltpu.CompilerParams(vmem_limit_bytes=4 * 2**20),
        name="add",
    )(left, right)


def finish_kernel(chips, keep_ref, first_ref, second_ref, *out_refs):
    chip, _ = own_place()
    rows = out_refs[0].shape[0]
    for offset in range(chips):
        here = block_at(chip ^ offset, rows)
        total = keep_ref[here, :].astype(F32) + first_ref[0, here, :].astype(F32) + second_ref[here, :].astype(F32)
        out_refs[offset][...] = total.astype(BF16)


def finish(keep, first, second, chips):
    rows, columns = keep.shape
    return pl.pallas_call(
        functools.partial(finish_kernel, chips),
        in_specs=[WHOLE] * 3,
        out_specs=[WHOLE] * chips,
        out_shape=[jax.ShapeDtypeStruct((rows // chips, columns), BF16)] * chips,
        cost_estimate=CHEAP,
        compiler_params=pltpu.CompilerParams(vmem_limit_bytes=4 * 2**20),
        name="finish",
    )(keep, first, second)


def join_kernel(chips, keep_ref, first_ref, second_ref, *refs):
    in_refs, out_ref = refs[:chips], refs[chips]
    chip, _ = own_place()
    share = in_refs[0].shape[1]
    for offset in range(chips):
        out_ref[:, block_at(chip ^ offset, share)] = in_refs[offset][...]
    total = keep_ref[...].astype(F32) + first_ref[...].astype(F32)
    total = total + second_ref[pl.ds(0, total.shape[0]), :].astype(F32)
    out_ref[:, pl.ds(chips * share, total.shape[1])] = total.astype(BF16)


def join(keep, first, second, blocks):
    chips = len(blocks)
    rows, share = blocks[0].shape
    return pl.pallas_call(
        functools.partial(join_kernel, chips),
        in_specs=[WHOLE] * (3 + chips),
        out_specs=WHOLE,
        out_shape=jax.ShapeDtypeStruct((rows, chips * share + keep.shape[1]), BF16),
        cost_estimate=CHEAP,
        compiler_params=pltpu.CompilerParams(vmem_limit_bytes=4 * 2**20),
        name="join",
    )(keep, first, second, *blocks)


def swapped(value, axis, offset):
    if not offset:
        return value
    return lax.ppermute(value, axis, [(source, source ^ offset) for source in range(lax.axis_size(axis))])


def to_chips(blocks):
    return [swapped(block, "seq", 2 * offset) for offset, block in enumerate(blocks)]


def after(value, *others):
    return lax.optimization_barrier((value, *others))[0]


def over_layers(passed, send):
    first = swapped(send, "chan", 1)
    passed = (passed.astype(F32) + first[1].astype(F32)).astype(BF16)
    return first, swapped(passed, "chan", 2)


def shards_direct(values_in, gate_values, filter_spectrum, skip_gain, out_weight):
    parts = lax.axis_size("seq")
    chips = parts // 2
    rows, width = values_in.shape
    tables = small_tables(parts, rows)

    values = pack_values(values_in, chips, 0)
    flat_filters = filter_spectrum.reshape(4, rows, width)
    near = pack_filters(after(flat_filters, values[0]), chips, (1, 2), 0)
    other_weight = swapped(out_weight, "seq", 1)
    *moved, mine = pack_moved(after(gate_values, near[0]), out_weight, other_weight, chips)
    own, far = pack_filters(after(flat_filters, moved[0]), chips, (0, 3), 0)
    values, filters = to_chips(values), to_chips([own, *near, far])
    own = stack([after(block, far) for block in values], rows)
    spectrum = forward(own, [swapped(part, "seq", 1) for part in own], tables)
    moved = to_chips([after(block, spectrum) for block in moved])
    keep, *send = backward(spectrum, filters, tables)
    gated, longer = gate(skip_gain[None, :], keep, [swapped(part, "seq", 1) for part in send], values, moved, 16)
    gathered = to_chips([gated, longer, longer, gated])

    others = [swapped(part, "seq", 1) for part in collect([after(block, gated) for block in moved[1:]], out_weight.shape[0] // 2)]
    keep, passed, send = project_moved(arrange(mine, moved[1:], others), gathered)
    blocks = to_chips(finish(keep, *over_layers(passed, send), chips))
    keep, near, passed, far = sort_blocks(to_chips(project_still(out_weight, other_weight, gathered)))
    second = swapped(add(after(passed, *blocks[1:3]), swapped(far, "chan", 1), 16), "chan", 2)
    return join(keep, swapped(near, "chan", 1), second, blocks)


def shards(values_in, gate_values, filter_spectrum, skip_gain, out_weight):
    parts, layers = lax.axis_size("seq"), lax.axis_size("chan")
    rows, width = values_in.shape
    share = out_weight.shape[1] // layers
    aligned = width // parts % 128 == 0 and share % 128 == 0 and rows % 32 == 0
    run = shards_direct if aligned and layers == 4 and parts == 8 else shards_general
    return run(values_in, gate_values, filter_spectrum, skip_gain, out_weight)


def solution(mesh):
    in_specs = (
        P("seq", "chan"),
        P("seq", "chan"),
        P(None, "seq", None, "chan"),
        P("chan"),
        P("chan", "seq"),
    )
    out_specs = P("seq", "chan")
    return jax.shard_map(shards, mesh=mesh, in_specs=in_specs, out_specs=out_specs, check_vma=False)
```

```python
import functools

import jax
import jax.numpy as jnp
import numpy as np
from jax import lax
from jax.experimental import pallas as pl
from jax.experimental.pallas import tpu as pltpu
from jax.sharding import PartitionSpec as P

BF16 = jnp.bfloat16
F32 = jnp.float32


def bit_reversed(number, width_bits):
    flipped = 0
    for bit_place in range(width_bits):
        flipped |= (number >> bit_place & 1) << (width_bits - 1 - bit_place)
    return flipped


def filter_row(residue, width_bits):
    return 2 * bit_reversed(residue // 2, width_bits) + residue % 2


def dft_tables(parts, rows):
    total = 2 * parts * rows
    residue = np.arange(2 * parts)[:, None, None]
    column = np.arange(rows)[None, :, None]
    position = np.arange(rows)[None, None, :]
    phase = 2.0 * np.pi * (position * (residue + 2 * parts * column) % total) / total
    cos, sin = np.cos(phase), np.sin(phase)
    forward = np.concatenate(
        [np.concatenate([cos, sin], axis=2), np.concatenate([-sin, cos], axis=2)], axis=1
    )
    inverse = np.transpose(forward, (0, 2, 1)) / total
    return forward.astype(BF16), inverse.astype(BF16)


def convolve_kernel(parts, rows, moved_ref, skip_ref, forward_ref, inverse_ref, out_ref, waves_ref, back_ref):
    width_bits = parts.bit_length() - 1
    chunk = 16

    def cosine(residue, block):
        return float(np.cos(np.pi * residue * block / parts))

    def sine(residue, block):
        return float(np.sin(np.pi * residue * block / parts))

    def spread(index, carry):
        here = pl.ds(index * chunk, chunk)
        there = pl.ds(rows + index * chunk, chunk)
        blocks = [moved_ref[block, here, :].astype(F32) for block in range(parts)]
        for residue in range(parts + 1):
            real = blocks[0]
            imag = jnp.zeros_like(real)
            for block in range(1, parts):
                real = real + cosine(residue, block) * blocks[block]
                imag = imag - sine(residue, block) * blocks[block]
            waves_ref[residue, here, :] = real.astype(BF16)
            waves_ref[residue, there, :] = imag.astype(BF16)
            if 0 < residue < parts:
                waves_ref[2 * parts - residue, here, :] = real.astype(BF16)
                waves_ref[2 * parts - residue, there, :] = (-imag).astype(BF16)
        return carry

    lax.fori_loop(0, rows // chunk, spread, 0)

    def through(residue):
        wave = jnp.dot(forward_ref[residue], waves_ref[residue], preferred_element_type=F32)
        source, odd = divmod(filter_row(residue, width_bits), 2)
        filter_real = moved_ref[source, pl.ds((2 + odd) * rows, rows), :].astype(F32)
        filter_imag = moved_ref[source, pl.ds((4 + odd) * rows, rows), :].astype(F32)
        real, imag = wave[:rows], wave[rows:]
        product = jnp.concatenate(
            [real * filter_real - imag * filter_imag, real * filter_imag + imag * filter_real], axis=0
        )
        return jnp.dot(inverse_ref[residue], product.astype(BF16), preferred_element_type=F32)

    for residue in range(parts + 1):
        back = through(residue)
        if 0 < residue < parts:
            other = through(2 * parts - residue)
            back_ref[residue, pl.ds(0, rows), :] = back[:rows] + other[:rows]
            back_ref[residue, pl.ds(rows, rows), :] = back[rows:] - other[rows:]
        else:
            back_ref[residue] = back

    skip = skip_ref[...]

    def gather(index, carry):
        here = pl.ds(index * chunk, chunk)
        there = pl.ds(rows + index * chunk, chunk)
        reals = [back_ref[residue, here, :] for residue in range(parts + 1)]
        imags = [back_ref[residue, there, :] for residue in range(parts + 1)]
        for block in range(parts):
            total = reals[0]
            for residue in range(1, parts + 1):
                total = total + cosine(residue, block) * reals[residue]
                if residue < parts and block:
                    total = total - sine(residue, block) * imags[residue]
            signal = moved_ref[block, here, :].astype(F32)
            gate = moved_ref[block, pl.ds(rows + index * chunk, chunk), :].astype(F32)
            out_ref[block, here, :] = (gate * (total + skip * signal)).astype(BF16)
        return carry

    lax.fori_loop(0, rows // chunk, gather, 0)


def convolve(moved, skip):
    parts, stacked, width = moved.shape
    rows = stacked // 6
    forward, inverse = dft_tables(parts, rows)
    whole = pl.BlockSpec(memory_space=pltpu.VMEM)
    return pl.pallas_call(
        functools.partial(convolve_kernel, parts, rows),
        out_shape=jax.ShapeDtypeStruct((parts, rows, width), BF16),
        in_specs=[whole] * 4,
        out_specs=whole,
        scratch_shapes=[
            pltpu.VMEM((2 * parts, 2 * rows, width), BF16),
            pltpu.VMEM((parts + 1, 2 * rows, width), F32),
        ],
        compiler_params=pltpu.CompilerParams(vmem_limit_bytes=40 * 2**20),
    )(moved, skip[None, :], forward, inverse)


def shards_general(values_in, gate_values, filter_spectrum, skip_gain, out_weight):
    parts = lax.axis_size("seq")
    layers = lax.axis_size("chan")
    rows, width = values_in.shape
    lanes = width // parts
    device = lax.axis_index("seq")

    def by_channel(array):
        return jnp.transpose(array.reshape(array.shape[0], parts, lanes), (1, 0, 2))

    filters = filter_spectrum.astype(BF16).reshape(4 * rows, width)
    packed = jnp.concatenate([by_channel(values_in), by_channel(gate_values), by_channel(filters)], axis=1)
    moved = lax.all_to_all(packed, "seq", 0, 0)
    skip = lax.dynamic_slice_in_dim(skip_gain, device * lanes, lanes)
    gated = convolve(moved, skip)
    gathered = lax.all_gather(gated.reshape(parts * rows, lanes), "seq", axis=1, tiled=True)

    own_cols = out_weight.shape[1]
    share = own_cols * parts // layers // parts
    per_block = parts // layers
    pieces = own_cols // share
    group = device % per_block
    member = device // per_block
    weight = jnp.zeros_like(out_weight)
    for step in range(pieces):
        piece = (member + step) % pieces
        sent = lax.dynamic_slice_in_dim(out_weight, piece * share, share, 1)
        pairs = [
            (source, source % per_block * pieces + (source // per_block + step) % pieces) for source in range(parts)
        ]
        arrived = lax.ppermute(sent, "seq", pairs)
        block = (device % pieces - step) % pieces
        weight = lax.dynamic_update_slice_in_dim(weight, arrived, block * share, 1)
    partials = jnp.dot(gathered, weight, preferred_element_type=F32).astype(BF16)
    mixed = lax.psum_scatter(partials, "chan", scatter_dimension=1, tiled=True)
    return lax.all_to_all(mixed, "seq", 0, 1, tiled=True)


WHOLE = pl.BlockSpec(memory_space=pltpu.VMEM)
CHEAP = pl.CostEstimate(flops=0, transcendentals=0, bytes_accessed=0)


def small_tables(parts, rows):
    total = 2 * parts * rows
    index = np.arange(rows)
    phase = 2.0 * np.pi * (index[:, None] * index[None, :] % rows) / rows
    cos, sin = np.cos(phase), np.sin(phase)
    forward = np.block([[cos, sin], [-sin, cos]])
    residue = np.arange(2 * parts).reshape(2, 1, parts)
    turn = 2.0 * np.pi * index[None, :, None] * residue / total
    return forward.astype(BF16), forward.T.astype(BF16), np.cos(turn).astype(F32), np.sin(turn).astype(F32)


def cosine(parts, residue, block):
    return float(np.cos(np.pi * residue * block / parts))


def sine(parts, residue, block):
    return float(np.sin(np.pi * residue * block / parts))


def weighted(terms):
    total = None
    for factor, term in terms:
        if abs(factor) < 1e-12:
            continue
        part = term if factor == 1.0 else factor * term
        total = part if total is None else total + part
    return total


def plus(left, right):
    return left if right is None else right if left is None else left + right


def minus(left, right):
    return left if right is None else -right if left is None else left - right


def own_place():
    device = lax.axis_index("seq")
    return device // 2, device % 2


def block_at(index, size):
    return pl.ds(pl.multiple_of(index * size, size), size)


def pack_filters_kernel(offsets, filter_ref, *refs):
    out_refs, (plane_ref, arrived) = refs[: len(offsets)], refs[len(offsets) :]
    chip, _ = own_place()
    planes, rows, _ = filter_ref.shape
    lanes = out_refs[0].shape[1]
    copies = []
    for place, offset in enumerate(offsets):
        here = block_at(chip ^ offset, lanes)
        for plane in range(planes):
            copies.append(
                pltpu.make_async_copy(filter_ref.at[plane, :, here], plane_ref.at[place, plane], arrived.at[place, plane])
            )
    for copy in copies:
        copy.start()
    for index, copy in enumerate(copies):
        copy.wait()
        place, plane = divmod(index, planes)
        out_refs[place][pl.ds(plane * rows, rows), :] = plane_ref[place, plane].astype(BF16)
    used = planes * rows
    for out_ref in out_refs:
        if out_ref.shape[0] > used:
            out_ref[pl.ds(used, out_ref.shape[0] - used), :] = out_ref[pl.ds(0, out_ref.shape[0] - used), :]


def pack_filters(filters, chips, offsets, spare):
    planes, rows, width = filters.shape
    lanes = width // chips
    return pl.pallas_call(
        functools.partial(pack_filters_kernel, offsets),
        in_specs=[pl.BlockSpec(memory_space=pltpu.HBM)],
        out_specs=[WHOLE] * len(offsets),
        out_shape=[jax.ShapeDtypeStruct((planes * rows + spare, lanes), BF16)] * len(offsets),
        scratch_shapes=[
            pltpu.VMEM((len(offsets), planes, rows, lanes), F32),
            pltpu.SemaphoreType.DMA((len(offsets), planes)),
        ],
        cost_estimate=CHEAP,
        compiler_params=pltpu.CompilerParams(vmem_limit_bytes=8 * 2**20),
        name="pack_filters",
    )(pltpu.with_memory_space_constraint(filters, pltpu.HBM))


def pack_values_kernel(chips, values_ref, *refs):
    out_refs, arrived = refs[:chips], refs[chips]
    rows = values_ref.shape[0]
    chip, _ = own_place()
    copies = []
    for offset, out_ref in enumerate(out_refs):
        values = values_ref.at[:, block_at(chip ^ offset, out_ref.shape[1])]
        copies.append(pltpu.make_async_copy(values, out_ref.at[pl.ds(0, rows)], arrived.at[offset]))
    for copy in copies:
        copy.start()
    for copy in copies:
        copy.wait()


def pack_values(values_in, chips, spare):
    rows, width = values_in.shape
    return pl.pallas_call(
        functools.partial(pack_values_kernel, chips),
        in_specs=[pl.BlockSpec(memory_space=pltpu.HBM)],
        out_specs=[WHOLE] * chips,
        out_shape=[jax.ShapeDtypeStruct((rows + spare, width // chips), BF16)] * chips,
        scratch_shapes=[pltpu.SemaphoreType.DMA((chips,))],
        cost_estimate=CHEAP,
        compiler_params=pltpu.CompilerParams(vmem_limit_bytes=4 * 2**20),
        name="pack_values",
    )(pltpu.with_memory_space_constraint(values_in, pltpu.HBM))


def pack_moved_kernel(chips, gate_ref, own_ref, other_ref, *refs):
    out_refs, (mine_ref, arrived) = refs[:chips], refs[chips:]
    chip, core = own_place()
    rows = gate_ref.shape[0]
    depth, held = own_ref.shape
    quarter, share = depth // 4, held // chips

    def copies_from(weight_ref):
        copies = [pltpu.make_async_copy(weight_ref.at[:, block_at(chip, share)], mine_ref, arrived.at[0, 0])]
        for offset in range(chips):
            out_ref, target = out_refs[offset], chip ^ offset
            gates = gate_ref.at[:, block_at(target, out_ref.shape[1])]
            copies.append(pltpu.make_async_copy(gates, out_ref.at[pl.ds(0, rows)], arrived.at[offset, 2]))
            for part in range(2 if offset else 0):
                source = weight_ref.at[block_at(2 * core + part, quarter), block_at(target, share)]
                sink = out_ref.at[pl.ds(rows, quarter), pl.ds(part * share, share)]
                copies.append(pltpu.make_async_copy(source, sink, arrived.at[offset, part]))
        for copy in copies:
            copy.start()
        for copy in copies:
            copy.wait()

    @pl.when(core == 0)
    def _():
        copies_from(own_ref)

    @pl.when(core == 1)
    def _():
        copies_from(other_ref)


def pack_moved(gate_values, own, other, chips):
    rows, width = gate_values.shape
    depth, held = own.shape
    share = held // chips
    return pl.pallas_call(
        functools.partial(pack_moved_kernel, chips),
        in_specs=[pl.BlockSpec(memory_space=pltpu.HBM)] * 2 + [pl.BlockSpec(memory_space=pl.ANY)],
        out_specs=[WHOLE] * (chips + 1),
        out_shape=[
            *(jax.ShapeDtypeStruct((rows + (depth // 4 if offset else 0), 2 * share), BF16) for offset in range(chips)),
            jax.ShapeDtypeStruct((depth, share), BF16),
        ],
        scratch_shapes=[pltpu.SemaphoreType.DMA((chips, 3))],
        cost_estimate=CHEAP,
        compiler_params=pltpu.CompilerParams(vmem_limit_bytes=8 * 2**20),
        name="pack_moved",
    )(*(pltpu.with_memory_space_constraint(array, pltpu.HBM) for array in (gate_values, own)), other)


def stack_kernel(chips, *refs):
    in_refs, out_refs = refs[:chips], refs[chips:]
    for offset, in_ref in enumerate(in_refs):
        part, place = divmod(offset, chips // 2)
        out_refs[part][place] = in_ref[pl.ds(0, out_refs[part].shape[1]), :]


def stack(blocks, rows):
    chips = len(blocks)
    half = jax.ShapeDtypeStruct((chips // 2, rows, blocks[0].shape[1]), BF16)
    return pl.pallas_call(
        functools.partial(stack_kernel, chips),
        in_specs=[WHOLE] * chips,
        out_specs=[WHOLE] * 2,
        out_shape=[half, half],
        cost_estimate=CHEAP,
        compiler_params=pltpu.CompilerParams(vmem_limit_bytes=4 * 2**20),
        name="stack",
    )(*blocks)


def forward_kernel(chips, cos_ref, sin_ref, table_ref, *refs):
    own_refs, other_refs, (out_ref, signal_ref, waves_ref) = refs[:2], refs[2:4], refs[4:]
    chip, core = own_place()
    parts = 2 * chips
    rows, lanes = own_refs[0].shape[1:]
    chunk, width = 16, 128
    for offset in range(chips):
        part, place = divmod(offset, chips // 2)
        signal_ref[2 * (chip ^ offset) + core] = own_refs[part][place]
        signal_ref[2 * (chip ^ offset) + 1 - core] = other_refs[part][place]
    sign = (1 - 2 * core).astype(F32)

    def spread(index, carry):
        here = block_at(index, chunk)
        there = pl.ds(pl.multiple_of(rows + index * chunk, chunk), chunk)
        cos_all, sin_all = cos_ref[core, here, :], sin_ref[core, here, :]
        for start in range(0, lanes, width):
            blocks = [signal_ref[block, here, pl.ds(start, width)].astype(F32) for block in range(parts)]
            blocks = [block * sign if place % 2 else block for place, block in enumerate(blocks)]

            def store(residue, real, imag):
                cos, sin = cos_all[:, residue : residue + 1], sin_all[:, residue : residue + 1]
                if imag is None:
                    real, imag = real * cos, -(real * sin)
                else:
                    real, imag = real * cos + imag * sin, imag * cos - real * sin
                columns = pl.ds(residue * lanes + start, width)
                waves_ref[here, columns] = real.astype(BF16)
                waves_ref[there, columns] = imag.astype(BF16)

            for residue in range(parts // 2 + 1):
                even, odd = range(0, parts, 2), range(1, parts, 2)
                cos_even = weighted([(cosine(parts, residue, block), blocks[block]) for block in even])
                cos_odd = weighted([(cosine(parts, residue, block), blocks[block]) for block in odd])
                sin_even = weighted([(sine(parts, residue, block), blocks[block]) for block in even])
                sin_odd = weighted([(sine(parts, residue, block), blocks[block]) for block in odd])
                sin_sum = plus(sin_even, sin_odd)
                store(residue, plus(cos_even, cos_odd), None if sin_sum is None else -sin_sum)
                if 0 < residue and 2 * residue != parts:
                    store(parts - residue, minus(cos_even, cos_odd), minus(sin_even, sin_odd))
        return carry

    lax.fori_loop(0, rows // chunk, spread, 0)
    for residue in range(parts):
        columns = pl.ds(residue * lanes, lanes)
        out_ref[:, columns] = jnp.dot(table_ref[...], waves_ref[:, columns], preferred_element_type=F32)


def forward(own, other, tables):
    chips, (_, rows, lanes) = 2 * own[0].shape[0], own[0].shape
    table, _, cos, sin = tables
    spectrum = (2 * rows, 2 * chips * lanes)
    return pl.pallas_call(
        functools.partial(forward_kernel, chips),
        in_specs=[WHOLE] * 7,
        out_specs=WHOLE,
        out_shape=jax.ShapeDtypeStruct(spectrum, F32),
        scratch_shapes=[pltpu.VMEM((2 * chips, rows, lanes), BF16), pltpu.VMEM(spectrum, BF16)],
        cost_estimate=CHEAP,
        compiler_params=pltpu.CompilerParams(vmem_limit_bytes=32 * 2**20),
        name="forward",
    )(cos, sin, table, *own, *other)


def backward_kernel(chips, cos_ref, sin_ref, table_ref, spectrum_ref, *refs):
    filter_refs, (keep_ref, *send_refs, filter_ref, product_ref, back_ref) = refs[:chips], refs[chips:]
    chip, core = own_place()
    parts = 2 * chips
    rows, lanes = keep_ref.shape[1:]
    chip_bits = chips.bit_length() - 1
    chunk, width = 16, 128
    for offset in range(chips):
        for plane in range(filter_ref.shape[1]):
            filter_ref[chip ^ offset, plane] = filter_refs[offset][pl.ds(plane * rows, rows), :]

    for residue in range(parts):
        source, odd = bit_reversed(residue // 2, chip_bits), residue % 2
        columns = pl.ds(residue * lanes, lanes)
        filter_real = filter_ref[source, odd].astype(F32)
        filter_imag = filter_ref[source, 2 + odd].astype(F32)
        real = spectrum_ref[pl.ds(0, rows), columns]
        imag = spectrum_ref[pl.ds(rows, rows), columns]
        product_ref[pl.ds(0, rows), columns] = (real * filter_real - imag * filter_imag).astype(BF16)
        product_ref[pl.ds(rows, rows), columns] = (real * filter_imag + imag * filter_real).astype(BF16)
        back_ref[:, columns] = jnp.dot(table_ref[...], product_ref[:, columns], preferred_element_type=F32)

    scale = 1.0 / (2 * parts * rows)
    sign = (1 - 2 * core).astype(F32)
    upper = core == 1

    def gather(index, carry):
        here = block_at(index, chunk)
        there = pl.ds(pl.multiple_of(rows + index * chunk, chunk), chunk)
        cos_all, sin_all = cos_ref[core, here, :] * scale, sin_ref[core, here, :] * scale
        for start in range(0, lanes, width):
            reals, imags = [], []
            for residue in range(parts):
                columns = pl.ds(residue * lanes + start, width)
                real, imag = back_ref[here, columns], back_ref[there, columns]
                cos, sin = cos_all[:, residue : residue + 1], sin_all[:, residue : residue + 1]
                reals.append(real * cos - imag * sin)
                imags.append(real * sin + imag * cos)
            totals = [None] * parts
            for block in range(parts // 2 + 1):
                even, odd = range(0, parts, 2), range(1, parts, 2)
                cos_even = weighted([(cosine(parts, residue, block), reals[residue]) for residue in even])
                cos_odd = weighted([(cosine(parts, residue, block), reals[residue]) for residue in odd])
                sin_even = weighted([(sine(parts, residue, block), imags[residue]) for residue in even])
                sin_odd = weighted([(sine(parts, residue, block), imags[residue]) for residue in odd])
                totals[block] = minus(plus(cos_even, cos_odd), plus(sin_even, sin_odd))
                if 0 < block and 2 * block != parts:
                    totals[parts - block] = plus(minus(cos_even, cos_odd), minus(sin_even, sin_odd))
            lane = pl.ds(start, width)
            for pair in range(chips):
                low, high = totals[2 * pair], totals[2 * pair + 1] * sign
                keep_ref[pair, here, lane] = jnp.where(upper, high, low)
                part, place = divmod(pair, chips // 2)
                send_refs[part][place, here, lane] = jnp.where(upper, low, high).astype(BF16)
        return carry

    lax.fori_loop(0, rows // chunk, gather, 0)


def backward(spectrum, first, tables):
    chips = len(first)
    rows, lanes = spectrum.shape[0] // 2, first[0].shape[1]
    _, table, cos, sin = tables
    half = jax.ShapeDtypeStruct((chips // 2, rows, lanes), BF16)
    return pl.pallas_call(
        functools.partial(backward_kernel, chips),
        in_specs=[WHOLE] * (4 + chips),
        out_specs=[WHOLE] * 3,
        out_shape=[jax.ShapeDtypeStruct((chips, rows, lanes), F32), half, half],
        scratch_shapes=[
            pltpu.VMEM((chips, 4, rows, lanes), BF16),
            pltpu.VMEM(spectrum.shape, BF16),
            pltpu.VMEM(spectrum.shape, F32),
        ],
        cost_estimate=CHEAP,
        compiler_params=pltpu.CompilerParams(vmem_limit_bytes=32 * 2**20),
        name="backward",
    )(cos, sin, table, spectrum, *first)


def gate_kernel(chips, skip_ref, keep_ref, low_ref, high_ref, *refs):
    signal_refs, gate_refs = refs[:chips], refs[chips : 2 * chips]
    out_ref, longer_ref, arrived_ref = refs[2 * chips :]
    chip, _ = own_place()
    rows, lanes = keep_ref.shape[1:]
    skip = skip_ref[:, block_at(chip, lanes)]
    arrived_ref[pl.ds(0, chips // 2)] = low_ref[...]
    arrived_ref[pl.ds(chips // 2, chips // 2)] = high_ref[...]
    for offset in range(chips):
        block = chip ^ offset
        convolved = keep_ref[block] + arrived_ref[block].astype(F32)
        signal = signal_refs[offset][pl.ds(0, rows), :].astype(F32)
        gate = gate_refs[offset][pl.ds(0, rows), :].astype(F32)
        gated = (gate * (convolved + skip * signal)).astype(BF16)
        out_ref[block_at(block, rows), :] = gated
        longer_ref[block_at(block, rows), :] = gated
    end = chips * rows
    longer_ref[pl.ds(end, longer_ref.shape[0] - end), :] = longer_ref[pl.ds(0, longer_ref.shape[0] - end), :]


def gate(skip, keep, arrived, first, gates, spare):
    chips, rows, lanes = keep.shape
    return pl.pallas_call(
        functools.partial(gate_kernel, chips),
        in_specs=[WHOLE] * (4 + 2 * chips),
        out_specs=[WHOLE] * 2,
        out_shape=[
            jax.ShapeDtypeStruct((chips * rows, lanes), BF16),
            jax.ShapeDtypeStruct((chips * rows + spare, lanes), BF16),
        ],
        scratch_shapes=[pltpu.VMEM((chips, rows, lanes), BF16)],
        cost_estimate=CHEAP,
        compiler_params=pltpu.CompilerParams(vmem_limit_bytes=6 * 2**20),
        name="gate",
    )(skip, keep, *arrived, *first, *gates)


def piece_of(ref, half, part):
    quarter, share = half // 2, ref.shape[1] // 2
    return ref[pl.ds(ref.shape[0] - quarter, quarter), pl.ds(part * share, share)]


def collect_kernel(in_refs, out_refs):
    rows = out_refs[0].shape[0]
    quarter = len(out_refs) * rows // (2 * len(in_refs))
    for place in range(2 * len(in_refs)):
        index, start = divmod(place * quarter, rows)
        out_refs[index][pl.ds(start, quarter), :] = piece_of(in_refs[place // 2], 2 * quarter, place % 2)


def collect(moved, half):
    count = len(moved)
    shape = (count * half // 2, moved[0].shape[1] // 2)
    return pl.pallas_call(
        lambda *refs: collect_kernel(refs[:count], refs[count:]),
        in_specs=[WHOLE] * count,
        out_specs=[WHOLE] * 2,
        out_shape=[jax.ShapeDtypeStruct(shape, BF16)] * 2,
        cost_estimate=CHEAP,
        compiler_params=pltpu.CompilerParams(vmem_limit_bytes=4 * 2**20),
        name="collect_weights",
    )(*moved)


def arrange_kernel(chips, mine_ref, *refs):
    moved_refs, (*other_refs, out_ref) = refs[: chips - 1], refs[chips - 1 :]
    chip, core = own_place()
    layer = lax.axis_index("chan")
    depth, share = mine_ref.shape
    quarter = depth // 4
    out_ref[:, block_at(chip ^ layer, share)] = mine_ref[...]
    for place in range(2 * (chips - 1)):
        offset, part = place // 2 + 1, place % 2
        columns = block_at(chip ^ layer ^ offset, share)
        index, start = divmod(place * quarter, other_refs[0].shape[0])
        out_ref[block_at(2 * core + part, quarter), columns] = piece_of(moved_refs[offset - 1], 2 * quarter, part)
        out_ref[block_at(2 * (1 - core) + part, quarter), columns] = other_refs[index][pl.ds(start, quarter), :]


def arrange(mine, moved, others):
    chips = len(moved) + 1
    depth, share = mine.shape
    return pl.pallas_call(
        functools.partial(arrange_kernel, chips),
        in_specs=[WHOLE] * (chips + len(others)),
        out_specs=WHOLE,
        out_shape=jax.ShapeDtypeStruct((depth, chips * share), BF16),
        cost_estimate=CHEAP,
        compiler_params=pltpu.CompilerParams(vmem_limit_bytes=8 * 2**20),
        name="arrange_weights",
    )(mine, *moved, *others)


def join_channels(chips, gated_refs, joined_ref):
    chip, _ = own_place()
    lanes = gated_refs[0].shape[1]
    for offset in range(chips):
        joined_ref[:, block_at(chip ^ offset, lanes)] = gated_refs[offset][pl.ds(0, joined_ref.shape[0]), :]


def project_moved_kernel(chips, weight_ref, *refs):
    gated_refs, (keep_ref, pass_ref, send_ref, joined_ref) = refs[:chips], refs[chips:]
    share = keep_ref.shape[1]
    join_channels(chips, gated_refs, joined_ref)
    partial = jnp.dot(joined_ref[...], weight_ref[...], preferred_element_type=F32).astype(BF16)
    keep_ref[...] = partial[:, :share]
    send_ref[0] = partial[:, share : 2 * share]
    pass_ref[...] = partial[:, 2 * share : 3 * share]
    send_ref[1] = partial[:, 3 * share :]


def project_moved(weight, gated):
    chips = len(gated)
    depth, columns = weight.shape
    rows = gated[0].shape[0]
    block = jax.ShapeDtypeStruct((rows, columns // chips), BF16)
    return pl.pallas_call(
        functools.partial(project_moved_kernel, chips),
        in_specs=[WHOLE] * (1 + chips),
        out_specs=[WHOLE] * 3,
        out_shape=[block, block, jax.ShapeDtypeStruct((2, rows, columns // chips), BF16)],
        scratch_shapes=[pltpu.VMEM((rows, depth), BF16)],
        cost_estimate=CHEAP,
        compiler_params=pltpu.CompilerParams(vmem_limit_bytes=8 * 2**20),
        name="project_moved",
    )(weight, *gated)


def project_still_kernel(chips, own_ref, other_ref, *refs):
    gated_refs, out_refs, joined_ref = refs[:chips], refs[chips : 2 * chips], refs[2 * chips]
    chip, core = own_place()
    rows = out_refs[0].shape[0]
    join_channels(chips, gated_refs, joined_ref)

    def project_with(weight_ref):
        for offset in range(chips):
            gated = joined_ref[block_at(chip ^ offset, rows), :]
            out_refs[offset][...] = jnp.dot(gated, weight_ref[...], preferred_element_type=F32).astype(BF16)

    @pl.when(core == 0)
    def _():
        project_with(other_ref)

    @pl.when(core == 1)
    def _():
        project_with(own_ref)


def project_still(own, other, gated):
    chips = len(gated)
    depth, held = own.shape
    rows = gated[0].shape[0] // chips
    return pl.pallas_call(
        functools.partial(project_still_kernel, chips),
        in_specs=[WHOLE] * (2 + chips),
        out_specs=[WHOLE] * chips,
        out_shape=[jax.ShapeDtypeStruct((rows, held), BF16)] * chips,
        scratch_shapes=[pltpu.VMEM((rows * chips, depth), BF16)],
        cost_estimate=CHEAP,
        compiler_params=pltpu.CompilerParams(vmem_limit_bytes=12 * 2**20),
        name="project_still",
    )(own, other, *gated)


def sort_kernel(chips, *refs):
    in_refs, (*out_refs, sorted_ref) = refs[:chips], refs[chips:]
    chip, _ = own_place()
    layer = lax.axis_index("chan")
    for offset in range(chips):
        sorted_ref[chip ^ layer ^ offset] = in_refs[offset][...]
    for target, out_ref in enumerate(out_refs):
        out_ref[...] = sorted_ref[target]


def sort_blocks(blocks):
    chips = len(blocks)
    block = jax.ShapeDtypeStruct(blocks[0].shape, BF16)
    return pl.pallas_call(
        functools.partial(sort_kernel, chips),
        in_specs=[WHOLE] * chips,
        out_specs=[WHOLE] * chips,
        out_shape=[block] * chips,
        scratch_shapes=[pltpu.VMEM((chips, *block.shape), BF16)],
        cost_estimate=CHEAP,
        compiler_params=pltpu.CompilerParams(vmem_limit_bytes=4 * 2**20),
        name="sort_blocks",
    )(*blocks)


def add_kernel(left_ref, right_ref, out_ref):
    rows = left_ref.shape[0]
    total = (left_ref[...].astype(F32) + right_ref[...].astype(F32)).astype(BF16)
    out_ref[pl.ds(0, rows), :] = total
    more = out_ref.shape[0] - rows
    if more:
        out_ref[pl.ds(rows, more), :] = total[:more]


def add(left, right, spare):
    rows, columns = left.shape
    return pl.pallas_call(
        add_kernel,
        in_specs=[WHOLE] * 2,
        out_specs=WHOLE,
        out_shape=jax.ShapeDtypeStruct((rows + spare, columns), BF16),
        cost_estimate=CHEAP,
        compiler_params=pltpu.CompilerParams(vmem_limit_bytes=4 * 2**20),
        name="add",
    )(left, right)


def finish_kernel(chips, keep_ref, first_ref, second_ref, *out_refs):
    chip, _ = own_place()
    rows = out_refs[0].shape[0]
    for offset in range(chips):
        here = block_at(chip ^ offset, rows)
        total = keep_ref[here, :].astype(F32) + first_ref[0, here, :].astype(F32) + second_ref[here, :].astype(F32)
        out_refs[offset][...] = total.astype(BF16)


def finish(keep, first, second, chips):
    rows, columns = keep.shape
    return pl.pallas_call(
        functools.partial(finish_kernel, chips),
        in_specs=[WHOLE] * 3,
        out_specs=[WHOLE] * chips,
        out_shape=[jax.ShapeDtypeStruct((rows // chips, columns), BF16)] * chips,
        cost_estimate=CHEAP,
        compiler_params=pltpu.CompilerParams(vmem_limit_bytes=4 * 2**20),
        name="finish",
    )(keep, first, second)


def join_kernel(chips, keep_ref, first_ref, second_ref, *refs):
    in_refs, out_ref = refs[:chips], refs[chips]
    chip, _ = own_place()
    share = in_refs[0].shape[1]
    for offset in range(chips):
        out_ref[:, block_at(chip ^ offset, share)] = in_refs[offset][...]
    total = keep_ref[...].astype(F32) + first_ref[...].astype(F32)
    total = total + second_ref[pl.ds(0, total.shape[0]), :].astype(F32)
    out_ref[:, pl.ds(chips * share, total.shape[1])] = total.astype(BF16)


def join(keep, first, second, blocks):
    chips = len(blocks)
    rows, share = blocks[0].shape
    return pl.pallas_call(
        functools.partial(join_kernel, chips),
        in_specs=[WHOLE] * (3 + chips),
        out_specs=WHOLE,
        out_shape=jax.ShapeDtypeStruct((rows, chips * share + keep.shape[1]), BF16),
        cost_estimate=CHEAP,
        compiler_params=pltpu.CompilerParams(vmem_limit_bytes=4 * 2**20),
        name="join",
    )(keep, first, second, *blocks)


def swapped(value, axis, offset):
    if not offset:
        return value
    return lax.ppermute(value, axis, [(source, source ^ offset) for source in range(lax.axis_size(axis))])


def to_chips(blocks):
    return [swapped(block, "seq", 2 * offset) for offset, block in enumerate(blocks)]


def after(value, *others):
    return lax.optimization_barrier((value, *others))[0]


def over_layers(passed, send):
    first = swapped(send, "chan", 1)
    passed = (passed.astype(F32) + first[1].astype(F32)).astype(BF16)
    return first, swapped(passed, "chan", 2)


def shards_direct(values_in, gate_values, filter_spectrum, skip_gain, out_weight):
    parts = lax.axis_size("seq")
    chips = parts // 2
    rows, width = values_in.shape
    tables = small_tables(parts, rows)

    values = pack_values(values_in, chips, 0)
    flat_filters = filter_spectrum.reshape(4, rows, width)
    near = pack_filters(after(flat_filters, values[0]), chips, (1, 2), 0)
    other_weight = swapped(out_weight, "seq", 1)
    *moved, mine = pack_moved(after(gate_values, near[0]), out_weight, other_weight, chips)
    own, far = pack_filters(after(flat_filters, moved[0]), chips, (0, 3), 0)
    values, filters = to_chips(values), to_chips([own, *near, far])
    own = stack([after(block, far) for block in values], rows)
    spectrum = forward(own, [swapped(part, "seq", 1) for part in own], tables)
    moved = to_chips([after(block, spectrum) for block in moved])
    keep, *send = backward(spectrum, filters, tables)
    gated, longer = gate(skip_gain[None, :], keep, [swapped(part, "seq", 1) for part in send], values, moved, 16)
    gathered = to_chips([gated, longer, longer, gated])

    others = [swapped(part, "seq", 1) for part in collect([after(block, gated) for block in moved[1:]], out_weight.shape[0] // 2)]
    keep, passed, send = project_moved(arrange(mine, moved[1:], others), gathered)
    blocks = to_chips(finish(keep, *over_layers(passed, send), chips))
    keep, near, passed, far = sort_blocks(to_chips(project_still(out_weight, other_weight, gathered)))
    second = swapped(add(after(passed, blocks[3]), swapped(far, "chan", 1), 0), "chan", 2)
    return join(keep, swapped(near, "chan", 1), second, blocks)


def shards(values_in, gate_values, filter_spectrum, skip_gain, out_weight):
    parts, layers = lax.axis_size("seq"), lax.axis_size("chan")
    rows, width = values_in.shape
    share = out_weight.shape[1] // layers
    aligned = width // parts % 128 == 0 and share % 128 == 0 and rows % 32 == 0
    run = shards_direct if aligned and layers == 4 and parts == 8 else shards_general
    return run(values_in, gate_values, filter_spectrum, skip_gain, out_weight)


def solution(mesh):
    in_specs = (
        P("seq", "chan"),
        P("seq", "chan"),
        P(None, "seq", None, "chan"),
        P("chan"),
        P("chan", "seq"),
    )
    out_specs = P("seq", "chan")
    return jax.shard_map(shards, mesh=mesh, in_specs=in_specs, out_specs=out_specs, check_vma=False)
```

```python
import functools

import jax
import jax.numpy as jnp
import numpy as np
from jax import lax
from jax.experimental import pallas as pl
from jax.experimental.pallas import tpu as pltpu
from jax.sharding import PartitionSpec as P

BF16 = jnp.bfloat16
F32 = jnp.float32


def bit_reversed(number, width_bits):
    flipped = 0
    for bit_place in range(width_bits):
        flipped |= (number >> bit_place & 1) << (width_bits - 1 - bit_place)
    return flipped


def filter_row(residue, width_bits):
    return 2 * bit_reversed(residue // 2, width_bits) + residue % 2


def dft_tables(parts, rows):
    total = 2 * parts * rows
    residue = np.arange(2 * parts)[:, None, None]
    column = np.arange(rows)[None, :, None]
    position = np.arange(rows)[None, None, :]
    phase = 2.0 * np.pi * (position * (residue + 2 * parts * column) % total) / total
    cos, sin = np.cos(phase), np.sin(phase)
    forward = np.concatenate(
        [np.concatenate([cos, sin], axis=2), np.concatenate([-sin, cos], axis=2)], axis=1
    )
    inverse = np.transpose(forward, (0, 2, 1)) / total
    return forward.astype(BF16), inverse.astype(BF16)


def convolve_kernel(parts, rows, moved_ref, skip_ref, forward_ref, inverse_ref, out_ref, waves_ref, back_ref):
    width_bits = parts.bit_length() - 1
    chunk = 16

    def cosine(residue, block):
        return float(np.cos(np.pi * residue * block / parts))

    def sine(residue, block):
        return float(np.sin(np.pi * residue * block / parts))

    def spread(index, carry):
        here = pl.ds(index * chunk, chunk)
        there = pl.ds(rows + index * chunk, chunk)
        blocks = [moved_ref[block, here, :].astype(F32) for block in range(parts)]
        for residue in range(parts + 1):
            real = blocks[0]
            imag = jnp.zeros_like(real)
            for block in range(1, parts):
                real = real + cosine(residue, block) * blocks[block]
                imag = imag - sine(residue, block) * blocks[block]
            waves_ref[residue, here, :] = real.astype(BF16)
            waves_ref[residue, there, :] = imag.astype(BF16)
            if 0 < residue < parts:
                waves_ref[2 * parts - residue, here, :] = real.astype(BF16)
                waves_ref[2 * parts - residue, there, :] = (-imag).astype(BF16)
        return carry

    lax.fori_loop(0, rows // chunk, spread, 0)

    def through(residue):
        wave = jnp.dot(forward_ref[residue], waves_ref[residue], preferred_element_type=F32)
        source, odd = divmod(filter_row(residue, width_bits), 2)
        filter_real = moved_ref[source, pl.ds((2 + odd) * rows, rows), :].astype(F32)
        filter_imag = moved_ref[source, pl.ds((4 + odd) * rows, rows), :].astype(F32)
        real, imag = wave[:rows], wave[rows:]
        product = jnp.concatenate(
            [real * filter_real - imag * filter_imag, real * filter_imag + imag * filter_real], axis=0
        )
        return jnp.dot(inverse_ref[residue], product.astype(BF16), preferred_element_type=F32)

    for residue in range(parts + 1):
        back = through(residue)
        if 0 < residue < parts:
            other = through(2 * parts - residue)
            back_ref[residue, pl.ds(0, rows), :] = back[:rows] + other[:rows]
            back_ref[residue, pl.ds(rows, rows), :] = back[rows:] - other[rows:]
        else:
            back_ref[residue] = back

    skip = skip_ref[...]

    def gather(index, carry):
        here = pl.ds(index * chunk, chunk)
        there = pl.ds(rows + index * chunk, chunk)
        reals = [back_ref[residue, here, :] for residue in range(parts + 1)]
        imags = [back_ref[residue, there, :] for residue in range(parts + 1)]
        for block in range(parts):
            total = reals[0]
            for residue in range(1, parts + 1):
                total = total + cosine(residue, block) * reals[residue]
                if residue < parts and block:
                    total = total - sine(residue, block) * imags[residue]
            signal = moved_ref[block, here, :].astype(F32)
            gate = moved_ref[block, pl.ds(rows + index * chunk, chunk), :].astype(F32)
            out_ref[block, here, :] = (gate * (total + skip * signal)).astype(BF16)
        return carry

    lax.fori_loop(0, rows // chunk, gather, 0)


def convolve(moved, skip):
    parts, stacked, width = moved.shape
    rows = stacked // 6
    forward, inverse = dft_tables(parts, rows)
    whole = pl.BlockSpec(memory_space=pltpu.VMEM)
    return pl.pallas_call(
        functools.partial(convolve_kernel, parts, rows),
        out_shape=jax.ShapeDtypeStruct((parts, rows, width), BF16),
        in_specs=[whole] * 4,
        out_specs=whole,
        scratch_shapes=[
            pltpu.VMEM((2 * parts, 2 * rows, width), BF16),
            pltpu.VMEM((parts + 1, 2 * rows, width), F32),
        ],
        compiler_params=pltpu.CompilerParams(vmem_limit_bytes=40 * 2**20),
    )(moved, skip[None, :], forward, inverse)


def shards_general(values_in, gate_values, filter_spectrum, skip_gain, out_weight):
    parts = lax.axis_size("seq")
    layers = lax.axis_size("chan")
    rows, width = values_in.shape
    lanes = width // parts
    device = lax.axis_index("seq")

    def by_channel(array):
        return jnp.transpose(array.reshape(array.shape[0], parts, lanes), (1, 0, 2))

    filters = filter_spectrum.astype(BF16).reshape(4 * rows, width)
    packed = jnp.concatenate([by_channel(values_in), by_channel(gate_values), by_channel(filters)], axis=1)
    moved = lax.all_to_all(packed, "seq", 0, 0)
    skip = lax.dynamic_slice_in_dim(skip_gain, device * lanes, lanes)
    gated = convolve(moved, skip)
    gathered = lax.all_gather(gated.reshape(parts * rows, lanes), "seq", axis=1, tiled=True)

    own_cols = out_weight.shape[1]
    share = own_cols * parts // layers // parts
    per_block = parts // layers
    pieces = own_cols // share
    group = device % per_block
    member = device // per_block
    weight = jnp.zeros_like(out_weight)
    for step in range(pieces):
        piece = (member + step) % pieces
        sent = lax.dynamic_slice_in_dim(out_weight, piece * share, share, 1)
        pairs = [
            (source, source % per_block * pieces + (source // per_block + step) % pieces) for source in range(parts)
        ]
        arrived = lax.ppermute(sent, "seq", pairs)
        block = (device % pieces - step) % pieces
        weight = lax.dynamic_update_slice_in_dim(weight, arrived, block * share, 1)
    partials = jnp.dot(gathered, weight, preferred_element_type=F32).astype(BF16)
    mixed = lax.psum_scatter(partials, "chan", scatter_dimension=1, tiled=True)
    return lax.all_to_all(mixed, "seq", 0, 1, tiled=True)


WHOLE = pl.BlockSpec(memory_space=pltpu.VMEM)
CHEAP = pl.CostEstimate(flops=0, transcendentals=0, bytes_accessed=0)


def small_tables(parts, rows):
    total = 2 * parts * rows
    index = np.arange(rows)
    phase = 2.0 * np.pi * (index[:, None] * index[None, :] % rows) / rows
    cos, sin = np.cos(phase), np.sin(phase)
    forward = np.block([[cos, sin], [-sin, cos]])
    residue = np.arange(2 * parts).reshape(2, 1, parts)
    turn = 2.0 * np.pi * index[None, :, None] * residue / total
    return forward.astype(BF16), forward.T.astype(BF16), np.cos(turn).astype(F32), np.sin(turn).astype(F32)


def cosine(parts, residue, block):
    return float(np.cos(np.pi * residue * block / parts))


def sine(parts, residue, block):
    return float(np.sin(np.pi * residue * block / parts))


def weighted(terms):
    total = None
    for factor, term in terms:
        if abs(factor) < 1e-12:
            continue
        part = term if factor == 1.0 else factor * term
        total = part if total is None else total + part
    return total


def plus(left, right):
    return left if right is None else right if left is None else left + right


def minus(left, right):
    return left if right is None else -right if left is None else left - right


def own_place():
    device = lax.axis_index("seq")
    return device // 2, device % 2


def block_at(index, size):
    return pl.ds(pl.multiple_of(index * size, size), size)


def pack_filters_kernel(offsets, filter_ref, *refs):
    out_refs, (plane_ref, arrived) = refs[: len(offsets)], refs[len(offsets) :]
    chip, _ = own_place()
    planes, rows, _ = filter_ref.shape
    lanes = out_refs[0].shape[1]
    copies = []
    for place, offset in enumerate(offsets):
        here = block_at(chip ^ offset, lanes)
        for plane in range(planes):
            copies.append(
                pltpu.make_async_copy(filter_ref.at[plane, :, here], plane_ref.at[place, plane], arrived.at[place, plane])
            )
    for copy in copies:
        copy.start()
    for index, copy in enumerate(copies):
        copy.wait()
        place, plane = divmod(index, planes)
        out_refs[place][pl.ds(plane * rows, rows), :] = plane_ref[place, plane].astype(BF16)
    used = planes * rows
    for out_ref in out_refs:
        if out_ref.shape[0] > used:
            out_ref[pl.ds(used, out_ref.shape[0] - used), :] = out_ref[pl.ds(0, out_ref.shape[0] - used), :]


def pack_filters(filters, chips, offsets, spare):
    planes, rows, width = filters.shape
    lanes = width // chips
    return pl.pallas_call(
        functools.partial(pack_filters_kernel, offsets),
        in_specs=[pl.BlockSpec(memory_space=pltpu.HBM)],
        out_specs=[WHOLE] * len(offsets),
        out_shape=[jax.ShapeDtypeStruct((planes * rows + spare, lanes), BF16)] * len(offsets),
        scratch_shapes=[
            pltpu.VMEM((len(offsets), planes, rows, lanes), F32),
            pltpu.SemaphoreType.DMA((len(offsets), planes)),
        ],
        cost_estimate=CHEAP,
        compiler_params=pltpu.CompilerParams(vmem_limit_bytes=8 * 2**20),
        name="pack_filters",
    )(pltpu.with_memory_space_constraint(filters, pltpu.HBM))


def pack_values_kernel(chips, values_ref, *refs):
    out_refs, arrived = refs[:chips], refs[chips]
    rows = values_ref.shape[0]
    chip, _ = own_place()
    copies = []
    for offset, out_ref in enumerate(out_refs):
        values = values_ref.at[:, block_at(chip ^ offset, out_ref.shape[1])]
        copies.append(pltpu.make_async_copy(values, out_ref.at[pl.ds(0, rows)], arrived.at[offset]))
    for copy in copies:
        copy.start()
    for copy in copies:
        copy.wait()


def pack_values(values_in, chips, spare):
    rows, width = values_in.shape
    return pl.pallas_call(
        functools.partial(pack_values_kernel, chips),
        in_specs=[pl.BlockSpec(memory_space=pltpu.HBM)],
        out_specs=[WHOLE] * chips,
        out_shape=[jax.ShapeDtypeStruct((rows + spare, width // chips), BF16)] * chips,
        scratch_shapes=[pltpu.SemaphoreType.DMA((chips,))],
        cost_estimate=CHEAP,
        compiler_params=pltpu.CompilerParams(vmem_limit_bytes=4 * 2**20),
        name="pack_values",
    )(pltpu.with_memory_space_constraint(values_in, pltpu.HBM))


def pack_moved_kernel(chips, gate_ref, own_ref, other_ref, *refs):
    out_refs, (mine_ref, arrived) = refs[:chips], refs[chips:]
    chip, core = own_place()
    rows = gate_ref.shape[0]
    depth, held = own_ref.shape
    quarter, share = depth // 4, held // chips

    def copies_from(weight_ref):
        copies = [pltpu.make_async_copy(weight_ref.at[:, block_at(chip, share)], mine_ref, arrived.at[0, 0])]
        for offset in range(chips):
            out_ref, target = out_refs[offset], chip ^ offset
            gates = gate_ref.at[:, block_at(target, out_ref.shape[1])]
            copies.append(pltpu.make_async_copy(gates, out_ref.at[pl.ds(0, rows)], arrived.at[offset, 2]))
            for part in range(2 if offset else 0):
                source = weight_ref.at[block_at(2 * core + part, quarter), block_at(target, share)]
                sink = out_ref.at[pl.ds(rows, quarter), pl.ds(part * share, share)]
                copies.append(pltpu.make_async_copy(source, sink, arrived.at[offset, part]))
        for copy in copies:
            copy.start()
        for copy in copies:
            copy.wait()

    @pl.when(core == 0)
    def _():
        copies_from(own_ref)

    @pl.when(core == 1)
    def _():
        copies_from(other_ref)


def pack_moved(gate_values, own, other, chips):
    rows, width = gate_values.shape
    depth, held = own.shape
    share = held // chips
    return pl.pallas_call(
        functools.partial(pack_moved_kernel, chips),
        in_specs=[pl.BlockSpec(memory_space=pltpu.HBM)] * 2 + [pl.BlockSpec(memory_space=pl.ANY)],
        out_specs=[WHOLE] * (chips + 1),
        out_shape=[
            *(jax.ShapeDtypeStruct((rows + (depth // 4 if offset else 0), 2 * share), BF16) for offset in range(chips)),
            jax.ShapeDtypeStruct((depth, share), BF16),
        ],
        scratch_shapes=[pltpu.SemaphoreType.DMA((chips, 3))],
        cost_estimate=CHEAP,
        compiler_params=pltpu.CompilerParams(vmem_limit_bytes=8 * 2**20),
        name="pack_moved",
    )(*(pltpu.with_memory_space_constraint(array, pltpu.HBM) for array in (gate_values, own)), other)


def stack_kernel(chips, *refs):
    in_refs, out_refs = refs[:chips], refs[chips:]
    for offset, in_ref in enumerate(in_refs):
        part, place = divmod(offset, chips // 2)
        out_refs[part][place] = in_ref[pl.ds(0, out_refs[part].shape[1]), :]


def stack(blocks, rows):
    chips = len(blocks)
    half = jax.ShapeDtypeStruct((chips // 2, rows, blocks[0].shape[1]), BF16)
    return pl.pallas_call(
        functools.partial(stack_kernel, chips),
        in_specs=[WHOLE] * chips,
        out_specs=[WHOLE] * 2,
        out_shape=[half, half],
        cost_estimate=CHEAP,
        compiler_params=pltpu.CompilerParams(vmem_limit_bytes=4 * 2**20),
        name="stack",
    )(*blocks)


def forward_kernel(chips, cos_ref, sin_ref, table_ref, *refs):
    own_refs, other_refs, (out_ref, signal_ref, waves_ref) = refs[:2], refs[2:4], refs[4:]
    chip, core = own_place()
    parts = 2 * chips
    rows, lanes = own_refs[0].shape[1:]
    chunk, width = 16, 128
    for offset in range(chips):
        part, place = divmod(offset, chips // 2)
        signal_ref[2 * (chip ^ offset) + core] = own_refs[part][place]
        signal_ref[2 * (chip ^ offset) + 1 - core] = other_refs[part][place]
    sign = (1 - 2 * core).astype(F32)

    def spread(index, carry):
        here = block_at(index, chunk)
        there = pl.ds(pl.multiple_of(rows + index * chunk, chunk), chunk)
        cos_all, sin_all = cos_ref[core, here, :], sin_ref[core, here, :]
        for start in range(0, lanes, width):
            blocks = [signal_ref[block, here, pl.ds(start, width)].astype(F32) for block in range(parts)]
            blocks = [block * sign if place % 2 else block for place, block in enumerate(blocks)]

            def store(residue, real, imag):
                cos, sin = cos_all[:, residue : residue + 1], sin_all[:, residue : residue + 1]
                if imag is None:
                    real, imag = real * cos, -(real * sin)
                else:
                    real, imag = real * cos + imag * sin, imag * cos - real * sin
                columns = pl.ds(residue * lanes + start, width)
                waves_ref[here, columns] = real.astype(BF16)
                waves_ref[there, columns] = imag.astype(BF16)

            for residue in range(parts // 2 + 1):
                even, odd = range(0, parts, 2), range(1, parts, 2)
                cos_even = weighted([(cosine(parts, residue, block), blocks[block]) for block in even])
                cos_odd = weighted([(cosine(parts, residue, block), blocks[block]) for block in odd])
                sin_even = weighted([(sine(parts, residue, block), blocks[block]) for block in even])
                sin_odd = weighted([(sine(parts, residue, block), blocks[block]) for block in odd])
                sin_sum = plus(sin_even, sin_odd)
                store(residue, plus(cos_even, cos_odd), None if sin_sum is None else -sin_sum)
                if 0 < residue and 2 * residue != parts:
                    store(parts - residue, minus(cos_even, cos_odd), minus(sin_even, sin_odd))
        return carry

    lax.fori_loop(0, rows // chunk, spread, 0)
    for residue in range(parts):
        columns = pl.ds(residue * lanes, lanes)
        out_ref[:, columns] = jnp.dot(table_ref[...], waves_ref[:, columns], preferred_element_type=F32)


def forward(own, other, tables):
    chips, (_, rows, lanes) = 2 * own[0].shape[0], own[0].shape
    table, _, cos, sin = tables
    spectrum = (2 * rows, 2 * chips * lanes)
    return pl.pallas_call(
        functools.partial(forward_kernel, chips),
        in_specs=[WHOLE] * 7,
        out_specs=WHOLE,
        out_shape=jax.ShapeDtypeStruct(spectrum, F32),
        scratch_shapes=[pltpu.VMEM((2 * chips, rows, lanes), BF16), pltpu.VMEM(spectrum, BF16)],
        cost_estimate=CHEAP,
        compiler_params=pltpu.CompilerParams(vmem_limit_bytes=32 * 2**20),
        name="forward",
    )(cos, sin, table, *own, *other)


def backward_kernel(chips, cos_ref, sin_ref, table_ref, spectrum_ref, *refs):
    filter_refs, (keep_ref, *send_refs, filter_ref, product_ref, back_ref) = refs[:chips], refs[chips:]
    chip, core = own_place()
    parts = 2 * chips
    rows, lanes = keep_ref.shape[1:]
    chip_bits = chips.bit_length() - 1
    chunk, width = 16, 128
    for offset in range(chips):
        for plane in range(filter_ref.shape[1]):
            filter_ref[chip ^ offset, plane] = filter_refs[offset][pl.ds(plane * rows, rows), :]

    for residue in range(parts):
        source, odd = bit_reversed(residue // 2, chip_bits), residue % 2
        columns = pl.ds(residue * lanes, lanes)
        filter_real = filter_ref[source, odd].astype(F32)
        filter_imag = filter_ref[source, 2 + odd].astype(F32)
        real = spectrum_ref[pl.ds(0, rows), columns]
        imag = spectrum_ref[pl.ds(rows, rows), columns]
        product_ref[pl.ds(0, rows), columns] = (real * filter_real - imag * filter_imag).astype(BF16)
        product_ref[pl.ds(rows, rows), columns] = (real * filter_imag + imag * filter_real).astype(BF16)
        back_ref[:, columns] = jnp.dot(table_ref[...], product_ref[:, columns], preferred_element_type=F32)

    scale = 1.0 / (2 * parts * rows)
    sign = (1 - 2 * core).astype(F32)
    upper = core == 1

    def gather(index, carry):
        here = block_at(index, chunk)
        there = pl.ds(pl.multiple_of(rows + index * chunk, chunk), chunk)
        cos_all, sin_all = cos_ref[core, here, :] * scale, sin_ref[core, here, :] * scale
        for start in range(0, lanes, width):
            reals, imags = [], []
            for residue in range(parts):
                columns = pl.ds(residue * lanes + start, width)
                real, imag = back_ref[here, columns], back_ref[there, columns]
                cos, sin = cos_all[:, residue : residue + 1], sin_all[:, residue : residue + 1]
                reals.append(real * cos - imag * sin)
                imags.append(real * sin + imag * cos)
            totals = [None] * parts
            for block in range(parts // 2 + 1):
                even, odd = range(0, parts, 2), range(1, parts, 2)
                cos_even = weighted([(cosine(parts, residue, block), reals[residue]) for residue in even])
                cos_odd = weighted([(cosine(parts, residue, block), reals[residue]) for residue in odd])
                sin_even = weighted([(sine(parts, residue, block), imags[residue]) for residue in even])
                sin_odd = weighted([(sine(parts, residue, block), imags[residue]) for residue in odd])
                totals[block] = minus(plus(cos_even, cos_odd), plus(sin_even, sin_odd))
                if 0 < block and 2 * block != parts:
                    totals[parts - block] = plus(minus(cos_even, cos_odd), minus(sin_even, sin_odd))
            lane = pl.ds(start, width)
            for pair in range(chips):
                low, high = totals[2 * pair], totals[2 * pair + 1] * sign
                keep_ref[pair, here, lane] = jnp.where(upper, high, low)
                part, place = divmod(pair, chips // 2)
                send_refs[part][place, here, lane] = jnp.where(upper, low, high).astype(BF16)
        return carry

    lax.fori_loop(0, rows // chunk, gather, 0)


def backward(spectrum, first, tables):
    chips = len(first)
    rows, lanes = spectrum.shape[0] // 2, first[0].shape[1]
    _, table, cos, sin = tables
    half = jax.ShapeDtypeStruct((chips // 2, rows, lanes), BF16)
    return pl.pallas_call(
        functools.partial(backward_kernel, chips),
        in_specs=[WHOLE] * (4 + chips),
        out_specs=[WHOLE] * 3,
        out_shape=[jax.ShapeDtypeStruct((chips, rows, lanes), F32), half, half],
        scratch_shapes=[
            pltpu.VMEM((chips, 4, rows, lanes), BF16),
            pltpu.VMEM(spectrum.shape, BF16),
            pltpu.VMEM(spectrum.shape, F32),
        ],
        cost_estimate=CHEAP,
        compiler_params=pltpu.CompilerParams(vmem_limit_bytes=32 * 2**20),
        name="backward",
    )(cos, sin, table, spectrum, *first)


def gate_kernel(chips, skip_ref, keep_ref, low_ref, high_ref, *refs):
    signal_refs, gate_refs = refs[:chips], refs[chips : 2 * chips]
    out_ref, longer_ref, arrived_ref = refs[2 * chips :]
    chip, _ = own_place()
    rows, lanes = keep_ref.shape[1:]
    skip = skip_ref[:, block_at(chip, lanes)]
    arrived_ref[pl.ds(0, chips // 2)] = low_ref[...]
    arrived_ref[pl.ds(chips // 2, chips // 2)] = high_ref[...]
    for offset in range(chips):
        block = chip ^ offset
        convolved = keep_ref[block] + arrived_ref[block].astype(F32)
        signal = signal_refs[offset][pl.ds(0, rows), :].astype(F32)
        gate = gate_refs[offset][pl.ds(0, rows), :].astype(F32)
        gated = (gate * (convolved + skip * signal)).astype(BF16)
        out_ref[block_at(block, rows), :] = gated
        longer_ref[block_at(block, rows), :] = gated
    end = chips * rows
    longer_ref[pl.ds(end, longer_ref.shape[0] - end), :] = longer_ref[pl.ds(0, longer_ref.shape[0] - end), :]


def gate(skip, keep, arrived, first, gates, spare):
    chips, rows, lanes = keep.shape
    return pl.pallas_call(
        functools.partial(gate_kernel, chips),
        in_specs=[WHOLE] * (4 + 2 * chips),
        out_specs=[WHOLE] * 2,
        out_shape=[
            jax.ShapeDtypeStruct((chips * rows, lanes), BF16),
            jax.ShapeDtypeStruct((chips * rows + spare, lanes), BF16),
        ],
        scratch_shapes=[pltpu.VMEM((chips, rows, lanes), BF16)],
        cost_estimate=CHEAP,
        compiler_params=pltpu.CompilerParams(vmem_limit_bytes=6 * 2**20),
        name="gate",
    )(skip, keep, *arrived, *first, *gates)


def piece_of(ref, half, part):
    quarter, share = half // 2, ref.shape[1] // 2
    return ref[pl.ds(ref.shape[0] - quarter, quarter), pl.ds(part * share, share)]


def collect_kernel(in_refs, out_refs):
    rows = out_refs[0].shape[0]
    quarter = len(out_refs) * rows // (2 * len(in_refs))
    for place in range(2 * len(in_refs)):
        index, start = divmod(place * quarter, rows)
        out_refs[index][pl.ds(start, quarter), :] = piece_of(in_refs[place // 2], 2 * quarter, place % 2)


def collect(moved, half):
    count = len(moved)
    shape = (count * half // 2, moved[0].shape[1] // 2)
    return pl.pallas_call(
        lambda *refs: collect_kernel(refs[:count], refs[count:]),
        in_specs=[WHOLE] * count,
        out_specs=[WHOLE] * 2,
        out_shape=[jax.ShapeDtypeStruct(shape, BF16)] * 2,
        cost_estimate=CHEAP,
        compiler_params=pltpu.CompilerParams(vmem_limit_bytes=4 * 2**20),
        name="collect_weights",
    )(*moved)


def arrange_kernel(chips, mine_ref, *refs):
    moved_refs, (*other_refs, out_ref) = refs[: chips - 1], refs[chips - 1 :]
    chip, core = own_place()
    layer = lax.axis_index("chan")
    depth, share = mine_ref.shape
    quarter = depth // 4
    out_ref[:, block_at(chip ^ layer, share)] = mine_ref[...]
    for place in range(2 * (chips - 1)):
        offset, part = place // 2 + 1, place % 2
        columns = block_at(chip ^ layer ^ offset, share)
        index, start = divmod(place * quarter, other_refs[0].shape[0])
        out_ref[block_at(2 * core + part, quarter), columns] = piece_of(moved_refs[offset - 1], 2 * quarter, part)
        out_ref[block_at(2 * (1 - core) + part, quarter), columns] = other_refs[index][pl.ds(start, quarter), :]


def arrange(mine, moved, others):
    chips = len(moved) + 1
    depth, share = mine.shape
    return pl.pallas_call(
        functools.partial(arrange_kernel, chips),
        in_specs=[WHOLE] * (chips + len(others)),
        out_specs=WHOLE,
        out_shape=jax.ShapeDtypeStruct((depth, chips * share), BF16),
        cost_estimate=CHEAP,
        compiler_params=pltpu.CompilerParams(vmem_limit_bytes=8 * 2**20),
        name="arrange_weights",
    )(mine, *moved, *others)


def join_channels(chips, gated_refs, joined_ref):
    chip, _ = own_place()
    lanes = gated_refs[0].shape[1]
    for offset in range(chips):
        joined_ref[:, block_at(chip ^ offset, lanes)] = gated_refs[offset][pl.ds(0, joined_ref.shape[0]), :]


def project_moved_kernel(chips, weight_ref, *refs):
    gated_refs, (keep_ref, pass_ref, send_ref, joined_ref) = refs[:chips], refs[chips:]
    share = keep_ref.shape[1]
    join_channels(chips, gated_refs, joined_ref)
    partial = jnp.dot(joined_ref[...], weight_ref[...], preferred_element_type=F32).astype(BF16)
    keep_ref[...] = partial[:, :share]
    send_ref[0] = partial[:, share : 2 * share]
    pass_ref[...] = partial[:, 2 * share : 3 * share]
    send_ref[1] = partial[:, 3 * share :]


def project_moved(weight, gated):
    chips = len(gated)
    depth, columns = weight.shape
    rows = gated[0].shape[0]
    block = jax.ShapeDtypeStruct((rows, columns // chips), BF16)
    return pl.pallas_call(
        functools.partial(project_moved_kernel, chips),
        in_specs=[WHOLE] * (1 + chips),
        out_specs=[WHOLE] * 3,
        out_shape=[block, block, jax.ShapeDtypeStruct((2, rows, columns // chips), BF16)],
        scratch_shapes=[pltpu.VMEM((rows, depth), BF16)],
        cost_estimate=CHEAP,
        compiler_params=pltpu.CompilerParams(vmem_limit_bytes=8 * 2**20),
        name="project_moved",
    )(weight, *gated)


def project_still_kernel(chips, own_ref, other_ref, *refs):
    gated_refs, out_refs, joined_ref = refs[:chips], refs[chips : 2 * chips], refs[2 * chips]
    chip, core = own_place()
    rows = out_refs[0].shape[0]
    join_channels(chips, gated_refs, joined_ref)

    def project_with(weight_ref):
        for offset in range(chips):
            gated = joined_ref[block_at(chip ^ offset, rows), :]
            out_refs[offset][...] = jnp.dot(gated, weight_ref[...], preferred_element_type=F32).astype(BF16)

    @pl.when(core == 0)
    def _():
        project_with(other_ref)

    @pl.when(core == 1)
    def _():
        project_with(own_ref)


def project_still(own, other, gated):
    chips = len(gated)
    depth, held = own.shape
    rows = gated[0].shape[0] // chips
    return pl.pallas_call(
        functools.partial(project_still_kernel, chips),
        in_specs=[WHOLE] * (2 + chips),
        out_specs=[WHOLE] * chips,
        out_shape=[jax.ShapeDtypeStruct((rows, held), BF16)] * chips,
        scratch_shapes=[pltpu.VMEM((rows * chips, depth), BF16)],
        cost_estimate=CHEAP,
        compiler_params=pltpu.CompilerParams(vmem_limit_bytes=12 * 2**20),
        name="project_still",
    )(own, other, *gated)


def sort_kernel(chips, *refs):
    in_refs, (*out_refs, sorted_ref) = refs[:chips], refs[chips:]
    chip, _ = own_place()
    layer = lax.axis_index("chan")
    for offset in range(chips):
        sorted_ref[chip ^ layer ^ offset] = in_refs[offset][...]
    for target, out_ref in enumerate(out_refs):
        out_ref[...] = sorted_ref[target]


def sort_blocks(blocks):
    chips = len(blocks)
    block = jax.ShapeDtypeStruct(blocks[0].shape, BF16)
    return pl.pallas_call(
        functools.partial(sort_kernel, chips),
        in_specs=[WHOLE] * chips,
        out_specs=[WHOLE] * chips,
        out_shape=[block] * chips,
        scratch_shapes=[pltpu.VMEM((chips, *block.shape), BF16)],
        cost_estimate=CHEAP,
        compiler_params=pltpu.CompilerParams(vmem_limit_bytes=4 * 2**20),
        name="sort_blocks",
    )(*blocks)


def add_kernel(left_ref, right_ref, out_ref):
    rows = left_ref.shape[0]
    total = (left_ref[...].astype(F32) + right_ref[...].astype(F32)).astype(BF16)
    out_ref[pl.ds(0, rows), :] = total
    more = out_ref.shape[0] - rows
    if more:
        out_ref[pl.ds(rows, more), :] = total[:more]


def add(left, right, spare):
    rows, columns = left.shape
    return pl.pallas_call(
        add_kernel,
        in_specs=[WHOLE] * 2,
        out_specs=WHOLE,
        out_shape=jax.ShapeDtypeStruct((rows + spare, columns), BF16),
        cost_estimate=CHEAP,
        compiler_params=pltpu.CompilerParams(vmem_limit_bytes=4 * 2**20),
        name="add",
    )(left, right)


def finish_kernel(chips, keep_ref, first_ref, second_ref, *out_refs):
    chip, _ = own_place()
    rows = out_refs[0].shape[0]
    for offset in range(chips):
        here = block_at(chip ^ offset, rows)
        total = keep_ref[here, :].astype(F32) + first_ref[0, here, :].astype(F32) + second_ref[here, :].astype(F32)
        out_refs[offset][...] = total.astype(BF16)


def finish(keep, first, second, chips):
    rows, columns = keep.shape
    return pl.pallas_call(
        functools.partial(finish_kernel, chips),
        in_specs=[WHOLE] * 3,
        out_specs=[WHOLE] * chips,
        out_shape=[jax.ShapeDtypeStruct((rows // chips, columns), BF16)] * chips,
        cost_estimate=CHEAP,
        compiler_params=pltpu.CompilerParams(vmem_limit_bytes=4 * 2**20),
        name="finish",
    )(keep, first, second)


def join_kernel(chips, keep_ref, first_ref, second_ref, *refs):
    in_refs, out_ref = refs[:chips], refs[chips]
    chip, _ = own_place()
    share = in_refs[0].shape[1]
    for offset in range(chips):
        out_ref[:, block_at(chip ^ offset, share)] = in_refs[offset][...]
    total = keep_ref[...].astype(F32) + first_ref[...].astype(F32)
    total = total + second_ref[pl.ds(0, total.shape[0]), :].astype(F32)
    out_ref[:, pl.ds(chips * share, total.shape[1])] = total.astype(BF16)


def join(keep, first, second, blocks):
    chips = len(blocks)
    rows, share = blocks[0].shape
    return pl.pallas_call(
        functools.partial(join_kernel, chips),
        in_specs=[WHOLE] * (3 + chips),
        out_specs=WHOLE,
        out_shape=jax.ShapeDtypeStruct((rows, chips * share + keep.shape[1]), BF16),
        cost_estimate=CHEAP,
        compiler_params=pltpu.CompilerParams(vmem_limit_bytes=4 * 2**20),
        name="join",
    )(keep, first, second, *blocks)


def swapped(value, axis, offset):
    if not offset:
        return value
    return lax.ppermute(value, axis, [(source, source ^ offset) for source in range(lax.axis_size(axis))])


def to_chips(blocks):
    return [swapped(block, "seq", 2 * offset) for offset, block in enumerate(blocks)]


def after(value, *others):
    return lax.optimization_barrier((value, *others))[0]


def over_layers(passed, send):
    first = swapped(send, "chan", 1)
    passed = (passed.astype(F32) + first[1].astype(F32)).astype(BF16)
    return first, swapped(passed, "chan", 2)


def shards_direct(values_in, gate_values, filter_spectrum, skip_gain, out_weight):
    parts = lax.axis_size("seq")
    chips = parts // 2
    rows, width = values_in.shape
    tables = small_tables(parts, rows)

    values = pack_values(values_in, chips, 0)
    flat_filters = filter_spectrum.reshape(4, rows, width)
    near = pack_filters(after(flat_filters, values[0]), chips, (1, 2), 0)
    other_weight = swapped(out_weight, "seq", 1)
    *moved, mine = pack_moved(after(gate_values, near[0]), out_weight, other_weight, chips)
    own, far = pack_filters(after(flat_filters, moved[0]), chips, (0, 3), 0)
    values, filters = to_chips(values), to_chips([own, *near, far])
    own = stack([after(block, far) for block in values], rows)
    spectrum = forward(own, [swapped(part, "seq", 1) for part in own], tables)
    moved = to_chips([after(block, spectrum) for block in moved])
    keep, *send = backward(spectrum, filters, tables)
    gated, longer = gate(skip_gain[None, :], keep, [swapped(part, "seq", 1) for part in send], values, moved, 16)
    gathered = to_chips([gated, longer, longer, gated])

    others = [swapped(part, "seq", 1) for part in collect([after(block, gated) for block in moved[1:]], out_weight.shape[0] // 2)]
    keep, passed, send = project_moved(arrange(mine, moved[1:], others), gathered)
    blocks = to_chips(finish(keep, *over_layers(passed, send), chips))
    keep, near, passed, far = sort_blocks(to_chips(project_still(out_weight, other_weight, gathered)))
    second = swapped(add(after(passed, blocks[3], blocks[1]), swapped(far, "chan", 1), 0), "chan", 2)
    return join(keep, swapped(near, "chan", 1), second, blocks)


def shards(values_in, gate_values, filter_spectrum, skip_gain, out_weight):
    parts, layers = lax.axis_size("seq"), lax.axis_size("chan")
    rows, width = values_in.shape
    share = out_weight.shape[1] // layers
    aligned = width // parts % 128 == 0 and share % 128 == 0 and rows % 32 == 0
    run = shards_direct if aligned and layers == 4 and parts == 8 else shards_general
    return run(values_in, gate_values, filter_spectrum, skip_gain, out_weight)


def solution(mesh):
    in_specs = (
        P("seq", "chan"),
        P("seq", "chan"),
        P(None, "seq", None, "chan"),
        P("chan"),
        P("chan", "seq"),
    )
    out_specs = P("seq", "chan")
    return jax.shard_map(shards, mesh=mesh, in_specs=in_specs, out_specs=out_specs, check_vma=False)
```

```python
import functools

import jax
import jax.numpy as jnp
import numpy as np
from jax import lax
from jax.experimental import pallas as pl
from jax.experimental.pallas import tpu as pltpu
from jax.sharding import PartitionSpec as P

BF16 = jnp.bfloat16
F32 = jnp.float32


def bit_reversed(number, width_bits):
    flipped = 0
    for bit_place in range(width_bits):
        flipped |= (number >> bit_place & 1) << (width_bits - 1 - bit_place)
    return flipped


def filter_row(residue, width_bits):
    return 2 * bit_reversed(residue // 2, width_bits) + residue % 2


def dft_tables(parts, rows):
    total = 2 * parts * rows
    residue = np.arange(2 * parts)[:, None, None]
    column = np.arange(rows)[None, :, None]
    position = np.arange(rows)[None, None, :]
    phase = 2.0 * np.pi * (position * (residue + 2 * parts * column) % total) / total
    cos, sin = np.cos(phase), np.sin(phase)
    forward = np.concatenate(
        [np.concatenate([cos, sin], axis=2), np.concatenate([-sin, cos], axis=2)], axis=1
    )
    inverse = np.transpose(forward, (0, 2, 1)) / total
    return forward.astype(BF16), inverse.astype(BF16)


def convolve_kernel(parts, rows, moved_ref, skip_ref, forward_ref, inverse_ref, out_ref, waves_ref, back_ref):
    width_bits = parts.bit_length() - 1
    chunk = 16

    def cosine(residue, block):
        return float(np.cos(np.pi * residue * block / parts))

    def sine(residue, block):
        return float(np.sin(np.pi * residue * block / parts))

    def spread(index, carry):
        here = pl.ds(index * chunk, chunk)
        there = pl.ds(rows + index * chunk, chunk)
        blocks = [moved_ref[block, here, :].astype(F32) for block in range(parts)]
        for residue in range(parts + 1):
            real = blocks[0]
            imag = jnp.zeros_like(real)
            for block in range(1, parts):
                real = real + cosine(residue, block) * blocks[block]
                imag = imag - sine(residue, block) * blocks[block]
            waves_ref[residue, here, :] = real.astype(BF16)
            waves_ref[residue, there, :] = imag.astype(BF16)
            if 0 < residue < parts:
                waves_ref[2 * parts - residue, here, :] = real.astype(BF16)
                waves_ref[2 * parts - residue, there, :] = (-imag).astype(BF16)
        return carry

    lax.fori_loop(0, rows // chunk, spread, 0)

    def through(residue):
        wave = jnp.dot(forward_ref[residue], waves_ref[residue], preferred_element_type=F32)
        source, odd = divmod(filter_row(residue, width_bits), 2)
        filter_real = moved_ref[source, pl.ds((2 + odd) * rows, rows), :].astype(F32)
        filter_imag = moved_ref[source, pl.ds((4 + odd) * rows, rows), :].astype(F32)
        real, imag = wave[:rows], wave[rows:]
        product = jnp.concatenate(
            [real * filter_real - imag * filter_imag, real * filter_imag + imag * filter_real], axis=0
        )
        return jnp.dot(inverse_ref[residue], product.astype(BF16), preferred_element_type=F32)

    for residue in range(parts + 1):
        back = through(residue)
        if 0 < residue < parts:
            other = through(2 * parts - residue)
            back_ref[residue, pl.ds(0, rows), :] = back[:rows] + other[:rows]
            back_ref[residue, pl.ds(rows, rows), :] = back[rows:] - other[rows:]
        else:
            back_ref[residue] = back

    skip = skip_ref[...]

    def gather(index, carry):
        here = pl.ds(index * chunk, chunk)
        there = pl.ds(rows + index * chunk, chunk)
        reals = [back_ref[residue, here, :] for residue in range(parts + 1)]
        imags = [back_ref[residue, there, :] for residue in range(parts + 1)]
        for block in range(parts):
            total = reals[0]
            for residue in range(1, parts + 1):
                total = total + cosine(residue, block) * reals[residue]
                if residue < parts and block:
                    total = total - sine(residue, block) * imags[residue]
            signal = moved_ref[block, here, :].astype(F32)
            gate = moved_ref[block, pl.ds(rows + index * chunk, chunk), :].astype(F32)
            out_ref[block, here, :] = (gate * (total + skip * signal)).astype(BF16)
        return carry

    lax.fori_loop(0, rows // chunk, gather, 0)


def convolve(moved, skip):
    parts, stacked, width = moved.shape
    rows = stacked // 6
    forward, inverse = dft_tables(parts, rows)
    whole = pl.BlockSpec(memory_space=pltpu.VMEM)
    return pl.pallas_call(
        functools.partial(convolve_kernel, parts, rows),
        out_shape=jax.ShapeDtypeStruct((parts, rows, width), BF16),
        in_specs=[whole] * 4,
        out_specs=whole,
        scratch_shapes=[
            pltpu.VMEM((2 * parts, 2 * rows, width), BF16),
            pltpu.VMEM((parts + 1, 2 * rows, width), F32),
        ],
        compiler_params=pltpu.CompilerParams(vmem_limit_bytes=40 * 2**20),
    )(moved, skip[None, :], forward, inverse)


def shards_general(values_in, gate_values, filter_spectrum, skip_gain, out_weight):
    parts = lax.axis_size("seq")
    layers = lax.axis_size("chan")
    rows, width = values_in.shape
    lanes = width // parts
    device = lax.axis_index("seq")

    def by_channel(array):
        return jnp.transpose(array.reshape(array.shape[0], parts, lanes), (1, 0, 2))

    filters = filter_spectrum.astype(BF16).reshape(4 * rows, width)
    packed = jnp.concatenate([by_channel(values_in), by_channel(gate_values), by_channel(filters)], axis=1)
    moved = lax.all_to_all(packed, "seq", 0, 0)
    skip = lax.dynamic_slice_in_dim(skip_gain, device * lanes, lanes)
    gated = convolve(moved, skip)
    gathered = lax.all_gather(gated.reshape(parts * rows, lanes), "seq", axis=1, tiled=True)

    own_cols = out_weight.shape[1]
    share = own_cols * parts // layers // parts
    per_block = parts // layers
    pieces = own_cols // share
    group = device % per_block
    member = device // per_block
    weight = jnp.zeros_like(out_weight)
    for step in range(pieces):
        piece = (member + step) % pieces
        sent = lax.dynamic_slice_in_dim(out_weight, piece * share, share, 1)
        pairs = [
            (source, source % per_block * pieces + (source // per_block + step) % pieces) for source in range(parts)
        ]
        arrived = lax.ppermute(sent, "seq", pairs)
        block = (device % pieces - step) % pieces
        weight = lax.dynamic_update_slice_in_dim(weight, arrived, block * share, 1)
    partials = jnp.dot(gathered, weight, preferred_element_type=F32).astype(BF16)
    mixed = lax.psum_scatter(partials, "chan", scatter_dimension=1, tiled=True)
    return lax.all_to_all(mixed, "seq", 0, 1, tiled=True)


WHOLE = pl.BlockSpec(memory_space=pltpu.VMEM)
CHEAP = pl.CostEstimate(flops=0, transcendentals=0, bytes_accessed=0)


def small_tables(parts, rows):
    total = 2 * parts * rows
    index = np.arange(rows)
    phase = 2.0 * np.pi * (index[:, None] * index[None, :] % rows) / rows
    cos, sin = np.cos(phase), np.sin(phase)
    forward = np.block([[cos, sin], [-sin, cos]])
    residue = np.arange(2 * parts).reshape(2, 1, parts)
    turn = 2.0 * np.pi * index[None, :, None] * residue / total
    return forward.astype(BF16), forward.T.astype(BF16), np.cos(turn).astype(F32), np.sin(turn).astype(F32)


def cosine(parts, residue, block):
    return float(np.cos(np.pi * residue * block / parts))


def sine(parts, residue, block):
    return float(np.sin(np.pi * residue * block / parts))


def weighted(terms):
    total = None
    for factor, term in terms:
        if abs(factor) < 1e-12:
            continue
        part = term if factor == 1.0 else factor * term
        total = part if total is None else total + part
    return total


def plus(left, right):
    return left if right is None else right if left is None else left + right


def minus(left, right):
    return left if right is None else -right if left is None else left - right


def own_place():
    device = lax.axis_index("seq")
    return device // 2, device % 2


def block_at(index, size):
    return pl.ds(pl.multiple_of(index * size, size), size)


def pack_filters_kernel(offsets, filter_ref, *refs):
    out_refs, (plane_ref, arrived) = refs[: len(offsets)], refs[len(offsets) :]
    chip, _ = own_place()
    planes, rows, _ = filter_ref.shape
    lanes = out_refs[0].shape[1]
    copies = []
    for place, offset in enumerate(offsets):
        here = block_at(chip ^ offset, lanes)
        for plane in range(planes):
            copies.append(
                pltpu.make_async_copy(filter_ref.at[plane, :, here], plane_ref.at[place, plane], arrived.at[place, plane])
            )
    for copy in copies:
        copy.start()
    for index, copy in enumerate(copies):
        copy.wait()
        place, plane = divmod(index, planes)
        out_refs[place][pl.ds(plane * rows, rows), :] = plane_ref[place, plane].astype(BF16)
    used = planes * rows
    for out_ref in out_refs:
        if out_ref.shape[0] > used:
            out_ref[pl.ds(used, out_ref.shape[0] - used), :] = out_ref[pl.ds(0, out_ref.shape[0] - used), :]


def pack_filters(filters, chips, offsets, spare):
    planes, rows, width = filters.shape
    lanes = width // chips
    return pl.pallas_call(
        functools.partial(pack_filters_kernel, offsets),
        in_specs=[pl.BlockSpec(memory_space=pltpu.HBM)],
        out_specs=[WHOLE] * len(offsets),
        out_shape=[jax.ShapeDtypeStruct((planes * rows + spare, lanes), BF16)] * len(offsets),
        scratch_shapes=[
            pltpu.VMEM((len(offsets), planes, rows, lanes), F32),
            pltpu.SemaphoreType.DMA((len(offsets), planes)),
        ],
        cost_estimate=CHEAP,
        compiler_params=pltpu.CompilerParams(vmem_limit_bytes=8 * 2**20),
        name="pack_filters",
    )(pltpu.with_memory_space_constraint(filters, pltpu.HBM))


def pack_values_kernel(chips, values_ref, *refs):
    out_refs, arrived = refs[:chips], refs[chips]
    rows = values_ref.shape[0]
    chip, _ = own_place()
    copies = []
    for offset, out_ref in enumerate(out_refs):
        values = values_ref.at[:, block_at(chip ^ offset, out_ref.shape[1])]
        copies.append(pltpu.make_async_copy(values, out_ref.at[pl.ds(0, rows)], arrived.at[offset]))
    for copy in copies:
        copy.start()
    for copy in copies:
        copy.wait()


def pack_values(values_in, chips, spare):
    rows, width = values_in.shape
    return pl.pallas_call(
        functools.partial(pack_values_kernel, chips),
        in_specs=[pl.BlockSpec(memory_space=pltpu.HBM)],
        out_specs=[WHOLE] * chips,
        out_shape=[jax.ShapeDtypeStruct((rows + spare, width // chips), BF16)] * chips,
        scratch_shapes=[pltpu.SemaphoreType.DMA((chips,))],
        cost_estimate=CHEAP,
        compiler_params=pltpu.CompilerParams(vmem_limit_bytes=4 * 2**20),
        name="pack_values",
    )(pltpu.with_memory_space_constraint(values_in, pltpu.HBM))


def pack_moved_kernel(chips, gate_ref, own_ref, other_ref, *refs):
    out_refs, (mine_ref, arrived) = refs[:chips], refs[chips:]
    chip, core = own_place()
    rows = gate_ref.shape[0]
    depth, held = own_ref.shape
    quarter, share = depth // 4, held // chips

    def copies_from(weight_ref):
        copies = [pltpu.make_async_copy(weight_ref.at[:, block_at(chip, share)], mine_ref, arrived.at[0, 0])]
        for offset in range(chips):
            out_ref, target = out_refs[offset], chip ^ offset
            gates = gate_ref.at[:, block_at(target, out_ref.shape[1])]
            copies.append(pltpu.make_async_copy(gates, out_ref.at[pl.ds(0, rows)], arrived.at[offset, 2]))
            for part in range(2 if offset else 0):
                source = weight_ref.at[block_at(2 * core + part, quarter), block_at(target, share)]
                sink = out_ref.at[pl.ds(rows, quarter), pl.ds(part * share, share)]
                copies.append(pltpu.make_async_copy(source, sink, arrived.at[offset, part]))
        for copy in copies:
            copy.start()
        for copy in copies:
            copy.wait()

    @pl.when(core == 0)
    def _():
        copies_from(own_ref)

    @pl.when(core == 1)
    def _():
        copies_from(other_ref)


def pack_moved(gate_values, own, other, chips):
    rows, width = gate_values.shape
    depth, held = own.shape
    share = held // chips
    return pl.pallas_call(
        functools.partial(pack_moved_kernel, chips),
        in_specs=[pl.BlockSpec(memory_space=pltpu.HBM)] * 2 + [pl.BlockSpec(memory_space=pl.ANY)],
        out_specs=[WHOLE] * (chips + 1),
        out_shape=[
            *(jax.ShapeDtypeStruct((rows + (depth // 4 if offset else 0), 2 * share), BF16) for offset in range(chips)),
            jax.ShapeDtypeStruct((depth, share), BF16),
        ],
        scratch_shapes=[pltpu.SemaphoreType.DMA((chips, 3))],
        cost_estimate=CHEAP,
        compiler_params=pltpu.CompilerParams(vmem_limit_bytes=8 * 2**20),
        name="pack_moved",
    )(*(pltpu.with_memory_space_constraint(array, pltpu.HBM) for array in (gate_values, own)), other)


def stack_kernel(chips, *refs):
    in_refs, out_refs = refs[:chips], refs[chips:]
    for offset, in_ref in enumerate(in_refs):
        part, place = divmod(offset, chips // 2)
        out_refs[part][place] = in_ref[pl.ds(0, out_refs[part].shape[1]), :]


def stack(blocks, rows):
    chips = len(blocks)
    half = jax.ShapeDtypeStruct((chips // 2, rows, blocks[0].shape[1]), BF16)
    return pl.pallas_call(
        functools.partial(stack_kernel, chips),
        in_specs=[WHOLE] * chips,
        out_specs=[WHOLE] * 2,
        out_shape=[half, half],
        cost_estimate=CHEAP,
        compiler_params=pltpu.CompilerParams(vmem_limit_bytes=4 * 2**20),
        name="stack",
    )(*blocks)


def forward_kernel(chips, cos_ref, sin_ref, table_ref, *refs):
    own_refs, other_refs, (out_ref, signal_ref, waves_ref) = refs[:2], refs[2:4], refs[4:]
    chip, core = own_place()
    parts = 2 * chips
    rows, lanes = own_refs[0].shape[1:]
    chunk, width = 16, 128
    for offset in range(chips):
        part, place = divmod(offset, chips // 2)
        signal_ref[2 * (chip ^ offset) + core] = own_refs[part][place]
        signal_ref[2 * (chip ^ offset) + 1 - core] = other_refs[part][place]
    sign = (1 - 2 * core).astype(F32)

    def spread(index, carry):
        here = block_at(index, chunk)
        there = pl.ds(pl.multiple_of(rows + index * chunk, chunk), chunk)
        cos_all, sin_all = cos_ref[core, here, :], sin_ref[core, here, :]
        for start in range(0, lanes, width):
            blocks = [signal_ref[block, here, pl.ds(start, width)].astype(F32) for block in range(parts)]
            blocks = [block * sign if place % 2 else block for place, block in enumerate(blocks)]

            def store(residue, real, imag):
                cos, sin = cos_all[:, residue : residue + 1], sin_all[:, residue : residue + 1]
                if imag is None:
                    real, imag = real * cos, -(real * sin)
                else:
                    real, imag = real * cos + imag * sin, imag * cos - real * sin
                columns = pl.ds(residue * lanes + start, width)
                waves_ref[here, columns] = real.astype(BF16)
                waves_ref[there, columns] = imag.astype(BF16)

            for residue in range(parts // 2 + 1):
                even, odd = range(0, parts, 2), range(1, parts, 2)
                cos_even = weighted([(cosine(parts, residue, block), blocks[block]) for block in even])
                cos_odd = weighted([(cosine(parts, residue, block), blocks[block]) for block in odd])
                sin_even = weighted([(sine(parts, residue, block), blocks[block]) for block in even])
                sin_odd = weighted([(sine(parts, residue, block), blocks[block]) for block in odd])
                sin_sum = plus(sin_even, sin_odd)
                store(residue, plus(cos_even, cos_odd), None if sin_sum is None else -sin_sum)
                if 0 < residue and 2 * residue != parts:
                    store(parts - residue, minus(cos_even, cos_odd), minus(sin_even, sin_odd))
        return carry

    lax.fori_loop(0, rows // chunk, spread, 0)
    for residue in range(parts):
        columns = pl.ds(residue * lanes, lanes)
        out_ref[:, columns] = jnp.dot(table_ref[...], waves_ref[:, columns], preferred_element_type=F32)


def forward(own, other, tables):
    chips, (_, rows, lanes) = 2 * own[0].shape[0], own[0].shape
    table, _, cos, sin = tables
    spectrum = (2 * rows, 2 * chips * lanes)
    return pl.pallas_call(
        functools.partial(forward_kernel, chips),
        in_specs=[WHOLE] * 7,
        out_specs=WHOLE,
        out_shape=jax.ShapeDtypeStruct(spectrum, F32),
        scratch_shapes=[pltpu.VMEM((2 * chips, rows, lanes), BF16), pltpu.VMEM(spectrum, BF16)],
        cost_estimate=CHEAP,
        compiler_params=pltpu.CompilerParams(vmem_limit_bytes=32 * 2**20),
        name="forward",
    )(cos, sin, table, *own, *other)


def backward_kernel(chips, cos_ref, sin_ref, table_ref, spectrum_ref, *refs):
    filter_refs, (keep_ref, *send_refs, filter_ref, product_ref, back_ref) = refs[:chips], refs[chips:]
    chip, core = own_place()
    parts = 2 * chips
    rows, lanes = keep_ref.shape[1:]
    chip_bits = chips.bit_length() - 1
    chunk, width = 16, 128
    for offset in range(chips):
        for plane in range(filter_ref.shape[1]):
            filter_ref[chip ^ offset, plane] = filter_refs[offset][pl.ds(plane * rows, rows), :]

    for residue in range(parts):
        source, odd = bit_reversed(residue // 2, chip_bits), residue % 2
        columns = pl.ds(residue * lanes, lanes)
        filter_real = filter_ref[source, odd].astype(F32)
        filter_imag = filter_ref[source, 2 + odd].astype(F32)
        real = spectrum_ref[pl.ds(0, rows), columns]
        imag = spectrum_ref[pl.ds(rows, rows), columns]
        product_ref[pl.ds(0, rows), columns] = (real * filter_real - imag * filter_imag).astype(BF16)
        product_ref[pl.ds(rows, rows), columns] = (real * filter_imag + imag * filter_real).astype(BF16)
        back_ref[:, columns] = jnp.dot(table_ref[...], product_ref[:, columns], preferred_element_type=F32)

    scale = 1.0 / (2 * parts * rows)
    sign = (1 - 2 * core).astype(F32)
    upper = core == 1

    def gather(index, carry):
        here = block_at(index, chunk)
        there = pl.ds(pl.multiple_of(rows + index * chunk, chunk), chunk)
        cos_all, sin_all = cos_ref[core, here, :] * scale, sin_ref[core, here, :] * scale
        for start in range(0, lanes, width):
            reals, imags = [], []
            for residue in range(parts):
                columns = pl.ds(residue * lanes + start, width)
                real, imag = back_ref[here, columns], back_ref[there, columns]
                cos, sin = cos_all[:, residue : residue + 1], sin_all[:, residue : residue + 1]
                reals.append(real * cos - imag * sin)
                imags.append(real * sin + imag * cos)
            totals = [None] * parts
            for block in range(parts // 2 + 1):
                even, odd = range(0, parts, 2), range(1, parts, 2)
                cos_even = weighted([(cosine(parts, residue, block), reals[residue]) for residue in even])
                cos_odd = weighted([(cosine(parts, residue, block), reals[residue]) for residue in odd])
                sin_even = weighted([(sine(parts, residue, block), imags[residue]) for residue in even])
                sin_odd = weighted([(sine(parts, residue, block), imags[residue]) for residue in odd])
                totals[block] = minus(plus(cos_even, cos_odd), plus(sin_even, sin_odd))
                if 0 < block and 2 * block != parts:
                    totals[parts - block] = plus(minus(cos_even, cos_odd), minus(sin_even, sin_odd))
            lane = pl.ds(start, width)
            for pair in range(chips):
                low, high = totals[2 * pair], totals[2 * pair + 1] * sign
                keep_ref[pair, here, lane] = jnp.where(upper, high, low)
                part, place = divmod(pair, chips // 2)
                send_refs[part][place, here, lane] = jnp.where(upper, low, high).astype(BF16)
        return carry

    lax.fori_loop(0, rows // chunk, gather, 0)


def backward(spectrum, first, tables):
    chips = len(first)
    rows, lanes = spectrum.shape[0] // 2, first[0].shape[1]
    _, table, cos, sin = tables
    half = jax.ShapeDtypeStruct((chips // 2, rows, lanes), BF16)
    return pl.pallas_call(
        functools.partial(backward_kernel, chips),
        in_specs=[WHOLE] * (4 + chips),
        out_specs=[WHOLE] * 3,
        out_shape=[jax.ShapeDtypeStruct((chips, rows, lanes), F32), half, half],
        scratch_shapes=[
            pltpu.VMEM((chips, 4, rows, lanes), BF16),
            pltpu.VMEM(spectrum.shape, BF16),
            pltpu.VMEM(spectrum.shape, F32),
        ],
        cost_estimate=CHEAP,
        compiler_params=pltpu.CompilerParams(vmem_limit_bytes=32 * 2**20),
        name="backward",
    )(cos, sin, table, spectrum, *first)


def gate_kernel(chips, offsets, skip_ref, keep_ref, low_ref, high_ref, *refs):
    signal_refs, gate_refs = refs[:chips], refs[chips : 2 * chips]
    out_ref, longer_ref, arrived_ref = refs[2 * chips :]
    chip, _ = own_place()
    rows, lanes = keep_ref.shape[1:]
    skip = skip_ref[:, block_at(chip, lanes)]
    arrived_ref[pl.ds(0, chips // 2)] = low_ref[...]
    arrived_ref[pl.ds(chips // 2, chips // 2)] = high_ref[...]
    for offset in range(chips):
        block = chip ^ offset
        convolved = keep_ref[block] + arrived_ref[block].astype(F32)
        signal = signal_refs[offset][pl.ds(0, rows), :].astype(F32)
        gate = gate_refs[offsets.index(offset)][pl.ds(0, rows), :].astype(F32)
        gated = (gate * (convolved + skip * signal)).astype(BF16)
        out_ref[block_at(block, rows), :] = gated
        longer_ref[block_at(block, rows), :] = gated
    end = chips * rows
    longer_ref[pl.ds(end, longer_ref.shape[0] - end), :] = longer_ref[pl.ds(0, longer_ref.shape[0] - end), :]


def gate(skip, keep, arrived, first, gates, offsets, spare):
    chips, rows, lanes = keep.shape
    return pl.pallas_call(
        functools.partial(gate_kernel, chips, offsets),
        in_specs=[WHOLE] * (4 + 2 * chips),
        out_specs=[WHOLE] * 2,
        out_shape=[
            jax.ShapeDtypeStruct((chips * rows, lanes), BF16),
            jax.ShapeDtypeStruct((chips * rows + spare, lanes), BF16),
        ],
        scratch_shapes=[pltpu.VMEM((chips, rows, lanes), BF16)],
        cost_estimate=CHEAP,
        compiler_params=pltpu.CompilerParams(vmem_limit_bytes=6 * 2**20),
        name="gate",
    )(skip, keep, *arrived, *first, *(gates[offset] for offset in offsets))


def piece_of(ref, half, part):
    quarter, share = half // 2, ref.shape[1] // 2
    return ref[pl.ds(ref.shape[0] - quarter, quarter), pl.ds(part * share, share)]


def collect_kernel(in_refs, out_refs):
    rows = out_refs[0].shape[0]
    quarter = len(out_refs) * rows // (2 * len(in_refs))
    for place in range(2 * len(in_refs)):
        index, start = divmod(place * quarter, rows)
        out_refs[index][pl.ds(start, quarter), :] = piece_of(in_refs[place // 2], 2 * quarter, place % 2)


def collect(moved, half):
    count = len(moved)
    shape = (count * half // 2, moved[0].shape[1] // 2)
    return pl.pallas_call(
        lambda *refs: collect_kernel(refs[:count], refs[count:]),
        in_specs=[WHOLE] * count,
        out_specs=[WHOLE] * 2,
        out_shape=[jax.ShapeDtypeStruct(shape, BF16)] * 2,
        cost_estimate=CHEAP,
        compiler_params=pltpu.CompilerParams(vmem_limit_bytes=4 * 2**20),
        name="collect_weights",
    )(*moved)


def arrange_kernel(chips, mine_ref, *refs):
    moved_refs, (*other_refs, out_ref) = refs[: chips - 1], refs[chips - 1 :]
    chip, core = own_place()
    layer = lax.axis_index("chan")
    depth, share = mine_ref.shape
    quarter = depth // 4
    out_ref[:, block_at(chip ^ layer, share)] = mine_ref[...]
    for place in range(2 * (chips - 1)):
        offset, part = place // 2 + 1, place % 2
        columns = block_at(chip ^ layer ^ offset, share)
        index, start = divmod(place * quarter, other_refs[0].shape[0])
        out_ref[block_at(2 * core + part, quarter), columns] = piece_of(moved_refs[offset - 1], 2 * quarter, part)
        out_ref[block_at(2 * (1 - core) + part, quarter), columns] = other_refs[index][pl.ds(start, quarter), :]


def arrange(mine, moved, others):
    chips = len(moved) + 1
    depth, share = mine.shape
    return pl.pallas_call(
        functools.partial(arrange_kernel, chips),
        in_specs=[WHOLE] * (chips + len(others)),
        out_specs=WHOLE,
        out_shape=jax.ShapeDtypeStruct((depth, chips * share), BF16),
        cost_estimate=CHEAP,
        compiler_params=pltpu.CompilerParams(vmem_limit_bytes=8 * 2**20),
        name="arrange_weights",
    )(mine, *moved, *others)


def join_channels(chips, gated_refs, joined_ref):
    chip, _ = own_place()
    lanes = gated_refs[0].shape[1]
    for offset in range(chips):
        joined_ref[:, block_at(chip ^ offset, lanes)] = gated_refs[offset][pl.ds(0, joined_ref.shape[0]), :]


def project_moved_kernel(chips, weight_ref, *refs):
    gated_refs, (keep_ref, pass_ref, send_ref, joined_ref) = refs[:chips], refs[chips:]
    share = keep_ref.shape[1]
    join_channels(chips, gated_refs, joined_ref)
    partial = jnp.dot(joined_ref[...], weight_ref[...], preferred_element_type=F32).astype(BF16)
    keep_ref[...] = partial[:, :share]
    send_ref[0] = partial[:, share : 2 * share]
    pass_ref[...] = partial[:, 2 * share : 3 * share]
    send_ref[1] = partial[:, 3 * share :]


def project_moved(weight, gated):
    chips = len(gated)
    depth, columns = weight.shape
    rows = gated[0].shape[0]
    block = jax.ShapeDtypeStruct((rows, columns // chips), BF16)
    return pl.pallas_call(
        functools.partial(project_moved_kernel, chips),
        in_specs=[WHOLE] * (1 + chips),
        out_specs=[WHOLE] * 3,
        out_shape=[block, block, jax.ShapeDtypeStruct((2, rows, columns // chips), BF16)],
        scratch_shapes=[pltpu.VMEM((rows, depth), BF16)],
        cost_estimate=CHEAP,
        compiler_params=pltpu.CompilerParams(vmem_limit_bytes=8 * 2**20),
        name="project_moved",
    )(weight, *gated)


def project_still_kernel(chips, own_ref, other_ref, *refs):
    gated_refs, out_refs, joined_ref = refs[:chips], refs[chips : 2 * chips], refs[2 * chips]
    chip, core = own_place()
    rows = out_refs[0].shape[0]
    join_channels(chips, gated_refs, joined_ref)

    def project_with(weight_ref):
        for offset in range(chips):
            gated = joined_ref[block_at(chip ^ offset, rows), :]
            out_refs[offset][...] = jnp.dot(gated, weight_ref[...], preferred_element_type=F32).astype(BF16)

    @pl.when(core == 0)
    def _():
        project_with(other_ref)

    @pl.when(core == 1)
    def _():
        project_with(own_ref)


def project_still(own, other, gated):
    chips = len(gated)
    depth, held = own.shape
    rows = gated[0].shape[0] // chips
    return pl.pallas_call(
        functools.partial(project_still_kernel, chips),
        in_specs=[WHOLE] * (2 + chips),
        out_specs=[WHOLE] * chips,
        out_shape=[jax.ShapeDtypeStruct((rows, held), BF16)] * chips,
        scratch_shapes=[pltpu.VMEM((rows * chips, depth), BF16)],
        cost_estimate=CHEAP,
        compiler_params=pltpu.CompilerParams(vmem_limit_bytes=12 * 2**20),
        name="project_still",
    )(own, other, *gated)


def sort_kernel(chips, *refs):
    in_refs, (*out_refs, sorted_ref) = refs[:chips], refs[chips:]
    chip, _ = own_place()
    layer = lax.axis_index("chan")
    for offset in range(chips):
        sorted_ref[chip ^ layer ^ offset] = in_refs[offset][...]
    for target, out_ref in enumerate(out_refs):
        out_ref[...] = sorted_ref[target]


def sort_blocks(blocks):
    chips = len(blocks)
    block = jax.ShapeDtypeStruct(blocks[0].shape, BF16)
    return pl.pallas_call(
        functools.partial(sort_kernel, chips),
        in_specs=[WHOLE] * chips,
        out_specs=[WHOLE] * chips,
        out_shape=[block] * chips,
        scratch_shapes=[pltpu.VMEM((chips, *block.shape), BF16)],
        cost_estimate=CHEAP,
        compiler_params=pltpu.CompilerParams(vmem_limit_bytes=4 * 2**20),
        name="sort_blocks",
    )(*blocks)


def add_kernel(left_ref, right_ref, out_ref):
    rows = left_ref.shape[0]
    total = (left_ref[...].astype(F32) + right_ref[...].astype(F32)).astype(BF16)
    out_ref[pl.ds(0, rows), :] = total
    more = out_ref.shape[0] - rows
    if more:
        out_ref[pl.ds(rows, more), :] = total[:more]


def add(left, right, spare):
    rows, columns = left.shape
    return pl.pallas_call(
        add_kernel,
        in_specs=[WHOLE] * 2,
        out_specs=WHOLE,
        out_shape=jax.ShapeDtypeStruct((rows + spare, columns), BF16),
        cost_estimate=CHEAP,
        compiler_params=pltpu.CompilerParams(vmem_limit_bytes=4 * 2**20),
        name="add",
    )(left, right)


def finish_kernel(chips, keep_ref, first_ref, second_ref, *out_refs):
    chip, _ = own_place()
    rows = out_refs[0].shape[0]
    for offset in range(chips):
        here = block_at(chip ^ offset, rows)
        total = keep_ref[here, :].astype(F32) + first_ref[0, here, :].astype(F32) + second_ref[here, :].astype(F32)
        out_refs[offset][...] = total.astype(BF16)


def finish(keep, first, second, chips):
    rows, columns = keep.shape
    return pl.pallas_call(
        functools.partial(finish_kernel, chips),
        in_specs=[WHOLE] * 3,
        out_specs=[WHOLE] * chips,
        out_shape=[jax.ShapeDtypeStruct((rows // chips, columns), BF16)] * chips,
        cost_estimate=CHEAP,
        compiler_params=pltpu.CompilerParams(vmem_limit_bytes=4 * 2**20),
        name="finish",
    )(keep, first, second)


def join_kernel(chips, keep_ref, first_ref, second_ref, *refs):
    in_refs, out_ref = refs[:chips], refs[chips]
    chip, _ = own_place()
    share = in_refs[0].shape[1]
    for offset in range(chips):
        out_ref[:, block_at(chip ^ offset, share)] = in_refs[offset][...]
    total = keep_ref[...].astype(F32) + first_ref[...].astype(F32)
    total = total + second_ref[pl.ds(0, total.shape[0]), :].astype(F32)
    out_ref[:, pl.ds(chips * share, total.shape[1])] = total.astype(BF16)


def join(keep, first, second, blocks):
    chips = len(blocks)
    rows, share = blocks[0].shape
    return pl.pallas_call(
        functools.partial(join_kernel, chips),
        in_specs=[WHOLE] * (3 + chips),
        out_specs=WHOLE,
        out_shape=jax.ShapeDtypeStruct((rows, chips * share + keep.shape[1]), BF16),
        cost_estimate=CHEAP,
        compiler_params=pltpu.CompilerParams(vmem_limit_bytes=4 * 2**20),
        name="join",
    )(keep, first, second, *blocks)


def swapped(value, axis, offset):
    if not offset:
        return value
    return lax.ppermute(value, axis, [(source, source ^ offset) for source in range(lax.axis_size(axis))])


def to_chips(blocks):
    return [swapped(block, "seq", 2 * offset) for offset, block in enumerate(blocks)]


def after(value, *others):
    return lax.optimization_barrier((value, *others))[0]


def over_layers(passed, send):
    first = swapped(send, "chan", 1)
    passed = (passed.astype(F32) + first[1].astype(F32)).astype(BF16)
    return first, swapped(passed, "chan", 2)


def shards_direct(values_in, gate_values, filter_spectrum, skip_gain, out_weight):
    parts = lax.axis_size("seq")
    chips = parts // 2
    rows, width = values_in.shape
    tables = small_tables(parts, rows)

    values = pack_values(values_in, chips, 0)
    flat_filters = filter_spectrum.reshape(4, rows, width)
    near = pack_filters(after(flat_filters, values[0]), chips, (1, 2), 0)
    other_weight = swapped(out_weight, "seq", 1)
    *moved, mine = pack_moved(after(gate_values, near[0]), out_weight, other_weight, chips)
    own, far = pack_filters(after(flat_filters, moved[0]), chips, (0, 3), 0)
    values, filters = to_chips(values), to_chips([own, *near, far])
    own = stack([after(block, far) for block in values], rows)
    spectrum = forward(own, [swapped(part, "seq", 1) for part in own], tables)
    moved = to_chips([after(block, spectrum) for block in moved])
    keep, *send = backward(spectrum, filters, tables)
    gated, longer = gate(skip_gain[None, :], keep, [swapped(part, "seq", 1) for part in send], values, moved, (0, 3, 1, 2), 16)
    gathered = to_chips([gated, longer, longer, gated])

    others = [swapped(part, "seq", 1) for part in collect([after(block, gated) for block in moved[1:]], out_weight.shape[0] // 2)]
    keep, passed, send = project_moved(arrange(mine, moved[1:], others), gathered)
    blocks = to_chips(finish(keep, *over_layers(passed, send), chips))
    keep, near, passed, far = sort_blocks(to_chips(project_still(out_weight, other_weight, gathered)))
    second = swapped(add(after(passed, blocks[3], blocks[1]), swapped(far, "chan", 1), 0), "chan", 2)
    return join(keep, swapped(near, "chan", 1), second, blocks)


def shards(values_in, gate_values, filter_spectrum, skip_gain, out_weight):
    parts, layers = lax.axis_size("seq"), lax.axis_size("chan")
    rows, width = values_in.shape
    share = out_weight.shape[1] // layers
    aligned = width // parts % 128 == 0 and share % 128 == 0 and rows % 32 == 0
    run = shards_direct if aligned and layers == 4 and parts == 8 else shards_general
    return run(values_in, gate_values, filter_spectrum, skip_gain, out_weight)


def solution(mesh):
    in_specs = (
        P("seq", "chan"),
        P("seq", "chan"),
        P(None, "seq", None, "chan"),
        P("chan"),
        P("chan", "seq"),
    )
    out_specs = P("seq", "chan")
    return jax.shard_map(shards, mesh=mesh, in_specs=in_specs, out_specs=out_specs, check_vma=False)
```

```python
import functools

import jax
import jax.numpy as jnp
import numpy as np
from jax import lax
from jax.experimental import pallas as pl
from jax.experimental.pallas import tpu as pltpu
from jax.sharding import PartitionSpec as P

BF16 = jnp.bfloat16
F32 = jnp.float32


def bit_reversed(number, width_bits):
    flipped = 0
    for bit_place in range(width_bits):
        flipped |= (number >> bit_place & 1) << (width_bits - 1 - bit_place)
    return flipped


def filter_row(residue, width_bits):
    return 2 * bit_reversed(residue // 2, width_bits) + residue % 2


def dft_tables(parts, rows):
    total = 2 * parts * rows
    residue = np.arange(2 * parts)[:, None, None]
    column = np.arange(rows)[None, :, None]
    position = np.arange(rows)[None, None, :]
    phase = 2.0 * np.pi * (position * (residue + 2 * parts * column) % total) / total
    cos, sin = np.cos(phase), np.sin(phase)
    forward = np.concatenate(
        [np.concatenate([cos, sin], axis=2), np.concatenate([-sin, cos], axis=2)], axis=1
    )
    inverse = np.transpose(forward, (0, 2, 1)) / total
    return forward.astype(BF16), inverse.astype(BF16)


def convolve_kernel(parts, rows, moved_ref, skip_ref, forward_ref, inverse_ref, out_ref, waves_ref, back_ref):
    width_bits = parts.bit_length() - 1
    chunk = 16

    def cosine(residue, block):
        return float(np.cos(np.pi * residue * block / parts))

    def sine(residue, block):
        return float(np.sin(np.pi * residue * block / parts))

    def spread(index, carry):
        here = pl.ds(index * chunk, chunk)
        there = pl.ds(rows + index * chunk, chunk)
        blocks = [moved_ref[block, here, :].astype(F32) for block in range(parts)]
        for residue in range(parts + 1):
            real = blocks[0]
            imag = jnp.zeros_like(real)
            for block in range(1, parts):
                real = real + cosine(residue, block) * blocks[block]
                imag = imag - sine(residue, block) * blocks[block]
            waves_ref[residue, here, :] = real.astype(BF16)
            waves_ref[residue, there, :] = imag.astype(BF16)
            if 0 < residue < parts:
                waves_ref[2 * parts - residue, here, :] = real.astype(BF16)
                waves_ref[2 * parts - residue, there, :] = (-imag).astype(BF16)
        return carry

    lax.fori_loop(0, rows // chunk, spread, 0)

    def through(residue):
        wave = jnp.dot(forward_ref[residue], waves_ref[residue], preferred_element_type=F32)
        source, odd = divmod(filter_row(residue, width_bits), 2)
        filter_real = moved_ref[source, pl.ds((2 + odd) * rows, rows), :].astype(F32)
        filter_imag = moved_ref[source, pl.ds((4 + odd) * rows, rows), :].astype(F32)
        real, imag = wave[:rows], wave[rows:]
        product = jnp.concatenate(
            [real * filter_real - imag * filter_imag, real * filter_imag + imag * filter_real], axis=0
        )
        return jnp.dot(inverse_ref[residue], product.astype(BF16), preferred_element_type=F32)

    for residue in range(parts + 1):
        back = through(residue)
        if 0 < residue < parts:
            other = through(2 * parts - residue)
            back_ref[residue, pl.ds(0, rows), :] = back[:rows] + other[:rows]
            back_ref[residue, pl.ds(rows, rows), :] = back[rows:] - other[rows:]
        else:
            back_ref[residue] = back

    skip = skip_ref[...]

    def gather(index, carry):
        here = pl.ds(index * chunk, chunk)
        there = pl.ds(rows + index * chunk, chunk)
        reals = [back_ref[residue, here, :] for residue in range(parts + 1)]
        imags = [back_ref[residue, there, :] for residue in range(parts + 1)]
        for block in range(parts):
            total = reals[0]
            for residue in range(1, parts + 1):
                total = total + cosine(residue, block) * reals[residue]
                if residue < parts and block:
                    total = total - sine(residue, block) * imags[residue]
            signal = moved_ref[block, here, :].astype(F32)
            gate = moved_ref[block, pl.ds(rows + index * chunk, chunk), :].astype(F32)
            out_ref[block, here, :] = (gate * (total + skip * signal)).astype(BF16)
        return carry

    lax.fori_loop(0, rows // chunk, gather, 0)


def convolve(moved, skip):
    parts, stacked, width = moved.shape
    rows = stacked // 6
    forward, inverse = dft_tables(parts, rows)
    whole = pl.BlockSpec(memory_space=pltpu.VMEM)
    return pl.pallas_call(
        functools.partial(convolve_kernel, parts, rows),
        out_shape=jax.ShapeDtypeStruct((parts, rows, width), BF16),
        in_specs=[whole] * 4,
        out_specs=whole,
        scratch_shapes=[
            pltpu.VMEM((2 * parts, 2 * rows, width), BF16),
            pltpu.VMEM((parts + 1, 2 * rows, width), F32),
        ],
        compiler_params=pltpu.CompilerParams(vmem_limit_bytes=40 * 2**20),
    )(moved, skip[None, :], forward, inverse)


def shards_general(values_in, gate_values, filter_spectrum, skip_gain, out_weight):
    parts = lax.axis_size("seq")
    layers = lax.axis_size("chan")
    rows, width = values_in.shape
    lanes = width // parts
    device = lax.axis_index("seq")

    def by_channel(array):
        return jnp.transpose(array.reshape(array.shape[0], parts, lanes), (1, 0, 2))

    filters = filter_spectrum.astype(BF16).reshape(4 * rows, width)
    packed = jnp.concatenate([by_channel(values_in), by_channel(gate_values), by_channel(filters)], axis=1)
    moved = lax.all_to_all(packed, "seq", 0, 0)
    skip = lax.dynamic_slice_in_dim(skip_gain, device * lanes, lanes)
    gated = convolve(moved, skip)
    gathered = lax.all_gather(gated.reshape(parts * rows, lanes), "seq", axis=1, tiled=True)

    own_cols = out_weight.shape[1]
    share = own_cols * parts // layers // parts
    per_block = parts // layers
    pieces = own_cols // share
    group = device % per_block
    member = device // per_block
    weight = jnp.zeros_like(out_weight)
    for step in range(pieces):
        piece = (member + step) % pieces
        sent = lax.dynamic_slice_in_dim(out_weight, piece * share, share, 1)
        pairs = [
            (source, source % per_block * pieces + (source // per_block + step) % pieces) for source in range(parts)
        ]
        arrived = lax.ppermute(sent, "seq", pairs)
        block = (device % pieces - step) % pieces
        weight = lax.dynamic_update_slice_in_dim(weight, arrived, block * share, 1)
    partials = jnp.dot(gathered, weight, preferred_element_type=F32).astype(BF16)
    mixed = lax.psum_scatter(partials, "chan", scatter_dimension=1, tiled=True)
    return lax.all_to_all(mixed, "seq", 0, 1, tiled=True)


WHOLE = pl.BlockSpec(memory_space=pltpu.VMEM)
CHEAP = pl.CostEstimate(flops=0, transcendentals=0, bytes_accessed=0)


def small_tables(parts, rows):
    total = 2 * parts * rows
    index = np.arange(rows)
    phase = 2.0 * np.pi * (index[:, None] * index[None, :] % rows) / rows
    cos, sin = np.cos(phase), np.sin(phase)
    forward = np.block([[cos, sin], [-sin, cos]])
    residue = np.arange(2 * parts).reshape(2, 1, parts)
    turn = 2.0 * np.pi * index[None, :, None] * residue / total
    return forward.astype(BF16), forward.T.astype(BF16), np.cos(turn).astype(F32), np.sin(turn).astype(F32)


def cosine(parts, residue, block):
    return float(np.cos(np.pi * residue * block / parts))


def sine(parts, residue, block):
    return float(np.sin(np.pi * residue * block / parts))


def weighted(terms):
    total = None
    for factor, term in terms:
        if abs(factor) < 1e-12:
            continue
        part = term if factor == 1.0 else factor * term
        total = part if total is None else total + part
    return total


def plus(left, right):
    return left if right is None else right if left is None else left + right


def minus(left, right):
    return left if right is None else -right if left is None else left - right


def own_place():
    device = lax.axis_index("seq")
    return device // 2, device % 2


def block_at(index, size):
    return pl.ds(pl.multiple_of(index * size, size), size)


def pack_filters_kernel(offsets, filter_ref, *refs):
    out_refs, (plane_ref, arrived) = refs[: len(offsets)], refs[len(offsets) :]
    chip, _ = own_place()
    planes, rows, _ = filter_ref.shape
    lanes = out_refs[0].shape[1]
    copies = []
    for place, offset in enumerate(offsets):
        here = block_at(chip ^ offset, lanes)
        for plane in range(planes):
            copies.append(
                pltpu.make_async_copy(filter_ref.at[plane, :, here], plane_ref.at[place, plane], arrived.at[place, plane])
            )
    for copy in copies:
        copy.start()
    for index, copy in enumerate(copies):
        copy.wait()
        place, plane = divmod(index, planes)
        out_refs[place][pl.ds(plane * rows, rows), :] = plane_ref[place, plane].astype(BF16)
    used = planes * rows
    for out_ref in out_refs:
        if out_ref.shape[0] > used:
            out_ref[pl.ds(used, out_ref.shape[0] - used), :] = out_ref[pl.ds(0, out_ref.shape[0] - used), :]


def pack_filters(filters, chips, offsets, spare):
    planes, rows, width = filters.shape
    lanes = width // chips
    return pl.pallas_call(
        functools.partial(pack_filters_kernel, offsets),
        in_specs=[pl.BlockSpec(memory_space=pltpu.HBM)],
        out_specs=[WHOLE] * len(offsets),
        out_shape=[jax.ShapeDtypeStruct((planes * rows + spare, lanes), BF16)] * len(offsets),
        scratch_shapes=[
            pltpu.VMEM((len(offsets), planes, rows, lanes), F32),
            pltpu.SemaphoreType.DMA((len(offsets), planes)),
        ],
        cost_estimate=CHEAP,
        compiler_params=pltpu.CompilerParams(vmem_limit_bytes=8 * 2**20),
        name="pack_filters",
    )(pltpu.with_memory_space_constraint(filters, pltpu.HBM))


def pack_values_kernel(chips, values_ref, *refs):
    out_refs, arrived = refs[:chips], refs[chips]
    rows = values_ref.shape[0]
    chip, _ = own_place()
    copies = []
    for offset, out_ref in enumerate(out_refs):
        values = values_ref.at[:, block_at(chip ^ offset, out_ref.shape[1])]
        copies.append(pltpu.make_async_copy(values, out_ref.at[pl.ds(0, rows)], arrived.at[offset]))
    for copy in copies:
        copy.start()
    for copy in copies:
        copy.wait()


def pack_values(values_in, chips, spare):
    rows, width = values_in.shape
    return pl.pallas_call(
        functools.partial(pack_values_kernel, chips),
        in_specs=[pl.BlockSpec(memory_space=pltpu.HBM)],
        out_specs=[WHOLE] * chips,
        out_shape=[jax.ShapeDtypeStruct((rows + spare, width // chips), BF16)] * chips,
        scratch_shapes=[pltpu.SemaphoreType.DMA((chips,))],
        cost_estimate=CHEAP,
        compiler_params=pltpu.CompilerParams(vmem_limit_bytes=4 * 2**20),
        name="pack_values",
    )(pltpu.with_memory_space_constraint(values_in, pltpu.HBM))


def pack_moved_kernel(chips, gate_ref, own_ref, other_ref, *refs):
    out_refs, (mine_ref, arrived) = refs[:chips], refs[chips:]
    chip, core = own_place()
    rows = gate_ref.shape[0]
    depth, held = own_ref.shape
    quarter, share = depth // 4, held // chips

    def copies_from(weight_ref):
        copies = [pltpu.make_async_copy(weight_ref.at[:, block_at(chip, share)], mine_ref, arrived.at[0, 0])]
        for offset in range(chips):
            out_ref, target = out_refs[offset], chip ^ offset
            gates = gate_ref.at[:, block_at(target, out_ref.shape[1])]
            copies.append(pltpu.make_async_copy(gates, out_ref.at[pl.ds(0, rows)], arrived.at[offset, 2]))
            for part in range(2 if offset else 0):
                source = weight_ref.at[block_at(2 * core + part, quarter), block_at(target, share)]
                sink = out_ref.at[pl.ds(rows, quarter), pl.ds(part * share, share)]
                copies.append(pltpu.make_async_copy(source, sink, arrived.at[offset, part]))
        for copy in copies:
            copy.start()
        for copy in copies:
            copy.wait()

    @pl.when(core == 0)
    def _():
        copies_from(own_ref)

    @pl.when(core == 1)
    def _():
        copies_from(other_ref)


def pack_moved(gate_values, own, other, chips):
    rows, width = gate_values.shape
    depth, held = own.shape
    share = held // chips
    return pl.pallas_call(
        functools.partial(pack_moved_kernel, chips),
        in_specs=[pl.BlockSpec(memory_space=pltpu.HBM)] * 2 + [pl.BlockSpec(memory_space=pl.ANY)],
        out_specs=[WHOLE] * (chips + 1),
        out_shape=[
            *(jax.ShapeDtypeStruct((rows + (depth // 4 if offset else 0), 2 * share), BF16) for offset in range(chips)),
            jax.ShapeDtypeStruct((depth, share), BF16),
        ],
        scratch_shapes=[pltpu.SemaphoreType.DMA((chips, 3))],
        cost_estimate=CHEAP,
        compiler_params=pltpu.CompilerParams(vmem_limit_bytes=8 * 2**20),
        name="pack_moved",
    )(*(pltpu.with_memory_space_constraint(array, pltpu.HBM) for array in (gate_values, own)), other)


def stack_kernel(chips, *refs):
    in_refs, out_refs = refs[:chips], refs[chips:]
    for offset, in_ref in enumerate(in_refs):
        part, place = divmod(offset, chips // 2)
        out_refs[part][place] = in_ref[pl.ds(0, out_refs[part].shape[1]), :]


def stack(blocks, rows):
    chips = len(blocks)
    half = jax.ShapeDtypeStruct((chips // 2, rows, blocks[0].shape[1]), BF16)
    return pl.pallas_call(
        functools.partial(stack_kernel, chips),
        in_specs=[WHOLE] * chips,
        out_specs=[WHOLE] * 2,
        out_shape=[half, half],
        cost_estimate=CHEAP,
        compiler_params=pltpu.CompilerParams(vmem_limit_bytes=4 * 2**20),
        name="stack",
    )(*blocks)


def forward_kernel(chips, cos_ref, sin_ref, table_ref, *refs):
    own_refs, other_refs, (out_ref, signal_ref, waves_ref) = refs[:2], refs[2:4], refs[4:]
    chip, core = own_place()
    parts = 2 * chips
    rows, lanes = own_refs[0].shape[1:]
    chunk, width = 16, 128
    for offset in range(chips):
        part, place = divmod(offset, chips // 2)
        signal_ref[2 * (chip ^ offset) + core] = own_refs[part][place]
        signal_ref[2 * (chip ^ offset) + 1 - core] = other_refs[part][place]
    sign = (1 - 2 * core).astype(F32)

    def spread(index, carry):
        here = block_at(index, chunk)
        there = pl.ds(pl.multiple_of(rows + index * chunk, chunk), chunk)
        cos_all, sin_all = cos_ref[core, here, :], sin_ref[core, here, :]
        for start in range(0, lanes, width):
            blocks = [signal_ref[block, here, pl.ds(start, width)].astype(F32) for block in range(parts)]
            blocks = [block * sign if place % 2 else block for place, block in enumerate(blocks)]

            def store(residue, real, imag):
                cos, sin = cos_all[:, residue : residue + 1], sin_all[:, residue : residue + 1]
                if imag is None:
                    real, imag = real * cos, -(real * sin)
                else:
                    real, imag = real * cos + imag * sin, imag * cos - real * sin
                columns = pl.ds(residue * lanes + start, width)
                waves_ref[here, columns] = real.astype(BF16)
                waves_ref[there, columns] = imag.astype(BF16)

            for residue in range(parts // 2 + 1):
                even, odd = range(0, parts, 2), range(1, parts, 2)
                cos_even = weighted([(cosine(parts, residue, block), blocks[block]) for block in even])
                cos_odd = weighted([(cosine(parts, residue, block), blocks[block]) for block in odd])
                sin_even = weighted([(sine(parts, residue, block), blocks[block]) for block in even])
                sin_odd = weighted([(sine(parts, residue, block), blocks[block]) for block in odd])
                sin_sum = plus(sin_even, sin_odd)
                store(residue, plus(cos_even, cos_odd), None if sin_sum is None else -sin_sum)
                if 0 < residue and 2 * residue != parts:
                    store(parts - residue, minus(cos_even, cos_odd), minus(sin_even, sin_odd))
        return carry

    lax.fori_loop(0, rows // chunk, spread, 0)
    for residue in range(parts):
        columns = pl.ds(residue * lanes, lanes)
        out_ref[:, columns] = jnp.dot(table_ref[...], waves_ref[:, columns], preferred_element_type=F32)


def forward(own, other, tables):
    chips, (_, rows, lanes) = 2 * own[0].shape[0], own[0].shape
    table, _, cos, sin = tables
    spectrum = (2 * rows, 2 * chips * lanes)
    return pl.pallas_call(
        functools.partial(forward_kernel, chips),
        in_specs=[WHOLE] * 7,
        out_specs=WHOLE,
        out_shape=jax.ShapeDtypeStruct(spectrum, F32),
        scratch_shapes=[pltpu.VMEM((2 * chips, rows, lanes), BF16), pltpu.VMEM(spectrum, BF16)],
        cost_estimate=CHEAP,
        compiler_params=pltpu.CompilerParams(vmem_limit_bytes=32 * 2**20),
        name="forward",
    )(cos, sin, table, *own, *other)


def backward_kernel(chips, cos_ref, sin_ref, table_ref, spectrum_ref, *refs):
    filter_refs, (keep_ref, *send_refs, filter_ref, product_ref, back_ref) = refs[:chips], refs[chips:]
    chip, core = own_place()
    parts = 2 * chips
    rows, lanes = keep_ref.shape[1:]
    chip_bits = chips.bit_length() - 1
    chunk, width = 16, 128
    for offset in range(chips):
        for plane in range(filter_ref.shape[1]):
            filter_ref[chip ^ offset, plane] = filter_refs[offset][pl.ds(plane * rows, rows), :]

    for residue in range(parts):
        source, odd = bit_reversed(residue // 2, chip_bits), residue % 2
        columns = pl.ds(residue * lanes, lanes)
        filter_real = filter_ref[source, odd].astype(F32)
        filter_imag = filter_ref[source, 2 + odd].astype(F32)
        real = spectrum_ref[pl.ds(0, rows), columns]
        imag = spectrum_ref[pl.ds(rows, rows), columns]
        product_ref[pl.ds(0, rows), columns] = (real * filter_real - imag * filter_imag).astype(BF16)
        product_ref[pl.ds(rows, rows), columns] = (real * filter_imag + imag * filter_real).astype(BF16)
        back_ref[:, columns] = jnp.dot(table_ref[...], product_ref[:, columns], preferred_element_type=F32)

    scale = 1.0 / (2 * parts * rows)
    sign = (1 - 2 * core).astype(F32)
    upper = core == 1

    def gather(index, carry):
        here = block_at(index, chunk)
        there = pl.ds(pl.multiple_of(rows + index * chunk, chunk), chunk)
        cos_all, sin_all = cos_ref[core, here, :] * scale, sin_ref[core, here, :] * scale
        for start in range(0, lanes, width):
            reals, imags = [], []
            for residue in range(parts):
                columns = pl.ds(residue * lanes + start, width)
                real, imag = back_ref[here, columns], back_ref[there, columns]
                cos, sin = cos_all[:, residue : residue + 1], sin_all[:, residue : residue + 1]
                reals.append(real * cos - imag * sin)
                imags.append(real * sin + imag * cos)
            totals = [None] * parts
            for block in range(parts // 2 + 1):
                even, odd = range(0, parts, 2), range(1, parts, 2)
                cos_even = weighted([(cosine(parts, residue, block), reals[residue]) for residue in even])
                cos_odd = weighted([(cosine(parts, residue, block), reals[residue]) for residue in odd])
                sin_even = weighted([(sine(parts, residue, block), imags[residue]) for residue in even])
                sin_odd = weighted([(sine(parts, residue, block), imags[residue]) for residue in odd])
                totals[block] = minus(plus(cos_even, cos_odd), plus(sin_even, sin_odd))
                if 0 < block and 2 * block != parts:
                    totals[parts - block] = plus(minus(cos_even, cos_odd), minus(sin_even, sin_odd))
            lane = pl.ds(start, width)
            for pair in range(chips):
                low, high = totals[2 * pair], totals[2 * pair + 1] * sign
                keep_ref[pair, here, lane] = jnp.where(upper, high, low)
                part, place = divmod(pair, chips // 2)
                send_refs[part][place, here, lane] = jnp.where(upper, low, high).astype(BF16)
        return carry

    lax.fori_loop(0, rows // chunk, gather, 0)


def backward(spectrum, first, tables):
    chips = len(first)
    rows, lanes = spectrum.shape[0] // 2, first[0].shape[1]
    _, table, cos, sin = tables
    half = jax.ShapeDtypeStruct((chips // 2, rows, lanes), BF16)
    return pl.pallas_call(
        functools.partial(backward_kernel, chips),
        in_specs=[WHOLE] * (4 + chips),
        out_specs=[WHOLE] * 3,
        out_shape=[jax.ShapeDtypeStruct((chips, rows, lanes), F32), half, half],
        scratch_shapes=[
            pltpu.VMEM((chips, 4, rows, lanes), BF16),
            pltpu.VMEM(spectrum.shape, BF16),
            pltpu.VMEM(spectrum.shape, F32),
        ],
        cost_estimate=CHEAP,
        compiler_params=pltpu.CompilerParams(vmem_limit_bytes=32 * 2**20),
        name="backward",
    )(cos, sin, table, spectrum, *first)


def gate_kernel(chips, skip_ref, keep_ref, low_ref, high_ref, *refs):
    signal_refs, gate_refs = refs[:chips], refs[chips : 2 * chips]
    out_ref, longer_ref, arrived_ref = refs[2 * chips :]
    chip, _ = own_place()
    rows, lanes = keep_ref.shape[1:]
    skip = skip_ref[:, block_at(chip, lanes)]
    arrived_ref[pl.ds(0, chips // 2)] = low_ref[...]
    arrived_ref[pl.ds(chips // 2, chips // 2)] = high_ref[...]
    for offset in range(chips):
        block = chip ^ offset
        convolved = keep_ref[block] + arrived_ref[block].astype(F32)
        signal = signal_refs[offset][pl.ds(0, rows), :].astype(F32)
        gate = gate_refs[offset][pl.ds(0, rows), :].astype(F32)
        gated = (gate * (convolved + skip * signal)).astype(BF16)
        out_ref[block_at(block, rows), :] = gated
        longer_ref[block_at(block, rows), :] = gated
    end = chips * rows
    longer_ref[pl.ds(end, longer_ref.shape[0] - end), :] = longer_ref[pl.ds(0, longer_ref.shape[0] - end), :]


def gate(skip, keep, arrived, first, gates, spare):
    chips, rows, lanes = keep.shape
    return pl.pallas_call(
        functools.partial(gate_kernel, chips),
        in_specs=[WHOLE] * (4 + 2 * chips),
        out_specs=[WHOLE] * 2,
        out_shape=[
            jax.ShapeDtypeStruct((chips * rows, lanes), BF16),
            jax.ShapeDtypeStruct((chips * rows + spare, lanes), BF16),
        ],
        scratch_shapes=[pltpu.VMEM((chips, rows, lanes), BF16)],
        cost_estimate=CHEAP,
        compiler_params=pltpu.CompilerParams(vmem_limit_bytes=6 * 2**20),
        name="gate",
    )(skip, keep, *arrived, *first, *gates)


def piece_of(ref, half, part):
    quarter, share = half // 2, ref.shape[1] // 2
    return ref[pl.ds(ref.shape[0] - quarter, quarter), pl.ds(part * share, share)]


def collect_kernel(in_refs, out_refs):
    rows = out_refs[0].shape[0]
    quarter = len(out_refs) * rows // (2 * len(in_refs))
    for place in range(2 * len(in_refs)):
        index, start = divmod(place * quarter, rows)
        out_refs[index][pl.ds(start, quarter), :] = piece_of(in_refs[place // 2], 2 * quarter, place % 2)


def collect(moved, half):
    count = len(moved)
    shape = (count * half // 2, moved[0].shape[1] // 2)
    return pl.pallas_call(
        lambda *refs: collect_kernel(refs[:count], refs[count:]),
        in_specs=[WHOLE] * count,
        out_specs=[WHOLE] * 2,
        out_shape=[jax.ShapeDtypeStruct(shape, BF16)] * 2,
        cost_estimate=CHEAP,
        compiler_params=pltpu.CompilerParams(vmem_limit_bytes=4 * 2**20),
        name="collect_weights",
    )(*moved)


def slot(target):
    return (1 - target % 2) * 2 + target // 2


def arrange_kernel(chips, mine_ref, *refs):
    moved_refs, (*other_refs, out_ref) = refs[: chips - 1], refs[chips - 1 :]
    chip, core = own_place()
    layer = lax.axis_index("chan")
    depth, share = mine_ref.shape
    quarter = depth // 4
    out_ref[:, block_at(slot(chip ^ layer), share)] = mine_ref[...]
    for place in range(2 * (chips - 1)):
        offset, part = place // 2 + 1, place % 2
        columns = block_at(slot(chip ^ layer ^ offset), share)
        index, start = divmod(place * quarter, other_refs[0].shape[0])
        out_ref[block_at(2 * core + part, quarter), columns] = piece_of(moved_refs[offset - 1], 2 * quarter, part)
        out_ref[block_at(2 * (1 - core) + part, quarter), columns] = other_refs[index][pl.ds(start, quarter), :]


def arrange(mine, moved, others):
    chips = len(moved) + 1
    depth, share = mine.shape
    return pl.pallas_call(
        functools.partial(arrange_kernel, chips),
        in_specs=[WHOLE] * (chips + len(others)),
        out_specs=WHOLE,
        out_shape=jax.ShapeDtypeStruct((depth, chips * share), BF16),
        cost_estimate=CHEAP,
        compiler_params=pltpu.CompilerParams(vmem_limit_bytes=8 * 2**20),
        name="arrange_weights",
    )(mine, *moved, *others)


def project_sent_kernel(chips, weight_ref, *refs):
    gated_refs, (send_ref, joined_ref) = refs[:chips], refs[chips:]
    chip, _ = own_place()
    lanes = gated_refs[0].shape[1]
    share = send_ref.shape[2]
    for offset in range(chips):
        joined_ref[:, block_at(chip ^ offset, lanes)] = gated_refs[offset][pl.ds(0, joined_ref.shape[0]), :]
    weight = weight_ref[:, pl.ds(0, 2 * share)]
    partial = jnp.dot(joined_ref[...], weight, preferred_element_type=F32).astype(BF16)
    send_ref[0] = partial[:, :share]
    send_ref[1] = partial[:, share:]


def project_sent(weight, gated):
    chips = len(gated)
    depth, columns = weight.shape
    rows = gated[0].shape[0]
    return pl.pallas_call(
        functools.partial(project_sent_kernel, chips),
        in_specs=[WHOLE] * (1 + chips),
        out_specs=[WHOLE] * 2,
        out_shape=[
            jax.ShapeDtypeStruct((2, rows, columns // chips), BF16),
            jax.ShapeDtypeStruct((rows, depth), BF16),
        ],
        cost_estimate=CHEAP,
        compiler_params=pltpu.CompilerParams(vmem_limit_bytes=8 * 2**20),
        name="project_sent",
    )(weight, *gated)


def project_kept_kernel(weight_ref, joined_ref, keep_ref, pass_ref):
    share = keep_ref.shape[1]
    weight = weight_ref[:, pl.ds(2 * share, 2 * share)]
    partial = jnp.dot(joined_ref[...], weight, preferred_element_type=F32).astype(BF16)
    keep_ref[...] = partial[:, :share]
    pass_ref[...] = partial[:, share:]


def project_kept(weight, joined):
    block = jax.ShapeDtypeStruct((joined.shape[0], weight.shape[1] // 4), BF16)
    return pl.pallas_call(
        project_kept_kernel,
        in_specs=[WHOLE] * 2,
        out_specs=[WHOLE] * 2,
        out_shape=[block, block],
        cost_estimate=CHEAP,
        compiler_params=pltpu.CompilerParams(vmem_limit_bytes=8 * 2**20),
        name="project_kept",
    )(weight, joined)


def project_still_kernel(chips, own_ref, other_ref, joined_ref, *out_refs):
    chip, core = own_place()
    rows = out_refs[0].shape[0]

    def project_with(weight_ref):
        for offset in range(chips):
            gated = joined_ref[block_at(chip ^ offset, rows), :]
            out_refs[offset][...] = jnp.dot(gated, weight_ref[...], preferred_element_type=F32).astype(BF16)

    @pl.when(core == 0)
    def _():
        project_with(other_ref)

    @pl.when(core == 1)
    def _():
        project_with(own_ref)


def project_still(own, other, joined, chips):
    held = own.shape[1]
    rows = joined.shape[0] // chips
    return pl.pallas_call(
        functools.partial(project_still_kernel, chips),
        in_specs=[WHOLE] * 3,
        out_specs=[WHOLE] * chips,
        out_shape=[jax.ShapeDtypeStruct((rows, held), BF16)] * chips,
        cost_estimate=CHEAP,
        compiler_params=pltpu.CompilerParams(vmem_limit_bytes=12 * 2**20),
        name="project_still",
    )(own, other, joined)


def sort_kernel(chips, *refs):
    in_refs, (*out_refs, sorted_ref) = refs[:chips], refs[chips:]
    chip, _ = own_place()
    layer = lax.axis_index("chan")
    for offset in range(chips):
        sorted_ref[chip ^ layer ^ offset] = in_refs[offset][...]
    for target, out_ref in enumerate(out_refs):
        out_ref[...] = sorted_ref[target]


def sort_blocks(blocks):
    chips = len(blocks)
    block = jax.ShapeDtypeStruct(blocks[0].shape, BF16)
    return pl.pallas_call(
        functools.partial(sort_kernel, chips),
        in_specs=[WHOLE] * chips,
        out_specs=[WHOLE] * chips,
        out_shape=[block] * chips,
        scratch_shapes=[pltpu.VMEM((chips, *block.shape), BF16)],
        cost_estimate=CHEAP,
        compiler_params=pltpu.CompilerParams(vmem_limit_bytes=4 * 2**20),
        name="sort_blocks",
    )(*blocks)


def add_kernel(left_ref, right_ref, out_ref):
    rows = left_ref.shape[0]
    total = (left_ref[...].astype(F32) + right_ref[...].astype(F32)).astype(BF16)
    out_ref[pl.ds(0, rows), :] = total
    more = out_ref.shape[0] - rows
    if more:
        out_ref[pl.ds(rows, more), :] = total[:more]


def add(left, right, spare):
    rows, columns = left.shape
    return pl.pallas_call(
        add_kernel,
        in_specs=[WHOLE] * 2,
        out_specs=WHOLE,
        out_shape=jax.ShapeDtypeStruct((rows + spare, columns), BF16),
        cost_estimate=CHEAP,
        compiler_params=pltpu.CompilerParams(vmem_limit_bytes=4 * 2**20),
        name="add",
    )(left, right)


def finish_kernel(chips, keep_ref, first_ref, second_ref, *out_refs):
    chip, _ = own_place()
    rows = out_refs[0].shape[0]
    for offset in range(chips):
        here = block_at(chip ^ offset, rows)
        total = keep_ref[here, :].astype(F32) + first_ref[0, here, :].astype(F32) + second_ref[here, :].astype(F32)
        out_refs[offset][...] = total.astype(BF16)


def finish(keep, first, second, chips):
    rows, columns = keep.shape
    return pl.pallas_call(
        functools.partial(finish_kernel, chips),
        in_specs=[WHOLE] * 3,
        out_specs=[WHOLE] * chips,
        out_shape=[jax.ShapeDtypeStruct((rows // chips, columns), BF16)] * chips,
        cost_estimate=CHEAP,
        compiler_params=pltpu.CompilerParams(vmem_limit_bytes=4 * 2**20),
        name="finish",
    )(keep, first, second)


def join_kernel(chips, keep_ref, first_ref, second_ref, *refs):
    in_refs, out_ref = refs[:chips], refs[chips]
    chip, _ = own_place()
    share = in_refs[0].shape[1]
    for offset in range(chips):
        out_ref[:, block_at(chip ^ offset, share)] = in_refs[offset][...]
    total = keep_ref[...].astype(F32) + first_ref[...].astype(F32)
    total = total + second_ref[pl.ds(0, total.shape[0]), :].astype(F32)
    out_ref[:, pl.ds(chips * share, total.shape[1])] = total.astype(BF16)


def join(keep, first, second, blocks):
    chips = len(blocks)
    rows, share = blocks[0].shape
    return pl.pallas_call(
        functools.partial(join_kernel, chips),
        in_specs=[WHOLE] * (3 + chips),
        out_specs=WHOLE,
        out_shape=jax.ShapeDtypeStruct((rows, chips * share + keep.shape[1]), BF16),
        cost_estimate=CHEAP,
        compiler_params=pltpu.CompilerParams(vmem_limit_bytes=4 * 2**20),
        name="join",
    )(keep, first, second, *blocks)


def swapped(value, axis, offset):
    if not offset:
        return value
    return lax.ppermute(value, axis, [(source, source ^ offset) for source in range(lax.axis_size(axis))])


def to_chips(blocks):
    return [swapped(block, "seq", 2 * offset) for offset, block in enumerate(blocks)]


def after(value, *others):
    return lax.optimization_barrier((value, *others))[0]


def after(value, *others):
    return lax.optimization_barrier((value, *others))[0]


def over_layers(passed, send):
    first = swapped(send, "chan", 1)
    passed = (passed.astype(F32) + first[1].astype(F32)).astype(BF16)
    return first, swapped(passed, "chan", 2)


def shards_direct(values_in, gate_values, filter_spectrum, skip_gain, out_weight):
    parts = lax.axis_size("seq")
    chips = parts // 2
    rows, width = values_in.shape
    tables = small_tables(parts, rows)

    values = pack_values(values_in, chips, 0)
    flat_filters = filter_spectrum.reshape(4, rows, width)
    near = pack_filters(after(flat_filters, values[0]), chips, (1, 2), 0)
    other_weight = swapped(out_weight, "seq", 1)
    *moved, mine = pack_moved(after(gate_values, near[0]), out_weight, other_weight, chips)
    own, far = pack_filters(after(flat_filters, moved[0]), chips, (0, 3), 0)
    values, filters = to_chips(values), to_chips([own, *near, far])
    own = stack([after(block, far) for block in values], rows)
    spectrum = forward(own, [swapped(part, "seq", 1) for part in own], tables)
    moved = to_chips([after(block, spectrum) for block in moved])
    keep, *send = backward(spectrum, filters, tables)
    gated, longer = gate(skip_gain[None, :], keep, [swapped(part, "seq", 1) for part in send], values, moved, 16)
    gathered = to_chips([gated, longer, longer, gated])

    others = [swapped(part, "seq", 1) for part in collect([after(block, gated) for block in moved[1:]], out_weight.shape[0] // 2)]
    moved_weight = arrange(mine, moved[1:], others)
    send, joined = project_sent(moved_weight, gathered)
    first = swapped(send, "chan", 1)
    keep, passed = project_kept(moved_weight, after(joined, first))
    passed = (passed.astype(F32) + first[1].astype(F32)).astype(BF16)
    blocks = to_chips(finish(keep, first, swapped(passed, "chan", 2), chips))
    keep, near, passed, far = sort_blocks(to_chips(project_still(out_weight, other_weight, joined, chips)))
    second = swapped(add(after(passed, blocks[3], blocks[1]), swapped(far, "chan", 1), 0), "chan", 2)
    return join(keep, swapped(near, "chan", 1), second, blocks)


def shards(values_in, gate_values, filter_spectrum, skip_gain, out_weight):
    parts, layers = lax.axis_size("seq"), lax.axis_size("chan")
    rows, width = values_in.shape
    share = out_weight.shape[1] // layers
    aligned = width // parts % 128 == 0 and share % 128 == 0 and rows % 32 == 0
    run = shards_direct if aligned and layers == 4 and parts == 8 else shards_general
    return run(values_in, gate_values, filter_spectrum, skip_gain, out_weight)


def solution(mesh):
    in_specs = (
        P("seq", "chan"),
        P("seq", "chan"),
        P(None, "seq", None, "chan"),
        P("chan"),
        P("chan", "seq"),
    )
    out_specs = P("seq", "chan")
    return jax.shard_map(shards, mesh=mesh, in_specs=in_specs, out_specs=out_specs, check_vma=False)
```

```python
import functools

import jax
import jax.numpy as jnp
import numpy as np
from jax import lax
from jax.experimental import pallas as pl
from jax.experimental.pallas import tpu as pltpu
from jax.sharding import PartitionSpec as P

BF16 = jnp.bfloat16
F32 = jnp.float32


def bit_reversed(number, width_bits):
    flipped = 0
    for bit_place in range(width_bits):
        flipped |= (number >> bit_place & 1) << (width_bits - 1 - bit_place)
    return flipped


def filter_row(residue, width_bits):
    return 2 * bit_reversed(residue // 2, width_bits) + residue % 2


def dft_tables(parts, rows):
    total = 2 * parts * rows
    residue = np.arange(2 * parts)[:, None, None]
    column = np.arange(rows)[None, :, None]
    position = np.arange(rows)[None, None, :]
    phase = 2.0 * np.pi * (position * (residue + 2 * parts * column) % total) / total
    cos, sin = np.cos(phase), np.sin(phase)
    forward = np.concatenate(
        [np.concatenate([cos, sin], axis=2), np.concatenate([-sin, cos], axis=2)], axis=1
    )
    inverse = np.transpose(forward, (0, 2, 1)) / total
    return forward.astype(BF16), inverse.astype(BF16)


def convolve_kernel(parts, rows, moved_ref, skip_ref, forward_ref, inverse_ref, out_ref, waves_ref, back_ref):
    width_bits = parts.bit_length() - 1
    chunk = 16

    def cosine(residue, block):
        return float(np.cos(np.pi * residue * block / parts))

    def sine(residue, block):
        return float(np.sin(np.pi * residue * block / parts))

    def spread(index, carry):
        here = pl.ds(index * chunk, chunk)
        there = pl.ds(rows + index * chunk, chunk)
        blocks = [moved_ref[block, here, :].astype(F32) for block in range(parts)]
        for residue in range(parts + 1):
            real = blocks[0]
            imag = jnp.zeros_like(real)
            for block in range(1, parts):
                real = real + cosine(residue, block) * blocks[block]
                imag = imag - sine(residue, block) * blocks[block]
            waves_ref[residue, here, :] = real.astype(BF16)
            waves_ref[residue, there, :] = imag.astype(BF16)
            if 0 < residue < parts:
                waves_ref[2 * parts - residue, here, :] = real.astype(BF16)
                waves_ref[2 * parts - residue, there, :] = (-imag).astype(BF16)
        return carry

    lax.fori_loop(0, rows // chunk, spread, 0)

    def through(residue):
        wave = jnp.dot(forward_ref[residue], waves_ref[residue], preferred_element_type=F32)
        source, odd = divmod(filter_row(residue, width_bits), 2)
        filter_real = moved_ref[source, pl.ds((2 + odd) * rows, rows), :].astype(F32)
        filter_imag = moved_ref[source, pl.ds((4 + odd) * rows, rows), :].astype(F32)
        real, imag = wave[:rows], wave[rows:]
        product = jnp.concatenate(
            [real * filter_real - imag * filter_imag, real * filter_imag + imag * filter_real], axis=0
        )
        return jnp.dot(inverse_ref[residue], product.astype(BF16), preferred_element_type=F32)

    for residue in range(parts + 1):
        back = through(residue)
        if 0 < residue < parts:
            other = through(2 * parts - residue)
            back_ref[residue, pl.ds(0, rows), :] = back[:rows] + other[:rows]
            back_ref[residue, pl.ds(rows, rows), :] = back[rows:] - other[rows:]
        else:
            back_ref[residue] = back

    skip = skip_ref[...]

    def gather(index, carry):
        here = pl.ds(index * chunk, chunk)
        there = pl.ds(rows + index * chunk, chunk)
        reals = [back_ref[residue, here, :] for residue in range(parts + 1)]
        imags = [back_ref[residue, there, :] for residue in range(parts + 1)]
        for block in range(parts):
            total = reals[0]
            for residue in range(1, parts + 1):
                total = total + cosine(residue, block) * reals[residue]
                if residue < parts and block:
                    total = total - sine(residue, block) * imags[residue]
            signal = moved_ref[block, here, :].astype(F32)
            gate = moved_ref[block, pl.ds(rows + index * chunk, chunk), :].astype(F32)
            out_ref[block, here, :] = (gate * (total + skip * signal)).astype(BF16)
        return carry

    lax.fori_loop(0, rows // chunk, gather, 0)


def convolve(moved, skip):
    parts, stacked, width = moved.shape
    rows = stacked // 6
    forward, inverse = dft_tables(parts, rows)
    whole = pl.BlockSpec(memory_space=pltpu.VMEM)
    return pl.pallas_call(
        functools.partial(convolve_kernel, parts, rows),
        out_shape=jax.ShapeDtypeStruct((parts, rows, width), BF16),
        in_specs=[whole] * 4,
        out_specs=whole,
        scratch_shapes=[
            pltpu.VMEM((2 * parts, 2 * rows, width), BF16),
            pltpu.VMEM((parts + 1, 2 * rows, width), F32),
        ],
        compiler_params=pltpu.CompilerParams(vmem_limit_bytes=40 * 2**20),
    )(moved, skip[None, :], forward, inverse)


def shards_general(values_in, gate_values, filter_spectrum, skip_gain, out_weight):
    parts = lax.axis_size("seq")
    layers = lax.axis_size("chan")
    rows, width = values_in.shape
    lanes = width // parts
    device = lax.axis_index("seq")

    def by_channel(array):
        return jnp.transpose(array.reshape(array.shape[0], parts, lanes), (1, 0, 2))

    filters = filter_spectrum.astype(BF16).reshape(4 * rows, width)
    packed = jnp.concatenate([by_channel(values_in), by_channel(gate_values), by_channel(filters)], axis=1)
    moved = lax.all_to_all(packed, "seq", 0, 0)
    skip = lax.dynamic_slice_in_dim(skip_gain, device * lanes, lanes)
    gated = convolve(moved, skip)
    gathered = lax.all_gather(gated.reshape(parts * rows, lanes), "seq", axis=1, tiled=True)

    own_cols = out_weight.shape[1]
    share = own_cols * parts // layers // parts
    per_block = parts // layers
    pieces = own_cols // share
    group = device % per_block
    member = device // per_block
    weight = jnp.zeros_like(out_weight)
    for step in range(pieces):
        piece = (member + step) % pieces
        sent = lax.dynamic_slice_in_dim(out_weight, piece * share, share, 1)
        pairs = [
            (source, source % per_block * pieces + (source // per_block + step) % pieces) for source in range(parts)
        ]
        arrived = lax.ppermute(sent, "seq", pairs)
        block = (device % pieces - step) % pieces
        weight = lax.dynamic_update_slice_in_dim(weight, arrived, block * share, 1)
    partials = jnp.dot(gathered, weight, preferred_element_type=F32).astype(BF16)
    mixed = lax.psum_scatter(partials, "chan", scatter_dimension=1, tiled=True)
    return lax.all_to_all(mixed, "seq", 0, 1, tiled=True)


WHOLE = pl.BlockSpec(memory_space=pltpu.VMEM)
CHEAP = pl.CostEstimate(flops=0, transcendentals=0, bytes_accessed=0)


def small_tables(parts, rows):
    total = 2 * parts * rows
    index = np.arange(rows)
    phase = 2.0 * np.pi * (index[:, None] * index[None, :] % rows) / rows
    cos, sin = np.cos(phase), np.sin(phase)
    forward = np.block([[cos, sin], [-sin, cos]])
    residue = np.arange(2 * parts).reshape(2, 1, parts)
    turn = 2.0 * np.pi * index[None, :, None] * residue / total
    return forward.astype(BF16), forward.T.astype(BF16), np.cos(turn).astype(F32), np.sin(turn).astype(F32)


def cosine(parts, residue, block):
    return float(np.cos(np.pi * residue * block / parts))


def sine(parts, residue, block):
    return float(np.sin(np.pi * residue * block / parts))


def weighted(terms):
    total = None
    for factor, term in terms:
        if abs(factor) < 1e-12:
            continue
        part = term if factor == 1.0 else factor * term
        total = part if total is None else total + part
    return total


def plus(left, right):
    return left if right is None else right if left is None else left + right


def minus(left, right):
    return left if right is None else -right if left is None else left - right


def own_place():
    device = lax.axis_index("seq")
    return device // 2, device % 2


def block_at(index, size):
    return pl.ds(pl.multiple_of(index * size, size), size)


def pack_filters_kernel(offsets, filter_ref, *refs):
    out_refs, (plane_ref, arrived) = refs[: len(offsets)], refs[len(offsets) :]
    chip, _ = own_place()
    planes, rows, _ = filter_ref.shape
    lanes = out_refs[0].shape[1]
    copies = []
    for place, offset in enumerate(offsets):
        here = block_at(chip ^ offset, lanes)
        for plane in range(planes):
            copies.append(
                pltpu.make_async_copy(filter_ref.at[plane, :, here], plane_ref.at[place, plane], arrived.at[place, plane])
            )
    for copy in copies:
        copy.start()
    for index, copy in enumerate(copies):
        copy.wait()
        place, plane = divmod(index, planes)
        out_refs[place][pl.ds(plane * rows, rows), :] = plane_ref[place, plane].astype(BF16)
    used = planes * rows
    for out_ref in out_refs:
        if out_ref.shape[0] > used:
            out_ref[pl.ds(used, out_ref.shape[0] - used), :] = out_ref[pl.ds(0, out_ref.shape[0] - used), :]


def pack_filters(filters, chips, offsets, spare):
    planes, rows, width = filters.shape
    lanes = width // chips
    return pl.pallas_call(
        functools.partial(pack_filters_kernel, offsets),
        in_specs=[pl.BlockSpec(memory_space=pltpu.HBM)],
        out_specs=[WHOLE] * len(offsets),
        out_shape=[jax.ShapeDtypeStruct((planes * rows + spare, lanes), BF16)] * len(offsets),
        scratch_shapes=[
            pltpu.VMEM((len(offsets), planes, rows, lanes), F32),
            pltpu.SemaphoreType.DMA((len(offsets), planes)),
        ],
        cost_estimate=CHEAP,
        compiler_params=pltpu.CompilerParams(vmem_limit_bytes=8 * 2**20),
        name="pack_filters",
    )(pltpu.with_memory_space_constraint(filters, pltpu.HBM))


def pack_values_kernel(chips, values_ref, *refs):
    out_refs, arrived = refs[:chips], refs[chips]
    rows = values_ref.shape[0]
    chip, _ = own_place()
    copies = []
    for offset, out_ref in enumerate(out_refs):
        values = values_ref.at[:, block_at(chip ^ offset, out_ref.shape[1])]
        copies.append(pltpu.make_async_copy(values, out_ref.at[pl.ds(0, rows)], arrived.at[offset]))
    for copy in copies:
        copy.start()
    for copy in copies:
        copy.wait()


def pack_values(values_in, chips, spare):
    rows, width = values_in.shape
    return pl.pallas_call(
        functools.partial(pack_values_kernel, chips),
        in_specs=[pl.BlockSpec(memory_space=pltpu.HBM)],
        out_specs=[WHOLE] * chips,
        out_shape=[jax.ShapeDtypeStruct((rows + spare, width // chips), BF16)] * chips,
        scratch_shapes=[pltpu.SemaphoreType.DMA((chips,))],
        cost_estimate=CHEAP,
        compiler_params=pltpu.CompilerParams(vmem_limit_bytes=4 * 2**20),
        name="pack_values",
    )(pltpu.with_memory_space_constraint(values_in, pltpu.HBM))


def pack_moved_kernel(chips, gate_ref, own_ref, other_ref, *refs):
    out_refs, (mine_ref, arrived) = refs[:chips], refs[chips:]
    chip, core = own_place()
    rows = gate_ref.shape[0]
    depth, held = own_ref.shape
    quarter, share = depth // 4, held // chips

    def copies_from(weight_ref):
        copies = [pltpu.make_async_copy(weight_ref.at[:, block_at(chip, share)], mine_ref, arrived.at[0, 0])]
        for offset in range(chips):
            out_ref, target = out_refs[offset], chip ^ offset
            gates = gate_ref.at[:, block_at(target, out_ref.shape[1])]
            copies.append(pltpu.make_async_copy(gates, out_ref.at[pl.ds(0, rows)], arrived.at[offset, 2]))
            for part in range(2 if offset else 0):
                source = weight_ref.at[block_at(2 * core + part, quarter), block_at(target, share)]
                sink = out_ref.at[pl.ds(rows, quarter), pl.ds(part * share, share)]
                copies.append(pltpu.make_async_copy(source, sink, arrived.at[offset, part]))
        for copy in copies:
            copy.start()
        for copy in copies:
            copy.wait()

    @pl.when(core == 0)
    def _():
        copies_from(own_ref)

    @pl.when(core == 1)
    def _():
        copies_from(other_ref)


def pack_moved(gate_values, own, other, chips):
    rows, width = gate_values.shape
    depth, held = own.shape
    share = held // chips
    return pl.pallas_call(
        functools.partial(pack_moved_kernel, chips),
        in_specs=[pl.BlockSpec(memory_space=pltpu.HBM)] * 2 + [pl.BlockSpec(memory_space=pl.ANY)],
        out_specs=[WHOLE] * (chips + 1),
        out_shape=[
            *(jax.ShapeDtypeStruct((rows + (depth // 4 if offset else 0), 2 * share), BF16) for offset in range(chips)),
            jax.ShapeDtypeStruct((depth, share), BF16),
        ],
        scratch_shapes=[pltpu.SemaphoreType.DMA((chips, 3))],
        cost_estimate=CHEAP,
        compiler_params=pltpu.CompilerParams(vmem_limit_bytes=8 * 2**20),
        name="pack_moved",
    )(*(pltpu.with_memory_space_constraint(array, pltpu.HBM) for array in (gate_values, own)), other)


def stack_kernel(chips, *refs):
    in_refs, out_refs = refs[:chips], refs[chips:]
    for offset, in_ref in enumerate(in_refs):
        part, place = divmod(offset, chips // 2)
        out_refs[part][place] = in_ref[pl.ds(0, out_refs[part].shape[1]), :]


def stack(blocks, rows):
    chips = len(blocks)
    half = jax.ShapeDtypeStruct((chips // 2, rows, blocks[0].shape[1]), BF16)
    return pl.pallas_call(
        functools.partial(stack_kernel, chips),
        in_specs=[WHOLE] * chips,
        out_specs=[WHOLE] * 2,
        out_shape=[half, half],
        cost_estimate=CHEAP,
        compiler_params=pltpu.CompilerParams(vmem_limit_bytes=4 * 2**20),
        name="stack",
    )(*blocks)


def forward_kernel(chips, cos_ref, sin_ref, table_ref, *refs):
    own_refs, other_refs, (out_ref, signal_ref, waves_ref) = refs[:2], refs[2:4], refs[4:]
    chip, core = own_place()
    parts = 2 * chips
    rows, lanes = own_refs[0].shape[1:]
    chunk, width = 16, 128
    for offset in range(chips):
        part, place = divmod(offset, chips // 2)
        signal_ref[2 * (chip ^ offset) + core] = own_refs[part][place]
        signal_ref[2 * (chip ^ offset) + 1 - core] = other_refs[part][place]
    sign = (1 - 2 * core).astype(F32)

    def spread(index, carry):
        here = block_at(index, chunk)
        there = pl.ds(pl.multiple_of(rows + index * chunk, chunk), chunk)
        cos_all, sin_all = cos_ref[core, here, :], sin_ref[core, here, :]
        for start in range(0, lanes, width):
            blocks = [signal_ref[block, here, pl.ds(start, width)].astype(F32) for block in range(parts)]
            blocks = [block * sign if place % 2 else block for place, block in enumerate(blocks)]

            def store(residue, real, imag):
                cos, sin = cos_all[:, residue : residue + 1], sin_all[:, residue : residue + 1]
                if imag is None:
                    real, imag = real * cos, -(real * sin)
                else:
                    real, imag = real * cos + imag * sin, imag * cos - real * sin
                columns = pl.ds(residue * lanes + start, width)
                waves_ref[here, columns] = real.astype(BF16)
                waves_ref[there, columns] = imag.astype(BF16)

            for residue in range(parts // 2 + 1):
                even, odd = range(0, parts, 2), range(1, parts, 2)
                cos_even = weighted([(cosine(parts, residue, block), blocks[block]) for block in even])
                cos_odd = weighted([(cosine(parts, residue, block), blocks[block]) for block in odd])
                sin_even = weighted([(sine(parts, residue, block), blocks[block]) for block in even])
                sin_odd = weighted([(sine(parts, residue, block), blocks[block]) for block in odd])
                sin_sum = plus(sin_even, sin_odd)
                store(residue, plus(cos_even, cos_odd), None if sin_sum is None else -sin_sum)
                if 0 < residue and 2 * residue != parts:
                    store(parts - residue, minus(cos_even, cos_odd), minus(sin_even, sin_odd))
        return carry

    lax.fori_loop(0, rows // chunk, spread, 0)
    for residue in range(parts):
        columns = pl.ds(residue * lanes, lanes)
        out_ref[:, columns] = jnp.dot(table_ref[...], waves_ref[:, columns], preferred_element_type=F32)


def forward(own, other, tables):
    chips, (_, rows, lanes) = 2 * own[0].shape[0], own[0].shape
    table, _, cos, sin = tables
    spectrum = (2 * rows, 2 * chips * lanes)
    return pl.pallas_call(
        functools.partial(forward_kernel, chips),
        in_specs=[WHOLE] * 7,
        out_specs=WHOLE,
        out_shape=jax.ShapeDtypeStruct(spectrum, F32),
        scratch_shapes=[pltpu.VMEM((2 * chips, rows, lanes), BF16), pltpu.VMEM(spectrum, BF16)],
        cost_estimate=CHEAP,
        compiler_params=pltpu.CompilerParams(vmem_limit_bytes=32 * 2**20),
        name="forward",
    )(cos, sin, table, *own, *other)


def backward_kernel(chips, cos_ref, sin_ref, table_ref, spectrum_ref, *refs):
    filter_refs, (keep_ref, *send_refs, filter_ref, product_ref, back_ref) = refs[:chips], refs[chips:]
    chip, core = own_place()
    parts = 2 * chips
    rows, lanes = keep_ref.shape[1:]
    chip_bits = chips.bit_length() - 1
    chunk, width = 16, 128
    for offset in range(chips):
        for plane in range(filter_ref.shape[1]):
            filter_ref[chip ^ offset, plane] = filter_refs[offset][pl.ds(plane * rows, rows), :]

    for residue in range(parts):
        source, odd = bit_reversed(residue // 2, chip_bits), residue % 2
        columns = pl.ds(residue * lanes, lanes)
        filter_real = filter_ref[source, odd].astype(F32)
        filter_imag = filter_ref[source, 2 + odd].astype(F32)
        real = spectrum_ref[pl.ds(0, rows), columns]
        imag = spectrum_ref[pl.ds(rows, rows), columns]
        product_ref[pl.ds(0, rows), columns] = (real * filter_real - imag * filter_imag).astype(BF16)
        product_ref[pl.ds(rows, rows), columns] = (real * filter_imag + imag * filter_real).astype(BF16)
        back_ref[:, columns] = jnp.dot(table_ref[...], product_ref[:, columns], preferred_element_type=F32)

    scale = 1.0 / (2 * parts * rows)
    sign = (1 - 2 * core).astype(F32)
    upper = core == 1

    def gather(index, carry):
        here = block_at(index, chunk)
        there = pl.ds(pl.multiple_of(rows + index * chunk, chunk), chunk)
        cos_all, sin_all = cos_ref[core, here, :] * scale, sin_ref[core, here, :] * scale
        for start in range(0, lanes, width):
            reals, imags = [], []
            for residue in range(parts):
                columns = pl.ds(residue * lanes + start, width)
                real, imag = back_ref[here, columns], back_ref[there, columns]
                cos, sin = cos_all[:, residue : residue + 1], sin_all[:, residue : residue + 1]
                reals.append(real * cos - imag * sin)
                imags.append(real * sin + imag * cos)
            totals = [None] * parts
            for block in range(parts // 2 + 1):
                even, odd = range(0, parts, 2), range(1, parts, 2)
                cos_even = weighted([(cosine(parts, residue, block), reals[residue]) for residue in even])
                cos_odd = weighted([(cosine(parts, residue, block), reals[residue]) for residue in odd])
                sin_even = weighted([(sine(parts, residue, block), imags[residue]) for residue in even])
                sin_odd = weighted([(sine(parts, residue, block), imags[residue]) for residue in odd])
                totals[block] = minus(plus(cos_even, cos_odd), plus(sin_even, sin_odd))
                if 0 < block and 2 * block != parts:
                    totals[parts - block] = plus(minus(cos_even, cos_odd), minus(sin_even, sin_odd))
            lane = pl.ds(start, width)
            for pair in range(chips):
                low, high = totals[2 * pair], totals[2 * pair + 1] * sign
                keep_ref[pair, here, lane] = jnp.where(upper, high, low)
                part, place = divmod(pair, chips // 2)
                send_refs[part][place, here, lane] = jnp.where(upper, low, high).astype(BF16)
        return carry

    lax.fori_loop(0, rows // chunk, gather, 0)


def backward(spectrum, first, tables):
    chips = len(first)
    rows, lanes = spectrum.shape[0] // 2, first[0].shape[1]
    _, table, cos, sin = tables
    half = jax.ShapeDtypeStruct((chips // 2, rows, lanes), BF16)
    return pl.pallas_call(
        functools.partial(backward_kernel, chips),
        in_specs=[WHOLE] * (4 + chips),
        out_specs=[WHOLE] * 3,
        out_shape=[jax.ShapeDtypeStruct((chips, rows, lanes), F32), half, half],
        scratch_shapes=[
            pltpu.VMEM((chips, 4, rows, lanes), BF16),
            pltpu.VMEM(spectrum.shape, BF16),
            pltpu.VMEM(spectrum.shape, F32),
        ],
        cost_estimate=CHEAP,
        compiler_params=pltpu.CompilerParams(vmem_limit_bytes=32 * 2**20),
        name="backward",
    )(cos, sin, table, spectrum, *first)


def gate_kernel(chips, skip_ref, keep_ref, low_ref, high_ref, *refs):
    signal_refs, gate_refs = refs[:chips], refs[chips : 2 * chips]
    out_ref, longer_ref, arrived_ref = refs[2 * chips :]
    chip, _ = own_place()
    rows, lanes = keep_ref.shape[1:]
    skip = skip_ref[:, block_at(chip, lanes)]
    arrived_ref[pl.ds(0, chips // 2)] = low_ref[...]
    arrived_ref[pl.ds(chips // 2, chips // 2)] = high_ref[...]
    for offset in range(chips):
        block = chip ^ offset
        convolved = keep_ref[block] + arrived_ref[block].astype(F32)
        signal = signal_refs[offset][pl.ds(0, rows), :].astype(F32)
        gate = gate_refs[offset][pl.ds(0, rows), :].astype(F32)
        gated = (gate * (convolved + skip * signal)).astype(BF16)
        out_ref[block_at(block, rows), :] = gated
        longer_ref[block_at(block, rows), :] = gated
    end = chips * rows
    longer_ref[pl.ds(end, longer_ref.shape[0] - end), :] = longer_ref[pl.ds(0, longer_ref.shape[0] - end), :]


def gate(skip, keep, arrived, first, gates, spare):
    chips, rows, lanes = keep.shape
    return pl.pallas_call(
        functools.partial(gate_kernel, chips),
        in_specs=[WHOLE] * (4 + 2 * chips),
        out_specs=[WHOLE] * 2,
        out_shape=[
            jax.ShapeDtypeStruct((chips * rows, lanes), BF16),
            jax.ShapeDtypeStruct((chips * rows + spare, lanes), BF16),
        ],
        scratch_shapes=[pltpu.VMEM((chips, rows, lanes), BF16)],
        cost_estimate=CHEAP,
        compiler_params=pltpu.CompilerParams(vmem_limit_bytes=6 * 2**20),
        name="gate",
    )(skip, keep, *arrived, *first, *gates)


def piece_of(ref, half, part):
    quarter, share = half // 2, ref.shape[1] // 2
    return ref[pl.ds(ref.shape[0] - quarter, quarter), pl.ds(part * share, share)]


def collect_kernel(in_refs, out_refs):
    rows = out_refs[0].shape[0]
    quarter = len(out_refs) * rows // (2 * len(in_refs))
    for place in range(2 * len(in_refs)):
        index, start = divmod(place * quarter, rows)
        out_refs[index][pl.ds(start, quarter), :] = piece_of(in_refs[place // 2], 2 * quarter, place % 2)


def collect(moved, half):
    count = len(moved)
    shape = (count * half // 2, moved[0].shape[1] // 2)
    return pl.pallas_call(
        lambda *refs: collect_kernel(refs[:count], refs[count:]),
        in_specs=[WHOLE] * count,
        out_specs=[WHOLE] * 2,
        out_shape=[jax.ShapeDtypeStruct(shape, BF16)] * 2,
        cost_estimate=CHEAP,
        compiler_params=pltpu.CompilerParams(vmem_limit_bytes=4 * 2**20),
        name="collect_weights",
    )(*moved)


def arrange_kernel(chips, mine_ref, *refs):
    moved_refs, (*other_refs, out_ref) = refs[: chips - 1], refs[chips - 1 :]
    chip, core = own_place()
    layer = lax.axis_index("chan")
    depth, share = mine_ref.shape
    quarter = depth // 4
    out_ref[:, block_at(chip ^ layer, share)] = mine_ref[...]
    for place in range(2 * (chips - 1)):
        offset, part = place // 2 + 1, place % 2
        columns = block_at(chip ^ layer ^ offset, share)
        index, start = divmod(place * quarter, other_refs[0].shape[0])
        out_ref[block_at(2 * core + part, quarter), columns] = piece_of(moved_refs[offset - 1], 2 * quarter, part)
        out_ref[block_at(2 * (1 - core) + part, quarter), columns] = other_refs[index][pl.ds(start, quarter), :]


def arrange(mine, moved, others):
    chips = len(moved) + 1
    depth, share = mine.shape
    return pl.pallas_call(
        functools.partial(arrange_kernel, chips),
        in_specs=[WHOLE] * (chips + len(others)),
        out_specs=WHOLE,
        out_shape=jax.ShapeDtypeStruct((depth, chips * share), BF16),
        cost_estimate=CHEAP,
        compiler_params=pltpu.CompilerParams(vmem_limit_bytes=8 * 2**20),
        name="arrange_weights",
    )(mine, *moved, *others)


def join_channels(chips, gated_refs, joined_ref):
    chip, _ = own_place()
    lanes = gated_refs[0].shape[1]
    for offset in range(chips):
        joined_ref[:, block_at(chip ^ offset, lanes)] = gated_refs[offset][pl.ds(0, joined_ref.shape[0]), :]


def project_moved_kernel(chips, weight_ref, *refs):
    gated_refs, (keep_ref, pass_ref, send_ref, joined_ref) = refs[:chips], refs[chips:]
    share = keep_ref.shape[1]
    join_channels(chips, gated_refs, joined_ref)
    partial = jnp.dot(joined_ref[...], weight_ref[...], preferred_element_type=F32).astype(BF16)
    keep_ref[...] = partial[:, :share]
    send_ref[0] = partial[:, share : 2 * share]
    pass_ref[...] = partial[:, 2 * share : 3 * share]
    send_ref[1] = partial[:, 3 * share :]


def project_moved(weight, gated):
    chips = len(gated)
    depth, columns = weight.shape
    rows = gated[0].shape[0]
    block = jax.ShapeDtypeStruct((rows, columns // chips), BF16)
    return pl.pallas_call(
        functools.partial(project_moved_kernel, chips),
        in_specs=[WHOLE] * (1 + chips),
        out_specs=[WHOLE] * 3,
        out_shape=[block, block, jax.ShapeDtypeStruct((2, rows, columns // chips), BF16)],
        scratch_shapes=[pltpu.VMEM((rows, depth), BF16)],
        cost_estimate=CHEAP,
        compiler_params=pltpu.CompilerParams(vmem_limit_bytes=8 * 2**20),
        name="project_moved",
    )(weight, *gated)


def project_still_kernel(chips, own_ref, other_ref, *refs):
    gated_refs, out_refs, joined_ref = refs[:chips], refs[chips : 2 * chips], refs[2 * chips]
    chip, core = own_place()
    rows = out_refs[0].shape[0]
    join_channels(chips, gated_refs, joined_ref)

    def project_with(weight_ref):
        for offset in range(chips):
            gated = joined_ref[block_at(chip ^ offset, rows), :]
            out_refs[offset][...] = jnp.dot(gated, weight_ref[...], preferred_element_type=F32).astype(BF16)

    @pl.when(core == 0)
    def _():
        project_with(other_ref)

    @pl.when(core == 1)
    def _():
        project_with(own_ref)


def project_still(own, other, gated):
    chips = len(gated)
    depth, held = own.shape
    rows = gated[0].shape[0] // chips
    return pl.pallas_call(
        functools.partial(project_still_kernel, chips),
        in_specs=[WHOLE] * (2 + chips),
        out_specs=[WHOLE] * chips,
        out_shape=[jax.ShapeDtypeStruct((rows, held), BF16)] * chips,
        scratch_shapes=[pltpu.VMEM((rows * chips, depth), BF16)],
        cost_estimate=CHEAP,
        compiler_params=pltpu.CompilerParams(vmem_limit_bytes=12 * 2**20),
        name="project_still",
    )(own, other, *gated)


def sort_kernel(chips, *refs):
    in_refs, (*out_refs, sorted_ref) = refs[:chips], refs[chips:]
    chip, _ = own_place()
    layer = lax.axis_index("chan")
    for offset in range(chips):
        sorted_ref[chip ^ layer ^ offset] = in_refs[offset][...]
    for target, out_ref in enumerate(out_refs):
        out_ref[...] = sorted_ref[target]


def sort_blocks(blocks):
    chips = len(blocks)
    block = jax.ShapeDtypeStruct(blocks[0].shape, BF16)
    return pl.pallas_call(
        functools.partial(sort_kernel, chips),
        in_specs=[WHOLE] * chips,
        out_specs=[WHOLE] * chips,
        out_shape=[block] * chips,
        scratch_shapes=[pltpu.VMEM((chips, *block.shape), BF16)],
        cost_estimate=CHEAP,
        compiler_params=pltpu.CompilerParams(vmem_limit_bytes=4 * 2**20),
        name="sort_blocks",
    )(*blocks)


def add_kernel(left_ref, right_ref, out_ref):
    rows = left_ref.shape[0]
    total = (left_ref[...].astype(F32) + right_ref[...].astype(F32)).astype(BF16)
    out_ref[pl.ds(0, rows), :] = total
    more = out_ref.shape[0] - rows
    if more:
        out_ref[pl.ds(rows, more), :] = total[:more]


def add(left, right, spare):
    rows, columns = left.shape
    return pl.pallas_call(
        add_kernel,
        in_specs=[WHOLE] * 2,
        out_specs=WHOLE,
        out_shape=jax.ShapeDtypeStruct((rows + spare, columns), BF16),
        cost_estimate=CHEAP,
        compiler_params=pltpu.CompilerParams(vmem_limit_bytes=4 * 2**20),
        name="add",
    )(left, right)


def finish_kernel(chips, keep_ref, first_ref, second_ref, *out_refs):
    chip, _ = own_place()
    rows = out_refs[0].shape[0]
    for offset in range(chips):
        here = block_at(chip ^ offset, rows)
        total = keep_ref[here, :].astype(F32) + first_ref[0, here, :].astype(F32) + second_ref[here, :].astype(F32)
        out_refs[offset][...] = total.astype(BF16)


def finish(keep, first, second, chips):
    rows, columns = keep.shape
    return pl.pallas_call(
        functools.partial(finish_kernel, chips),
        in_specs=[WHOLE] * 3,
        out_specs=[WHOLE] * chips,
        out_shape=[jax.ShapeDtypeStruct((rows // chips, columns), BF16)] * chips,
        cost_estimate=CHEAP,
        compiler_params=pltpu.CompilerParams(vmem_limit_bytes=4 * 2**20),
        name="finish",
    )(keep, first, second)


def join_kernel(chips, keep_ref, first_ref, second_ref, *refs):
    in_refs, out_ref = refs[:chips], refs[chips]
    chip, _ = own_place()
    share = in_refs[0].shape[1]
    for offset in range(chips):
        out_ref[:, block_at(chip ^ offset, share)] = in_refs[offset][...]
    total = keep_ref[...].astype(F32) + first_ref[...].astype(F32)
    total = total + second_ref[pl.ds(0, total.shape[0]), :].astype(F32)
    out_ref[:, pl.ds(chips * share, total.shape[1])] = total.astype(BF16)


def join(keep, first, second, blocks):
    chips = len(blocks)
    rows, share = blocks[0].shape
    return pl.pallas_call(
        functools.partial(join_kernel, chips),
        in_specs=[WHOLE] * (3 + chips),
        out_specs=WHOLE,
        out_shape=jax.ShapeDtypeStruct((rows, chips * share + keep.shape[1]), BF16),
        cost_estimate=CHEAP,
        compiler_params=pltpu.CompilerParams(vmem_limit_bytes=4 * 2**20),
        name="join",
    )(keep, first, second, *blocks)


def swapped(value, axis, offset):
    if not offset:
        return value
    return lax.ppermute(value, axis, [(source, source ^ offset) for source in range(lax.axis_size(axis))])


def to_chips(blocks):
    return [swapped(block, "seq", 2 * offset) for offset, block in enumerate(blocks)]


def after(value, *others):
    return lax.optimization_barrier((value, *others))[0]


def over_layers(passed, send):
    first = swapped(send, "chan", 1)
    passed = (passed.astype(F32) + first[1].astype(F32)).astype(BF16)
    return first, swapped(passed, "chan", 2)


def shards_direct(values_in, gate_values, filter_spectrum, skip_gain, out_weight):
    parts = lax.axis_size("seq")
    chips = parts // 2
    rows, width = values_in.shape
    tables = small_tables(parts, rows)

    values = pack_values(values_in, chips, 0)
    flat_filters = filter_spectrum.reshape(4, rows, width)
    near = pack_filters(after(flat_filters, values[0]), chips, (1, 2), 0)
    other_weight = swapped(out_weight, "seq", 1)
    *moved, mine = pack_moved(after(gate_values, near[0]), out_weight, other_weight, chips)
    own, far = pack_filters(after(flat_filters, moved[0]), chips, (0, 3), 0)
    values, filters = to_chips(values), to_chips([own, *near, far])
    own = stack([after(block, far) for block in values], rows)
    spectrum = forward(own, [swapped(part, "seq", 1) for part in own], tables)
    moved = to_chips([after(block, spectrum) for block in moved])
    keep, *send = backward(spectrum, filters, tables)
    gated, longer = gate(skip_gain[None, :], keep, [swapped(part, "seq", 1) for part in send], values, moved, 16)
    gathered = to_chips([gated, longer, longer, gated])

    others = [swapped(part, "seq", 1) for part in collect([after(block, gated) for block in moved[1:]], out_weight.shape[0] // 2)]
    keep, passed, send = project_moved(arrange(mine, moved[1:], others), gathered)
    blocks = to_chips(finish(keep, *over_layers(passed, send), chips))
    keep, near, passed, far = sort_blocks(to_chips(project_still(out_weight, other_weight, gathered)))
    second = swapped(add(after(passed, blocks[3], blocks[2]), swapped(far, "chan", 1), 0), "chan", 2)
    return join(keep, swapped(near, "chan", 1), second, blocks)


def shards(values_in, gate_values, filter_spectrum, skip_gain, out_weight):
    parts, layers = lax.axis_size("seq"), lax.axis_size("chan")
    rows, width = values_in.shape
    share = out_weight.shape[1] // layers
    aligned = width // parts % 128 == 0 and share % 128 == 0 and rows % 32 == 0
    run = shards_direct if aligned and layers == 4 and parts == 8 else shards_general
    return run(values_in, gate_values, filter_spectrum, skip_gain, out_weight)


def solution(mesh):
    in_specs = (
        P("seq", "chan"),
        P("seq", "chan"),
        P(None, "seq", None, "chan"),
        P("chan"),
        P("chan", "seq"),
    )
    out_specs = P("seq", "chan")
    return jax.shard_map(shards, mesh=mesh, in_specs=in_specs, out_specs=out_specs, check_vma=False)
```
